32 devices in a mesh: sky: 16 (over z, x, core), en: 2 (over y).
Axes of the slice: x: 2, y: 2, z: 4, core: 2. Of those that a mesh axis runs over, the one named last changes fastest.
Arguments:
- flux: float32 [64, 128, 2048], P('en', None, 'sky'), may hold values from 0.1 to 10
- exposure: float32 [64, 128, 2048], P('en', None, 'sky'), may hold values from 0.3 to 3
- background: float32 [64, 128, 2048], P('en', None, 'sky'), may hold values from 0.05 to 1
- observed: int32 [64, 128, 2048], P('en', None, 'sky'), may hold values from 0 to 23
- psf_radius: int32 [64], replicated, may hold values from 2 to 32, as said below
- band_low: int32 [64], replicated, may hold values from -2 to 0
- band_high: int32 [64], replicated, may hold values from 0 to 2
- disp_raw: float32 [64, 64], replicated, may hold values from 0.2 to 1
Outputs:
- grad_flux: float32 [64, 128, 2048], P('en', None, 'sky')
- mean_loss: float32 [], replicated
The draws below stay inside these ranges and needn't reach their ends.
Inputs may be any that keep to these rules, and one draw needn't show every extreme that they name: `psf_radius`: the first true bin has radius 32.
All inputs are finite; a program needn't handle non-finite values.
Results may differ from the reference program's by a relative error of at most 0.0003.
Values sent between devices are 32-bit elements; how exact they have to be, the bound alone decides.
No kernel may reach another device: no remote copies, remote signals or barrier semaphores. Data moves between devices by JAX's collectives and lax.ppermute only.
A program may use at most 64 MiB of HBM per device.

```python
import math
import jax
import jax.numpy as jnp
from jax import lax

E = 64
LAT = 128
RMAX = 32
REACH = 2
LON = 2048


def draw_psf_radius(key, part):
    key = jax.random.fold_in(key, 11)
    steps = jnp.arange(E)
    base = RMAX - steps * (RMAX - 2) // max(E - 1, 1)
    jitter = jax.random.randint(key, (E,), -2, 1)
    radius = jnp.clip(base + jitter, 2, RMAX)
    radius = radius.at[0].set(RMAX)
    return radius.astype(jnp.int32)


def ends_draw(key, lowest, highest, extreme, other):
    first, second = jax.random.split(key)
    values = jax.random.randint(first, (E,), lowest, highest + 1)
    where_at = jax.random.randint(second, (), 0, E)
    values = values.at[where_at].set(extreme)
    values = values.at[(where_at + 1) % E].set(other)
    return values.astype(jnp.int32)


def draw_band_low(key, part):
    key = jax.random.fold_in(key, 23)
    return ends_draw(key, -REACH, 0, -REACH, 0)


def draw_band_high(key, part):
    key = jax.random.fold_in(key, 37)
    return ends_draw(key, 0, REACH, REACH, 0)


def with_ends(array, own_key, low, largest):
    longest = array.shape.index(max(array.shape))
    spots = []
    for shift in (0, 1):
        where = [jax.random.randint(jax.random.fold_in(own_key, axis), (), 0, length) for axis, length in enumerate(array.shape)]
        where[longest] = (where[longest] + shift) % array.shape[longest]
        spots.append(tuple(where))
    return array.at[spots[0]].set(low).at[spots[1]].set(largest)


def levels(own_key, dims, cuts, low, high):
    def one(position, parts):
        steps = jax.random.uniform(jax.random.fold_in(jax.random.fold_in(own_key, 6), position), (parts,), jnp.float32, low / len(cuts), high / len(cuts))
        return jnp.repeat(jnp.exp(steps), dims[position] // parts).reshape((-1,) + (1,) * (len(dims) - position - 1))

    gain = one(*cuts[0])
    for cut in cuts[1:]:
        gain = gain * one(*cut)
    return gain


def setup_inputs(seed: int = 0) -> dict:
    keys = jax.random.split(jax.random.key(seed), 9)
    flux = jnp.clip(jnp.exp(math.log(10.0) - 4.6051702 * jax.random.uniform(keys[0], (E, LAT, LON), jnp.float32) ** levels(keys[0], (E, LAT, LON), ((0, 2), (2, 16)), -0.2, 0.2)), 0.1, 10.0)
    exposure = jnp.clip(jnp.exp(math.log(3.0) - 2.3025851 * jax.random.uniform(keys[1], (E, LAT, LON), jnp.float32) ** levels(keys[1], (E, LAT, LON), ((0, 2), (2, 16)), -0.2, 0.2)), 0.3, 3.0)
    background = jnp.clip(jnp.exp(math.log(1.0) - 2.9957323 * jax.random.uniform(keys[2], (E, LAT, LON), jnp.float32) ** levels(keys[2], (E, LAT, LON), ((0, 2), (2, 16)), -0.2, 0.2)), 0.05, 1.0)
    observed = with_ends(jax.random.randint(keys[3], (E, LAT, LON), 0, 24), jax.random.fold_in(keys[3], 1), 0, 23).astype(jnp.int32)
    psf_radius = draw_psf_radius(jax.random.fold_in(keys[8], 71), 0)
    band_low = draw_band_low(jax.random.fold_in(keys[8], 71), 0)
    band_high = draw_band_high(jax.random.fold_in(keys[8], 71), 0)
    disp_raw = jnp.clip(jax.random.uniform(keys[7], (E, E), jnp.float32, 0.2, 1.0), 0.2, 1.0)
    return dict(flux=flux, exposure=exposure, background=background, observed=observed, psf_radius=psf_radius, band_low=band_low, band_high=band_high, disp_raw=disp_raw)


def psf_norm(radius):
    offsets = jnp.arange(-RMAX, RMAX + 1).astype(jnp.float32)
    spread = 0.5 * radius
    values = jnp.exp(-offsets * offsets / (2.0 * spread * spread))
    values = jnp.where(jnp.abs(offsets) <= radius, values, jnp.float32(0.0))
    return jnp.sum(values)


def taper(diff, radius, norm):
    spread = 0.5 * radius
    values = jnp.exp(-diff * diff / (2.0 * spread * spread)) / norm
    return jnp.where(jnp.abs(diff) <= radius, values, jnp.float32(0.0))


def blur_one(args):
    field, radius = args
    radius = radius.astype(jnp.float32)
    norm = psf_norm(radius)
    rows = jnp.arange(LAT)
    diff = (rows[:, None] - rows[None, :]).astype(jnp.float32)
    lat_matrix = taper(diff, radius, norm)
    blurred = jnp.dot(lat_matrix, field, precision=lax.Precision.HIGHEST, preferred_element_type=jnp.float32)
    result = jnp.zeros_like(blurred)
    for shift_by in range(-RMAX, RMAX + 1):
        weight = taper(jnp.float32(shift_by), radius, norm)
        result = result + weight * jnp.roll(blurred, -shift_by, axis=1)
    return result


def dispersion(disp_raw, band_low, band_high):
    rows = jnp.arange(E)
    offset = rows[None, :] - rows[:, None]
    inside = (offset >= band_low[:, None]) & (offset <= band_high[:, None])
    masked = jnp.where(inside, disp_raw, jnp.float32(0.0))
    return masked / jnp.sum(masked, axis=0, keepdims=True)


def reference(flux, exposure, background, observed, psf_radius, band_low, band_high, disp_raw):
    weighted_flux = flux * exposure
    blurred = lax.map(blur_one, (weighted_flux, psf_radius))
    matrix = dispersion(disp_raw, band_low, band_high)
    folded = jnp.einsum("ij,jlc->ilc", matrix, blurred, precision=lax.Precision.HIGHEST)
    mu = folded + background
    counts = observed.astype(jnp.float32)
    total = jnp.sum(mu - counts * jnp.log(mu))
    mean_loss = total / jnp.float32(E * LAT * LON)
    resid = 1.0 - counts / mu
    back = jnp.einsum("ij,ilc->jlc", matrix, resid, precision=lax.Precision.HIGHEST)
    spread_back = lax.map(blur_one, (back, psf_radius))
    return exposure * spread_back, mean_loss
```

```python
import functools

import jax
import jax.numpy as jnp
from jax import lax
from jax.experimental import pallas as pl
from jax.experimental.pallas import tpu as pltpu
from jax.sharding import PartitionSpec as P

RMAX = 32
REACH = 2
F32 = jnp.float32
BF16 = jnp.bfloat16
SMEM = pl.BlockSpec(memory_space=pltpu.SMEM)
ANY = pl.BlockSpec(memory_space=pl.ANY)


def split(x):
    hi = x.astype(BF16)
    return hi, (x - hi.astype(F32)).astype(BF16)


def blocks(count, rows, cols):
    return pl.BlockSpec((count, rows, cols), lambda i: (i, 0, 0))


def params(mib=32):
    return pltpu.CompilerParams(vmem_limit_bytes=mib * 2**20)


def pack_edges(tile):
    lane = lax.broadcasted_iota(jnp.int32, (RMAX, 4 * RMAX), 1)
    last = first = None
    for q in range(4):
        rows = tile[q * RMAX:(q + 1) * RMAX]
        to_last = pltpu.roll(rows, (q + 1) * RMAX % 128, 1) if q != 3 else rows
        to_first = pltpu.roll(rows, q * RMAX, 1) if q else rows
        last = to_last if last is None else jnp.where(lane >= q * RMAX, to_last, last)
        first = to_first if first is None else jnp.where(lane >= q * RMAX, to_first, first)
    return last, first


def unpack_edges(before, after):
    lane = lax.broadcasted_iota(jnp.int32, (RMAX, 4 * RMAX), 1)
    parts = []
    for q in range(4):
        left = pltpu.roll(before, 128 - q * RMAX, 1) if q else before
        right = pltpu.roll(after, (96 - q * RMAX) % 128, 1) if q != 3 else after
        parts.append(jnp.where(lane < 64, left, right))
    return jnp.concatenate(parts, axis=0)


def lon_product(tile, weights):
    hi, lo = split(tile)
    both = jnp.concatenate([weights, weights], axis=0)
    out = jnp.dot(jnp.concatenate([hi, lo], axis=1), both, preferred_element_type=F32)
    return out[:, :128] + out[:, 128:]


def lat_product(weights, tile):
    hi, lo = split(tile)
    row = jnp.concatenate([hi, lo], axis=1)
    both = jnp.concatenate([row, row], axis=0)
    out = jnp.dot(weights, both, preferred_element_type=F32)
    return out[:, :128] + out[:, 128:]


def taper_weights(diff, ok, scale, norm, reach2):
    square = diff * diff
    values = jnp.where((square <= reach2) & ok, jnp.exp(square * scale) * norm, 0.0)
    hi, lo = split(values)
    return jnp.concatenate([hi, lo], axis=1)


def pack_kernel(flux, exposure, last, first):
    def one(b, carry):
        last[b], first[b] = pack_edges(flux[b] * exposure[b])
        return carry

    lax.fori_loop(0, flux.shape[0], one, 0, unroll=2)


def weights_kernel(chunk, extra, block, taps, flux, exposure, centre, band, edge, centre_x, edge_x):
    step = pl.program_id(0)
    row = lax.broadcasted_iota(jnp.int32, (128, 128), 0)
    col = lax.broadcasted_iota(jnp.int32, (128, 128), 1)
    near = (row - col).astype(F32)
    far = jnp.where(row < 64, row - col - RMAX, row - col + RMAX).astype(F32)
    held = (row < RMAX) | (row >= 128 - RMAX)
    always = row >= 0

    def make(position):
        numbers = [taps[3 * position + n] for n in range(3)]
        return taper_weights(near, always, *numbers), taper_weights(far, held, *numbers)

    def one(b, carry):
        band[b], edge[b] = make(step * chunk + b)
        centre[b] = lon_product(flux[b] * exposure[b], band[b])
        return carry

    lax.fori_loop(0, chunk, one, 0, unroll=2)

    def one_extra(b, carry):
        centre_x[b], edge_x[b] = make(block + step * extra + b)
        return carry

    lax.fori_loop(0, extra, one_extra, 0)


def middle_kernel(block, extra, near, parts, fold, where, centre, band, edge, before, after, background, observed,
                  band_x, edge_x, before_x, after_x, energy, back_out, last_out, first_out, loss_out,
                  blurred, resid, *rest):
    count = 11
    held, sems, outs, out_sem = rest[:count], rest[count], rest[count + 1:count + 4], rest[count + 4]
    sources = (centre, band, edge, before, after, background, observed, band_x, edge_x, before_x, after_x)
    v_centre, v_band, v_edge, v_before, v_after, v_background, v_observed, v_band_x, v_edge_x, v_before_x, v_after_x = held
    v_energy, e_sem = rest[count + 5], rest[count + 6]
    chunk = block // parts

    def copy(n, c):
        if n < 7:
            return pltpu.make_async_copy(sources[n].at[pl.ds(c * chunk, chunk)], held[n].at[pl.ds(c * chunk, chunk)], sems.at[n, c])
        return pltpu.make_async_copy(sources[n], held[n], sems.at[n, 0])

    energy_copy = pltpu.make_async_copy(energy, v_energy, e_sem)
    for c in range(parts):
        for n in range(5):
            copy(n, c).start()
    for n in range(7, count):
        copy(n, 0).start()
    energy_copy.start()
    for c in range(parts):
        for n in (5, 6):
            copy(n, c).start()

    own = where[0]
    slots = block + extra
    zero = jnp.zeros((128, 128), F32)
    for s in (0, 1, slots + 2, slots + 3):
        blurred[s] = zero
        resid[s] = zero
    for s in (2, 3, slots, slots + 1):
        resid[s] = zero

    def blur(slot, middle, wide, narrow, left, right):
        whole = middle + lon_product(unpack_edges(left, right), narrow)
        blurred[slot + 2] = lat_product(wide, whole)

    for c in range(parts):
        for n in range(5):
            copy(n, c).wait()

        def one(b, carry):
            blur(b + own, v_centre[b], v_band[b], v_edge[b], v_before[b], v_after[b])
            return carry

        lax.fori_loop(c * chunk, (c + 1) * chunk, one, 0, unroll=2)
    for n in range(7, count):
        copy(n, 0).wait()
    energy_copy.wait()

    def one_extra(k, carry):
        middle = lon_product(v_energy[k], v_band_x[k])
        blur(where[1 + k], middle, v_band_x[k], v_edge_x[k], v_before_x[k], v_after_x[k])
        return carry

    lax.fori_loop(0, extra, one_extra, 0, unroll=2)

    def mean_counts(slot, ground):
        mu = ground
        for o in range(5):
            mu = mu + fold[5 * (slot + 2) + o] * blurred[slot + o]
        return mu

    for c in range(parts):
        for n in (5, 6):
            copy(n, c).wait()

    def one_resid(b, total):
        slot = b + own
        mu = mean_counts(slot, v_background[b])
        counts = v_observed[b].astype(F32)
        resid[slot + 2] = 1.0 - counts / mu
        return total + (mu - counts * jnp.log(mu)).reshape(16, 8, 128).sum(0)

    loss_out[...] = lax.fori_loop(0, block, one_resid, jnp.zeros((8, 128), F32), unroll=2)

    def one_extra_resid(k, carry):
        slot = where[1 + extra + k]
        mu = mean_counts(slot, v_energy[extra + k])
        resid[slot + 2] = 1.0 - v_energy[extra + near + k] / mu
        return carry

    lax.fori_loop(0, near, one_extra_resid, 0)

    def one_back(b, carry):
        slot = b + own
        total = None
        for o in range(5):
            term = fold[5 * (slot + 4 - o) + o] * resid[slot + 4 - o]
            total = term if total is None else total + term
        outs[0][b] = total
        outs[1][b], outs[2][b] = pack_edges(total)
        return carry

    lax.fori_loop(0, block, one_back, 0, unroll=2)
    copies = [pltpu.make_async_copy(src, dst, out_sem.at[n]) for n, (src, dst) in enumerate(zip(outs, (back_out, last_out, first_out)))]
    for one_copy in copies:
        one_copy.start()
    for one_copy in copies:
        one_copy.wait()


def centre_kernel(back, band, out):
    def one(b, carry):
        out[b] = lon_product(back[b], band[b])
        return carry

    lax.fori_loop(0, back.shape[0], one, 0, unroll=2)


def final_kernel(centre, band, edge, before, after, exposure, out):
    def one(b, carry):
        whole = centre[b] + lon_product(unpack_edges(before[b], after[b]), edge[b])
        out[b] = lat_product(band[b], whole) * exposure[b]
        return carry

    lax.fori_loop(0, out.shape[0], one, 0, unroll=2)


def ring(size, shift):
    return [(i, (i + shift) % size) for i in range(size)]


def grid_ring(sky, en, sky_shift, en_shift):
    return [(s * en + e, (s + sky_shift) % sky * en + (e + en_shift) % en) for s in range(sky) for e in range(en)]


def total_over(value, axis):
    size, shift = lax.axis_size(axis), 1
    while shift < size:
        value = value + lax.ppermute(value, axis, [(i, i ^ shift) for i in range(size)])
        shift *= 2
    return value


def dispersion_band(disp_raw, band_low, band_high):
    count = disp_raw.shape[0]
    rows = jnp.arange(count)
    offset = rows[None, :] - rows[:, None]
    inside = (offset >= band_low[:, None]) & (offset <= band_high[:, None])
    masked = jnp.where(inside, disp_raw, F32(0.0))
    matrix = masked / jnp.sum(masked, axis=0, keepdims=True)
    return jnp.stack([jnp.sum(jnp.where(offset == o, matrix, 0.0), axis=1) for o in range(-REACH, REACH + 1)], axis=1)


def local(flux, exposure, background, observed, psf_radius, band_low, band_high, disp_raw):
    block, rows, width = flux.shape
    bins = disp_raw.shape[0]
    sky, en = lax.axis_size("sky"), lax.axis_size("en")
    me = lax.axis_index("en")
    wide, near = 2 * REACH, REACH
    tile = jax.ShapeDtypeStruct((block, rows, width), F32)
    edges = jax.ShapeDtypeStruct((block, RMAX, 128), F32)
    parts = 4
    chunk = block // parts

    if en == 2:
        shifts = [1]
        starts = [jnp.where(me == 0, block - wide, 0)]
        near_starts = [jnp.where(me == 0, block - near, 0)]
        own = jnp.where(me == 0, 0, wide)
        extra_slots = jnp.where(me == 0, block, 0) + jnp.arange(wide)
        near_slots = jnp.where(me == 0, block, near) + jnp.arange(near)
    else:
        shifts = [1, -1]
        starts = [block - wide, 0]
        near_starts = [block - near, 0]
        own = jnp.int32(wide)
        extra_slots = jnp.concatenate([jnp.arange(wide), wide + block + jnp.arange(wide)])
        near_slots = jnp.concatenate([near + jnp.arange(near), wide + block + jnp.arange(near)])
    extra, nears = wide * len(shifts), near * len(shifts)
    slots = block + extra
    first_bin = me * block - own

    last, first = pl.pallas_call(
        pack_kernel,
        grid=(parts,),
        in_specs=[blocks(chunk, rows, width)] * 2,
        out_specs=[blocks(chunk, RMAX, 128)] * 2,
        out_shape=[edges] * 2,
        compiler_params=params(),
        name="pack_edges",
    )(flux, exposure)
    before = lax.ppermute(last, "sky", ring(sky, 1))
    after = lax.ppermute(first, "sky", ring(sky, -1))
    energies, befores, afters = [], [], []
    for shift, start, near_start in zip(shifts, starts, near_starts):
        def cut(array, at, size):
            return lax.dynamic_slice_in_dim(array, at, size, axis=0)

        sent = jnp.concatenate([
            cut(flux, start, wide) * cut(exposure, start, wide),
            cut(background, near_start, near),
            cut(observed, near_start, near).astype(F32),
        ])
        energies.append(lax.ppermute(sent, "en", ring(en, shift)))
        befores.append(lax.ppermute(cut(last, start, wide), ("sky", "en"), grid_ring(sky, en, 1, shift)))
        afters.append(lax.ppermute(cut(first, start, wide), ("sky", "en"), grid_ring(sky, en, -1, shift)))
    energy = jnp.concatenate(
        [e[:wide] for e in energies] + [e[wide:wide + near] for e in energies] + [e[wide + near:] for e in energies]
    ) if len(shifts) > 1 else energies[0]
    before_x, after_x = [jnp.concatenate(a) if len(a) > 1 else a[0] for a in (befores, afters)]

    positions = jnp.concatenate([own + jnp.arange(block), extra_slots])
    radius = psf_radius[(first_bin + positions) % bins].astype(F32)
    squares = (jnp.arange(RMAX + 1) ** 2).astype(F32)
    factor = -2.0 / (radius * radius)
    values = jnp.where(squares[None] <= (radius * radius)[:, None], jnp.exp(squares[None] * factor[:, None]), 0.0)
    norm = 2.0 * jnp.sum(values, axis=1) - 1.0
    taps = jnp.stack([factor, 1.0 / norm, radius * radius], axis=1).reshape(-1)
    bands = dispersion_band(disp_raw, band_low, band_high)
    fold = bands[(first_bin - REACH + jnp.arange(slots + 2 * REACH)) % bins].reshape(-1)
    where = jnp.concatenate([own[None], extra_slots, near_slots]).astype(jnp.int32)

    wide_weights = jax.ShapeDtypeStruct((block, 128, 256), BF16)
    extra_weights = jax.ShapeDtypeStruct((extra, 128, 256), BF16)
    centre, band, edge, band_x, edge_x = pl.pallas_call(
        functools.partial(weights_kernel, chunk, extra // parts, block),
        grid=(parts,),
        in_specs=[SMEM, blocks(chunk, rows, width), blocks(chunk, rows, width)],
        out_specs=[blocks(chunk, rows, width)] + [blocks(chunk, 128, 256)] * 2 + [blocks(extra // parts, 128, 256)] * 2,
        out_shape=[tile, wide_weights, wide_weights, extra_weights, extra_weights],
        compiler_params=params(),
        cost_estimate=pl.CostEstimate(flops=block * 2 * 128 * 256 * 256, bytes_accessed=block * 10 * 2**16, transcendentals=block * 2**15),
        name="weights_and_centre",
    )(taps, flux, exposure)

    def vmem(count, dtype, *shape):
        return pltpu.VMEM((count, *shape), dtype)

    back, last, first, partial = pl.pallas_call(
        functools.partial(middle_kernel, block, extra, nears, parts),
        in_specs=[SMEM, SMEM] + [ANY] * 12,
        out_specs=[ANY] * 3 + [pl.BlockSpec(memory_space=pltpu.VMEM)],
        out_shape=[tile, edges, edges, jax.ShapeDtypeStruct((8, 128), F32)],
        scratch_shapes=[
            vmem(slots + 4, F32, rows, width), vmem(slots + 4, F32, rows, width),
            vmem(block, F32, rows, width), vmem(block, BF16, 128, 256), vmem(block, BF16, 128, 256),
            vmem(block, F32, RMAX, 128), vmem(block, F32, RMAX, 128),
            vmem(block, F32, rows, width), vmem(block, jnp.int32, rows, width),
            vmem(extra, BF16, 128, 256), vmem(extra, BF16, 128, 256), vmem(extra, F32, RMAX, 128), vmem(extra, F32, RMAX, 128),
            pltpu.SemaphoreType.DMA((11, parts)),
            vmem(block, F32, rows, width), vmem(block, F32, RMAX, 128), vmem(block, F32, RMAX, 128),
            pltpu.SemaphoreType.DMA((3,)),
            vmem(extra + 2 * nears, F32, rows, width), pltpu.SemaphoreType.DMA,
        ],
        compiler_params=params(40),
        cost_estimate=pl.CostEstimate(flops=block * 4 * 128 * 256 * 256, bytes_accessed=block * 8 * 2**16, transcendentals=block * 2**15),
        name="blur_fold_residual_fold",
    )(fold, where, centre, band, edge, before, after, background, observed, band_x, edge_x, before_x, after_x, energy)

    before = lax.ppermute(last, "sky", ring(sky, 1))
    after = lax.ppermute(first, "sky", ring(sky, -1))
    total = total_over(total_over(jnp.sum(partial).reshape(1, 1), "sky"), "en")
    mean_loss = total[0, 0] / F32(rows * width * bins * sky)

    centre = pl.pallas_call(
        centre_kernel,
        grid=(parts,),
        in_specs=[blocks(chunk, rows, width), blocks(chunk, 128, 256)],
        out_specs=blocks(chunk, rows, width),
        out_shape=tile,
        compiler_params=params(),
        cost_estimate=pl.CostEstimate(flops=block * 2 * 128 * 256 * 256, bytes_accessed=block * 3 * 2**16, transcendentals=0),
        name="back_centre",
    )(back, band)
    grad = pl.pallas_call(
        final_kernel,
        grid=(parts,),
        in_specs=[blocks(chunk, rows, width)] + [blocks(chunk, 128, 256)] * 2 + [blocks(chunk, RMAX, 128)] * 2 + [blocks(chunk, rows, width)],
        out_specs=blocks(chunk, rows, width),
        out_shape=tile,
        compiler_params=params(),
        cost_estimate=pl.CostEstimate(flops=block * 4 * 128 * 256 * 256, bytes_accessed=block * 6 * 2**16, transcendentals=0),
        name="back_edges_lat_exposure",
    )(centre, band, edge, before, after, exposure)
    return grad, mean_loss


def solution(mesh):
    placed = (P("en", None, "sky"),) * 4 + (P(),) * 4
    return jax.shard_map(local, mesh=mesh, in_specs=placed, out_specs=(P("en", None, "sky"), P()), check_vma=False)
```

```python
import functools

import jax
import jax.numpy as jnp
from jax import lax
from jax.experimental import pallas as pl
from jax.experimental.pallas import tpu as pltpu
from jax.sharding import PartitionSpec as P

RMAX = 32
REACH = 2
F32 = jnp.float32
BF16 = jnp.bfloat16
SMEM = pl.BlockSpec(memory_space=pltpu.SMEM)
ANY = pl.BlockSpec(memory_space=pl.ANY)
VMEM = pl.BlockSpec(memory_space=pltpu.VMEM)


def split(x):
    hi = x.astype(BF16)
    return hi, (x - hi.astype(F32)).astype(BF16)


def params(mib):
    return pltpu.CompilerParams(vmem_limit_bytes=mib * 2**20)


def cost(tiles, products, transcendentals=0):
    return pl.CostEstimate(flops=tiles * products * 2 * 128 * 256 * 256, bytes_accessed=tiles * 2**16, transcendentals=transcendentals)


def pack_edges(tile):
    lane = lax.broadcasted_iota(jnp.int32, (RMAX, 4 * RMAX), 1)
    last = first = None
    for q in range(4):
        rows = tile[q * RMAX:(q + 1) * RMAX]
        to_last = pltpu.roll(rows, (q + 1) * RMAX % 128, 1) if q != 3 else rows
        to_first = pltpu.roll(rows, q * RMAX, 1) if q else rows
        last = to_last if last is None else jnp.where(lane >= q * RMAX, to_last, last)
        first = to_first if first is None else jnp.where(lane >= q * RMAX, to_first, first)
    return last, first


def unpack_edges(before, after):
    lane = lax.broadcasted_iota(jnp.int32, (RMAX, 4 * RMAX), 1)
    parts = []
    for q in range(4):
        left = pltpu.roll(before, 128 - q * RMAX, 1) if q else before
        right = pltpu.roll(after, (96 - q * RMAX) % 128, 1) if q != 3 else after
        parts.append(jnp.where(lane < 64, left, right))
    return jnp.concatenate(parts, axis=0)


def lon_product(tile, weights):
    hi, lo = split(tile)
    both = jnp.concatenate([weights, weights], axis=0)
    out = jnp.dot(jnp.concatenate([hi, lo], axis=1), both, preferred_element_type=F32)
    return out[:, :128] + out[:, 128:]


def lat_product(weights, tile):
    hi, lo = split(tile)
    row = jnp.concatenate([hi, lo], axis=1)
    both = jnp.concatenate([row, row], axis=0)
    out = jnp.dot(weights, both, preferred_element_type=F32)
    return out[:, :128] + out[:, 128:]


def taper_weights(diff, ok, scale, norm, reach2):
    square = diff * diff
    values = jnp.where((square <= reach2) & ok, jnp.exp(square * scale) * norm, 0.0)
    hi, lo = split(values)
    return jnp.concatenate([hi, lo], axis=1)


def pack_kernel(parts, wide, near, starts, flux, exposure, background, observed, weighted, last, first, *rest):
    dirs = starts.shape[0] // 2
    sent, last_x, first_x = rest[:dirs], rest[dirs:2 * dirs], rest[2 * dirs:3 * dirs]
    v_flux, v_exposure, v_observed, sems, near_sems = rest[3 * dirs:]
    chunk = flux.shape[0] // parts

    def copy(n, c):
        source, held = ((flux, v_flux), (exposure, v_exposure))[n]
        return pltpu.make_async_copy(source.at[pl.ds(c * chunk, chunk)], held.at[pl.ds(c * chunk, chunk)], sems.at[n, c])

    def near_copies(d):
        at = pl.ds(starts[2 * d + 1], near)
        return (
            pltpu.make_async_copy(background.at[at], sent[d].at[pl.ds(wide, near)], near_sems.at[d, 0]),
            pltpu.make_async_copy(observed.at[at], v_observed.at[pl.ds(d * near, near)], near_sems.at[d, 1]),
        )

    for c in range(parts):
        copy(0, c).start()
        copy(1, c).start()
    for d in range(dirs):
        for one_copy in near_copies(d):
            one_copy.start()
    for c in range(parts):
        copy(0, c).wait()
        copy(1, c).wait()

        def one(b, carry):
            tile = v_flux[b] * v_exposure[b]
            weighted[b] = tile
            last[b], first[b] = pack_edges(tile)
            return carry

        lax.fori_loop(c * chunk, (c + 1) * chunk, one, 0, unroll=2)
    for d in range(dirs):
        for one_copy in near_copies(d):
            one_copy.wait()
        for k in range(wide):
            b = starts[2 * d] + k
            sent[d][k] = weighted[b]
            last_x[d][k] = last[b]
            first_x[d][k] = first[b]
        for k in range(near):
            sent[d][wide + near + k] = v_observed[d * near + k].astype(F32)


def weights_kernel(where, taps, weighted, centre, band, edge):
    row = lax.broadcasted_iota(jnp.int32, (128, 128), 0)
    col = lax.broadcasted_iota(jnp.int32, (128, 128), 1)
    near = (row - col).astype(F32)
    far = jnp.where(row < 64, row - col - RMAX, row - col + RMAX).astype(F32)
    held = (row < RMAX) | (row >= 128 - RMAX)
    always = row >= 0

    def make(s, carry):
        numbers = [taps[3 * s + n] for n in range(3)]
        band[s] = taper_weights(near, always, *numbers)
        edge[s] = taper_weights(far, held, *numbers)
        return carry

    lax.fori_loop(0, band.shape[0], make, 0, unroll=2)

    def one(b, carry):
        centre[b] = lon_product(weighted[b], band[b + where[0]])
        return carry

    lax.fori_loop(0, weighted.shape[0], one, 0, unroll=4)


def middle_kernel(extra, nears, fold, where, centre, band, edge, before, after, background, observed, before_x, after_x, energy,
                  back, last, first, loss, whole, blurred, resid):
    block = centre.shape[0]
    slots = block + extra
    own = where[0]
    zero = jnp.zeros((128, 128), F32)
    for s in (0, 1, slots + 2, slots + 3):
        blurred[s] = zero
        resid[s] = zero
    loss[...] = jnp.zeros((8, 128), F32)

    edges = [unpack_edges(before_x[k], after_x[k]) for k in range(extra)]
    at = [where[1 + k] for k in range(extra)]
    sums = [lon_product(energy[k], band[at[k]]) + lon_product(edges[k], edge[at[k]]) for k in range(extra)]
    for k in range(extra):
        blurred[at[k] + 2] = lat_product(band[at[k]], sums[k])

    def lon(b):
        whole[b] = centre[b] + lon_product(unpack_edges(before[b], after[b]), edge[b + own])

    def lat(b):
        blurred[b + own + 2] = lat_product(band[b + own], whole[b])

    def mean_counts(slot, ground):
        mu = ground
        for o in range(5):
            mu = mu + fold[5 * (slot + 2) + o] * blurred[slot + o]
        return mu

    def residual(b):
        slot = b + own
        mu = mean_counts(slot, background[b])
        counts = observed[b].astype(F32)
        resid[slot + 2] = 1.0 - counts / mu
        loss[...] += (mu - counts * jnp.log(mu)).reshape(16, 8, 128).sum(0)

    def extra_residuals():
        for k in range(nears):
            slot = where[1 + extra + k]
            mu = mean_counts(slot, energy[extra + k])
            resid[slot + 2] = 1.0 - energy[extra + nears + k] / mu

    def fold_back(b):
        slot = b + own
        total = None
        for o in range(5):
            term = fold[5 * (slot + 4 - o) + o] * resid[slot + 4 - o]
            total = term if total is None else total + term
        back[b] = total
        last[b], first[b] = pack_edges(total)

    def loop(start, stop, stages, unroll=1):
        def body(b, carry):
            for stage, lag in stages:
                stage(b - lag)
            return carry

        if stop > start:
            lax.fori_loop(start, stop, body, 0, unroll=unroll)

    lon(0)
    loop(1, 4, [(lon, 0), (lat, 1)])
    loop(4, 8, [(lon, 0), (lat, 1), (residual, 4)])
    extra_residuals()
    loop(8, block, [(lon, 0), (lat, 1), (residual, 4), (fold_back, 8)], 2)
    lat(block - 1)
    loop(block - 4, block, [(residual, 0)])
    extra_residuals()
    loop(block - 8, block, [(fold_back, 0)], 2)


def centre_kernel(where, back, band, out):
    def one(b, carry):
        out[b] = lon_product(back[b], band[b + where[0]])
        return carry

    lax.fori_loop(0, back.shape[0], one, 0, unroll=4)


def final_kernel(parts, where, centre, band, edge, before, after, exposure, out, whole, held, sems):
    block = centre.shape[0]
    chunk = block // parts
    own = where[0]

    def lon(b):
        whole[b] = centre[b] + lon_product(unpack_edges(before[b], after[b]), edge[b + own])

    def lat(b):
        held[b] = lat_product(band[b + own], whole[b]) * exposure[b]

    def copy(c):
        return pltpu.make_async_copy(held.at[pl.ds(c * chunk, chunk)], out.at[pl.ds(c * chunk, chunk)], sems.at[c])

    def body(b, carry):
        lon(b + 2)
        lat(b)
        return carry

    lon(0)
    lon(1)
    for c in range(parts):
        lax.fori_loop(c * chunk, (c + 1) * chunk - 2 * (c == parts - 1), body, 0, unroll=2)
        if c == parts - 1:
            lat(block - 2)
            lat(block - 1)
        copy(c).start()
    for c in range(parts):
        copy(c).wait()


def ring(size, shift):
    return [(i, (i + shift) % size) for i in range(size)]


def grid_ring(sky, en, sky_shift, en_shift):
    return [(s * en + e, (s + sky_shift) % sky * en + (e + en_shift) % en) for s in range(sky) for e in range(en)]


def dispersion_band(disp_raw, band_low, band_high):
    count = disp_raw.shape[0]
    rows = jnp.arange(count)
    offset = rows[None, :] - rows[:, None]
    inside = (offset >= band_low[:, None]) & (offset <= band_high[:, None])
    masked = jnp.where(inside, disp_raw, F32(0.0))
    matrix = masked / jnp.sum(masked, axis=0, keepdims=True)
    return jnp.stack([jnp.sum(jnp.where(offset == o, matrix, 0.0), axis=1) for o in range(-REACH, REACH + 1)], axis=1)


def local(flux, exposure, background, observed, psf_radius, band_low, band_high, disp_raw):
    block, rows, width = flux.shape
    bins = disp_raw.shape[0]
    sky, en = lax.axis_size("sky"), lax.axis_size("en")
    me = lax.axis_index("en")
    wide, near = 2 * REACH, REACH
    parts = 4

    def tiles(count):
        return pltpu.VMEM((count, rows, width), F32)

    def edges(count):
        return pltpu.VMEM((count, RMAX, 128), F32)

    if en == 2:
        shifts = [1]
        starts = [jnp.where(me == 0, block - wide, 0), jnp.where(me == 0, block - near, 0)]
        own = jnp.where(me == 0, 0, wide)
        extra_slots = jnp.where(me == 0, block, 0) + jnp.arange(wide)
        near_slots = jnp.where(me == 0, block, near) + jnp.arange(near)
    else:
        shifts = [1, -1]
        starts = [block - wide, block - near, 0, 0]
        own = jnp.int32(wide)
        extra_slots = jnp.concatenate([jnp.arange(wide), wide + block + jnp.arange(wide)])
        near_slots = jnp.concatenate([near + jnp.arange(near), wide + block + jnp.arange(near)])
    dirs = len(shifts)
    extra, nears = wide * dirs, near * dirs
    slots = block + extra

    packed = pl.pallas_call(
        functools.partial(pack_kernel, parts, wide, near),
        in_specs=[SMEM] + [ANY] * 4,
        out_specs=[VMEM] * (3 + 3 * dirs),
        out_shape=[tiles(block), edges(block), edges(block)] + [tiles(wide + 2 * near)] * dirs + [edges(wide)] * (2 * dirs),
        scratch_shapes=[
            tiles(block), tiles(block), pltpu.VMEM((nears, rows, width), jnp.int32),
            pltpu.SemaphoreType.DMA((2, parts)), pltpu.SemaphoreType.DMA((dirs, 2)),
        ],
        compiler_params=params(8),
        name="weight_and_pack",
    )(jnp.stack(starts).astype(jnp.int32) if en == 2 else jnp.array(starts, jnp.int32), flux, exposure, background, observed)
    weighted, last, first = packed[:3]
    before = lax.ppermute(last, "sky", ring(sky, 1))
    after = lax.ppermute(first, "sky", ring(sky, -1))
    energies, befores, afters = [], [], []
    for d, shift in enumerate(shifts):
        energies.append(lax.ppermute(packed[3 + d], "en", ring(en, shift)))
        befores.append(lax.ppermute(packed[3 + dirs + d], ("sky", "en"), grid_ring(sky, en, 1, shift)))
        afters.append(lax.ppermute(packed[3 + 2 * dirs + d], ("sky", "en"), grid_ring(sky, en, -1, shift)))
    if dirs > 1:
        energy = jnp.concatenate(
            [e[:wide] for e in energies] + [e[wide:wide + near] for e in energies] + [e[wide + near:] for e in energies]
        )
        before_x, after_x = jnp.concatenate(befores), jnp.concatenate(afters)
    else:
        energy, before_x, after_x = energies[0], befores[0], afters[0]

    first_bin = me * block - own
    radius = psf_radius[(first_bin + jnp.arange(slots)) % bins].astype(F32)
    squares = (jnp.arange(RMAX + 1) ** 2).astype(F32)
    factor = -2.0 / (radius * radius)
    values = jnp.where(squares[None] <= (radius * radius)[:, None], jnp.exp(squares[None] * factor[:, None]), 0.0)
    norm = 2.0 * jnp.sum(values, axis=1) - 1.0
    taps = jnp.stack([factor, 1.0 / norm, radius * radius], axis=1).reshape(-1)
    bands = dispersion_band(disp_raw, band_low, band_high)
    fold = bands[(first_bin - REACH + jnp.arange(slots + 2 * REACH)) % bins].reshape(-1)
    where = jnp.concatenate([own[None], extra_slots, near_slots]).astype(jnp.int32)

    weights = pltpu.VMEM((slots, 128, 256), BF16)
    centre, band, edge = pl.pallas_call(
        weights_kernel,
        in_specs=[SMEM, SMEM, VMEM],
        out_specs=[VMEM] * 3,
        out_shape=[tiles(block), weights, weights],
        compiler_params=params(2),
        cost_estimate=cost(block, 1, block * 2**15),
        name="weights_and_centre",
    )(where, taps, weighted)
    back, last, first, partial = pl.pallas_call(
        functools.partial(middle_kernel, extra, nears),
        in_specs=[SMEM, SMEM] + [VMEM] * 10,
        out_specs=[VMEM] * 4,
        out_shape=[tiles(block), edges(block), edges(block), pltpu.VMEM((8, 128), F32)],
        scratch_shapes=[tiles(block), tiles(slots + 4), tiles(slots + 4)],
        compiler_params=params(12),
        cost_estimate=cost(block, 2, block * 2**15),
        name="blur_fold_residual_fold",
    )(fold, where, centre, band, edge, before, after, background, observed, before_x, after_x, energy)

    before = lax.ppermute(last, "sky", ring(sky, 1))
    after = lax.ppermute(first, "sky", ring(sky, -1))
    total = jnp.sum(lax.all_gather(partial, ("sky", "en")))
    mean_loss = total / F32(rows * width * bins * sky)

    centre = pl.pallas_call(
        centre_kernel,
        in_specs=[SMEM, VMEM, VMEM],
        out_specs=VMEM,
        out_shape=tiles(block),
        compiler_params=params(2),
        cost_estimate=cost(block, 1),
        name="back_centre",
    )(where, back, band)
    grad = pl.pallas_call(
        functools.partial(final_kernel, parts),
        in_specs=[SMEM] + [VMEM] * 6,
        out_specs=ANY,
        out_shape=jax.ShapeDtypeStruct((block, rows, width), F32),
        scratch_shapes=[tiles(block), tiles(block), pltpu.SemaphoreType.DMA((parts,))],
        compiler_params=params(8),
        cost_estimate=cost(block, 2),
        name="back_edges_lat_exposure",
    )(where, centre, band, edge, before, after, exposure)
    return grad, mean_loss


def solution(mesh):
    placed = (P("en", None, "sky"),) * 4 + (P(),) * 4
    return jax.shard_map(local, mesh=mesh, in_specs=placed, out_specs=(P("en", None, "sky"), P()), check_vma=False)
```

```python
import functools

import jax
import jax.numpy as jnp
from jax import lax
from jax.experimental import pallas as pl
from jax.experimental.pallas import tpu as pltpu
from jax.sharding import PartitionSpec as P

RMAX = 32
REACH = 2
F32 = jnp.float32
BF16 = jnp.bfloat16
SMEM = pl.BlockSpec(memory_space=pltpu.SMEM)
ANY = pl.BlockSpec(memory_space=pl.ANY)
VMEM = pl.BlockSpec(memory_space=pltpu.VMEM)


def split(x):
    hi = x.astype(BF16)
    return hi, (x - hi.astype(F32)).astype(BF16)


def params(mib=56):
    return pltpu.CompilerParams(vmem_limit_bytes=mib * 2**20)


def blocks(count, rows, cols):
    return pl.BlockSpec((count, rows, cols), lambda i: (i, 0, 0))


def chunk_copy(source, target, sem, c, size):
    at = pl.ds(c * size, size)
    return pltpu.make_async_copy(source.at[at], target.at[at], sem)


def run_stages(groups, size, stages, events=(), arrive=None):
    marks = {0} | {lag for _, lag in stages} | {lag + groups for _, lag in stages} | {at for at, _ in events}
    marks = sorted(marks)
    for start, stop in zip(marks, marks[1:] + [marks[-1]]):
        for at, event in events:
            if at == start:
                event()
        active = [(n, stage, lag) for n, (stage, lag) in enumerate(stages) if lag <= start < lag + groups]
        if stop == start or not active:
            continue

        def step(p, carry):
            if arrive is not None:
                for n, _, lag in active:
                    arrive(n, p - lag)
            stores = []
            for _, stage, lag in active:
                for i in range(size):
                    stores += stage((p - lag) * size + i)
            for ref, index, value in stores:
                if index is None:
                    ref[...] += value
                else:
                    ref[index] = value
            return carry

        lax.fori_loop(start, stop, step, 0)


def cost(tiles, products, transcendentals=0):
    return pl.CostEstimate(flops=tiles * products * 2 * 128 * 256 * 256, bytes_accessed=tiles * 2**16, transcendentals=transcendentals)


def pack_edges(tile):
    lane = lax.broadcasted_iota(jnp.int32, (RMAX, 4 * RMAX), 1)
    last = first = None
    for q in range(4):
        rows = tile[q * RMAX:(q + 1) * RMAX]
        to_last = pltpu.roll(rows, (q + 1) * RMAX % 128, 1) if q != 3 else rows
        to_first = pltpu.roll(rows, q * RMAX, 1) if q else rows
        last = to_last if last is None else jnp.where(lane >= q * RMAX, to_last, last)
        first = to_first if first is None else jnp.where(lane >= q * RMAX, to_first, first)
    return last, first


def unpack_edges(before, after):
    lane = lax.broadcasted_iota(jnp.int32, (RMAX, 4 * RMAX), 1)
    parts = []
    for q in range(4):
        left = pltpu.roll(before, 128 - q * RMAX, 1) if q else before
        right = pltpu.roll(after, (96 - q * RMAX) % 128, 1) if q != 3 else after
        parts.append(jnp.where(lane < 64, left, right))
    return jnp.concatenate(parts, axis=0)


def lon_product(tile, weights):
    hi, lo = split(tile)
    both = jnp.concatenate([weights, weights], axis=0)
    out = jnp.dot(jnp.concatenate([hi, lo], axis=1), both, preferred_element_type=F32)
    return out[:, :128] + out[:, 128:]


def lat_product(weights, tile):
    hi, lo = split(tile)
    row = jnp.concatenate([hi, lo], axis=1)
    both = jnp.concatenate([row, row], axis=0)
    out = jnp.dot(weights, both, preferred_element_type=F32)
    return out[:, :128] + out[:, 128:]


def taper_weights(diff, ok, scale, norm, reach2):
    square = diff * diff
    values = jnp.where((square <= reach2) & ok, jnp.exp(square * scale) * norm, 0.0)
    hi, lo = split(values)
    return jnp.concatenate([hi, lo], axis=1)


def pack_kernel(parts, wide, near, starts, flux, exposure, background, observed, last, first, *rest):
    dirs = starts.shape[0] // 2
    outs, rest = rest[:3 * dirs], rest[3 * dirs:]
    v_flux, v_exposure, v_observed, v_last, v_first, v_sent, sems, near_sems, out_sems, near_out_sems = rest
    block = flux.shape[0]
    chunk = block // parts

    def arrivals(c):
        return [chunk_copy(a, b, sems.at[n, c], c, chunk) for n, (a, b) in enumerate(((flux, v_flux), (exposure, v_exposure)))]

    def departures(c):
        return [chunk_copy(a, b, out_sems.at[n, c], c, chunk) for n, (a, b) in enumerate(((v_last, last), (v_first, first)))]

    def near_arrivals(d):
        at = pl.ds(starts[2 * d + 1], near)
        return [
            pltpu.make_async_copy(background.at[at], v_sent.at[d, pl.ds(wide, near)], near_sems.at[d, 0]),
            pltpu.make_async_copy(observed.at[at], v_observed.at[d], near_sems.at[d, 1]),
        ]

    def near_departures(d):
        at = pl.ds(starts[2 * d], wide)
        return [
            pltpu.make_async_copy(v_sent.at[d], outs[d], near_out_sems.at[d, 0]),
            pltpu.make_async_copy(v_last.at[at], outs[dirs + d], near_out_sems.at[d, 1]),
            pltpu.make_async_copy(v_first.at[at], outs[2 * dirs + d], near_out_sems.at[d, 2]),
        ]

    for c in range(parts):
        for copy in arrivals(c):
            copy.start()
    for d in range(dirs):
        for copy in near_arrivals(d):
            copy.start()
    for c in range(parts):
        for copy in arrivals(c):
            copy.wait()

        def four(g, carry):
            packed = [pack_edges(v_flux[4 * g + i] * v_exposure[4 * g + i]) for i in range(4)]
            for i in range(4):
                v_last[4 * g + i], v_first[4 * g + i] = packed[i]
            return carry

        if chunk % 4 == 0:
            lax.fori_loop(c * chunk // 4, (c + 1) * chunk // 4, four, 0)
        else:
            for b in range(c * chunk, (c + 1) * chunk):
                v_last[b], v_first[b] = pack_edges(v_flux[b] * v_exposure[b])
        for copy in departures(c):
            copy.start()
    for d in range(dirs):
        for copy in near_arrivals(d):
            copy.wait()
        for k in range(wide):
            b = starts[2 * d] + k
            v_sent[d, k] = v_flux[b] * v_exposure[b]
        for k in range(near):
            v_sent[d, wide + near + k] = v_observed[d, k].astype(F32)
        for copy in near_departures(d):
            copy.start()
    for c in range(parts):
        for copy in departures(c):
            copy.wait()
    for d in range(dirs):
        for copy in near_departures(d):
            copy.wait()


def weights_kernel(chunk, extra, block, taps, flux, exposure, centre, band, edge, band_x, edge_x):
    step = pl.program_id(0)
    row = lax.broadcasted_iota(jnp.int32, (128, 128), 0)
    col = lax.broadcasted_iota(jnp.int32, (128, 128), 1)
    near = (row - col).astype(F32)
    far = jnp.where(row < 64, row - col - RMAX, row - col + RMAX).astype(F32)
    held = (row < RMAX) | (row >= 128 - RMAX)
    always = row >= 0

    def make(position):
        numbers = [taps[3 * position + n] for n in range(3)]
        return taper_weights(near, always, *numbers), taper_weights(far, held, *numbers)

    def two(g, carry):
        made = [make(step * chunk + 2 * g + i) for i in range(2)]
        sums = [lon_product(flux[2 * g + i] * exposure[2 * g + i], made[i][0]) for i in range(2)]
        for i in range(2):
            centre[2 * g + i] = sums[i]
            band[2 * g + i], edge[2 * g + i] = made[i]
        return carry

    lax.fori_loop(0, chunk // 2, two, 0)
    for k in range(extra):
        band_x[k], edge_x[k] = make(block + step * extra + k)


def middle_kernel(parts, fold, where, centre, band, edge, before, after, background, observed,
                  band_x, edge_x, before_x, after_x, energy, back, last, first, loss,
                  whole, blurred, resid, *rest):
    block, extra = centre.shape[0], band_x.shape[0]
    nears = (energy.shape[0] - extra) // 2
    chunk, slots, own = block // parts, block + extra, where[0]
    held, rest = rest[:7], rest[7:]
    held_x, rest = rest[:5], rest[5:]
    v_back, v_last, v_first, sems, sems_x, out_sems = rest
    sources = (centre, band, edge, before, after, background, observed)
    sources_x = (band_x, edge_x, before_x, after_x, energy)
    v_centre, v_band, v_edge, v_before, v_after, v_background, v_observed = held
    x_band, x_edge, x_before, x_after, x_energy = held_x

    def copy(n, c):
        return chunk_copy(sources[n], held[n], sems.at[n, c], c, chunk)

    def copy_x(n):
        return pltpu.make_async_copy(sources_x[n], held_x[n], sems_x.at[n])

    def copy_out(n, c):
        return chunk_copy((v_back, v_last, v_first)[n], (back, last, first)[n], out_sems.at[n, c], c, chunk)

    for n in range(5):
        copy_x(n).start()
    for c in range(parts):
        for n in range(7):
            copy(n, c).start()
    zero = jnp.zeros((128, 128), F32)
    for s in (0, 1, slots + 2, slots + 3):
        blurred[s] = zero
        resid[s] = zero
    loss[...] = jnp.zeros((8, 128), F32)

    for n in range(5):
        copy_x(n).wait()
    edges = [unpack_edges(x_before[k], x_after[k]) for k in range(extra)]
    sums = [lon_product(x_energy[k], x_band[k]) + lon_product(edges[k], x_edge[k]) for k in range(extra)]
    sums = [lat_product(x_band[k], sums[k]) for k in range(extra)]
    for k in range(extra):
        blurred[where[1 + k] + 2] = sums[k]

    def lon(b):
        return [(whole, b, v_centre[b] + lon_product(unpack_edges(v_before[b], v_after[b]), v_edge[b]))]

    def lat(b):
        return [(blurred, b + own + 2, lat_product(v_band[b], whole[b]))]

    def mean_counts(slot, ground):
        mu = ground
        for o in range(5):
            mu = mu + fold[5 * (slot + 2) + o] * blurred[slot + o]
        return mu

    def residual(b):
        slot = b + own
        mu = mean_counts(slot, v_background[b])
        counts = v_observed[b].astype(F32)
        terms = (mu - counts * jnp.log(mu)).reshape(16, 8, 128).sum(0)
        return [(resid, slot + 2, 1.0 - counts / mu), (loss, None, terms)]

    def extra_residuals():
        values = []
        for k in range(nears):
            mu = mean_counts(where[1 + extra + k], x_energy[extra + k])
            values.append(1.0 - x_energy[extra + nears + k] / mu)
        for k in range(nears):
            resid[where[1 + extra + k] + 2] = values[k]

    def fold_back(b):
        slot = b + own
        total = None
        for o in range(5):
            term = fold[5 * (slot + 4 - o) + o] * resid[slot + 4 - o]
            total = term if total is None else total + term
        ends = pack_edges(total)
        return [(v_back, b, total), (v_last, b, ends[0]), (v_first, b, ends[1])]

    size = 2
    groups, per_chunk = block // size, chunk // size

    def arrive(n, p):
        needs = {0: (0, 1, 2, 3, 4), 2: (5, 6)}.get(n, ())
        if not needs:
            return

        @pl.when(lax.rem(p, per_chunk) == 0)
        def _():
            for m in needs:
                copy(m, lax.div(p, per_chunk)).wait()

    run_stages(
        groups, size, [(lon, 0), (lat, 1), (residual, 3), (fold_back, 5)],
        events=[(3, extra_residuals), (groups + 1, extra_residuals)], arrive=arrive,
    )
    for c in range(parts):
        for n in range(3):
            copy_out(n, c).start()
    for c in range(parts):
        for n in range(3):
            copy_out(n, c).wait()


def centre_kernel(back, band, out):
    def four(g, carry):
        sums = [lon_product(back[4 * g + i], band[4 * g + i]) for i in range(4)]
        for i in range(4):
            out[4 * g + i] = sums[i]
        return carry

    if back.shape[0] % 4 == 0:
        lax.fori_loop(0, back.shape[0] // 4, four, 0)
    else:
        for b in range(back.shape[0]):
            out[b] = lon_product(back[b], band[b])


def final_kernel(parts, centre, band, edge, before, after, exposure, out, whole, v_out, *rest):
    block = centre.shape[0]
    chunk = block // parts
    held, sems, out_sems = rest[:6], rest[6], rest[7]
    sources = (centre, band, edge, before, after, exposure)
    v_centre, v_band, v_edge, v_before, v_after, v_exposure = held

    def copy(n, c):
        return chunk_copy(sources[n], held[n], sems.at[n, c], c, chunk)

    def copy_out(c):
        return chunk_copy(v_out, out, out_sems.at[c], c, chunk)

    for c in range(parts):
        for n in range(6):
            copy(n, c).start()

    def lon(b):
        return [(whole, b, v_centre[b] + lon_product(unpack_edges(v_before[b], v_after[b]), v_edge[b]))]

    def lat(b):
        return [(v_out, b, lat_product(v_band[b], whole[b]) * v_exposure[b])]

    size = 2
    groups, per_chunk = block // size, chunk // size

    def arrive(n, p):
        @pl.when(lax.rem(p, per_chunk) == 0)
        def _():
            for m in (0, 1, 2, 3, 4) if n == 0 else (5,):
                copy(m, lax.div(p, per_chunk)).wait()

        if n == 1:
            @pl.when((lax.rem(p, per_chunk) == 0) & (p > 0))
            def _():
                copy_out(lax.div(p, per_chunk) - 1).start()

    run_stages(groups, size, [(lon, 0), (lat, 1)], arrive=arrive)
    copy_out(parts - 1).start()
    for c in range(parts):
        copy_out(c).wait()


def ring(size, shift):
    return [(i, (i + shift) % size) for i in range(size)]


def grid_ring(sky, en, sky_shift, en_shift):
    return [(s * en + e, (s + sky_shift) % sky * en + (e + en_shift) % en) for s in range(sky) for e in range(en)]


def total_over(value, axis):
    size, shift = lax.axis_size(axis), 1
    while shift < size:
        base = min(4, size // shift)
        moved = [
            lax.ppermute(value, axis, [(i, i + ((i // shift + k) % base - i // shift % base) * shift) for i in range(size)])
            for k in range(1, base)
        ]
        for other in moved:
            value = value + other
        shift *= base
    return value


def dispersion_band(disp_raw, band_low, band_high):
    count = disp_raw.shape[0]
    rows = jnp.arange(count)
    offset = rows[None, :] - rows[:, None]
    inside = (offset >= band_low[:, None]) & (offset <= band_high[:, None])
    masked = jnp.where(inside, disp_raw, F32(0.0))
    matrix = masked / jnp.sum(masked, axis=0, keepdims=True)
    return jnp.stack([jnp.sum(jnp.where(offset == o, matrix, 0.0), axis=1) for o in range(-REACH, REACH + 1)], axis=1)


def local(flux, exposure, background, observed, psf_radius, band_low, band_high, disp_raw):
    block, rows, width = flux.shape
    bins = disp_raw.shape[0]
    sky, en = lax.axis_size("sky"), lax.axis_size("en")
    me = lax.axis_index("en")
    wide, near = 2 * REACH, REACH
    parts = 4

    tile = jax.ShapeDtypeStruct((block, rows, width), F32)
    ends = jax.ShapeDtypeStruct((block, RMAX, 128), F32)
    chunk = block // parts

    def tiles(count, dtype=F32):
        return pltpu.VMEM((count, rows, width), dtype)

    def edges(count):
        return pltpu.VMEM((count, RMAX, 128), F32)

    def weights(count):
        return pltpu.VMEM((count, 128, 256), BF16)

    if en == 2:
        shifts = [1]
        starts = [jnp.where(me == 0, block - wide, 0), jnp.where(me == 0, block - near, 0)]
        own = jnp.where(me == 0, 0, wide)
        extra_slots = jnp.where(me == 0, block, 0) + jnp.arange(wide)
        near_slots = jnp.where(me == 0, block, near) + jnp.arange(near)
    else:
        shifts = [1, -1]
        starts = [block - wide, block - near, 0, 0]
        own = jnp.int32(wide)
        extra_slots = jnp.concatenate([jnp.arange(wide), wide + block + jnp.arange(wide)])
        near_slots = jnp.concatenate([near + jnp.arange(near), wide + block + jnp.arange(near)])
    dirs = len(shifts)
    extra, nears = wide * dirs, near * dirs
    slots = block + extra

    packed = pl.pallas_call(
        functools.partial(pack_kernel, parts, wide, near),
        in_specs=[SMEM] + [ANY] * 4,
        out_specs=[ANY] * (2 + 3 * dirs),
        out_shape=[ends, ends] + [jax.ShapeDtypeStruct((wide + 2 * near, rows, width), F32)] * dirs
        + [jax.ShapeDtypeStruct((wide, RMAX, 128), F32)] * (2 * dirs),
        scratch_shapes=[
            tiles(block), tiles(block), pltpu.VMEM((dirs, near, rows, width), jnp.int32), edges(block), edges(block),
            pltpu.VMEM((dirs, wide + 2 * near, rows, width), F32),
            pltpu.SemaphoreType.DMA((2, parts)), pltpu.SemaphoreType.DMA((dirs, 2)),
            pltpu.SemaphoreType.DMA((2, parts)), pltpu.SemaphoreType.DMA((dirs, 3)),
        ],
        compiler_params=params(),
        name="weight_and_pack",
    )(jnp.stack(starts).astype(jnp.int32) if en == 2 else jnp.array(starts, jnp.int32), flux, exposure, background, observed)
    last, first = packed[:2]
    before = lax.ppermute(last, "sky", ring(sky, 1))
    after = lax.ppermute(first, "sky", ring(sky, -1))
    energies, befores, afters = [], [], []
    for d, shift in enumerate(shifts):
        energies.append(lax.ppermute(packed[2 + d], "en", ring(en, shift)))
        befores.append(lax.ppermute(packed[2 + dirs + d], ("sky", "en"), grid_ring(sky, en, 1, shift)))
        afters.append(lax.ppermute(packed[2 + 2 * dirs + d], ("sky", "en"), grid_ring(sky, en, -1, shift)))
    if dirs > 1:
        energy = jnp.concatenate(
            [e[:wide] for e in energies] + [e[wide:wide + near] for e in energies] + [e[wide + near:] for e in energies]
        )
        before_x, after_x = jnp.concatenate(befores), jnp.concatenate(afters)
    else:
        energy, before_x, after_x = energies[0], befores[0], afters[0]

    first_bin = me * block - own
    positions = jnp.concatenate([own + jnp.arange(block), extra_slots])
    radius = psf_radius[(first_bin + positions) % bins].astype(F32)
    squares = (jnp.arange(RMAX + 1) ** 2).astype(F32)
    factor = -2.0 / (radius * radius)
    values = jnp.where(squares[None] <= (radius * radius)[:, None], jnp.exp(squares[None] * factor[:, None]), 0.0)
    norm = 2.0 * jnp.sum(values, axis=1) - 1.0
    taps = jnp.stack([factor, 1.0 / norm, radius * radius], axis=1).reshape(-1)
    bands = dispersion_band(disp_raw, band_low, band_high)
    fold = bands[(first_bin - REACH + jnp.arange(slots + 2 * REACH)) % bins].reshape(-1)
    where = jnp.concatenate([own[None], extra_slots, near_slots]).astype(jnp.int32)

    own_weights = jax.ShapeDtypeStruct((block, 128, 256), BF16)
    extra_weights = jax.ShapeDtypeStruct((extra, 128, 256), BF16)
    centre, band, edge, band_x, edge_x = pl.pallas_call(
        functools.partial(weights_kernel, chunk, extra // parts, block),
        grid=(parts,),
        in_specs=[SMEM, blocks(chunk, rows, width), blocks(chunk, rows, width)],
        out_specs=[blocks(chunk, rows, width)] + [blocks(chunk, 128, 256)] * 2 + [blocks(extra // parts, 128, 256)] * 2,
        out_shape=[tile, own_weights, own_weights, extra_weights, extra_weights],
        compiler_params=params(),
        cost_estimate=cost(block, 1, block * 2**15),
        name="weights_and_centre",
    )(taps, flux, exposure)
    back, last, first, partial = pl.pallas_call(
        functools.partial(middle_kernel, parts),
        in_specs=[SMEM, SMEM] + [ANY] * 12,
        out_specs=[ANY] * 3 + [VMEM],
        out_shape=[tile, ends, ends, jax.ShapeDtypeStruct((8, 128), F32)],
        scratch_shapes=[
            tiles(block), tiles(slots + 4), tiles(slots + 4),
            tiles(block), weights(block), weights(block), edges(block), edges(block), tiles(block), tiles(block, jnp.int32),
            weights(extra), weights(extra), edges(extra), edges(extra), tiles(extra + 2 * nears),
            tiles(block), edges(block), edges(block),
            pltpu.SemaphoreType.DMA((7, parts)), pltpu.SemaphoreType.DMA((5,)), pltpu.SemaphoreType.DMA((3, parts)),
        ],
        compiler_params=params(48),
        cost_estimate=cost(block, 2, block * 2**15),
        name="blur_fold_residual_fold",
    )(fold, where, centre, band, edge, before, after, background, observed, band_x, edge_x, before_x, after_x, energy)

    before = lax.ppermute(last, "sky", ring(sky, 1))
    after = lax.ppermute(first, "sky", ring(sky, -1))
    total = total_over(total_over(jnp.sum(partial).reshape(1, 1), "sky"), "en")
    mean_loss = total[0, 0] / F32(rows * width * bins * sky)

    centre = pl.pallas_call(
        centre_kernel,
        grid=(parts,),
        in_specs=[blocks(chunk, rows, width), blocks(chunk, 128, 256)],
        out_specs=blocks(chunk, rows, width),
        out_shape=tile,
        compiler_params=params(),
        cost_estimate=cost(block, 1),
        name="back_centre",
    )(back, band)
    grad = pl.pallas_call(
        functools.partial(final_kernel, parts),
        in_specs=[ANY] * 6,
        out_specs=ANY,
        out_shape=tile,
        scratch_shapes=[
            tiles(block), tiles(block),
            tiles(block), weights(block), weights(block), edges(block), edges(block), tiles(block),
            pltpu.SemaphoreType.DMA((6, parts)), pltpu.SemaphoreType.DMA((parts,)),
        ],
        compiler_params=params(48),
        cost_estimate=cost(block, 2),
        name="back_edges_lat_exposure",
    )(centre, band, edge, before, after, exposure)
    return grad, mean_loss


def solution(mesh):
    placed = (P("en", None, "sky"),) * 4 + (P(),) * 4
    return jax.shard_map(local, mesh=mesh, in_specs=placed, out_specs=(P("en", None, "sky"), P()), check_vma=False)
```

```python
import functools

import jax
import jax.numpy as jnp
from jax import lax
from jax.experimental import pallas as pl
from jax.experimental.pallas import tpu as pltpu
from jax.sharding import PartitionSpec as P

RMAX = 32
REACH = 2
F32 = jnp.float32
BF16 = jnp.bfloat16
SMEM = pl.BlockSpec(memory_space=pltpu.SMEM)
ANY = pl.BlockSpec(memory_space=pl.ANY)
VMEM = pl.BlockSpec(memory_space=pltpu.VMEM)
HBM = pl.BlockSpec(memory_space=pltpu.HBM)


def split(x):
    hi = x.astype(BF16)
    return hi, (x - hi.astype(F32)).astype(BF16)


def params(mib=56):
    return pltpu.CompilerParams(vmem_limit_bytes=mib * 2**20)


def blocks(count, rows, cols):
    return pl.BlockSpec((count, rows, cols), lambda i: (i, 0, 0))


def chunk_copy(source, target, sem, c, size):
    at = pl.ds(c * size, size)
    return pltpu.make_async_copy(source.at[at], target.at[at], sem)


def run_stages(groups, size, stages, events=(), arrive=None):
    marks = {0} | {lag for _, lag in stages} | {lag + groups for _, lag in stages} | {at for at, _ in events}
    marks = sorted(marks)
    for start, stop in zip(marks, marks[1:] + [marks[-1]]):
        for at, event in events:
            if at == start:
                event()
        active = [(n, stage, lag) for n, (stage, lag) in enumerate(stages) if lag <= start < lag + groups]
        if stop == start or not active:
            continue

        def step(p, carry):
            if arrive is not None:
                for n, _, lag in active:
                    arrive(n, p - lag)
            stores = []
            for _, stage, lag in active:
                for i in range(size):
                    stores += stage((p - lag) * size + i)
            for ref, index, value in stores:
                if index is None:
                    ref[...] += value
                else:
                    ref[index] = value
            return carry

        lax.fori_loop(start, stop, step, 0)


def cost(tiles, products, transcendentals=0):
    return pl.CostEstimate(flops=tiles * products * 2 * 128 * 256 * 256, bytes_accessed=tiles * 2**16, transcendentals=transcendentals)


class Place:
    def __init__(self, block, en):
        self.block, self.en = block, en
        self.me = lax.axis_index("en")
        self.wide, self.near = 2 * REACH, REACH
        self.dirs = 1 if en == 2 else 2
        self.extra, self.nears = self.wide * self.dirs, self.near * self.dirs
        self.slots, self.bins = block + self.extra, block * en
        self.own = jnp.where(self.me == 0, 0, self.wide) if en == 2 else self.wide
        self.first_bin = self.me * block - self.own

    def start(self, d, width):
        if self.en == 2:
            return jnp.where(self.me == 0, self.block - width, 0)
        return self.block - width if d == 0 else 0

    def slot(self, k, width):
        if self.en == 2:
            return jnp.where(self.me == 0, self.block, self.wide - width) + k
        return self.wide - width + k if k < width else self.wide + self.block + k - width

    def clamp(self, g):
        return jnp.clip(g, 0, self.bins - 1)


def pack_edges(tile):
    lane = lax.broadcasted_iota(jnp.int32, (RMAX, 4 * RMAX), 1)
    last = first = None
    for q in range(4):
        rows = tile[q * RMAX:(q + 1) * RMAX]
        to_last = pltpu.roll(rows, (q + 1) * RMAX % 128, 1) if q != 3 else rows
        to_first = pltpu.roll(rows, q * RMAX, 1) if q else rows
        last = to_last if last is None else jnp.where(lane >= q * RMAX, to_last, last)
        first = to_first if first is None else jnp.where(lane >= q * RMAX, to_first, first)
    return last, first


def unpack_edges(before, after):
    lane = lax.broadcasted_iota(jnp.int32, (RMAX, 4 * RMAX), 1)
    parts = []
    for q in range(4):
        left = pltpu.roll(before, 128 - q * RMAX, 1) if q else before
        right = pltpu.roll(after, (96 - q * RMAX) % 128, 1) if q != 3 else after
        parts.append(jnp.where(lane < 64, left, right))
    return jnp.concatenate(parts, axis=0)


def lon_product(tile, weights):
    hi, lo = split(tile)
    both = jnp.concatenate([weights, weights], axis=0)
    out = jnp.dot(jnp.concatenate([hi, lo], axis=1), both, preferred_element_type=F32)
    return out[:, :128] + out[:, 128:]


def lat_product(weights, tile):
    hi, lo = split(tile)
    row = jnp.concatenate([hi, lo], axis=1)
    both = jnp.concatenate([row, row], axis=0)
    out = jnp.dot(weights, both, preferred_element_type=F32)
    return out[:, :128] + out[:, 128:]


def profile(radius):
    wide = jnp.full((1, 128), radius, jnp.int32).astype(F32)
    reach = wide * wide
    factor = -2.0 / reach
    lane = lax.broadcasted_iota(jnp.int32, (1, 128), 1)
    square = (lane * lane).astype(F32)
    values = jnp.where(square <= reach, jnp.exp(square * factor), 0.0)
    total = jnp.sum(values, axis=1, keepdims=True)
    return factor[:, :1], 1.0 / (2.0 * total - 1.0), reach[:, :1]


def taper_weights(diff, ok, factor, scale, reach):
    square = diff * diff
    values = jnp.where((square <= reach) & ok, jnp.exp(square * factor) * scale, 0.0)
    hi, lo = split(values)
    return jnp.concatenate([hi, lo], axis=1)


def pack_kernel(parts, en, flux, exposure, background, observed, weighted, last, first, *rest):
    place = Place(flux.shape[0], en)
    dirs, wide, near, block = place.dirs, place.wide, place.near, place.block
    sent, last_x, first_x = rest[:dirs], rest[dirs:2 * dirs], rest[2 * dirs:3 * dirs]
    v_flux, v_exposure, v_observed, sems, near_sems = rest[3 * dirs:]
    chunk = block // parts

    def arrivals(c):
        return [chunk_copy(a, b, sems.at[n, c], c, chunk) for n, (a, b) in enumerate(((flux, v_flux), (exposure, v_exposure)))]

    def near_arrivals(d):
        at = pl.ds(place.start(d, near), near)
        return [
            pltpu.make_async_copy(background.at[at], sent[d].at[pl.ds(wide, near)], near_sems.at[d, 0]),
            pltpu.make_async_copy(observed.at[at], v_observed.at[d], near_sems.at[d, 1]),
        ]

    for c in range(parts):
        for copy in arrivals(c):
            copy.start()
    for d in range(dirs):
        for copy in near_arrivals(d):
            copy.start()
    size = 4 if chunk % 4 == 0 else 2
    for c in range(parts):
        for copy in arrivals(c):
            copy.wait()

        def some(g, carry):
            tiles = [v_flux[size * g + i] * v_exposure[size * g + i] for i in range(size)]
            packed = [pack_edges(tile) for tile in tiles]
            for i in range(size):
                weighted[size * g + i] = tiles[i]
                last[size * g + i], first[size * g + i] = packed[i]
            return carry

        lax.fori_loop(c * chunk // size, (c + 1) * chunk // size, some, 0)
    for d in range(dirs):
        for copy in near_arrivals(d):
            copy.wait()
        start = place.start(d, wide)
        for k in range(wide):
            sent[d][k] = weighted[start + k]
            last_x[d][k] = last[start + k]
            first_x[d][k] = first[start + k]
        for k in range(near):
            sent[d][wide + near + k] = v_observed[d, k].astype(F32)


def weights_kernel(en, radius, low, high, disp, weighted, centre, band, edge, band_x, edge_x, fold, raw, column):
    block = weighted.shape[0]
    place = Place(block, en)
    row = lax.broadcasted_iota(jnp.int32, (128, 128), 0)
    col = lax.broadcasted_iota(jnp.int32, (128, 128), 1)
    near = (row - col).astype(F32)
    far = jnp.where(row < 64, row - col - RMAX, row - col + RMAX).astype(F32)
    held = (row < RMAX) | (row >= 128 - RMAX)
    always = row >= 0

    def make(g):
        numbers = profile(radius[place.clamp(g)])
        return taper_weights(near, always, *numbers), taper_weights(far, held, *numbers)

    def two(g, carry):
        made = [make(place.me * block + 2 * g + i) for i in range(2)]
        sums = [lon_product(weighted[2 * g + i], made[i][0]) for i in range(2)]
        for i in range(2):
            centre[2 * g + i] = sums[i]
            band[2 * g + i], edge[2 * g + i] = made[i]
        return carry

    lax.fori_loop(0, block // 2, two, 0)
    for k in range(place.extra):
        band_x[k], edge_x[k] = make(place.first_bin + place.slot(k, place.wide))

    def dispersion_row(s, carry):
        g = place.first_bin - 4 + s
        at = place.clamp(g)
        for o in range(-REACH, REACH + 1):
            j = g + o
            inside = (g == at) & (j >= 0) & (j < place.bins) & (low[at] <= o) & (o <= high[at])
            raw[5 * s + o + REACH] = jnp.where(inside, disp[at, place.clamp(j)], 0.0)
        return carry

    lax.fori_loop(0, place.slots + 8, dispersion_row, 0)

    def column_sum(s, carry):
        total = raw[5 * s + REACH]
        for o in (-2, -1, 1, 2):
            total = total + raw[5 * (s - o) + o + REACH]
        column[s] = jnp.where(total > 0.0, total, 1.0)
        return carry

    lax.fori_loop(2, place.slots + 6, column_sum, 0)

    def normalise(s, carry):
        for o in range(-REACH, REACH + 1):
            at = jnp.clip(s + 2 + o, 2, place.slots + 5)
            fold[5 * s + o + REACH] = raw[5 * (s + 2) + o + REACH] / column[at]
        return carry

    lax.fori_loop(0, place.slots + 4, normalise, 0)


def middle_kernel(en, fold, centre, band, edge, before, after, background, observed, band_x, edge_x, before_x, after_x, energy,
                  back, last, first, loss, whole, blurred, resid, sums):
    block = centre.shape[0]
    place = Place(block, en)
    extra, nears, slots, own = place.extra, place.nears, place.slots, place.own
    zero = jnp.zeros((128, 128), F32)
    for s in (0, 1, slots + 2, slots + 3):
        blurred[s] = zero
        resid[s] = zero
    sums[...] = jnp.zeros((8, 128), F32)

    edges = [unpack_edges(before_x[k], after_x[k]) for k in range(extra)]
    done = [lon_product(energy[k], band_x[k]) + lon_product(edges[k], edge_x[k]) for k in range(extra)]
    done = [lat_product(band_x[k], done[k]) for k in range(extra)]
    for k in range(extra):
        blurred[place.slot(k, place.wide) + 2] = done[k]

    def lon(b):
        return [(whole, b, centre[b] + lon_product(unpack_edges(before[b], after[b]), edge[b]))]

    def lat(b):
        return [(blurred, b + own + 2, lat_product(band[b], whole[b]))]

    def mean_counts(slot, ground):
        mu = ground
        for o in range(5):
            mu = mu + fold[5 * (slot + 2) + o] * blurred[slot + o]
        return mu

    def residual(b):
        slot = b + own
        mu = mean_counts(slot, background[b])
        counts = observed[b].astype(F32)
        terms = (mu - counts * jnp.log(mu)).reshape(16, 8, 128).sum(0)
        return [(resid, slot + 2, 1.0 - counts / mu), (sums, None, terms)]

    def extra_residuals():
        values = []
        for k in range(nears):
            mu = mean_counts(place.slot(k, place.near), energy[extra + k])
            values.append(1.0 - energy[extra + nears + k] / mu)
        for k in range(nears):
            resid[place.slot(k, place.near) + 2] = values[k]

    def fold_back(b):
        slot = b + own
        total = None
        for o in range(5):
            term = fold[5 * (slot + 4 - o) + o] * resid[slot + 4 - o]
            total = term if total is None else total + term
        ends = pack_edges(total)
        return [(back, b, total), (last, b, ends[0]), (first, b, ends[1])]

    size = 2
    groups = block // size
    run_stages(
        groups, size, [(lon, 0), (lat, 1), (residual, 3), (fold_back, 5)],
        events=[(3, extra_residuals), (groups + 1, extra_residuals)],
    )
    loss[...] = jnp.full((1, 128), jnp.sum(sums[...]), F32)


def centre_kernel(back, band, out):
    size = 4 if back.shape[0] % 4 == 0 else 2

    def some(g, carry):
        sums = [lon_product(back[size * g + i], band[size * g + i]) for i in range(size)]
        for i in range(size):
            out[size * g + i] = sums[i]
        return carry

    lax.fori_loop(0, back.shape[0] // size, some, 0)


def final_kernel(parts, centre, band, edge, before, after, exposure, total, moved, out, passed, whole, v_out, out_sems):
    block = centre.shape[0]
    chunk = block // parts
    passed[...] = total[...] + moved[...]

    def copy_out(c):
        return chunk_copy(v_out, out, out_sems.at[c], c, chunk)

    def lon(b):
        return [(whole, b, centre[b] + lon_product(unpack_edges(before[b], after[b]), edge[b]))]

    def lat(b):
        return [(v_out, b, lat_product(band[b], whole[b]) * exposure[b])]

    size = 2
    groups, per_chunk = block // size, chunk // size

    def arrive(n, p):
        if n == 1:
            @pl.when((lax.rem(p, per_chunk) == 0) & (p > 0))
            def _():
                copy_out(lax.div(p, per_chunk) - 1).start()

    run_stages(groups, size, [(lon, 0), (lat, 1)], arrive=arrive)
    copy_out(parts - 1).start()
    for c in range(parts):
        copy_out(c).wait()


def ring(size, shift):
    return [(i, (i + shift) % size) for i in range(size)]


def grid_ring(sky, en, sky_shift, en_shift):
    return [(s * en + e, (s + sky_shift) % sky * en + (e + en_shift) % en) for s in range(sky) for e in range(en)]


def exchange(value, axis, shift):
    return lax.ppermute(value, axis, [(i, i ^ shift) for i in range(lax.axis_size(axis))])


def local(flux, exposure, background, observed, psf_radius, band_low, band_high, disp_raw):
    block, rows, width = flux.shape
    bins = disp_raw.shape[0]
    sky, en = lax.axis_size("sky"), lax.axis_size("en")
    wide, near = 2 * REACH, REACH
    shifts = [1] if en == 2 else [1, -1]
    dirs = len(shifts)
    extra, nears = wide * dirs, near * dirs
    slots = block + extra
    parts = 4

    def tiles(count, dtype=F32):
        return jax.ShapeDtypeStruct((count, rows, width), dtype)

    def edges(count):
        return jax.ShapeDtypeStruct((count, RMAX, 128), F32)

    def weights(count):
        return jax.ShapeDtypeStruct((count, 128, 256), BF16)

    def scratch(shape):
        return pltpu.VMEM(shape.shape, shape.dtype)

    lanes = jax.ShapeDtypeStruct((1, 128), F32)

    packed = pl.pallas_call(
        functools.partial(pack_kernel, parts, en),
        in_specs=[HBM] * 4,
        out_specs=[VMEM] * (3 + 3 * dirs),
        out_shape=[tiles(block), edges(block), edges(block)] + [tiles(wide + 2 * near)] * dirs + [edges(wide)] * (2 * dirs),
        scratch_shapes=[
            scratch(tiles(block)), scratch(tiles(block)), pltpu.VMEM((dirs, near, rows, width), jnp.int32),
            pltpu.SemaphoreType.DMA((2, parts)), pltpu.SemaphoreType.DMA((dirs, 2)),
        ],
        compiler_params=params(12),
        name="weight_and_pack",
    )(*[pltpu.with_memory_space_constraint(array, pltpu.HBM) for array in (flux, exposure, background, observed)])
    weighted, last, first = packed[:3]
    before = lax.ppermute(last, "sky", ring(sky, 1))
    after = lax.ppermute(first, "sky", ring(sky, -1))
    energies, befores, afters = [], [], []
    for d, shift in enumerate(shifts):
        energies.append(lax.ppermute(packed[3 + d], "en", ring(en, shift)))
        befores.append(lax.ppermute(packed[3 + dirs + d], ("sky", "en"), grid_ring(sky, en, 1, shift)))
        afters.append(lax.ppermute(packed[3 + 2 * dirs + d], ("sky", "en"), grid_ring(sky, en, -1, shift)))
    if dirs > 1:
        energy = jnp.concatenate(
            [e[:wide] for e in energies] + [e[wide:wide + near] for e in energies] + [e[wide + near:] for e in energies]
        )
        before_x, after_x = jnp.concatenate(befores), jnp.concatenate(afters)
    else:
        energy, before_x, after_x = energies[0], befores[0], afters[0]

    centre, band, edge, band_x, edge_x, fold = pl.pallas_call(
        functools.partial(weights_kernel, en),
        in_specs=[SMEM] * 4 + [VMEM],
        out_specs=[VMEM] * 5 + [SMEM],
        out_shape=[tiles(block), weights(block), weights(block), weights(extra), weights(extra), jax.ShapeDtypeStruct((5 * (slots + 4),), F32)],
        scratch_shapes=[pltpu.SMEM((5 * (slots + 8),), F32), pltpu.SMEM((slots + 8,), F32)],
        compiler_params=params(4),
        cost_estimate=cost(block, 1, block * 2**15),
        name="weights_and_centre",
    )(psf_radius, band_low, band_high, disp_raw, weighted)
    back, last, first, total = pl.pallas_call(
        functools.partial(middle_kernel, en),
        in_specs=[SMEM] + [VMEM] * 12,
        out_specs=[VMEM] * 4,
        out_shape=[tiles(block), edges(block), edges(block), lanes],
        scratch_shapes=[scratch(tiles(block)), scratch(tiles(slots + 4)), scratch(tiles(slots + 4)), pltpu.VMEM((8, 128), F32)],
        compiler_params=params(14),
        cost_estimate=cost(block, 2, block * 2**15),
        name="blur_fold_residual_fold",
    )(fold, centre, band, edge, before, after, background, observed, band_x, edge_x, before_x, after_x, energy)

    before = lax.ppermute(last, "sky", ring(sky, 1))
    after = lax.ppermute(first, "sky", ring(sky, -1))
    rounds = [(axis, 1 << n) for axis, size in (("sky", sky), ("en", en)) for n in range(size.bit_length() - 1)]
    for axis, shift in rounds[:-2]:
        total = total + exchange(total, axis, shift)
    moved = exchange(total, *rounds[-2])
    centre = pl.pallas_call(
        centre_kernel,
        in_specs=[VMEM, VMEM],
        out_specs=VMEM,
        out_shape=tiles(block),
        compiler_params=params(4),
        cost_estimate=cost(block, 1),
        name="back_centre",
    )(back, band)
    grad, passed = pl.pallas_call(
        functools.partial(final_kernel, parts),
        in_specs=[VMEM] * 8,
        out_specs=[ANY, VMEM],
        out_shape=[tiles(block), lanes],
        scratch_shapes=[scratch(tiles(block)), scratch(tiles(block)), pltpu.SemaphoreType.DMA((parts,))],
        compiler_params=params(8),
        cost_estimate=cost(block, 2),
        name="back_edges_lat_exposure",
    )(centre, band, edge, before, after, exposure, total, moved)
    total = passed + exchange(total + moved, *rounds[-1])
    return grad, total[0, 0] / F32(rows * width * bins * sky)


def solution(mesh):
    placed = (P("en", None, "sky"),) * 4 + (P(),) * 4
    return jax.shard_map(local, mesh=mesh, in_specs=placed, out_specs=(P("en", None, "sky"), P()), check_vma=False)
```

```python
import functools

import jax
import jax.numpy as jnp
from jax import lax
from jax.experimental import pallas as pl
from jax.experimental.pallas import tpu as pltpu
from jax.sharding import PartitionSpec as P

RMAX = 32
REACH = 2
F32 = jnp.float32
BF16 = jnp.bfloat16
SMEM = pl.BlockSpec(memory_space=pltpu.SMEM)
ANY = pl.BlockSpec(memory_space=pl.ANY)
VMEM = pl.BlockSpec(memory_space=pltpu.VMEM)
HBM = pl.BlockSpec(memory_space=pltpu.HBM)


def split(x):
    hi = x.astype(BF16)
    return hi, (x - hi.astype(F32)).astype(BF16)


def params(mib=56):
    return pltpu.CompilerParams(vmem_limit_bytes=mib * 2**20)


def blocks(count, rows, cols):
    return pl.BlockSpec((count, rows, cols), lambda i: (i, 0, 0))


def chunk_copy(source, target, sem, c, size):
    at = pl.ds(c * size, size)
    return pltpu.make_async_copy(source.at[at], target.at[at], sem)


def run_stages(groups, size, stages, events=(), arrive=None):
    marks = {0} | {lag for _, lag in stages} | {lag + groups for _, lag in stages} | {at for at, _ in events}
    marks = sorted(marks)
    for start, stop in zip(marks, marks[1:] + [marks[-1]]):
        for at, event in events:
            if at == start:
                event()
        active = [(n, stage, lag) for n, (stage, lag) in enumerate(stages) if lag <= start < lag + groups]
        if stop == start or not active:
            continue

        def step(p, carry):
            if arrive is not None:
                for n, _, lag in active:
                    arrive(n, p - lag)
            stores = []
            for _, stage, lag in active:
                for i in range(size):
                    stores += stage((p - lag) * size + i)
            for ref, index, value in stores:
                if index is None:
                    ref[...] += value
                else:
                    ref[index] = value
            return carry

        lax.fori_loop(start, stop, step, 0)


def cost(tiles, products, transcendentals=0):
    return pl.CostEstimate(flops=tiles * products * 2 * 128 * 256 * 256, bytes_accessed=tiles * 2**16, transcendentals=transcendentals)


class Place:
    def __init__(self, block, en):
        self.block, self.en = block, en
        self.me = lax.axis_index("en")
        self.wide, self.near = 2 * REACH, REACH
        self.dirs = 1 if en == 2 else 2
        self.extra, self.nears = self.wide * self.dirs, self.near * self.dirs
        self.slots, self.bins = block + self.extra, block * en
        self.own = jnp.where(self.me == 0, 0, self.wide) if en == 2 else self.wide
        self.first_bin = self.me * block - self.own

    def start(self, d, width):
        if self.en == 2:
            return jnp.where(self.me == 0, self.block - width, 0)
        return self.block - width if d == 0 else 0

    def slot(self, k, width):
        if self.en == 2:
            return jnp.where(self.me == 0, self.block, self.wide - width) + k
        return self.wide - width + k if k < width else self.wide + self.block + k - width

    def clamp(self, g):
        return jnp.clip(g, 0, self.bins - 1)


def pack_edges(tile):
    lane = lax.broadcasted_iota(jnp.int32, (RMAX, 4 * RMAX), 1)
    last = first = None
    for q in range(4):
        rows = tile[q * RMAX:(q + 1) * RMAX]
        to_last = pltpu.roll(rows, (q + 1) * RMAX % 128, 1) if q != 3 else rows
        to_first = pltpu.roll(rows, q * RMAX, 1) if q else rows
        last = to_last if last is None else jnp.where(lane >= q * RMAX, to_last, last)
        first = to_first if first is None else jnp.where(lane >= q * RMAX, to_first, first)
    return last, first


def unpack_edges(before, after):
    lane = lax.broadcasted_iota(jnp.int32, (RMAX, 4 * RMAX), 1)
    parts = []
    for q in range(4):
        left = pltpu.roll(before, 128 - q * RMAX, 1) if q else before
        right = pltpu.roll(after, (96 - q * RMAX) % 128, 1) if q != 3 else after
        parts.append(jnp.where(lane < 64, left, right))
    return jnp.concatenate(parts, axis=0)


def twice(x, axis):
    return jnp.concatenate([x, x], axis=axis)


def lon_product(tile, weights):
    out = jnp.dot(jnp.concatenate(split(tile), axis=1), twice(weights, 0), preferred_element_type=F32)
    return out[:, :128] + out[:, 128:]


def lat_product(weights, tile):
    out = jnp.dot(weights, twice(jnp.concatenate(split(tile), axis=1), 0), preferred_element_type=F32)
    return out[:, :128] + out[:, 128:]


def lon_edges(tile, weights):
    out = jnp.dot(jnp.concatenate(split(tile), axis=1), twice(weights, 0), preferred_element_type=F32)
    return out + pltpu.roll(out, 64, 1)


def lat_edges(weights, tile):
    lane = lax.broadcasted_iota(jnp.int32, (128, 128), 1)
    hi = tile.astype(BF16).astype(F32)
    parts = jnp.where(lane < 64, hi, tile - hi).astype(BF16)
    out = jnp.dot(weights, twice(parts, 0), preferred_element_type=F32)
    out = out + pltpu.roll(out, 64, 1)
    return jnp.where((lane < RMAX) | (lane >= 128 - RMAX), out, 0.0)


def profile(radius, column):
    wide = jnp.full((1, 128), radius, jnp.int32).astype(F32)
    reach = wide * wide
    factor = -2.0 / reach
    lane = lax.broadcasted_iota(jnp.int32, (1, 128), 1)
    square = (lane * lane).astype(F32)
    values = jnp.where(square <= reach, jnp.exp(square * factor), 0.0)
    norm = 2.0 * jnp.sum(values, axis=1, keepdims=True) - 1.0
    root = jnp.sqrt(jnp.full((1, 128), column, F32))[:, :1]
    return factor[:, :1], 1.0 / (norm * root), reach[:, :1]


def taper_values(diff, ok, factor, scale, reach):
    square = diff * diff
    return jnp.where((square <= reach) & ok, jnp.exp(square * factor) * scale, 0.0)


def pack_kernel(parts, en, flux, exposure, background, observed, weighted, last, first, *rest):
    place = Place(flux.shape[0], en)
    dirs, wide, near, block = place.dirs, place.wide, place.near, place.block
    sent, last_x, first_x = rest[:dirs], rest[dirs:2 * dirs], rest[2 * dirs:3 * dirs]
    v_flux, v_exposure, v_observed, sems, near_sems = rest[3 * dirs:]
    chunk = block // parts

    def arrivals(c):
        return [chunk_copy(a, b, sems.at[n, c], c, chunk) for n, (a, b) in enumerate(((flux, v_flux), (exposure, v_exposure)))]

    def near_arrivals(d):
        at = pl.ds(place.start(d, near), near)
        return [
            pltpu.make_async_copy(background.at[at], sent[d].at[pl.ds(wide, near)], near_sems.at[d, 0]),
            pltpu.make_async_copy(observed.at[at], v_observed.at[d], near_sems.at[d, 1]),
        ]

    for c in range(parts):
        for copy in arrivals(c):
            copy.start()
    for d in range(dirs):
        for copy in near_arrivals(d):
            copy.start()
    size = 4 if chunk % 4 == 0 else 2
    for c in range(parts):
        for copy in arrivals(c):
            copy.wait()

        def some(g, carry):
            tiles = [v_flux[size * g + i] * v_exposure[size * g + i] for i in range(size)]
            packed = [pack_edges(tile) for tile in tiles]
            for i in range(size):
                weighted[size * g + i] = tiles[i]
                last[size * g + i], first[size * g + i] = packed[i]
            return carry

        lax.fori_loop(c * chunk // size, (c + 1) * chunk // size, some, 0)
    for d in range(dirs):
        for copy in near_arrivals(d):
            copy.wait()
        start = place.start(d, wide)
        for k in range(wide):
            sent[d][k] = weighted[start + k]
            last_x[d][k] = last[start + k]
            first_x[d][k] = first[start + k]
        for k in range(near):
            sent[d][wide + near + k] = v_observed[d, k].astype(F32)


def weights_kernel(en, radius, low, high, disp, weighted, centre, band, edge, band_x, edge_x, fold):
    block = weighted.shape[0]
    place = Place(block, en)
    row = lax.broadcasted_iota(jnp.int32, (128, 128), 0)
    col = lax.broadcasted_iota(jnp.int32, (128, 128), 1)
    near = (row - col).astype(F32)
    target = jnp.where(col % 64 < RMAX, col % 64, col % 64 + 64)
    far = jnp.where(row < 64, row - target - RMAX, row - target + RMAX).astype(F32)
    held = (row < RMAX) | (row >= 128 - RMAX)
    always = row >= 0

    def weight(i, j):
        at, to = place.clamp(i), place.clamp(j)
        inside = (i == at) & (j == to) & (low[at] <= j - i) & (j - i <= high[at])
        return jnp.where(inside, disp[at, to], 0.0)

    def make(g):
        for o in range(-REACH, REACH + 1):
            fold[5 * (g - place.first_bin + REACH) + o + REACH] = weight(g, g + o)
        column = weight(g, g)
        for o in (-2, -1, 1, 2):
            column = column + weight(g - o, g)
        numbers = profile(radius[place.clamp(g)], jnp.where(column > 0.0, column, 1.0))
        wide = jnp.concatenate(split(taper_values(near, always, *numbers)), axis=1)
        ends = taper_values(far, held, *numbers)
        hi = ends.astype(BF16).astype(F32)
        return wide, jnp.where(col < 64, hi, ends - hi).astype(BF16)

    for s in (0, 1, place.slots + 2, place.slots + 3):
        for o in range(5):
            fold[5 * s + o] = 0.0

    def some(b):
        made = make(place.me * block + b)
        return [(band, b, made[0]), (edge, b, made[1])]

    def lon(b):
        return [(centre, b, lon_product(weighted[b], band[b]))]

    def lat(b):
        return [(centre, b, lat_product(band[b], centre[b]))]

    run_stages(block // 2, 2, [(some, 0), (lon, 1), (lat, 2)])
    for k in range(place.extra):
        band_x[k], edge_x[k] = make(place.first_bin + place.slot(k, place.wide))


def middle_kernel(en, fold, centre, band, edge, before, after, background, observed, band_x, edge_x, before_x, after_x, energy,
                  back, last, first, loss, whole, blurred, resid, sums):
    block = centre.shape[0]
    place = Place(block, en)
    extra, nears, slots, own = place.extra, place.nears, place.slots, place.own
    zero = jnp.zeros((128, 128), F32)
    for s in (0, 1, slots + 2, slots + 3):
        blurred[s] = zero
        resid[s] = zero
    sums[...] = jnp.zeros((8, 128), F32)

    done = [lon_product(energy[k], band_x[k]) for k in range(extra)]
    ends = [lon_edges(unpack_edges(before_x[k], after_x[k]), edge_x[k]) for k in range(extra)]
    done = [lat_product(band_x[k], done[k]) + lat_edges(band_x[k], ends[k]) for k in range(extra)]
    for k in range(extra):
        blurred[place.slot(k, place.wide) + 2] = done[k]

    def lon(b):
        return [(whole, b, lon_edges(unpack_edges(before[b], after[b]), edge[b]))]

    def lat(b):
        return [(blurred, b + own + 2, centre[b] + lat_edges(band[b], whole[b]))]

    def mean_counts(slot, ground):
        mu = ground
        for o in range(5):
            mu = mu + fold[5 * (slot + 2) + o] * blurred[slot + o]
        return mu

    def residual(b):
        slot = b + own
        mu = mean_counts(slot, background[b])
        counts = observed[b].astype(F32)
        terms = (mu - counts * jnp.log(mu)).reshape(16, 8, 128).sum(0)
        return [(resid, slot + 2, 1.0 - counts / mu), (sums, None, terms)]

    def extra_residuals():
        values = []
        for k in range(nears):
            mu = mean_counts(place.slot(k, place.near), energy[extra + k])
            values.append(1.0 - energy[extra + nears + k] / mu)
        for k in range(nears):
            resid[place.slot(k, place.near) + 2] = values[k]

    def fold_back(b):
        slot = b + own
        total = None
        for o in range(5):
            term = fold[5 * (slot + 4 - o) + o] * resid[slot + 4 - o]
            total = term if total is None else total + term
        ends = pack_edges(total)
        return [(back, b, total), (last, b, ends[0]), (first, b, ends[1])]

    size = 2
    groups = block // size
    run_stages(
        groups, size, [(lon, 0), (lat, 1), (residual, 3), (fold_back, 5)],
        events=[(3, extra_residuals), (groups + 1, extra_residuals)],
    )
    loss[...] = jnp.full((1, 128), jnp.sum(sums[...]), F32)


def centre_kernel(back, band, out):
    def lon(b):
        return [(out, b, lon_product(back[b], band[b]))]

    def lat(b):
        return [(out, b, lat_product(band[b], out[b]))]

    run_stages(back.shape[0] // 2, 2, [(lon, 0), (lat, 1)])


def tree_sum(values):
    while len(values) > 1:
        values = [a + b for a, b in zip(values[::2], values[1::2])]
    return values[0]


def final_kernel(parts, pixels, centre, band, edge, before, after, exposure, *rest):
    terms, (out, loss, whole, v_out, out_sems) = rest[:-5], rest[-5:]
    block = centre.shape[0]
    chunk = block // parts
    loss[...] = tree_sum([term[...] for term in terms])[:, :1] / pixels

    def copy_out(c):
        return chunk_copy(v_out, out, out_sems.at[c], c, chunk)

    def lon(b):
        return [(whole, b, lon_edges(unpack_edges(before[b], after[b]), edge[b]))]

    def lat(b):
        return [(v_out, b, (centre[b] + lat_edges(band[b], whole[b])) * exposure[b])]

    size = 2
    groups, per_chunk = block // size, chunk // size

    def arrive(n, p):
        if n == 1:
            @pl.when((lax.rem(p, per_chunk) == 0) & (p > 0))
            def _():
                copy_out(lax.div(p, per_chunk) - 1).start()

    run_stages(groups, size, [(lon, 0), (lat, 1)], arrive=arrive)
    copy_out(parts - 1).start()
    for c in range(parts):
        copy_out(c).wait()


def ring(size, shift):
    return [(i, (i + shift) % size) for i in range(size)]


def grid_ring(sky, en, sky_shift, en_shift):
    return [(s * en + e, (s + sky_shift) % sky * en + (e + en_shift) % en) for s in range(sky) for e in range(en)]


def local(flux, exposure, background, observed, psf_radius, band_low, band_high, disp_raw):
    block, rows, width = flux.shape
    bins = disp_raw.shape[0]
    sky, en = lax.axis_size("sky"), lax.axis_size("en")
    wide, near = 2 * REACH, REACH
    shifts = [1] if en == 2 else [1, -1]
    dirs = len(shifts)
    extra, nears = wide * dirs, near * dirs
    slots = block + extra
    parts = 4

    def tiles(count, dtype=F32):
        return jax.ShapeDtypeStruct((count, rows, width), dtype)

    def edges(count):
        return jax.ShapeDtypeStruct((count, RMAX, 128), F32)

    def weights(count):
        return jax.ShapeDtypeStruct((count, 128, 256), BF16)

    def halves(count):
        return jax.ShapeDtypeStruct((count, 128, 128), BF16)

    def scratch(shape):
        return pltpu.VMEM(shape.shape, shape.dtype)

    lanes = jax.ShapeDtypeStruct((1, 128), F32)

    packed = pl.pallas_call(
        functools.partial(pack_kernel, parts, en),
        in_specs=[HBM] * 4,
        out_specs=[VMEM] * (3 + 3 * dirs),
        out_shape=[tiles(block), edges(block), edges(block)] + [tiles(wide + 2 * near)] * dirs + [edges(wide)] * (2 * dirs),
        scratch_shapes=[
            scratch(tiles(block)), scratch(tiles(block)), pltpu.VMEM((dirs, near, rows, width), jnp.int32),
            pltpu.SemaphoreType.DMA((2, parts)), pltpu.SemaphoreType.DMA((dirs, 2)),
        ],
        compiler_params=params(12),
        name="weight_and_pack",
    )(*[pltpu.with_memory_space_constraint(array, pltpu.HBM) for array in (flux, exposure, background, observed)])
    weighted, last, first = packed[:3]
    before = lax.ppermute(last, "sky", ring(sky, 1))
    after = lax.ppermute(first, "sky", ring(sky, -1))
    energies, befores, afters = [], [], []
    for d, shift in enumerate(shifts):
        energies.append(lax.ppermute(packed[3 + d], "en", ring(en, shift)))
        befores.append(lax.ppermute(packed[3 + dirs + d], ("sky", "en"), grid_ring(sky, en, 1, shift)))
        afters.append(lax.ppermute(packed[3 + 2 * dirs + d], ("sky", "en"), grid_ring(sky, en, -1, shift)))
    if dirs > 1:
        energy = jnp.concatenate(
            [e[:wide] for e in energies] + [e[wide:wide + near] for e in energies] + [e[wide + near:] for e in energies]
        )
        before_x, after_x = jnp.concatenate(befores), jnp.concatenate(afters)
    else:
        energy, before_x, after_x = energies[0], befores[0], afters[0]

    centre, band, edge, band_x, edge_x, fold = pl.pallas_call(
        functools.partial(weights_kernel, en),
        in_specs=[SMEM] * 4 + [VMEM],
        out_specs=[VMEM] * 5 + [SMEM],
        out_shape=[tiles(block), weights(block), halves(block), weights(extra), halves(extra), jax.ShapeDtypeStruct((5 * (slots + 4),), F32)],
        compiler_params=params(4),
        cost_estimate=cost(block, 2, block * 2**15),
        name="weights_and_centre",
    )(psf_radius, band_low, band_high, disp_raw, weighted)
    back, last, first, total = pl.pallas_call(
        functools.partial(middle_kernel, en),
        in_specs=[SMEM] + [VMEM] * 12,
        out_specs=[VMEM] * 4,
        out_shape=[tiles(block), edges(block), edges(block), lanes],
        scratch_shapes=[scratch(tiles(block)), scratch(tiles(slots + 4)), scratch(tiles(slots + 4)), pltpu.VMEM((8, 128), F32)],
        compiler_params=params(14),
        cost_estimate=cost(block, 2, block * 2**15),
        name="blur_fold_residual_fold",
    )(fold, centre, band, edge, before, after, background, observed, band_x, edge_x, before_x, after_x, energy)

    before = lax.ppermute(last, "sky", ring(sky, 1))
    after = lax.ppermute(first, "sky", ring(sky, -1))
    def partners(value, step, count):
        pairs = [[(i, i ^ (step * k)) for i in range(sky * en)] for k in range(1, count)]
        return [value] + [lax.ppermute(value, ("sky", "en"), pair) for pair in pairs]

    terms = partners(tree_sum(partners(total, 1, 2 * en)), 2 * en, sky // 2)
    centre = pl.pallas_call(
        centre_kernel,
        in_specs=[VMEM, VMEM],
        out_specs=VMEM,
        out_shape=tiles(block),
        compiler_params=params(4),
        cost_estimate=cost(block, 2),
        name="back_centre",
    )(back, band)
    grad, loss = pl.pallas_call(
        functools.partial(final_kernel, parts, float(rows * width * bins * sky)),
        in_specs=[VMEM] * (6 + len(terms)),
        out_specs=[ANY, VMEM],
        out_shape=[tiles(block), jax.ShapeDtypeStruct((1, 1), F32)],
        scratch_shapes=[scratch(tiles(block)), scratch(tiles(block)), pltpu.SemaphoreType.DMA((parts,))],
        compiler_params=params(8),
        cost_estimate=cost(block, 1),
        name="back_edges_exposure",
    )(centre, band, edge, before, after, exposure, *terms)
    return grad, loss.reshape(())


def solution(mesh):
    placed = (P("en", None, "sky"),) * 4 + (P(),) * 4
    return jax.shard_map(local, mesh=mesh, in_specs=placed, out_specs=(P("en", None, "sky"), P()), check_vma=False)
```

```python
import functools

import jax
import jax.numpy as jnp
from jax import lax
from jax.experimental import pallas as pl
from jax.experimental.pallas import tpu as pltpu
from jax.sharding import PartitionSpec as P

RMAX = 32
REACH = 2
F32 = jnp.float32
BF16 = jnp.bfloat16
SMEM = pl.BlockSpec(memory_space=pltpu.SMEM)
ANY = pl.BlockSpec(memory_space=pl.ANY)
VMEM = pl.BlockSpec(memory_space=pltpu.VMEM)
HBM = pl.BlockSpec(memory_space=pltpu.HBM)


def split(x):
    hi = x.astype(BF16)
    return hi, (x - hi.astype(F32)).astype(BF16)


def params(mib=56):
    return pltpu.CompilerParams(vmem_limit_bytes=mib * 2**20)


def blocks(count, rows, cols):
    return pl.BlockSpec((count, rows, cols), lambda i: (i, 0, 0))


def chunk_copy(source, target, sem, c, size):
    at = pl.ds(c * size, size)
    return pltpu.make_async_copy(source.at[at], target.at[at], sem)


def run_stages(groups, size, stages, events=(), arrive=None):
    marks = {0} | {lag for _, lag in stages} | {lag + groups for _, lag in stages} | {at for at, _ in events}
    marks = sorted(marks)
    for start, stop in zip(marks, marks[1:] + [marks[-1]]):
        for at, event in events:
            if at == start:
                event()
        active = [(n, stage, lag) for n, (stage, lag) in enumerate(stages) if lag <= start < lag + groups]
        if stop == start or not active:
            continue

        def step(p, carry):
            if arrive is not None:
                for n, _, lag in active:
                    arrive(n, p - lag)
            stores = []
            for _, stage, lag in active:
                for i in range(size):
                    stores += stage((p - lag) * size + i)
            for ref, index, value in stores:
                if index is None:
                    ref[...] += value
                else:
                    ref[index] = value
            return carry

        lax.fori_loop(start, stop, step, 0)


def cost(tiles, products, transcendentals=0):
    return pl.CostEstimate(flops=tiles * products * 2 * 128 * 256 * 256, bytes_accessed=tiles * 2**16, transcendentals=transcendentals)


class Place:
    def __init__(self, block, en):
        self.block, self.en = block, en
        self.me = lax.axis_index("en")
        self.wide, self.near = 2 * REACH, REACH
        self.dirs = 1 if en == 2 else 2
        self.extra, self.nears = self.wide * self.dirs, self.near * self.dirs
        self.slots, self.bins = block + self.extra, block * en
        self.own = jnp.where(self.me == 0, 0, self.wide) if en == 2 else self.wide
        self.first_bin = self.me * block - self.own

    def start(self, d, width):
        if self.en == 2:
            return jnp.where(self.me == 0, self.block - width, 0)
        return self.block - width if d == 0 else 0

    def slot(self, k, width):
        if self.en == 2:
            return jnp.where(self.me == 0, self.block, self.wide - width) + k
        return self.wide - width + k if k < width else self.wide + self.block + k - width

    def clamp(self, g):
        return jnp.clip(g, 0, self.bins - 1)


def pack_edges(tile):
    lane = lax.broadcasted_iota(jnp.int32, (RMAX, 4 * RMAX), 1)
    last = first = None
    for q in range(4):
        rows = tile[q * RMAX:(q + 1) * RMAX]
        to_last = pltpu.roll(rows, (q + 1) * RMAX % 128, 1) if q != 3 else rows
        to_first = pltpu.roll(rows, q * RMAX, 1) if q else rows
        last = to_last if last is None else jnp.where(lane >= q * RMAX, to_last, last)
        first = to_first if first is None else jnp.where(lane >= q * RMAX, to_first, first)
    return last, first


def unpack_edges(before, after):
    lane = lax.broadcasted_iota(jnp.int32, (RMAX, 4 * RMAX), 1)
    parts = []
    for q in range(4):
        left = pltpu.roll(before, 128 - q * RMAX, 1) if q else before
        right = pltpu.roll(after, (96 - q * RMAX) % 128, 1) if q != 3 else after
        parts.append(jnp.where(lane < 64, left, right))
    return jnp.concatenate(parts, axis=0)


def quarters(out):
    return out[:128, :128] + (out[:128, 128:] + out[128:, :128])


def lon_product(tile, weights):
    return quarters(jnp.dot(jnp.concatenate(split(tile), axis=0), weights, preferred_element_type=F32))


def lat_product(weights, tile):
    halves = jnp.concatenate([weights[:, :128], weights[:, 128:]], axis=0)
    return quarters(jnp.dot(halves, jnp.concatenate(split(tile), axis=1), preferred_element_type=F32))


def profile(radius, column):
    wide = jnp.full((1, 128), radius, jnp.int32).astype(F32)
    reach = wide * wide
    factor = -2.0 / reach
    lane = lax.broadcasted_iota(jnp.int32, (1, 128), 1)
    square = (lane * lane).astype(F32)
    values = jnp.where(square <= reach, jnp.exp(square * factor), 0.0)
    norm = 2.0 * jnp.sum(values, axis=1, keepdims=True) - 1.0
    root = jnp.sqrt(jnp.full((1, 128), column, F32))[:, :1]
    return factor[:, :1], 1.0 / (norm * root), reach[:, :1]


def taper_values(diff, ok, factor, scale, reach):
    square = diff * diff
    return jnp.where((square <= reach) & ok, jnp.exp(square * factor) * scale, 0.0)


def pack_kernel(parts, en, flux, exposure, background, observed, weighted, last, first, *rest):
    place = Place(flux.shape[0], en)
    dirs, wide, near, block = place.dirs, place.wide, place.near, place.block
    sent, last_x, first_x = rest[:dirs], rest[dirs:2 * dirs], rest[2 * dirs:3 * dirs]
    v_flux, v_exposure, v_observed, sems, near_sems = rest[3 * dirs:]
    chunk = block // parts

    def arrivals(c):
        return [chunk_copy(a, b, sems.at[n, c], c, chunk) for n, (a, b) in enumerate(((flux, v_flux), (exposure, v_exposure)))]

    def near_arrivals(d):
        at = pl.ds(place.start(d, near), near)
        return [
            pltpu.make_async_copy(background.at[at], sent[d].at[pl.ds(wide, near)], near_sems.at[d, 0]),
            pltpu.make_async_copy(observed.at[at], v_observed.at[d], near_sems.at[d, 1]),
        ]

    for c in range(parts):
        for copy in arrivals(c):
            copy.start()
    for d in range(dirs):
        for copy in near_arrivals(d):
            copy.start()
    size = 4 if chunk % 4 == 0 else 2
    for c in range(parts):
        for copy in arrivals(c):
            copy.wait()

        def some(g, carry):
            tiles = [v_flux[size * g + i] * v_exposure[size * g + i] for i in range(size)]
            packed = [pack_edges(tile) for tile in tiles]
            for i in range(size):
                weighted[size * g + i] = tiles[i]
                last[size * g + i], first[size * g + i] = packed[i]
            return carry

        lax.fori_loop(c * chunk // size, (c + 1) * chunk // size, some, 0)
    for d in range(dirs):
        for copy in near_arrivals(d):
            copy.wait()
        start = place.start(d, wide)
        for k in range(wide):
            sent[d][k] = weighted[start + k]
            last_x[d][k] = last[start + k]
            first_x[d][k] = first[start + k]
        for k in range(near):
            sent[d][wide + near + k] = v_observed[d, k].astype(F32)


def weights_kernel(en, radius, low, high, disp, weighted, centre, band, edge, band_x, edge_x, fold):
    block = weighted.shape[0]
    place = Place(block, en)
    row = lax.broadcasted_iota(jnp.int32, (128, 128), 0)
    col = lax.broadcasted_iota(jnp.int32, (128, 128), 1)
    near = (row - col).astype(F32)
    far = jnp.where(row < 64, row - col - RMAX, row - col + RMAX).astype(F32)
    held = (row < RMAX) | (row >= 128 - RMAX)
    always = row >= 0

    def weight(i, j):
        at, to = place.clamp(i), place.clamp(j)
        inside = (i == at) & (j == to) & (low[at] <= j - i) & (j - i <= high[at])
        return jnp.where(inside, disp[at, to], 0.0)

    def make(g):
        for o in range(-REACH, REACH + 1):
            fold[5 * (g - place.first_bin + REACH) + o + REACH] = weight(g, g + o)
        column = weight(g, g)
        for o in (-2, -1, 1, 2):
            column = column + weight(g - o, g)
        numbers = profile(radius[place.clamp(g)], jnp.where(column > 0.0, column, 1.0))
        return tuple(
            jnp.concatenate(split(taper_values(diff, ok, *numbers)), axis=1) for diff, ok in ((near, always), (far, held))
        )

    for s in (0, 1, place.slots + 2, place.slots + 3):
        for o in range(5):
            fold[5 * s + o] = 0.0

    def some(b):
        made = make(place.me * block + b)
        return [(band, b, made[0]), (edge, b, made[1])]

    def lon(b):
        return [(centre, b, lon_product(weighted[b], band[b]))]

    run_stages(block // 2, 2, [(some, 0), (lon, 1)])
    for k in range(place.extra):
        band_x[k], edge_x[k] = make(place.first_bin + place.slot(k, place.wide))


def middle_kernel(en, fold, centre, band, edge, before, after, background, observed, band_x, edge_x, before_x, after_x, energy,
                  back, last, first, loss, whole, blurred, resid, sums):
    block = centre.shape[0]
    place = Place(block, en)
    extra, nears, slots, own = place.extra, place.nears, place.slots, place.own
    zero = jnp.zeros((128, 128), F32)
    for s in (0, 1, slots + 2, slots + 3):
        blurred[s] = zero
        resid[s] = zero
    sums[...] = jnp.zeros((8, 128), F32)

    done = [lon_product(energy[k], band_x[k]) for k in range(extra)]
    done = [done[k] + lon_product(unpack_edges(before_x[k], after_x[k]), edge_x[k]) for k in range(extra)]
    done = [lat_product(band_x[k], done[k]) for k in range(extra)]
    for k in range(extra):
        blurred[place.slot(k, place.wide) + 2] = done[k]

    def lon(b):
        return [(whole, b, centre[b] + lon_product(unpack_edges(before[b], after[b]), edge[b]))]

    def lat(b):
        return [(blurred, b + own + 2, lat_product(band[b], whole[b]))]

    def mean_counts(slot, ground):
        mu = ground
        for o in range(5):
            mu = mu + fold[5 * (slot + 2) + o] * blurred[slot + o]
        return mu

    def residual(b):
        slot = b + own
        mu = mean_counts(slot, background[b])
        counts = observed[b].astype(F32)
        terms = (mu - counts * jnp.log(mu)).reshape(16, 8, 128).sum(0)
        return [(resid, slot + 2, 1.0 - counts / mu), (sums, None, terms)]

    def extra_residuals():
        values = []
        for k in range(nears):
            mu = mean_counts(place.slot(k, place.near), energy[extra + k])
            values.append(1.0 - energy[extra + nears + k] / mu)
        for k in range(nears):
            resid[place.slot(k, place.near) + 2] = values[k]

    def fold_back(b):
        slot = b + own
        total = None
        for o in range(5):
            term = fold[5 * (slot + 4 - o) + o] * resid[slot + 4 - o]
            total = term if total is None else total + term
        ends = pack_edges(total)
        return [(back, b, total), (last, b, ends[0]), (first, b, ends[1])]

    size = 2
    groups = block // size
    run_stages(
        groups, size, [(lon, 0), (lat, 1), (residual, 3), (fold_back, 5)],
        events=[(3, extra_residuals), (groups + 1, extra_residuals)],
    )
    loss[...] = jnp.full((1, 128), jnp.sum(sums[...]), F32)


def centre_kernel(back, band, total, moved, out, passed):
    passed[...] = total[...] + moved[...]
    size = 4 if back.shape[0] % 4 == 0 else 2

    def some(g, carry):
        sums = [lon_product(back[size * g + i], band[size * g + i]) for i in range(size)]
        for i in range(size):
            out[size * g + i] = sums[i]
        return carry

    lax.fori_loop(0, back.shape[0] // size, some, 0)


def final_kernel(parts, centre, band, edge, before, after, exposure, total, out, passed, whole, v_out, out_sems):
    block = centre.shape[0]
    chunk = block // parts
    passed[...] = total[...]

    def copy_out(c):
        return chunk_copy(v_out, out, out_sems.at[c], c, chunk)

    def lon(b):
        return [(whole, b, centre[b] + lon_product(unpack_edges(before[b], after[b]), edge[b]))]

    def lat(b):
        return [(v_out, b, lat_product(band[b], whole[b]) * exposure[b])]

    size = 2
    groups, per_chunk = block // size, chunk // size

    def arrive(n, p):
        if n == 1:
            @pl.when((lax.rem(p, per_chunk) == 0) & (p > 0))
            def _():
                copy_out(lax.div(p, per_chunk) - 1).start()

    run_stages(groups, size, [(lon, 0), (lat, 1)], arrive=arrive)
    copy_out(parts - 1).start()
    for c in range(parts):
        copy_out(c).wait()


def ring(size, shift):
    return [(i, (i + shift) % size) for i in range(size)]


def grid_ring(sky, en, sky_shift, en_shift):
    return [(s * en + e, (s + sky_shift) % sky * en + (e + en_shift) % en) for s in range(sky) for e in range(en)]


def local(flux, exposure, background, observed, psf_radius, band_low, band_high, disp_raw):
    block, rows, width = flux.shape
    bins = disp_raw.shape[0]
    sky, en = lax.axis_size("sky"), lax.axis_size("en")
    wide, near = 2 * REACH, REACH
    shifts = [1] if en == 2 else [1, -1]
    dirs = len(shifts)
    extra, nears = wide * dirs, near * dirs
    slots = block + extra
    parts = 4

    def tiles(count, dtype=F32):
        return jax.ShapeDtypeStruct((count, rows, width), dtype)

    def edges(count):
        return jax.ShapeDtypeStruct((count, RMAX, 128), F32)

    def weights(count):
        return jax.ShapeDtypeStruct((count, 128, 256), BF16)

    def scratch(shape):
        return pltpu.VMEM(shape.shape, shape.dtype)

    lanes = jax.ShapeDtypeStruct((1, 128), F32)

    packed = pl.pallas_call(
        functools.partial(pack_kernel, parts, en),
        in_specs=[HBM] * 4,
        out_specs=[VMEM] * (3 + 3 * dirs),
        out_shape=[tiles(block), edges(block), edges(block)] + [tiles(wide + 2 * near)] * dirs + [edges(wide)] * (2 * dirs),
        scratch_shapes=[
            scratch(tiles(block)), scratch(tiles(block)), pltpu.VMEM((dirs, near, rows, width), jnp.int32),
            pltpu.SemaphoreType.DMA((2, parts)), pltpu.SemaphoreType.DMA((dirs, 2)),
        ],
        compiler_params=params(12),
        name="weight_and_pack",
    )(*[pltpu.with_memory_space_constraint(array, pltpu.HBM) for array in (flux, exposure, background, observed)])
    weighted, last, first = packed[:3]
    before = lax.ppermute(last, "sky", ring(sky, 1))
    after = lax.ppermute(first, "sky", ring(sky, -1))
    energies, befores, afters = [], [], []
    for d, shift in enumerate(shifts):
        energies.append(lax.ppermute(packed[3 + d], "en", ring(en, shift)))
        befores.append(lax.ppermute(packed[3 + dirs + d], ("sky", "en"), grid_ring(sky, en, 1, shift)))
        afters.append(lax.ppermute(packed[3 + 2 * dirs + d], ("sky", "en"), grid_ring(sky, en, -1, shift)))
    if dirs > 1:
        energy = jnp.concatenate(
            [e[:wide] for e in energies] + [e[wide:wide + near] for e in energies] + [e[wide + near:] for e in energies]
        )
        before_x, after_x = jnp.concatenate(befores), jnp.concatenate(afters)
    else:
        energy, before_x, after_x = energies[0], befores[0], afters[0]

    centre, band, edge, band_x, edge_x, fold = pl.pallas_call(
        functools.partial(weights_kernel, en),
        in_specs=[SMEM] * 4 + [VMEM],
        out_specs=[VMEM] * 5 + [SMEM],
        out_shape=[tiles(block), weights(block), weights(block), weights(extra), weights(extra), jax.ShapeDtypeStruct((5 * (slots + 4),), F32)],
        compiler_params=params(4),
        cost_estimate=cost(block, 1, block * 2**15),
        name="weights_and_centre",
    )(psf_radius, band_low, band_high, disp_raw, weighted)
    back, last, first, total = pl.pallas_call(
        functools.partial(middle_kernel, en),
        in_specs=[SMEM] + [VMEM] * 12,
        out_specs=[VMEM] * 4,
        out_shape=[tiles(block), edges(block), edges(block), lanes],
        scratch_shapes=[scratch(tiles(block)), scratch(tiles(slots + 4)), scratch(tiles(slots + 4)), pltpu.VMEM((8, 128), F32)],
        compiler_params=params(14),
        cost_estimate=cost(block, 2, block * 2**15),
        name="blur_fold_residual_fold",
    )(fold, centre, band, edge, before, after, background, observed, band_x, edge_x, before_x, after_x, energy)

    before = lax.ppermute(last, "sky", ring(sky, 1))
    after = lax.ppermute(first, "sky", ring(sky, -1))
    masks = [en] + [1 << n for n in range(en.bit_length() - 1)]
    masks += [en << n for n in range(2, sky.bit_length() - 1)] + [2 * en]

    def partner(value, mask):
        return lax.ppermute(value, ("sky", "en"), [(i, i ^ mask) for i in range(sky * en)])

    centre, total = pl.pallas_call(
        centre_kernel,
        in_specs=[VMEM] * 4,
        out_specs=[VMEM] * 2,
        out_shape=[tiles(block), lanes],
        compiler_params=params(4),
        cost_estimate=cost(block, 1),
        name="back_centre",
    )(back, band, total, partner(total, masks[0]))
    for mask in masks[1:-1]:
        total = total + partner(total, mask)
    moved = partner(total, masks[-1])
    grad, passed = pl.pallas_call(
        functools.partial(final_kernel, parts),
        in_specs=[VMEM] * 7,
        out_specs=[ANY, VMEM],
        out_shape=[tiles(block), lanes],
        scratch_shapes=[scratch(tiles(block)), scratch(tiles(block)), pltpu.SemaphoreType.DMA((parts,))],
        compiler_params=params(8),
        cost_estimate=cost(block, 2),
        name="back_edges_lat_exposure",
    )(centre, band, edge, before, after, exposure, total)
    return grad, (passed + moved)[0, 0] / F32(rows * width * bins * sky)


def solution(mesh):
    placed = (P("en", None, "sky"),) * 4 + (P(),) * 4
    return jax.shard_map(local, mesh=mesh, in_specs=placed, out_specs=(P("en", None, "sky"), P()), check_vma=False)
```

```python
import functools

import jax
import jax.numpy as jnp
from jax import lax
from jax.experimental import pallas as pl
from jax.experimental.pallas import tpu as pltpu
from jax.sharding import PartitionSpec as P

RMAX = 32
REACH = 2
F32 = jnp.float32
BF16 = jnp.bfloat16
SMEM = pl.BlockSpec(memory_space=pltpu.SMEM)
ANY = pl.BlockSpec(memory_space=pl.ANY)
VMEM = pl.BlockSpec(memory_space=pltpu.VMEM)
HBM = pl.BlockSpec(memory_space=pltpu.HBM)


def split(x):
    hi = x.astype(BF16)
    return hi, (x - hi.astype(F32)).astype(BF16)


def params(mib=56):
    return pltpu.CompilerParams(vmem_limit_bytes=mib * 2**20)


def blocks(count, rows, cols):
    return pl.BlockSpec((count, rows, cols), lambda i: (i, 0, 0))


def chunk_copy(source, target, sem, c, size):
    at = pl.ds(c * size, size)
    return pltpu.make_async_copy(source.at[at], target.at[at], sem)


def run_stages(groups, size, stages, events=(), arrive=None):
    marks = {0} | {lag for _, lag in stages} | {lag + groups for _, lag in stages} | {at for at, _ in events}
    marks = sorted(marks)
    for start, stop in zip(marks, marks[1:] + [marks[-1]]):
        for at, event in events:
            if at == start:
                event()
        active = [(n, stage, lag) for n, (stage, lag) in enumerate(stages) if lag <= start < lag + groups]
        if stop == start or not active:
            continue

        def step(p, carry):
            if arrive is not None:
                for n, _, lag in active:
                    arrive(n, p - lag)
            stores = []
            for _, stage, lag in active:
                for i in range(size):
                    stores += stage((p - lag) * size + i)
            for ref, index, value in stores:
                if index is None:
                    ref[...] += value
                else:
                    ref[index] = value
            return carry

        lax.fori_loop(start, stop, step, 0)


def cost(tiles, products, transcendentals=0):
    return pl.CostEstimate(flops=tiles * products * 2 * 128 * 256 * 256, bytes_accessed=tiles * 2**16, transcendentals=transcendentals)


class Place:
    def __init__(self, block, en):
        self.block, self.en = block, en
        self.me = lax.axis_index("en")
        self.wide, self.near = 2 * REACH, REACH
        self.dirs = 1 if en == 2 else 2
        self.extra, self.nears = self.wide * self.dirs, self.near * self.dirs
        self.slots, self.bins = block + self.extra, block * en
        self.own = jnp.where(self.me == 0, 0, self.wide) if en == 2 else self.wide
        self.first_bin = self.me * block - self.own

    def start(self, d, width):
        if self.en == 2:
            return jnp.where(self.me == 0, self.block - width, 0)
        return self.block - width if d == 0 else 0

    def slot(self, k, width):
        if self.en == 2:
            return jnp.where(self.me == 0, self.block, self.wide - width) + k
        return self.wide - width + k if k < width else self.wide + self.block + k - width

    def clamp(self, g):
        return jnp.clip(g, 0, self.bins - 1)


def pack_edges(tile):
    lane = lax.broadcasted_iota(jnp.int32, (RMAX, 4 * RMAX), 1)
    last = first = None
    for q in range(4):
        rows = tile[q * RMAX:(q + 1) * RMAX]
        to_last = pltpu.roll(rows, (q + 1) * RMAX % 128, 1) if q != 3 else rows
        to_first = pltpu.roll(rows, q * RMAX, 1) if q else rows
        last = to_last if last is None else jnp.where(lane >= q * RMAX, to_last, last)
        first = to_first if first is None else jnp.where(lane >= q * RMAX, to_first, first)
    return last, first


def unpack_edges(before, after):
    lane = lax.broadcasted_iota(jnp.int32, (RMAX, 4 * RMAX), 1)
    parts = []
    for q in range(4):
        left = pltpu.roll(before, 128 - q * RMAX, 1) if q else before
        right = pltpu.roll(after, (96 - q * RMAX) % 128, 1) if q != 3 else after
        parts.append(jnp.where(lane < 64, left, right))
    return jnp.concatenate(parts, axis=0)


def twice(x):
    return jnp.concatenate([x, x], axis=0)


def lon_product(tile, weights):
    out = jnp.dot(jnp.concatenate(split(tile), axis=1), twice(weights), preferred_element_type=F32)
    return out[:, :128] + out[:, 128:]


def lat_product(weights, tile):
    out = jnp.dot(weights, twice(jnp.concatenate(split(tile), axis=1)), preferred_element_type=F32)
    return out[:, :128] + out[:, 128:]


def profile(radius, column):
    wide = jnp.full((1, 128), radius, jnp.int32).astype(F32)
    reach = wide * wide
    factor = -2.0 / reach
    lane = lax.broadcasted_iota(jnp.int32, (1, 128), 1)
    square = (lane * lane).astype(F32)
    values = jnp.where(square <= reach, jnp.exp(square * factor), 0.0)
    norm = 2.0 * jnp.sum(values, axis=1, keepdims=True) - 1.0
    root = jnp.sqrt(jnp.full((1, 128), column, F32))[:, :1]
    return factor[:, :1], 1.0 / (norm * root), reach[:, :1]


def taper_values(diff, ok, factor, scale, reach):
    square = diff * diff
    return jnp.where((square <= reach) & ok, jnp.exp(square * factor) * scale, 0.0)


def pack_kernel(parts, en, flux, exposure, background, observed, weighted, last, first, *rest):
    place = Place(flux.shape[0], en)
    dirs, wide, near, block = place.dirs, place.wide, place.near, place.block
    sent, last_x, first_x = rest[:dirs], rest[dirs:2 * dirs], rest[2 * dirs:3 * dirs]
    v_flux, v_exposure, v_observed, sems, near_sems = rest[3 * dirs:]
    chunk = block // parts

    def arrivals(c):
        return [chunk_copy(a, b, sems.at[n, c], c, chunk) for n, (a, b) in enumerate(((flux, v_flux), (exposure, v_exposure)))]

    def near_arrivals(d):
        at = pl.ds(place.start(d, near), near)
        return [
            pltpu.make_async_copy(background.at[at], sent[d].at[pl.ds(wide, near)], near_sems.at[d, 0]),
            pltpu.make_async_copy(observed.at[at], v_observed.at[d], near_sems.at[d, 1]),
        ]

    for c in range(parts):
        for copy in arrivals(c):
            copy.start()
    for d in range(dirs):
        for copy in near_arrivals(d):
            copy.start()
    size = 4 if chunk % 4 == 0 else 2
    for c in range(parts):
        for copy in arrivals(c):
            copy.wait()

        def some(g, carry):
            tiles = [v_flux[size * g + i] * v_exposure[size * g + i] for i in range(size)]
            packed = [pack_edges(tile) for tile in tiles]
            for i in range(size):
                weighted[size * g + i] = tiles[i]
                last[size * g + i], first[size * g + i] = packed[i]
            return carry

        lax.fori_loop(c * chunk // size, (c + 1) * chunk // size, some, 0)
    for d in range(dirs):
        for copy in near_arrivals(d):
            copy.wait()
        start = place.start(d, wide)
        for k in range(wide):
            sent[d][k] = weighted[start + k]
            last_x[d][k] = last[start + k]
            first_x[d][k] = first[start + k]
        for k in range(near):
            sent[d][wide + near + k] = v_observed[d, k].astype(F32)


def weights_kernel(en, radius, low, high, disp, weighted, centre, band, edge, band_x, edge_x, fold):
    block = weighted.shape[0]
    place = Place(block, en)
    row = lax.broadcasted_iota(jnp.int32, (128, 128), 0)
    col = lax.broadcasted_iota(jnp.int32, (128, 128), 1)
    near = (row - col).astype(F32)
    far = jnp.where(row < 64, row - col - RMAX, row - col + RMAX).astype(F32)
    held = (row < RMAX) | (row >= 128 - RMAX)
    always = row >= 0

    def weight(i, j):
        at, to = place.clamp(i), place.clamp(j)
        inside = (i == at) & (j == to) & (low[at] <= j - i) & (j - i <= high[at])
        return jnp.where(inside, disp[at, to], 0.0)

    def make(g):
        for o in range(-REACH, REACH + 1):
            fold[5 * (g - place.first_bin + REACH) + o + REACH] = weight(g, g + o)
        column = weight(g, g)
        for o in (-2, -1, 1, 2):
            column = column + weight(g - o, g)
        numbers = profile(radius[place.clamp(g)], jnp.where(column > 0.0, column, 1.0))
        return tuple(
            jnp.concatenate(split(taper_values(diff, ok, *numbers)), axis=1) for diff, ok in ((near, always), (far, held))
        )

    for s in (0, 1, place.slots + 2, place.slots + 3):
        for o in range(5):
            fold[5 * s + o] = 0.0

    def some(b):
        made = make(place.me * block + b)
        return [(band, b, made[0]), (edge, b, made[1])]

    def lon(b):
        return [(centre, b, lon_product(weighted[b], band[b]))]

    run_stages(block // 4, 4, [(some, 0), (lon, 1)])
    for k in range(place.extra):
        band_x[k], edge_x[k] = make(place.first_bin + place.slot(k, place.wide))


def middle_kernel(en, fold, centre, band, edge, before, after, background, observed, band_x, edge_x, before_x, after_x, energy,
                  back, last, first, loss, whole, blurred, resid, sums):
    block = centre.shape[0]
    place = Place(block, en)
    extra, nears, slots, own = place.extra, place.nears, place.slots, place.own
    zero = jnp.zeros((128, 128), F32)
    for s in (0, 1, slots + 2, slots + 3):
        blurred[s] = zero
        resid[s] = zero
    sums[...] = jnp.zeros((8, 128), F32)

    done = [lon_product(energy[k], band_x[k]) for k in range(extra)]
    done = [done[k] + lon_product(unpack_edges(before_x[k], after_x[k]), edge_x[k]) for k in range(extra)]
    done = [lat_product(band_x[k], done[k]) for k in range(extra)]
    for k in range(extra):
        blurred[place.slot(k, place.wide) + 2] = done[k]

    def lon(b):
        return [(whole, b, centre[b] + lon_product(unpack_edges(before[b], after[b]), edge[b]))]

    def lat(b):
        return [(blurred, b + own + 2, lat_product(band[b], whole[b]))]

    def mean_counts(slot, ground):
        mu = ground
        for o in range(5):
            mu = mu + fold[5 * (slot + 2) + o] * blurred[slot + o]
        return mu

    def residual(b):
        slot = b + own
        mu = mean_counts(slot, background[b])
        counts = observed[b].astype(F32)
        terms = (mu - counts * jnp.log(mu)).reshape(16, 8, 128).sum(0)
        return [(resid, slot + 2, 1.0 - counts / mu), (sums, None, terms)]

    def extra_residuals():
        values = []
        for k in range(nears):
            mu = mean_counts(place.slot(k, place.near), energy[extra + k])
            values.append(1.0 - energy[extra + nears + k] / mu)
        for k in range(nears):
            resid[place.slot(k, place.near) + 2] = values[k]

    def fold_back(b):
        slot = b + own
        total = None
        for o in range(5):
            term = fold[5 * (slot + 4 - o) + o] * resid[slot + 4 - o]
            total = term if total is None else total + term
        ends = pack_edges(total)
        return [(back, b, total), (last, b, ends[0]), (first, b, ends[1])]

    size = 4
    groups = block // size
    run_stages(
        groups, size, [(lon, 0), (lat, 1), (residual, 3), (fold_back, 5)],
        events=[(3, extra_residuals), (groups + 1, extra_residuals)],
    )
    loss[...] = jnp.full((1, 128), jnp.sum(sums[...]), F32)


def centre_kernel(back, band, total, moved, out, passed):
    passed[...] = total[...] + moved[...]
    size = 8

    def some(g, carry):
        sums = [lon_product(back[size * g + i], band[size * g + i]) for i in range(size)]
        for i in range(size):
            out[size * g + i] = sums[i]
        return carry

    lax.fori_loop(0, back.shape[0] // size, some, 0)


def final_kernel(parts, centre, band, edge, before, after, exposure, total, out, passed, whole, v_out, out_sems):
    block = centre.shape[0]
    passed[...] = total[...]

    size = 4
    parts = min(parts, block // size)
    chunk = block // parts

    def copy_out(c):
        return chunk_copy(v_out, out, out_sems.at[c], c, chunk)

    def lon(b):
        return [(whole, b, centre[b] + lon_product(unpack_edges(before[b], after[b]), edge[b]))]

    def lat(b):
        return [(v_out, b, lat_product(band[b], whole[b]) * exposure[b])]

    groups, per_chunk = block // size, chunk // size

    def arrive(n, p):
        if n == 1:
            @pl.when((lax.rem(p, per_chunk) == 0) & (p > 0))
            def _():
                copy_out(lax.div(p, per_chunk) - 1).start()

    run_stages(groups, size, [(lon, 0), (lat, 1)], arrive=arrive)
    copy_out(parts - 1).start()
    for c in range(parts):
        copy_out(c).wait()


def ring(size, shift):
    return [(i, (i + shift) % size) for i in range(size)]


def grid_ring(sky, en, sky_shift, en_shift):
    return [(s * en + e, (s + sky_shift) % sky * en + (e + en_shift) % en) for s in range(sky) for e in range(en)]


def local(flux, exposure, background, observed, psf_radius, band_low, band_high, disp_raw):
    block, rows, width = flux.shape
    bins = disp_raw.shape[0]
    sky, en = lax.axis_size("sky"), lax.axis_size("en")
    wide, near = 2 * REACH, REACH
    shifts = [1] if en == 2 else [1, -1]
    dirs = len(shifts)
    extra, nears = wide * dirs, near * dirs
    slots = block + extra
    parts = 4

    def tiles(count, dtype=F32):
        return jax.ShapeDtypeStruct((count, rows, width), dtype)

    def edges(count):
        return jax.ShapeDtypeStruct((count, RMAX, 128), F32)

    def weights(count):
        return jax.ShapeDtypeStruct((count, 128, 256), BF16)

    def scratch(shape):
        return pltpu.VMEM(shape.shape, shape.dtype)

    lanes = jax.ShapeDtypeStruct((1, 128), F32)

    packed = pl.pallas_call(
        functools.partial(pack_kernel, parts, en),
        in_specs=[HBM] * 4,
        out_specs=[VMEM] * (3 + 3 * dirs),
        out_shape=[tiles(block), edges(block), edges(block)] + [tiles(wide + 2 * near)] * dirs + [edges(wide)] * (2 * dirs),
        scratch_shapes=[
            scratch(tiles(block)), scratch(tiles(block)), pltpu.VMEM((dirs, near, rows, width), jnp.int32),
            pltpu.SemaphoreType.DMA((2, parts)), pltpu.SemaphoreType.DMA((dirs, 2)),
        ],
        compiler_params=params(12),
        name="weight_and_pack",
    )(*[pltpu.with_memory_space_constraint(array, pltpu.HBM) for array in (flux, exposure, background, observed)])
    weighted, last, first = packed[:3]
    before = lax.ppermute(last, "sky", ring(sky, 1))
    after = lax.ppermute(first, "sky", ring(sky, -1))
    energies, befores, afters = [], [], []
    for d, shift in enumerate(shifts):
        energies.append(lax.ppermute(packed[3 + d], "en", ring(en, shift)))
        befores.append(lax.ppermute(packed[3 + dirs + d], ("sky", "en"), grid_ring(sky, en, 1, shift)))
        afters.append(lax.ppermute(packed[3 + 2 * dirs + d], ("sky", "en"), grid_ring(sky, en, -1, shift)))
    if dirs > 1:
        energy = jnp.concatenate(
            [e[:wide] for e in energies] + [e[wide:wide + near] for e in energies] + [e[wide + near:] for e in energies]
        )
        before_x, after_x = jnp.concatenate(befores), jnp.concatenate(afters)
    else:
        energy, before_x, after_x = energies[0], befores[0], afters[0]

    centre, band, edge, band_x, edge_x, fold = pl.pallas_call(
        functools.partial(weights_kernel, en),
        in_specs=[SMEM] * 4 + [VMEM],
        out_specs=[VMEM] * 5 + [SMEM],
        out_shape=[tiles(block), weights(block), weights(block), weights(extra), weights(extra), jax.ShapeDtypeStruct((5 * (slots + 4),), F32)],
        compiler_params=params(4),
        cost_estimate=cost(block, 1, block * 2**15),
        name="weights_and_centre",
    )(psf_radius, band_low, band_high, disp_raw, weighted)
    back, last, first, total = pl.pallas_call(
        functools.partial(middle_kernel, en),
        in_specs=[SMEM] + [VMEM] * 12,
        out_specs=[VMEM] * 4,
        out_shape=[tiles(block), edges(block), edges(block), lanes],
        scratch_shapes=[scratch(tiles(block)), scratch(tiles(slots + 4)), scratch(tiles(slots + 4)), pltpu.VMEM((8, 128), F32)],
        compiler_params=params(14),
        cost_estimate=cost(block, 2, block * 2**15),
        name="blur_fold_residual_fold",
    )(fold, centre, band, edge, before, after, background, observed, band_x, edge_x, before_x, after_x, energy)

    before = lax.ppermute(last, "sky", ring(sky, 1))
    after = lax.ppermute(first, "sky", ring(sky, -1))
    masks = [en] + [1 << n for n in range(en.bit_length() - 1)]
    masks += [en << n for n in range(2, sky.bit_length() - 1)] + [2 * en]

    def partner(value, mask):
        return lax.ppermute(value, ("sky", "en"), [(i, i ^ mask) for i in range(sky * en)])

    centre, total = pl.pallas_call(
        centre_kernel,
        in_specs=[VMEM] * 4,
        out_specs=[VMEM] * 2,
        out_shape=[tiles(block), lanes],
        compiler_params=params(4),
        cost_estimate=cost(block, 1),
        name="back_centre",
    )(back, band, total, partner(total, masks[0]))
    for mask in masks[1:-1]:
        total = total + partner(total, mask)
    moved = partner(total, masks[-1])
    grad, passed = pl.pallas_call(
        functools.partial(final_kernel, parts),
        in_specs=[VMEM] * 7,
        out_specs=[ANY, VMEM],
        out_shape=[tiles(block), lanes],
        scratch_shapes=[scratch(tiles(block)), scratch(tiles(block)), pltpu.SemaphoreType.DMA((parts,))],
        compiler_params=params(8),
        cost_estimate=cost(block, 2),
        name="back_edges_lat_exposure",
    )(centre, band, edge, before, after, exposure, total)
    return grad, (passed + moved)[0, 0] / F32(rows * width * bins * sky)


def solution(mesh):
    placed = (P("en", None, "sky"),) * 4 + (P(),) * 4
    return jax.shard_map(local, mesh=mesh, in_specs=placed, out_specs=(P("en", None, "sky"), P()), check_vma=False)
```

```python
import functools

import jax
import jax.numpy as jnp
from jax import lax
from jax.experimental import pallas as pl
from jax.experimental.pallas import tpu as pltpu
from jax.sharding import PartitionSpec as P

RMAX = 32
REACH = 2
F32 = jnp.float32
BF16 = jnp.bfloat16
SMEM = pl.BlockSpec(memory_space=pltpu.SMEM)
ANY = pl.BlockSpec(memory_space=pl.ANY)
VMEM = pl.BlockSpec(memory_space=pltpu.VMEM)
HBM = pl.BlockSpec(memory_space=pltpu.HBM)


def split(x):
    hi = x.astype(BF16)
    return hi, (x - hi.astype(F32)).astype(BF16)


def params(mib=56):
    return pltpu.CompilerParams(vmem_limit_bytes=mib * 2**20)


def blocks(count, rows, cols):
    return pl.BlockSpec((count, rows, cols), lambda i: (i, 0, 0))


def chunk_copy(source, target, sem, c, size):
    at = pl.ds(c * size, size)
    return pltpu.make_async_copy(source.at[at], target.at[at], sem)


def run_stages(groups, size, stages, events=(), arrive=None):
    marks = {0} | {lag for _, lag in stages} | {lag + groups for _, lag in stages} | {at for at, _ in events}
    marks = sorted(marks)
    for start, stop in zip(marks, marks[1:] + [marks[-1]]):
        for at, event in events:
            if at == start:
                event()
        active = [(n, stage, lag) for n, (stage, lag) in enumerate(stages) if lag <= start < lag + groups]
        if stop == start or not active:
            continue

        def step(p, carry):
            if arrive is not None:
                for n, _, lag in active:
                    arrive(n, p - lag)
            stores = []
            for _, stage, lag in active:
                for i in range(size):
                    stores += stage((p - lag) * size + i)
            for ref, index, value in stores:
                if index is None:
                    ref[...] += value
                else:
                    ref[index] = value
            return carry

        lax.fori_loop(start, stop, step, 0)


def cost(tiles, products, transcendentals=0):
    return pl.CostEstimate(flops=tiles * products * 2 * 128 * 256 * 256, bytes_accessed=tiles * 2**16, transcendentals=transcendentals)


class Place:
    def __init__(self, block, en):
        self.block, self.en = block, en
        self.me = lax.axis_index("en")
        self.dirs = 1 if en == 2 else 2
        self.extra = REACH * self.dirs
        self.slots, self.bins = block + self.extra, block * en
        self.own = jnp.where(self.me == 0, 0, REACH) if en == 2 else REACH
        self.first_bin = self.me * block - self.own

    def start(self, d):
        if self.en == 2:
            return jnp.where(self.me == 0, self.block - REACH, 0)
        return self.block - REACH if d == 0 else 0

    def slot(self, k):
        if self.en == 2:
            return jnp.where(self.me == 0, self.block, 0) + k
        return k if k < REACH else self.block + k

    def beside(self, d):
        if self.en == 2:
            return self.start(0)
        return 0 if d == 0 else self.block - REACH

    def clamp(self, g):
        return jnp.clip(g, 0, self.bins - 1)


def pack_edges(tile):
    lane = lax.broadcasted_iota(jnp.int32, (RMAX, 4 * RMAX), 1)
    last = first = None
    for q in range(4):
        rows = tile[q * RMAX:(q + 1) * RMAX]
        to_last = pltpu.roll(rows, (q + 1) * RMAX % 128, 1) if q != 3 else rows
        to_first = pltpu.roll(rows, q * RMAX, 1) if q else rows
        last = to_last if last is None else jnp.where(lane >= q * RMAX, to_last, last)
        first = to_first if first is None else jnp.where(lane >= q * RMAX, to_first, first)
    return last, first


def unpack_edges(before, after):
    lane = lax.broadcasted_iota(jnp.int32, (RMAX, 4 * RMAX), 1)
    parts = []
    for q in range(4):
        left = pltpu.roll(before, 128 - q * RMAX, 1) if q else before
        right = pltpu.roll(after, (96 - q * RMAX) % 128, 1) if q != 3 else after
        parts.append(jnp.where(lane < 64, left, right))
    return jnp.concatenate(parts, axis=0)


def twice(x):
    return jnp.concatenate([x, x], axis=0)


def lon_product(tile, weights):
    out = jnp.dot(jnp.concatenate(split(tile), axis=1), twice(weights), preferred_element_type=F32)
    return out[:, :128] + out[:, 128:]


def lat_product(weights, tile):
    out = jnp.dot(weights, twice(jnp.concatenate(split(tile), axis=1)), preferred_element_type=F32)
    return out[:, :128] + out[:, 128:]


def profile(radius, column):
    wide = jnp.full((1, 128), radius, jnp.int32).astype(F32)
    reach = wide * wide
    factor = -2.0 / reach
    lane = lax.broadcasted_iota(jnp.int32, (1, 128), 1)
    square = (lane * lane).astype(F32)
    values = jnp.where(square <= reach, jnp.exp(square * factor), 0.0)
    norm = 2.0 * jnp.sum(values, axis=1, keepdims=True) - 1.0
    root = jnp.sqrt(jnp.full((1, 128), column, F32))[:, :1]
    return factor[:, :1], 1.0 / (norm * root), reach[:, :1]


def taper_values(diff, ok, factor, scale, reach):
    square = diff * diff
    return jnp.where((square <= reach) & ok, jnp.exp(square * factor) * scale, 0.0)


def pack_kernel(parts, en, flux, exposure, weighted, last, first, *rest):
    place = Place(flux.shape[0], en)
    dirs, block = place.dirs, place.block
    sent, last_x, first_x = rest[:dirs], rest[dirs:2 * dirs], rest[2 * dirs:3 * dirs]
    v_flux, v_exposure, sems = rest[3 * dirs:]
    chunk = block // parts

    def arrivals(c):
        return [chunk_copy(a, b, sems.at[n, c], c, chunk) for n, (a, b) in enumerate(((flux, v_flux), (exposure, v_exposure)))]

    for c in range(parts):
        for copy in arrivals(c):
            copy.start()
    size = 4 if chunk % 4 == 0 else 2
    for c in range(parts):
        for copy in arrivals(c):
            copy.wait()

        def some(g, carry):
            tiles = [v_flux[size * g + i] * v_exposure[size * g + i] for i in range(size)]
            packed = [pack_edges(tile) for tile in tiles]
            for i in range(size):
                weighted[size * g + i] = tiles[i]
                last[size * g + i], first[size * g + i] = packed[i]
            return carry

        lax.fori_loop(c * chunk // size, (c + 1) * chunk // size, some, 0)
    for d in range(dirs):
        start = place.start(d)
        for k in range(REACH):
            sent[d][k] = weighted[start + k]
            last_x[d][k] = last[start + k]
            first_x[d][k] = first[start + k]


def weights_kernel(en, radius, low, high, disp, weighted, centre, band, edge, band_x, edge_x, fold):
    block = weighted.shape[0]
    place = Place(block, en)
    row = lax.broadcasted_iota(jnp.int32, (128, 128), 0)
    col = lax.broadcasted_iota(jnp.int32, (128, 128), 1)
    near = (row - col).astype(F32)
    far = jnp.where(row < 64, row - col - RMAX, row - col + RMAX).astype(F32)
    held = (row < RMAX) | (row >= 128 - RMAX)
    always = row >= 0

    def weight(i, j):
        at, to = place.clamp(i), place.clamp(j)
        inside = (i == at) & (j == to) & (low[at] <= j - i) & (j - i <= high[at])
        return jnp.where(inside, disp[at, to], 0.0)

    def make(g):
        for o in range(-REACH, REACH + 1):
            fold[5 * (g - place.first_bin + REACH) + o + REACH] = weight(g, g + o)
        column = weight(g, g)
        for o in (-2, -1, 1, 2):
            column = column + weight(g - o, g)
        numbers = profile(radius[place.clamp(g)], jnp.where(column > 0.0, column, 1.0))
        return tuple(
            jnp.concatenate(split(taper_values(diff, ok, *numbers)), axis=1) for diff, ok in ((near, always), (far, held))
        )

    for s in (0, 1, place.slots + 2, place.slots + 3):
        for o in range(5):
            fold[5 * s + o] = 0.0

    def some(b):
        made = make(place.me * block + b)
        return [(band, b, made[0]), (edge, b, made[1])]

    def lon(b):
        return [(centre, b, lon_product(weighted[b], band[b]))]

    run_stages(block // 4, 4, [(some, 0), (lon, 1)])
    for k in range(place.extra):
        band_x[k], edge_x[k] = make(place.first_bin + place.slot(k))


def middle_kernel(en, fold, centre, band, edge, before, after, background, observed, band_x, edge_x, before_x, after_x, energy,
                  resid, loss, *rest):
    block = centre.shape[0]
    place = Place(block, en)
    extra, slots, own = place.extra, place.slots, place.own
    sent, (whole, blurred, sums) = rest[:place.dirs], rest[place.dirs:]
    zero = jnp.zeros((128, 128), F32)
    for s in (0, 1, slots + 2, slots + 3):
        blurred[s] = zero
    sums[...] = jnp.zeros((8, 128), F32)

    done = [lon_product(energy[k], band_x[k]) for k in range(extra)]
    done = [done[k] + lon_product(unpack_edges(before_x[k], after_x[k]), edge_x[k]) for k in range(extra)]
    done = [lat_product(band_x[k], done[k]) for k in range(extra)]
    for k in range(extra):
        blurred[place.slot(k) + 2] = done[k]

    def lon(b):
        return [(whole, b, centre[b] + lon_product(unpack_edges(before[b], after[b]), edge[b]))]

    def lat(b):
        return [(blurred, b + own + 2, lat_product(band[b], whole[b]))]

    def residual(b):
        slot = b + own
        mu = background[b]
        for o in range(5):
            mu = mu + fold[5 * (slot + 2) + o] * blurred[slot + o]
        counts = observed[b].astype(F32)
        terms = (mu - counts * jnp.log(mu)).reshape(16, 8, 128).sum(0)
        return [(resid, b, 1.0 - counts / mu), (sums, None, terms)]

    run_stages(block // 4, 4, [(lon, 0), (lat, 1), (residual, 3)])
    loss[...] = jnp.full((1, 128), jnp.sum(sums[...]), F32)
    for d in range(place.dirs):
        for k in range(REACH):
            sent[d][k] = resid[place.start(d) + k]


def fold_kernel(en, fold, resid, back, last, first):
    block = resid.shape[0]
    place = Place(block, en)

    def fold_back(b):
        total = None
        for o in range(5):
            i = b + 2 - o
            at = jnp.clip(i, 0, block - 1)
            term = jnp.where(i == at, fold[5 * (at + place.own + 2) + o], 0.0) * resid[at]
            total = term if total is None else total + term
        ends = pack_edges(total)
        return [(back, b, total), (last, b, ends[0]), (first, b, ends[1])]

    run_stages(block // 4, 4, [(fold_back, 0)])


def border_kernel(en, fold, received, back_in, last_in, first_in, total, moved, back, last, first, passed):
    place = Place(back_in.shape[0], en)
    passed[...] = total[...] + moved[...]
    for d in range(place.dirs):
        for j in range(REACH):
            b = place.beside(d) + j
            tile = back_in[b]
            for k in range(d * REACH, (d + 1) * REACH):
                o = b + place.own - place.slot(k)
                at = jnp.clip(o + REACH, 0, 2 * REACH)
                tile = tile + jnp.where(o + REACH == at, fold[5 * (place.slot(k) + 2) + at], 0.0) * received[k]
            back[b] = tile
            last[b], first[b] = pack_edges(tile)


def centre_kernel(back, band, total, moved, out, passed):
    passed[...] = total[...] + moved[...]
    size = 8

    def some(g, carry):
        sums = [lon_product(back[size * g + i], band[size * g + i]) for i in range(size)]
        for i in range(size):
            out[size * g + i] = sums[i]
        return carry

    lax.fori_loop(0, back.shape[0] // size, some, 0)


def final_kernel(parts, centre, band, edge, before, after, exposure, total, out, passed, whole, v_out, out_sems):
    block = centre.shape[0]
    passed[...] = total[...]

    size = 8
    parts = min(parts, block // size)
    chunk = block // parts

    def copy_out(c):
        return chunk_copy(v_out, out, out_sems.at[c], c, chunk)

    def lon(b):
        return [(whole, b, centre[b] + lon_product(unpack_edges(before[b], after[b]), edge[b]))]

    def lat(b):
        return [(v_out, b, lat_product(band[b], whole[b]) * exposure[b])]

    groups, per_chunk = block // size, chunk // size

    def arrive(n, p):
        if n == 1:
            @pl.when((lax.rem(p, per_chunk) == 0) & (p > 0))
            def _():
                copy_out(lax.div(p, per_chunk) - 1).start()

    run_stages(groups, size, [(lon, 0), (lat, 1)], arrive=arrive)
    copy_out(parts - 1).start()
    for c in range(parts):
        copy_out(c).wait()


def ring(size, shift):
    return [(i, (i + shift) % size) for i in range(size)]


def grid_ring(sky, en, sky_shift, en_shift):
    return [(s * en + e, (s + sky_shift) % sky * en + (e + en_shift) % en) for s in range(sky) for e in range(en)]


def local(flux, exposure, background, observed, psf_radius, band_low, band_high, disp_raw):
    block, rows, width = flux.shape
    bins = disp_raw.shape[0]
    sky, en = lax.axis_size("sky"), lax.axis_size("en")
    shifts = [1] if en == 2 else [1, -1]
    dirs = len(shifts)
    extra = REACH * dirs
    slots = block + extra
    parts = 4

    def tiles(count, dtype=F32):
        return jax.ShapeDtypeStruct((count, rows, width), dtype)

    def edges(count):
        return jax.ShapeDtypeStruct((count, RMAX, 128), F32)

    def weights(count):
        return jax.ShapeDtypeStruct((count, 128, 256), BF16)

    def scratch(shape):
        return pltpu.VMEM(shape.shape, shape.dtype)

    lanes = jax.ShapeDtypeStruct((1, 128), F32)

    packed = pl.pallas_call(
        functools.partial(pack_kernel, parts, en),
        in_specs=[ANY] * 2,
        out_specs=[VMEM] * (3 + 3 * dirs),
        out_shape=[tiles(block), edges(block), edges(block)] + [tiles(REACH)] * dirs + [edges(REACH)] * (2 * dirs),
        scratch_shapes=[scratch(tiles(block)), scratch(tiles(block)), pltpu.SemaphoreType.DMA((2, parts))],
        compiler_params=params(12),
        name="weight_and_pack",
    )(*[pltpu.with_memory_space_constraint(array, pltpu.HBM) for array in (flux, exposure)])
    weighted, last, first = packed[:3]
    before = lax.ppermute(last, "sky", ring(sky, 1))
    after = lax.ppermute(first, "sky", ring(sky, -1))
    energies, befores, afters = [], [], []
    for d, shift in enumerate(shifts):
        energies.append(lax.ppermute(packed[3 + d], "en", ring(en, shift)))
        befores.append(lax.ppermute(packed[3 + dirs + d], ("sky", "en"), grid_ring(sky, en, 1, shift)))
        afters.append(lax.ppermute(packed[3 + 2 * dirs + d], ("sky", "en"), grid_ring(sky, en, -1, shift)))
    def joined(arrays):
        return jnp.concatenate(arrays) if dirs > 1 else arrays[0]

    energy, before_x, after_x = joined(energies), joined(befores), joined(afters)

    centre, band, edge, band_x, edge_x, fold = pl.pallas_call(
        functools.partial(weights_kernel, en),
        in_specs=[SMEM] * 4 + [VMEM],
        out_specs=[VMEM] * 5 + [SMEM],
        out_shape=[tiles(block), weights(block), weights(block), weights(extra), weights(extra), jax.ShapeDtypeStruct((5 * (slots + 4),), F32)],
        compiler_params=params(4),
        cost_estimate=cost(block, 1, block * 2**15),
        name="weights_and_centre",
    )(psf_radius, band_low, band_high, disp_raw, weighted)
    resid, total, *sent = pl.pallas_call(
        functools.partial(middle_kernel, en),
        in_specs=[SMEM] + [VMEM] * 12,
        out_specs=[VMEM] * (2 + dirs),
        out_shape=[tiles(block), lanes] + [tiles(REACH)] * dirs,
        scratch_shapes=[scratch(tiles(block)), scratch(tiles(slots + 4)), pltpu.VMEM((8, 128), F32)],
        compiler_params=params(10),
        cost_estimate=cost(block, 2, block * 2**15),
        name="blur_fold_residual",
    )(fold, centre, band, edge, before, after, background, observed, band_x, edge_x, before_x, after_x, energy)
    masks = [en] + [1 << n for n in range(en.bit_length() - 1)]
    masks += [en << n for n in range(2, sky.bit_length() - 1)] + [2 * en]

    def partner(value, mask):
        return lax.ppermute(value, ("sky", "en"), [(i, i ^ mask) for i in range(sky * en)])

    received = joined([lax.ppermute(rows, "en", ring(en, shift)) for rows, shift in zip(sent, shifts)])
    shapes = [tiles(block), edges(block), edges(block)]
    folded = pl.pallas_call(
        functools.partial(fold_kernel, en),
        in_specs=[SMEM, VMEM],
        out_specs=[VMEM] * 3,
        out_shape=shapes,
        compiler_params=params(4),
        cost_estimate=cost(block, 1),
        name="fold_back",
    )(fold, resid)
    back, last, first, total = pl.pallas_call(
        functools.partial(border_kernel, en),
        in_specs=[SMEM] + [VMEM] * 6,
        out_specs=[VMEM] * 4,
        out_shape=shapes + [lanes],
        input_output_aliases={2: 0, 3: 1, 4: 2},
        compiler_params=params(4),
        name="fold_back_border",
    )(fold, received, *folded, total, partner(total, masks[0]))

    before = lax.ppermute(last, "sky", ring(sky, 1))
    after = lax.ppermute(first, "sky", ring(sky, -1))
    centre, total = pl.pallas_call(
        centre_kernel,
        in_specs=[VMEM] * 4,
        out_specs=[VMEM] * 2,
        out_shape=[tiles(block), lanes],
        compiler_params=params(4),
        cost_estimate=cost(block, 1),
        name="back_centre",
    )(back, band, total, partner(total, masks[1]))
    for mask in masks[2:-1]:
        total = total + partner(total, mask)
    moved = partner(total, masks[-1])
    grad, passed = pl.pallas_call(
        functools.partial(final_kernel, parts),
        in_specs=[VMEM] * 7,
        out_specs=[ANY, VMEM],
        out_shape=[tiles(block), lanes],
        scratch_shapes=[scratch(tiles(block)), scratch(tiles(block)), pltpu.SemaphoreType.DMA((parts,))],
        compiler_params=params(8),
        cost_estimate=cost(block, 2),
        name="back_edges_lat_exposure",
    )(centre, band, edge, before, after, exposure, total)
    return grad, (passed + moved)[0, 0] / F32(rows * width * bins * sky)


def solution(mesh):
    placed = (P("en", None, "sky"),) * 4 + (P(),) * 4
    return jax.shard_map(local, mesh=mesh, in_specs=placed, out_specs=(P("en", None, "sky"), P()), check_vma=False)
```

```python
import functools

import jax
import jax.numpy as jnp
from jax import lax
from jax.experimental import pallas as pl
from jax.experimental.pallas import tpu as pltpu
from jax.sharding import PartitionSpec as P

RMAX = 32
REACH = 2
F32 = jnp.float32
BF16 = jnp.bfloat16
SMEM = pl.BlockSpec(memory_space=pltpu.SMEM)
ANY = pl.BlockSpec(memory_space=pl.ANY)
VMEM = pl.BlockSpec(memory_space=pltpu.VMEM)
HBM = pl.BlockSpec(memory_space=pltpu.HBM)


def split(x):
    hi = x.astype(BF16)
    return hi, (x - hi.astype(F32)).astype(BF16)


def params(mib=56):
    return pltpu.CompilerParams(vmem_limit_bytes=mib * 2**20)


def blocks(count, rows, cols):
    return pl.BlockSpec((count, rows, cols), lambda i: (i, 0, 0))


def chunk_copy(source, target, sem, c, size):
    at = pl.ds(c * size, size)
    return pltpu.make_async_copy(source.at[at], target.at[at], sem)


def run_stages(groups, size, stages, events=(), arrive=None):
    marks = {0} | {lag for _, lag in stages} | {lag + groups for _, lag in stages} | {at for at, _ in events}
    marks = sorted(marks)
    for start, stop in zip(marks, marks[1:] + [marks[-1]]):
        for at, event in events:
            if at == start:
                event()
        active = [(n, stage, lag) for n, (stage, lag) in enumerate(stages) if lag <= start < lag + groups]
        if stop == start or not active:
            continue

        def step(p, carry):
            if arrive is not None:
                for n, _, lag in active:
                    arrive(n, p - lag)
            stores = []
            for _, stage, lag in active:
                for i in range(size):
                    stores += stage((p - lag) * size + i)
            for ref, index, value in stores:
                if index is None:
                    ref[...] += value
                else:
                    ref[index] = value
            return carry

        lax.fori_loop(start, stop, step, 0)


def cost(tiles, products, transcendentals=0):
    return pl.CostEstimate(flops=tiles * products * 2 * 128 * 256 * 256, bytes_accessed=tiles * 2**16, transcendentals=transcendentals)


class Place:
    def __init__(self, block, en):
        self.block, self.en = block, en
        self.me = lax.axis_index("en")
        self.wide, self.near = 2 * REACH, REACH
        self.dirs = 1 if en == 2 else 2
        self.extra, self.nears = self.wide * self.dirs, self.near * self.dirs
        self.slots, self.bins = block + self.extra, block * en
        self.own = jnp.where(self.me == 0, 0, self.wide) if en == 2 else self.wide
        self.first_bin = self.me * block - self.own

    def start(self, d, width):
        if self.en == 2:
            return jnp.where(self.me == 0, self.block - width, 0)
        return self.block - width if d == 0 else 0

    def slot(self, k, width):
        if self.en == 2:
            return jnp.where(self.me == 0, self.block, self.wide - width) + k
        return self.wide - width + k if k < width else self.wide + self.block + k - width

    def clamp(self, g):
        return jnp.clip(g, 0, self.bins - 1)


def pack_edges(tile):
    lane = lax.broadcasted_iota(jnp.int32, (RMAX, 4 * RMAX), 1)
    last = first = None
    for q in range(4):
        rows = tile[q * RMAX:(q + 1) * RMAX]
        to_last = pltpu.roll(rows, (q + 1) * RMAX % 128, 1) if q != 3 else rows
        to_first = pltpu.roll(rows, q * RMAX, 1) if q else rows
        last = to_last if last is None else jnp.where(lane >= q * RMAX, to_last, last)
        first = to_first if first is None else jnp.where(lane >= q * RMAX, to_first, first)
    return last, first


def unpack_edges(before, after):
    lane = lax.broadcasted_iota(jnp.int32, (RMAX, 4 * RMAX), 1)
    parts = []
    for q in range(4):
        left = pltpu.roll(before, 128 - q * RMAX, 1) if q else before
        right = pltpu.roll(after, (96 - q * RMAX) % 128, 1) if q != 3 else after
        parts.append(jnp.where(lane < 64, left, right))
    return jnp.concatenate(parts, axis=0)


def twice(x):
    return jnp.concatenate([x, x], axis=0)


def lon_product(tile, weights):
    out = jnp.dot(jnp.concatenate(split(tile), axis=1), twice(weights), preferred_element_type=F32)
    return out[:, :128] + out[:, 128:]


def lat_product(weights, tile):
    out = jnp.dot(weights, twice(jnp.concatenate(split(tile), axis=1)), preferred_element_type=F32)
    return out[:, :128] + out[:, 128:]


def profile(radius, column):
    wide = jnp.full((1, 128), radius, jnp.int32).astype(F32)
    reach = wide * wide
    factor = -2.0 / reach
    lane = lax.broadcasted_iota(jnp.int32, (1, 128), 1)
    square = (lane * lane).astype(F32)
    values = jnp.where(square <= reach, jnp.exp(square * factor), 0.0)
    norm = 2.0 * jnp.sum(values, axis=1, keepdims=True) - 1.0
    root = jnp.sqrt(jnp.full((1, 128), column, F32))[:, :1]
    return factor[:, :1], 1.0 / (norm * root), reach[:, :1]


def taper_values(diff, ok, factor, scale, reach):
    square = diff * diff
    return jnp.where((square <= reach) & ok, jnp.exp(square * factor) * scale, 0.0)


def pack_kernel(parts, en, flux, exposure, background, observed, weighted, last, first, *rest):
    place = Place(flux.shape[0], en)
    dirs, wide, near, block = place.dirs, place.wide, place.near, place.block
    sent, last_x, first_x = rest[:dirs], rest[dirs:2 * dirs], rest[2 * dirs:3 * dirs]
    v_flux, v_exposure, v_observed, sems, near_sems = rest[3 * dirs:]
    chunk = block // parts

    def arrivals(c):
        return [chunk_copy(a, b, sems.at[n, c], c, chunk) for n, (a, b) in enumerate(((flux, v_flux), (exposure, v_exposure)))]

    def near_arrivals(d):
        at = pl.ds(place.start(d, near), near)
        return [
            pltpu.make_async_copy(background.at[at], sent[d].at[pl.ds(wide, near)], near_sems.at[d, 0]),
            pltpu.make_async_copy(observed.at[at], v_observed.at[d], near_sems.at[d, 1]),
        ]

    for c in range(parts):
        for copy in arrivals(c):
            copy.start()
    for d in range(dirs):
        for copy in near_arrivals(d):
            copy.start()
    size = 4 if chunk % 4 == 0 else 2
    for c in range(parts):
        for copy in arrivals(c):
            copy.wait()

        def some(g, carry):
            tiles = [v_flux[size * g + i] * v_exposure[size * g + i] for i in range(size)]
            packed = [pack_edges(tile) for tile in tiles]
            for i in range(size):
                weighted[size * g + i] = tiles[i]
                last[size * g + i], first[size * g + i] = packed[i]
            return carry

        lax.fori_loop(c * chunk // size, (c + 1) * chunk // size, some, 0)
    for d in range(dirs):
        for copy in near_arrivals(d):
            copy.wait()
        start = place.start(d, wide)
        for k in range(wide):
            sent[d][k] = weighted[start + k]
            last_x[d][k] = last[start + k]
            first_x[d][k] = first[start + k]
        for k in range(near):
            sent[d][wide + near + k] = v_observed[d, k].astype(F32)


def weights_kernel(en, radius, low, high, disp, weighted, background, observed, centre, band, edge, band_x, edge_x, fold,
                   near_background, near_observed, sems):
    fetches = [
        pltpu.make_async_copy(background, near_background, sems.at[0]),
        pltpu.make_async_copy(observed, near_observed, sems.at[1]),
    ]
    for fetch in fetches:
        fetch.start()
    block = weighted.shape[0]
    place = Place(block, en)
    row = lax.broadcasted_iota(jnp.int32, (128, 128), 0)
    col = lax.broadcasted_iota(jnp.int32, (128, 128), 1)
    near = (row - col).astype(F32)
    far = jnp.where(row < 64, row - col - RMAX, row - col + RMAX).astype(F32)
    held = (row < RMAX) | (row >= 128 - RMAX)
    always = row >= 0

    def weight(i, j):
        at, to = place.clamp(i), place.clamp(j)
        inside = (i == at) & (j == to) & (low[at] <= j - i) & (j - i <= high[at])
        return jnp.where(inside, disp[at, to], 0.0)

    def make(g):
        for o in range(-REACH, REACH + 1):
            fold[5 * (g - place.first_bin + REACH) + o + REACH] = weight(g, g + o)
        column = weight(g, g)
        for o in (-2, -1, 1, 2):
            column = column + weight(g - o, g)
        numbers = profile(radius[place.clamp(g)], jnp.where(column > 0.0, column, 1.0))
        return tuple(
            jnp.concatenate(split(taper_values(diff, ok, *numbers)), axis=1) for diff, ok in ((near, always), (far, held))
        )

    for s in (0, 1, place.slots + 2, place.slots + 3):
        for o in range(5):
            fold[5 * s + o] = 0.0

    def some(b):
        made = make(place.me * block + b)
        return [(band, b, made[0]), (edge, b, made[1])]

    def lon(b):
        return [(centre, b, lon_product(weighted[b], band[b]))]

    run_stages(block // 4, 4, [(some, 0), (lon, 1)])
    for k in range(place.extra):
        band_x[k], edge_x[k] = make(place.first_bin + place.slot(k, place.wide))
    for fetch in fetches:
        fetch.wait()


def middle_kernel(en, fold, centre, band, edge, before, after, background, observed, band_x, edge_x, before_x, after_x, energy,
                  back, last, first, loss, whole, blurred, resid, sums):
    block = centre.shape[0]
    place = Place(block, en)
    extra, nears, slots, own = place.extra, place.nears, place.slots, place.own
    zero = jnp.zeros((128, 128), F32)
    for s in (0, 1, slots + 2, slots + 3):
        blurred[s] = zero
        resid[s] = zero
    sums[...] = jnp.zeros((8, 128), F32)

    done = [lon_product(energy[k], band_x[k]) for k in range(extra)]
    done = [done[k] + lon_product(unpack_edges(before_x[k], after_x[k]), edge_x[k]) for k in range(extra)]
    done = [lat_product(band_x[k], done[k]) for k in range(extra)]
    for k in range(extra):
        blurred[place.slot(k, place.wide) + 2] = done[k]

    def lon(b):
        return [(whole, b, centre[b] + lon_product(unpack_edges(before[b], after[b]), edge[b]))]

    def lat(b):
        return [(blurred, b + own + 2, lat_product(band[b], whole[b]))]

    def mean_counts(slot, ground):
        mu = ground
        for o in range(5):
            mu = mu + fold[5 * (slot + 2) + o] * blurred[slot + o]
        return mu

    def residual(b):
        slot = b + own
        mu = mean_counts(slot, background[b])
        counts = observed[b].astype(F32)
        terms = (mu - counts * jnp.log(mu)).reshape(16, 8, 128).sum(0)
        return [(resid, slot + 2, 1.0 - counts / mu), (sums, None, terms)]

    def extra_residuals():
        values = []
        for k in range(nears):
            mu = mean_counts(place.slot(k, place.near), energy[extra + k])
            values.append(1.0 - energy[extra + nears + k] / mu)
        for k in range(nears):
            resid[place.slot(k, place.near) + 2] = values[k]

    def fold_back(b):
        slot = b + own
        total = None
        for o in range(5):
            term = fold[5 * (slot + 4 - o) + o] * resid[slot + 4 - o]
            total = term if total is None else total + term
        ends = pack_edges(total)
        return [(back, b, total), (last, b, ends[0]), (first, b, ends[1])]

    size = 8
    groups = block // size
    run_stages(
        groups, size, [(lon, 0), (lat, 1), (residual, 3), (fold_back, 5)],
        events=[(3, extra_residuals), (groups + 1, extra_residuals)],
    )
    loss[...] = jnp.full((1, 128), jnp.sum(sums[...]), F32)


def centre_kernel(back, band, total, out, passed):
    passed[...] = total[...]
    size = 8

    def some(g, carry):
        sums = [lon_product(back[size * g + i], band[size * g + i]) for i in range(size)]
        for i in range(size):
            out[size * g + i] = sums[i]
        return carry

    lax.fori_loop(0, back.shape[0] // size, some, 0)


def final_kernel(part, centre, band, edge, before, after, exposure, total, *rest):
    out, passed, whole, v_out, out_sems = rest[part:]
    block = centre.shape[0]
    size = min(8, block // 2)
    groups = block // 2 // size
    first = part * (block // 2)
    passed[...] = total[...]

    def copy_out(g):
        return pltpu.make_async_copy(v_out.at[pl.ds(g * size, size)], out.at[pl.ds(first + g * size, size)], out_sems.at[g])

    def lon(i):
        b = first + i
        return [(whole, i, centre[b] + lon_product(unpack_edges(before[b], after[b]), edge[b]))]

    def lat(i):
        return [(v_out, i, lat_product(band[first + i], whole[i]) * exposure[first + i])]

    run_stages(groups, size, [(lon, 0), (lat, 1)])
    for g in range(groups):
        copy_out(g).start()
    for g in range(groups):
        copy_out(g).wait()


def ring(size, shift):
    return [(i, (i + shift) % size) for i in range(size)]


def grid_ring(sky, en, sky_shift, en_shift):
    return [(s * en + e, (s + sky_shift) % sky * en + (e + en_shift) % en) for s in range(sky) for e in range(en)]


def local(flux, exposure, background, observed, psf_radius, band_low, band_high, disp_raw):
    block, rows, width = flux.shape
    bins = disp_raw.shape[0]
    sky, en = lax.axis_size("sky"), lax.axis_size("en")
    wide, near = 2 * REACH, REACH
    shifts = [1] if en == 2 else [1, -1]
    dirs = len(shifts)
    extra, nears = wide * dirs, near * dirs
    slots = block + extra
    parts = 4

    def tiles(count, dtype=F32):
        return jax.ShapeDtypeStruct((count, rows, width), dtype)

    def edges(count):
        return jax.ShapeDtypeStruct((count, RMAX, 128), F32)

    def weights(count):
        return jax.ShapeDtypeStruct((count, 128, 256), BF16)

    def scratch(shape):
        return pltpu.VMEM(shape.shape, shape.dtype)

    lanes = jax.ShapeDtypeStruct((1, 128), F32)

    flux, exposure_in, background, observed = [
        pltpu.with_memory_space_constraint(array, pltpu.HBM) for array in (flux, exposure, background, observed)
    ]
    packed = pl.pallas_call(
        functools.partial(pack_kernel, parts, en),
        in_specs=[HBM] * 4,
        out_specs=[VMEM] * (3 + 3 * dirs),
        out_shape=[tiles(block), edges(block), edges(block)] + [tiles(wide + 2 * near)] * dirs + [edges(wide)] * (2 * dirs),
        scratch_shapes=[
            scratch(tiles(block)), scratch(tiles(block)), pltpu.VMEM((dirs, near, rows, width), jnp.int32),
            pltpu.SemaphoreType.DMA((2, parts)), pltpu.SemaphoreType.DMA((dirs, 2)),
        ],
        compiler_params=params(12),
        name="weight_and_pack",
    )(flux, exposure_in, background, observed)
    weighted, last, first = packed[:3]
    before = lax.ppermute(last, "sky", ring(sky, 1))
    after = lax.ppermute(first, "sky", ring(sky, -1))
    energies, befores, afters = [], [], []
    for d, shift in enumerate(shifts):
        energies.append(lax.ppermute(packed[3 + d], "en", ring(en, shift)))
        befores.append(lax.ppermute(packed[3 + dirs + d], ("sky", "en"), grid_ring(sky, en, 1, shift)))
        afters.append(lax.ppermute(packed[3 + 2 * dirs + d], ("sky", "en"), grid_ring(sky, en, -1, shift)))
    if dirs > 1:
        energy = jnp.concatenate(
            [e[:wide] for e in energies] + [e[wide:wide + near] for e in energies] + [e[wide + near:] for e in energies]
        )
        before_x, after_x = jnp.concatenate(befores), jnp.concatenate(afters)
    else:
        energy, before_x, after_x = energies[0], befores[0], afters[0]

    centre, band, edge, band_x, edge_x, fold, background, observed = pl.pallas_call(
        functools.partial(weights_kernel, en),
        in_specs=[SMEM] * 4 + [VMEM] + [ANY] * 2,
        out_specs=[VMEM] * 5 + [SMEM] + [VMEM] * 2,
        out_shape=[tiles(block), weights(block), weights(block), weights(extra), weights(extra), jax.ShapeDtypeStruct((5 * (slots + 4),), F32), tiles(block), tiles(block, jnp.int32)],
        scratch_shapes=[pltpu.SemaphoreType.DMA((2,))],
        compiler_params=params(4),
        cost_estimate=cost(block, 1, block * 2**15),
        name="weights_and_centre",
    )(psf_radius, band_low, band_high, disp_raw, weighted, background, observed)
    back, last, first, total = pl.pallas_call(
        functools.partial(middle_kernel, en),
        in_specs=[SMEM] + [VMEM] * 12,
        out_specs=[VMEM] * 4,
        out_shape=[tiles(block), edges(block), edges(block), lanes],
        scratch_shapes=[scratch(tiles(block)), scratch(tiles(slots + 4)), scratch(tiles(slots + 4)), pltpu.VMEM((8, 128), F32)],
        compiler_params=params(14),
        cost_estimate=cost(block, 2, block * 2**15),
        name="blur_fold_residual_fold",
    )(fold, centre, band, edge, before, after, background, observed, band_x, edge_x, before_x, after_x, energy)

    before = lax.ppermute(last, "sky", ring(sky, 1))
    after = lax.ppermute(first, "sky", ring(sky, -1))
    masks = [en] + [1 << n for n in range(en.bit_length() - 1)]
    masks += [en << n for n in range(2, sky.bit_length() - 1)] + [2 * en]

    def partner(value, mask):
        return lax.ppermute(value, ("sky", "en"), [(i, i ^ mask) for i in range(sky * en)])

    moved = partner(total, masks[0])
    centre, total = pl.pallas_call(
        centre_kernel,
        in_specs=[VMEM] * 3,
        out_specs=[VMEM] * 2,
        out_shape=[tiles(block), lanes],
        compiler_params=params(4),
        cost_estimate=cost(block, 1),
        name="back_centre",
    )(back, band, total)
    total = total + moved
    for mask in masks[1:-2]:
        total = total + partner(total, mask)
    grad = []
    for part, mask in enumerate(masks[-2:]):
        moved = partner(total, mask)
        *grad, passed = pl.pallas_call(
            functools.partial(final_kernel, part),
            in_specs=[VMEM] * 7 + [ANY] * part,
            out_specs=[ANY, VMEM],
            out_shape=[tiles(block), lanes],
            scratch_shapes=[scratch(tiles(block // 2)), scratch(tiles(block // 2)), pltpu.SemaphoreType.DMA((block // 2,))],
            input_output_aliases={7: 0} if part else {},
            compiler_params=params(8),
            cost_estimate=cost(block // 2, 2),
            name="back_edges_lat_exposure",
        )(centre, band, edge, before, after, exposure, total, *grad)
        total = passed + moved
    return grad[0], total[0, 0] / F32(rows * width * bins * sky)


def solution(mesh):
    placed = (P("en", None, "sky"),) * 4 + (P(),) * 4
    return jax.shard_map(local, mesh=mesh, in_specs=placed, out_specs=(P("en", None, "sky"), P()), check_vma=False)
```

```python
import functools

import jax
import jax.numpy as jnp
from jax import lax
from jax.experimental import pallas as pl
from jax.experimental.pallas import tpu as pltpu
from jax.sharding import PartitionSpec as P

RMAX = 32
REACH = 2
F32 = jnp.float32
BF16 = jnp.bfloat16
SMEM = pl.BlockSpec(memory_space=pltpu.SMEM)
ANY = pl.BlockSpec(memory_space=pl.ANY)
VMEM = pl.BlockSpec(memory_space=pltpu.VMEM)
HBM = pl.BlockSpec(memory_space=pltpu.HBM)


def split(x):
    hi = x.astype(BF16)
    return hi, (x - hi.astype(F32)).astype(BF16)


def params(mib=56):
    return pltpu.CompilerParams(vmem_limit_bytes=mib * 2**20)


def blocks(count, rows, cols):
    return pl.BlockSpec((count, rows, cols), lambda i: (i, 0, 0))


def chunk_copy(source, target, sem, c, size):
    at = pl.ds(c * size, size)
    return pltpu.make_async_copy(source.at[at], target.at[at], sem)


def run_stages(groups, size, stages, events=(), arrive=None):
    stages = [(*stage, groups)[:3] for stage in stages]
    marks = {0} | {lag for _, lag, _ in stages} | {lag + count for _, lag, count in stages} | {at for at, _ in events}
    marks = sorted(marks)
    for start, stop in zip(marks, marks[1:] + [marks[-1]]):
        for at, event in events:
            if at == start:
                event()
        active = [(n, stage, lag) for n, (stage, lag, count) in enumerate(stages) if lag <= start < lag + count]
        if stop == start or not active:
            continue

        def step(p, carry):
            if arrive is not None:
                for n, _, lag in active:
                    arrive(n, p - lag)
            stores = []
            for _, stage, lag in active:
                for i in range(size):
                    stores += stage((p - lag) * size + i)
            for ref, index, value in stores:
                if index is None:
                    ref[...] += value
                else:
                    ref[index] = value
            return carry

        lax.fori_loop(start, stop, step, 0)


def cost(tiles, products, transcendentals=0):
    return pl.CostEstimate(flops=tiles * products * 2 * 128 * 256 * 256, bytes_accessed=tiles * 2**16, transcendentals=transcendentals)


class Place:
    def __init__(self, block, en):
        self.block, self.en = block, en
        self.me = lax.axis_index("en")
        self.wide, self.near = 2 * REACH, REACH
        self.dirs = 1 if en == 2 else 2
        self.extra, self.nears = self.wide * self.dirs, self.near * self.dirs
        self.slots, self.bins = block + self.extra, block * en
        self.own = jnp.where(self.me == 0, 0, self.wide) if en == 2 else self.wide
        self.first_bin = self.me * block - self.own

    def start(self, d, width):
        if self.en == 2:
            return jnp.where(self.me == 0, self.block - width, 0)
        return self.block - width if d == 0 else 0

    def slot(self, k, width):
        if self.en == 2:
            return jnp.where(self.me == 0, self.block, self.wide - width) + k
        return self.wide - width + k if k < width else self.wide + self.block + k - width

    def clamp(self, g):
        return jnp.clip(g, 0, self.bins - 1)


def pack_edges(tile):
    lane = lax.broadcasted_iota(jnp.int32, (RMAX, 4 * RMAX), 1)
    last = first = None
    for q in range(4):
        rows = tile[q * RMAX:(q + 1) * RMAX]
        to_last = pltpu.roll(rows, (q + 1) * RMAX % 128, 1) if q != 3 else rows
        to_first = pltpu.roll(rows, q * RMAX, 1) if q else rows
        last = to_last if last is None else jnp.where(lane >= q * RMAX, to_last, last)
        first = to_first if first is None else jnp.where(lane >= q * RMAX, to_first, first)
    return last, first


def unpack_edges(before, after):
    lane = lax.broadcasted_iota(jnp.int32, (RMAX, 4 * RMAX), 1)
    parts = []
    for q in range(4):
        left = pltpu.roll(before, 128 - q * RMAX, 1) if q else before
        right = pltpu.roll(after, (96 - q * RMAX) % 128, 1) if q != 3 else after
        parts.append(jnp.where(lane < 64, left, right))
    return jnp.concatenate(parts, axis=0)


def twice(x):
    return jnp.concatenate([x, x], axis=0)


def lon_product(tile, weights):
    out = jnp.dot(jnp.concatenate(split(tile), axis=1), twice(weights), preferred_element_type=F32)
    return out[:, :128] + out[:, 128:]


def lat_product(weights, tile):
    out = jnp.dot(weights, twice(jnp.concatenate(split(tile), axis=1)), preferred_element_type=F32)
    return out[:, :128] + out[:, 128:]


def profile(radius, column):
    wide = jnp.full((1, 128), radius, jnp.int32).astype(F32)
    reach = wide * wide
    factor = -2.0 / reach
    lane = lax.broadcasted_iota(jnp.int32, (1, 128), 1)
    square = (lane * lane).astype(F32)
    values = jnp.where(square <= reach, jnp.exp(square * factor), 0.0)
    norm = 2.0 * jnp.sum(values, axis=1, keepdims=True) - 1.0
    root = jnp.sqrt(jnp.full((1, 128), column, F32))[:, :1]
    return factor[:, :1], 1.0 / (norm * root), reach[:, :1]


def taper_values(diff, ok, factor, scale, reach):
    square = diff * diff
    return jnp.where((square <= reach) & ok, jnp.exp(square * factor) * scale, 0.0)


def pack_kernel(part, en, flux, exposure, *rest):
    block = flux.shape[0]
    half, place = block // 2, Place(block, en)
    dirs, wide, near = (place.dirs if part else 0), place.wide, place.near
    counts, rest = rest[:2 * part], rest[3 * part:]
    weighted, last, first = rest[:3]
    sent, last_x, first_x = rest[3:3 + dirs], rest[3 + dirs:3 + 2 * dirs], rest[3 + 2 * dirs:3 + 3 * dirs]
    v_flux, v_exposure, sems, *more = rest[3 + 3 * dirs:]
    size = min(4, half)
    parts = max(half // 8, 1)
    chunk = half // parts

    def arrivals(c):
        at, to = pl.ds(part * half + c * chunk, chunk), pl.ds(c * chunk, chunk)
        return [
            pltpu.make_async_copy(source.at[at], target.at[to], sems.at[n, c])
            for n, (source, target) in enumerate(((flux, v_flux), (exposure, v_exposure)))
        ]

    copies = []
    for c in range(parts):
        for copy in arrivals(c):
            copy.start()
    if part:
        x_flux, x_exposure, x_observed, near_sems = more
        for d in range(dirs):
            at, at_near = pl.ds(place.start(d, wide), wide), pl.ds(place.start(d, near), near)
            pairs = (
                (flux.at[at], x_flux.at[d]), (exposure.at[at], x_exposure.at[d]),
                (counts[0].at[at_near], sent[d].at[pl.ds(wide, near)]), (counts[1].at[at_near], x_observed.at[d]),
            )
            copies += [pltpu.make_async_copy(source, target, near_sems.at[d, n]) for n, (source, target) in enumerate(pairs)]
    for copy in copies:
        copy.start()
    for c in range(parts):
        for copy in arrivals(c):
            copy.wait()

        def some(g, carry):
            tiles = [v_flux[size * g + i] * v_exposure[size * g + i] for i in range(size)]
            packed = [pack_edges(tile) for tile in tiles]
            for i in range(size):
                weighted[size * g + i] = tiles[i]
                last[size * g + i], first[size * g + i] = packed[i]
            return carry

        lax.fori_loop(c * chunk // size, (c + 1) * chunk // size, some, 0)
    for copy in copies:
        copy.wait()
    for d in range(dirs):
        tiles = [x_flux[d, k] * x_exposure[d, k] for k in range(wide)]
        packed = [pack_edges(tile) for tile in tiles]
        for k in range(wide):
            sent[d][k] = tiles[k]
            last_x[d][k], first_x[d][k] = packed[k]
        for k in range(near):
            sent[d][wide + near + k] = x_observed[d, k].astype(F32)


def weights_kernel(en, radius, low, high, disp, weighted_a, weighted_b, background, observed, *rest):
    through = (len(rest) - 9) // 2
    centre, band, edge, band_x, edge_x, fold, near_background, near_observed = rest[through:through + 8]
    sems = rest[-1]
    fetches = [
        pltpu.make_async_copy(background, near_background, sems.at[0]),
        pltpu.make_async_copy(observed, near_observed, sems.at[1]),
    ]
    for fetch in fetches:
        fetch.start()
    half = weighted_a.shape[0]
    block = 2 * half
    place = Place(block, en)
    row = lax.broadcasted_iota(jnp.int32, (128, 128), 0)
    col = lax.broadcasted_iota(jnp.int32, (128, 128), 1)
    near = (row - col).astype(F32)
    far = jnp.where(row < 64, row - col - RMAX, row - col + RMAX).astype(F32)
    held = (row < RMAX) | (row >= 128 - RMAX)
    always = row >= 0

    def weight(i, j):
        at, to = place.clamp(i), place.clamp(j)
        inside = (i == at) & (j == to) & (low[at] <= j - i) & (j - i <= high[at])
        return jnp.where(inside, disp[at, to], 0.0)

    def make(g):
        for o in range(-REACH, REACH + 1):
            fold[5 * (g - place.first_bin + REACH) + o + REACH] = weight(g, g + o)
        column = weight(g, g)
        for o in (-2, -1, 1, 2):
            column = column + weight(g - o, g)
        numbers = profile(radius[place.clamp(g)], jnp.where(column > 0.0, column, 1.0))
        return tuple(
            jnp.concatenate(split(taper_values(diff, ok, *numbers)), axis=1) for diff, ok in ((near, always), (far, held))
        )

    for s in (0, 1, place.slots + 2, place.slots + 3):
        for o in range(5):
            fold[5 * s + o] = 0.0

    def some(b):
        made = make(place.me * block + b)
        return [(band, b, made[0]), (edge, b, made[1])]

    for weighted, start in ((weighted_a, 0), (weighted_b, half)):
        def lon(i, weighted=weighted, start=start):
            return [(centre, start + i, lon_product(weighted[i], band[start + i]))]

        run_stages(half // 4, 4, [(lambda i, start=start: some(start + i), 0), (lon, 1)])
    for k in range(place.extra):
        band_x[k], edge_x[k] = make(place.first_bin + place.slot(k, place.wide))
    for fetch in fetches:
        fetch.wait()


def blur_kernel(centre, band, edge, before, after, blurred, whole):
    def lon(b):
        return [(whole, b, centre[b] + lon_product(unpack_edges(before[b], after[b]), edge[b]))]

    def lat(b):
        return [(blurred, b, lat_product(band[b], whole[b]))]

    size = min(8, before.shape[0])
    run_stages(before.shape[0] // size, size, [(lon, 0), (lat, 1)])


def middle_kernel(en, fold, centre, band, edge, blurred_a, before, after, background, observed, band_x, edge_x, before_x, after_x, energy,
                  back, last_a, first_a, last_b, first_b, loss, whole, blurred, resid, ends, sums):
    half = before.shape[0]
    block = 2 * half
    place = Place(block, en)
    extra, nears, slots, own = place.extra, place.nears, place.slots, place.own
    zero = jnp.zeros((128, 128), F32)
    for s in (0, 1, slots + 2, slots + 3):
        blurred[s] = zero
        resid[s] = zero
    sums[...] = jnp.zeros((8, 128), F32)
    blurred[pl.ds(own + 2, half)] = blurred_a[...]

    done = [lon_product(energy[k], band_x[k]) for k in range(extra)]
    done = [done[k] + lon_product(unpack_edges(before_x[k], after_x[k]), edge_x[k]) for k in range(extra)]
    done = [lat_product(band_x[k], done[k]) for k in range(extra)]
    for k in range(extra):
        blurred[place.slot(k, place.wide) + 2] = done[k]

    def lon(i):
        return [(whole, i, centre[half + i] + lon_product(unpack_edges(before[i], after[i]), edge[half + i]))]

    def lat(i):
        return [(blurred, half + i + own + 2, lat_product(band[half + i], whole[i]))]

    def mean_counts(slot, ground):
        mu = ground
        for o in range(5):
            mu = mu + fold[5 * (slot + 2) + o] * blurred[slot + o]
        return mu

    def residual(b):
        slot = b + own
        mu = mean_counts(slot, background[b])
        counts = observed[b].astype(F32)
        terms = (mu - counts * jnp.log(mu)).reshape(16, 8, 128).sum(0)
        return [(resid, slot + 2, 1.0 - counts / mu), (sums, None, terms)]

    def extra_residuals():
        values = []
        for k in range(nears):
            mu = mean_counts(place.slot(k, place.near), energy[extra + k])
            values.append(1.0 - energy[extra + nears + k] / mu)
        for k in range(nears):
            resid[place.slot(k, place.near) + 2] = values[k]

    def fold_back(b):
        slot = b + own
        total = None
        for o in range(5):
            term = fold[5 * (slot + 4 - o) + o] * resid[slot + 4 - o]
            total = term if total is None else total + term
        packed = pack_edges(total)
        return [(back, b, total), (ends, b, jnp.concatenate(packed, axis=0))]

    size = 4
    groups = half // size
    run_stages(
        groups, size,
        [(lon, 0, groups), (lat, 1, groups), (residual, 3 - groups if groups < 3 else 0, 2 * groups), (fold_back, 5 - groups if groups < 3 else 2, 2 * groups)],
        events=[(0, extra_residuals), (groups + 1, extra_residuals)],
    )
    for start, last, first in ((0, last_a, first_a), (half, last_b, first_b)):
        last[...] = ends[pl.ds(start, half), :RMAX]
        first[...] = ends[pl.ds(start, half), RMAX:]
    loss[...] = jnp.full((1, 128), jnp.sum(sums[...]), F32)


def centre_kernel(back, band, total, last_in, first_in, out, passed, last, first):
    del last_in, first_in, last, first
    passed[...] = total[...]
    size = 8

    def some(g, carry):
        sums = [lon_product(back[size * g + i], band[size * g + i]) for i in range(size)]
        for i in range(size):
            out[size * g + i] = sums[i]
        return carry

    lax.fori_loop(0, back.shape[0] // size, some, 0)


def final_kernel(part, centre, band, edge, before, after, exposure, total, *rest):
    out, passed, whole, v_out, out_sems = rest[part:]
    block = centre.shape[0]
    size = min(8, block // 2)
    groups = block // 2 // size
    first = part * (block // 2)
    passed[...] = total[...]

    def copy_out(g):
        return pltpu.make_async_copy(v_out.at[pl.ds(g * size, size)], out.at[pl.ds(first + g * size, size)], out_sems.at[g])

    def lon(i):
        b = first + i
        return [(whole, i, centre[b] + lon_product(unpack_edges(before[i], after[i]), edge[b]))]

    def lat(i):
        return [(v_out, i, lat_product(band[first + i], whole[i]) * exposure[first + i])]

    run_stages(groups, size, [(lon, 0), (lat, 1)])
    for g in range(groups):
        copy_out(g).start()
    for g in range(groups):
        copy_out(g).wait()


def ring(size, shift):
    return [(i, (i + shift) % size) for i in range(size)]


def grid_ring(sky, en, sky_shift, en_shift):
    return [(s * en + e, (s + sky_shift) % sky * en + (e + en_shift) % en) for s in range(sky) for e in range(en)]


def local(flux, exposure, background, observed, psf_radius, band_low, band_high, disp_raw):
    block, rows, width = flux.shape
    bins = disp_raw.shape[0]
    sky, en = lax.axis_size("sky"), lax.axis_size("en")
    wide, near = 2 * REACH, REACH
    shifts = [1] if en == 2 else [1, -1]
    dirs = len(shifts)
    extra, nears = wide * dirs, near * dirs
    slots = block + extra
    parts = 4

    def tiles(count, dtype=F32):
        return jax.ShapeDtypeStruct((count, rows, width), dtype)

    def edges(count):
        return jax.ShapeDtypeStruct((count, RMAX, 128), F32)

    def weights(count):
        return jax.ShapeDtypeStruct((count, 128, 256), BF16)

    def scratch(shape):
        return pltpu.VMEM(shape.shape, shape.dtype)

    lanes = jax.ShapeDtypeStruct((1, 128), F32)

    flux, exposure_in, background, observed = [
        pltpu.with_memory_space_constraint(array, pltpu.HBM) for array in (flux, exposure, background, observed)
    ]
    half = block // 2

    def pack(part, *earlier):
        more = [
            pltpu.VMEM((dirs, wide, rows, width), F32), pltpu.VMEM((dirs, wide, rows, width), F32),
            pltpu.VMEM((dirs, near, rows, width), jnp.int32), pltpu.SemaphoreType.DMA((dirs, 4)),
        ]
        shapes = [tiles(half), edges(half), edges(half)]
        if part:
            shapes += [tiles(wide + 2 * near)] * dirs + [edges(wide)] * (2 * dirs)
        return pl.pallas_call(
            functools.partial(pack_kernel, part, en),
            in_specs=[ANY] * (2 + 3 * part),
            out_specs=[VMEM] * len(shapes),
            out_shape=shapes,
            scratch_shapes=[scratch(tiles(half)), scratch(tiles(half)), pltpu.SemaphoreType.DMA((2, half))] + more * part,
            compiler_params=params(12),
            name="weight_and_pack",
        )(flux, exposure_in, *[background, observed] * part, *earlier)

    def halo(last, first):
        return lax.ppermute(last, "sky", ring(sky, 1)), lax.ppermute(first, "sky", ring(sky, -1))

    weighted_a, last, first = pack(0)
    halo_a = halo(last, first)
    weighted_b, last, first, *packed = pack(1, first)
    halo_b = halo(last, first)
    centre, band, edge, band_x, edge_x, fold, near_background, near_observed = rest[through:through + 8]
    sems = rest[-1]
    fetches = [
        pltpu.make_async_copy(background, near_background, sems.at[0]),
        pltpu.make_async_copy(observed, near_observed, sems.at[1]),
    ]
    for fetch in fetches:
        fetch.start()
    half = weighted_a.shape[0]
    block = 2 * half
    place = Place(block, en)
    row = lax.broadcasted_iota(jnp.int32, (128, 128), 0)
    col = lax.broadcasted_iota(jnp.int32, (128, 128), 1)
    near = (row - col).astype(F32)
    far = jnp.where(row < 64, row - col - RMAX, row - col + RMAX).astype(F32)
    held = (row < RMAX) | (row >= 128 - RMAX)
    always = row >= 0

    def weight(i, j):
        at, to = place.clamp(i), place.clamp(j)
        inside = (i == at) & (j == to) & (low[at] <= j - i) & (j - i <= high[at])
        return jnp.where(inside, disp[at, to], 0.0)

    def make(g):
        for o in range(-REACH, REACH + 1):
            fold[5 * (g - place.first_bin + REACH) + o + REACH] = weight(g, g + o)
        column = weight(g, g)
        for o in (-2, -1, 1, 2):
            column = column + weight(g - o, g)
        numbers = profile(radius[place.clamp(g)], jnp.where(column > 0.0, column, 1.0))
        return tuple(
            jnp.concatenate(split(taper_values(diff, ok, *numbers)), axis=1) for diff, ok in ((near, always), (far, held))
        )

    for s in (0, 1, place.slots + 2, place.slots + 3):
        for o in range(5):
            fold[5 * s + o] = 0.0

    def some(b):
        made = make(place.me * block + b)
        return [(band, b, made[0]), (edge, b, made[1])]

    for weighted, start in ((weighted_a, 0), (weighted_b, half)):
        def lon(i, weighted=weighted, start=start):
            return [(centre, start + i, lon_product(weighted[i], band[start + i]))]

        run_stages(half // 4, 4, [(lambda i, start=start: some(start + i), 0), (lon, 1)])
    for k in range(place.extra):
        band_x[k], edge_x[k] = make(place.first_bin + place.slot(k, place.wide))
    for fetch in fetches:
        fetch.wait()


def blur_kernel(centre, band, edge, before, after, blurred, whole):
    def lon(b):
        return [(whole, b, centre[b] + lon_product(unpack_edges(before[b], after[b]), edge[b]))]

    def lat(b):
        return [(blurred, b, lat_product(band[b], whole[b]))]

    size = min(8, before.shape[0])
    run_stages(before.shape[0] // size, size, [(lon, 0), (lat, 1)])


def middle_kernel(en, fold, centre, band, edge, blurred_a, before, after, background, observed, band_x, edge_x, before_x, after_x, energy,
                  back, last_a, first_a, last_b, first_b, loss, whole, blurred, resid, ends, sums):
    half = before.shape[0]
    block = 2 * half
    place = Place(block, en)
    extra, nears, slots, own = place.extra, place.nears, place.slots, place.own
    zero = jnp.zeros((128, 128), F32)
    for s in (0, 1, slots + 2, slots + 3):
        blurred[s] = zero
        resid[s] = zero
    sums[...] = jnp.zeros((8, 128), F32)
    blurred[pl.ds(own + 2, half)] = blurred_a[...]

    done = [lon_product(energy[k], band_x[k]) for k in range(extra)]
    done = [done[k] + lon_product(unpack_edges(before_x[k], after_x[k]), edge_x[k]) for k in range(extra)]
    done = [lat_product(band_x[k], done[k]) for k in range(extra)]
    for k in range(extra):
        blurred[place.slot(k, place.wide) + 2] = done[k]

    def lon(i):
        return [(whole, i, centre[half + i] + lon_product(unpack_edges(before[i], after[i]), edge[half + i]))]

    def lat(i):
        return [(blurred, half + i + own + 2, lat_product(band[half + i], whole[i]))]

    def mean_counts(slot, ground):
        mu = ground
        for o in range(5):
            mu = mu + fold[5 * (slot + 2) + o] * blurred[slot + o]
        return mu

    def residual(b):
        slot = b + own
        mu = mean_counts(slot, background[b])
        counts = observed[b].astype(F32)
        terms = (mu - counts * jnp.log(mu)).reshape(16, 8, 128).sum(0)
        return [(resid, slot + 2, 1.0 - counts / mu), (sums, None, terms)]

    def extra_residuals():
        values = []
        for k in range(nears):
            mu = mean_counts(place.slot(k, place.near), energy[extra + k])
            values.append(1.0 - energy[extra + nears + k] / mu)
        for k in range(nears):
            resid[place.slot(k, place.near) + 2] = values[k]

    def fold_back(b):
        slot = b + own
        total = None
        for o in range(5):
            term = fold[5 * (slot + 4 - o) + o] * resid[slot + 4 - o]
            total = term if total is None else total + term
        packed = pack_edges(total)
        return [(back, b, total), (ends, b, jnp.concatenate(packed, axis=0))]

    size = 4
    groups = half // size
    run_stages(
        groups, size,
        [(lon, 0, groups), (lat, 1, groups), (residual, 3 - groups if groups < 3 else 0, 2 * groups), (fold_back, 5 - groups if groups < 3 else 2, 2 * groups)],
        events=[(0, extra_residuals), (groups + 1, extra_residuals)],
    )
    for start, last, first in ((0, last_a, first_a), (half, last_b, first_b)):
        last[...] = ends[pl.ds(start, half), :RMAX]
        first[...] = ends[pl.ds(start, half), RMAX:]
    loss[...] = jnp.full((1, 128), jnp.sum(sums[...]), F32)


def centre_kernel(back, band, total, last_in, first_in, out, passed, last, first):
    del last_in, first_in, last, first
    passed[...] = total[...]
    size = 8

    def some(g, carry):
        sums = [lon_product(back[size * g + i], band[size * g + i]) for i in range(size)]
        for i in range(size):
            out[size * g + i] = sums[i]
        return carry

    lax.fori_loop(0, back.shape[0] // size, some, 0)


def final_kernel(part, centre, band, edge, before, after, exposure, total, *rest):
    out, passed, whole, v_out, out_sems = rest[part:]
    block = centre.shape[0]
    size = min(8, block // 2)
    groups = block // 2 // size
    first = part * (block // 2)
    passed[...] = total[...]

    def copy_out(g):
        return pltpu.make_async_copy(v_out.at[pl.ds(g * size, size)], out.at[pl.ds(first + g * size, size)], out_sems.at[g])

    def lon(i):
        b = first + i
        return [(whole, i, centre[b] + lon_product(unpack_edges(before[i], after[i]), edge[b]))]

    def lat(i):
        return [(v_out, i, lat_product(band[first + i], whole[i]) * exposure[first + i])]

    run_stages(groups, size, [(lon, 0), (lat, 1)])
    for g in range(groups):
        copy_out(g).start()
    for g in range(groups):
        copy_out(g).wait()


def ring(size, shift):
    return [(i, (i + shift) % size) for i in range(size)]


def grid_ring(sky, en, sky_shift, en_shift):
    return [(s * en + e, (s + sky_shift) % sky * en + (e + en_shift) % en) for s in range(sky) for e in range(en)]


def local(flux, exposure, background, observed, psf_radius, band_low, band_high, disp_raw):
    block, rows, width = flux.shape
    bins = disp_raw.shape[0]
    sky, en = lax.axis_size("sky"), lax.axis_size("en")
    wide, near = 2 * REACH, REACH
    shifts = [1] if en == 2 else [1, -1]
    dirs = len(shifts)
    extra, nears = wide * dirs, near * dirs
    slots = block + extra
    parts = 4

    def tiles(count, dtype=F32):
        return jax.ShapeDtypeStruct((count, rows, width), dtype)

    def edges(count):
        return jax.ShapeDtypeStruct((count, RMAX, 128), F32)

    def weights(count):
        return jax.ShapeDtypeStruct((count, 128, 256), BF16)

    def scratch(shape):
        return pltpu.VMEM(shape.shape, shape.dtype)

    lanes = jax.ShapeDtypeStruct((1, 128), F32)

    flux, exposure_in, background, observed = [
        pltpu.with_memory_space_constraint(array, pltpu.HBM) for array in (flux, exposure, background, observed)
    ]
    half = block // 2

    def pack(part, *earlier):
        more = [
            pltpu.VMEM((dirs, wide, rows, width), F32), pltpu.VMEM((dirs, wide, rows, width), F32),
            pltpu.VMEM((dirs, near, rows, width), jnp.int32), pltpu.SemaphoreType.DMA((dirs, 4)),
        ]
        shapes = [tiles(half), edges(half), edges(half)]
        if part:
            shapes += [tiles(wide + 2 * near)] * dirs + [edges(wide)] * (2 * dirs)
        return pl.pallas_call(
            functools.partial(pack_kernel, part, en),
            in_specs=[ANY] * (2 + 3 * part),
            out_specs=[VMEM] * len(shapes),
            out_shape=shapes,
            scratch_shapes=[scratch(tiles(half)), scratch(tiles(half)), pltpu.SemaphoreType.DMA((2, half))] + more * part,
            compiler_params=params(12),
            name="weight_and_pack",
        )(flux, exposure_in, *[background, observed] * part, *earlier)

    def halo(last, first):
        return lax.ppermute(last, "sky", ring(sky, 1)), lax.ppermute(first, "sky", ring(sky, -1))

    weighted_a, last, first = pack(0)
    halo_a = halo(last, first)
    weighted_b, last, first, *packed = pack(1, first)
    halo_b = halo(last, first)
    energies = []
    for d, shift in enumerate(shifts):
        energies.append(lax.ppermute(packed[d], "en", ring(en, shift)))
    if dirs > 1:
        energy = jnp.concatenate(
            [e[:wide] for e in energies] + [e[wide:wide + near] for e in energies] + [e[wide + near:] for e in energies]
        )
    else:
        energy = energies[0]

    centre, band, edge, band_x, edge_x, fold, background, observed, *packed = pl.pallas_call(
        functools.partial(weights_kernel, en),
        in_specs=[SMEM] * 4 + [VMEM] * 2 + [ANY] * (2 + 3 * dirs),
        out_specs=[VMEM] * 5 + [SMEM] + [VMEM] * 2 + [ANY] * (3 * dirs),
        out_shape=[tiles(block), weights(block), weights(block), weights(extra), weights(extra), jax.ShapeDtypeStruct((5 * (slots + 4),), F32), tiles(block), tiles(block, jnp.int32)]
        + [tiles(wide + 2 * near)] * dirs + [edges(wide)] * (2 * dirs),
        input_output_aliases={8 + n: 8 + n for n in range(3 * dirs)},
        scratch_shapes=[pltpu.SemaphoreType.DMA((2,))],
        compiler_params=params(4),
        cost_estimate=cost(block, 1, block * 2**15),
        name="weights_and_centre",
    )(psf_radius, band_low, band_high, disp_raw, weighted_a, weighted_b, background, observed, *packed)
    energies = [lax.ppermute(packed[d], "en", ring(en, shift)) for d, shift in enumerate(shifts)]
    befores = [lax.ppermute(packed[dirs + d], ("sky", "en"), grid_ring(sky, en, 1, shift)) for d, shift in enumerate(shifts)]
    afters = [lax.ppermute(packed[2 * dirs + d], ("sky", "en"), grid_ring(sky, en, -1, shift)) for d, shift in enumerate(shifts)]
    if dirs > 1:
        energy = jnp.concatenate(
            [e[:wide] for e in energies] + [e[wide:wide + near] for e in energies] + [e[wide + near:] for e in energies]
        )
        before_x, after_x = jnp.concatenate(befores), jnp.concatenate(afters)
    else:
        energy, before_x, after_x = energies[0], befores[0], afters[0]

    blurred_a = pl.pallas_call(
        blur_kernel,
        in_specs=[VMEM] * 5,
        out_specs=VMEM,
        out_shape=tiles(half),
        scratch_shapes=[scratch(tiles(half))],
        compiler_params=params(6),
        cost_estimate=cost(half, 2),
        name="blur_first_half",
    )(centre, band, edge, *halo_a)
    back, *ends, total = pl.pallas_call(
        functools.partial(middle_kernel, en),
        in_specs=[SMEM] + [VMEM] * 13,
        out_specs=[VMEM] * 6,
        out_shape=[tiles(block)] + [edges(half)] * 4 + [lanes],
        scratch_shapes=[
            scratch(tiles(half)), scratch(tiles(slots + 4)), scratch(tiles(slots + 4)),
            pltpu.VMEM((block, 2 * RMAX, 128), F32), pltpu.VMEM((8, 128), F32),
        ],
        compiler_params=params(14),
        cost_estimate=cost(block, 2, block * 2**15),
        name="blur_fold_residual_fold",
    )(fold, centre, band, edge, blurred_a, *halo_b, background, observed, band_x, edge_x, before_x, after_x, energy)

    masks = [en] + [1 << n for n in range(en.bit_length() - 1)]
    masks += [en << n for n in range(2, sky.bit_length() - 1)] + [2 * en]

    def partner(value, mask):
        return lax.ppermute(value, ("sky", "en"), [(i, i ^ mask) for i in range(sky * en)])

    halo_a = halo(*ends[:2])
    moved = partner(total, masks[0])
    centre, total, *ends = pl.pallas_call(
        centre_kernel,
        in_specs=[VMEM] * 3 + [ANY] * 2,
        out_specs=[VMEM] * 2 + [ANY] * 2,
        out_shape=[tiles(block), lanes, edges(half), edges(half)],
        input_output_aliases={3: 2, 4: 3},
        compiler_params=params(4),
        cost_estimate=cost(block, 1),
        name="back_centre",
    )(back, band, total, *ends[2:])
    halo_b = halo(*ends)
    total = total + moved
    for mask in masks[1:-2]:
        total = total + partner(total, mask)
    grad = []
    for part, (before, after) in enumerate((halo_a, halo_b)):
        moved = partner(total, masks[part - 2])
        *grad, passed = pl.pallas_call(
            functools.partial(final_kernel, part),
            in_specs=[VMEM] * 7 + [ANY] * part,
            out_specs=[ANY, VMEM],
            out_shape=[tiles(block), lanes],
            scratch_shapes=[scratch(tiles(half)), scratch(tiles(half)), pltpu.SemaphoreType.DMA((half,))],
            input_output_aliases={7: 0} if part else {},
            compiler_params=params(8),
            cost_estimate=cost(half, 2),
            name="back_edges_lat_exposure",
        )(centre, band, edge, before, after, exposure, total, *grad)
        total = passed + moved
    return grad[0], total[0, 0] / F32(rows * width * bins * sky)


def solution(mesh):
    placed = (P("en", None, "sky"),) * 4 + (P(),) * 4
    return jax.shard_map(local, mesh=mesh, in_specs=placed, out_specs=(P("en", None, "sky"), P()), check_vma=False)
```

```python
import functools

import jax
import jax.numpy as jnp
from jax import lax
from jax.experimental import pallas as pl
from jax.experimental.pallas import tpu as pltpu
from jax.sharding import PartitionSpec as P

RMAX = 32
REACH = 2
F32 = jnp.float32
BF16 = jnp.bfloat16
SMEM = pl.BlockSpec(memory_space=pltpu.SMEM)
ANY = pl.BlockSpec(memory_space=pl.ANY)
VMEM = pl.BlockSpec(memory_space=pltpu.VMEM)
HBM = pl.BlockSpec(memory_space=pltpu.HBM)


def split(x):
    hi = x.astype(BF16)
    return hi, (x - hi.astype(F32)).astype(BF16)


def params(mib=56):
    return pltpu.CompilerParams(vmem_limit_bytes=mib * 2**20)


def blocks(count, rows, cols):
    return pl.BlockSpec((count, rows, cols), lambda i: (i, 0, 0))


def chunk_copy(source, target, sem, c, size):
    at = pl.ds(c * size, size)
    return pltpu.make_async_copy(source.at[at], target.at[at], sem)


def run_stages(groups, size, stages, events=(), arrive=None):
    stages = [(*stage, groups)[:3] for stage in stages]
    marks = {0} | {lag for _, lag, _ in stages} | {lag + count for _, lag, count in stages} | {at for at, _ in events}
    marks = sorted(marks)
    for start, stop in zip(marks, marks[1:] + [marks[-1]]):
        for at, event in events:
            if at == start:
                event()
        active = [(n, stage, lag) for n, (stage, lag, count) in enumerate(stages) if lag <= start < lag + count]
        if stop == start or not active:
            continue

        def step(p, carry):
            if arrive is not None:
                for n, _, lag in active:
                    arrive(n, p - lag)
            stores = []
            for _, stage, lag in active:
                for i in range(size):
                    stores += stage((p - lag) * size + i)
            for ref, index, value in stores:
                if index is None:
                    ref[...] += value
                else:
                    ref[index] = value
            return carry

        lax.fori_loop(start, stop, step, 0)


def cost(tiles, products, transcendentals=0):
    return pl.CostEstimate(flops=tiles * products * 2 * 128 * 256 * 256, bytes_accessed=tiles * 2**16, transcendentals=transcendentals)


class Place:
    def __init__(self, block, en):
        self.block, self.en = block, en
        self.me = lax.axis_index("en")
        self.wide, self.near = 2 * REACH, REACH
        self.dirs = 1 if en == 2 else 2
        self.extra, self.nears = self.wide * self.dirs, self.near * self.dirs
        self.slots, self.bins = block + self.extra, block * en
        self.own = jnp.where(self.me == 0, 0, self.wide) if en == 2 else self.wide
        self.first_bin = self.me * block - self.own

    def start(self, d, width):
        if self.en == 2:
            return jnp.where(self.me == 0, self.block - width, 0)
        return self.block - width if d == 0 else 0

    def slot(self, k, width):
        if self.en == 2:
            return jnp.where(self.me == 0, self.block, self.wide - width) + k
        return self.wide - width + k if k < width else self.wide + self.block + k - width

    def clamp(self, g):
        return jnp.clip(g, 0, self.bins - 1)


def lanes_of(shape=(128, 128)):
    return lax.broadcasted_iota(jnp.int32, shape, 1)


def pack_edges(tiles):
    lane = lanes_of()
    outer = (lane < RMAX) | (lane >= 128 - RMAX)
    odd = (lane // RMAX) % 2 == 1
    early, late = [jnp.where(outer, tiles[n], pltpu.roll(tiles[n + 1], 64, 1)) for n in (0, 2)]
    late = pltpu.roll(late, RMAX, 1)
    return jnp.where(odd, early, late), jnp.where(odd, late, early)


LEFT = (3, 1, 0, 2)
RIGHT = (0, 2, 1, 3)


def edge_tile(before, after, n):
    lane = lanes_of()
    if LEFT[n] < RIGHT[n]:
        return jnp.where(lane < RMAX * RIGHT[n], before, after)
    return jnp.where(lane < RMAX * LEFT[n], after, before)


def twice(x):
    return jnp.concatenate([x, x], axis=0)


def lon_product(tile, weights):
    out = jnp.dot(jnp.concatenate(split(tile), axis=1), twice(weights), preferred_element_type=F32)
    return out[:, :128] + out[:, 128:]


def lat_product(weights, tile):
    out = jnp.dot(weights, twice(jnp.concatenate(split(tile), axis=1)), preferred_element_type=F32)
    return out[:, :128] + out[:, 128:]


def profile(radius, column):
    wide = jnp.full((1, 128), radius, jnp.int32).astype(F32)
    reach = wide * wide
    factor = -2.0 / reach
    lane = lax.broadcasted_iota(jnp.int32, (1, 128), 1)
    square = (lane * lane).astype(F32)
    values = jnp.where(square <= reach, jnp.exp(square * factor), 0.0)
    norm = 2.0 * jnp.sum(values, axis=1, keepdims=True) - 1.0
    root = jnp.sqrt(jnp.full((1, 128), column, F32))[:, :1]
    return factor[:, :1], 1.0 / (norm * root), reach[:, :1]


def taper_values(diff, ok, factor, scale, reach):
    square = diff * diff
    return jnp.where((square <= reach) & ok, jnp.exp(square * factor) * scale, 0.0)


def pack_kernel(parts, en, flux, exposure, background, observed, weighted, last_a, first_a, last_b, first_b, *rest):
    place = Place(flux.shape[0], en)
    dirs, wide, near, block = place.dirs, place.wide, place.near, place.block
    sent, last_x, first_x = rest[:dirs], rest[dirs:2 * dirs], rest[2 * dirs:3 * dirs]
    v_flux, v_exposure, v_observed, v_last, v_first, sems, near_sems = rest[3 * dirs:]
    chunk = block // parts

    def arrivals(c):
        return [chunk_copy(a, b, sems.at[n, c], c, chunk) for n, (a, b) in enumerate(((flux, v_flux), (exposure, v_exposure)))]

    def near_arrivals(d):
        at = pl.ds(place.start(d, near), near)
        return [
            pltpu.make_async_copy(background.at[at], sent[d].at[pl.ds(wide, near)], near_sems.at[d, 0]),
            pltpu.make_async_copy(observed.at[at], v_observed.at[d], near_sems.at[d, 1]),
        ]

    for c in range(parts):
        for copy in arrivals(c):
            copy.start()
    for d in range(dirs):
        for copy in near_arrivals(d):
            copy.start()

    def some(g, carry):
        tiles = [v_flux[4 * g + i] * v_exposure[4 * g + i] for i in range(4)]
        packed = pack_edges(tiles)
        for i in range(4):
            weighted[4 * g + i] = tiles[i]
        v_last[g], v_first[g] = packed
        return carry

    for c in range(parts):
        for copy in arrivals(c):
            copy.wait()
        lax.fori_loop(c * chunk // 4, (c + 1) * chunk // 4, some, 0)
    half = block // 8
    last_a[...], last_b[...] = v_last[:half], v_last[half:]
    first_a[...], first_b[...] = v_first[:half], v_first[half:]
    for d in range(dirs):
        for copy in near_arrivals(d):
            copy.wait()
        start = place.start(d, wide)
        group = lax.div(start, 4) if en == 2 else start // 4
        last_x[d][0] = v_last[group]
        first_x[d][0] = v_first[group]
        for k in range(wide):
            sent[d][k] = weighted[start + k]
        for k in range(near):
            sent[d][wide + near + k] = v_observed[d, k].astype(F32)


def weights_kernel(en, radius, low, high, disp, weighted, background, observed, *rest):
    through = (len(rest) - 9) // 2
    centre, band, edge, band_x, edge_x, fold, near_background, near_observed = rest[through:through + 8]
    sems = rest[-1]
    fetches = [
        pltpu.make_async_copy(background, near_background, sems.at[0]),
        pltpu.make_async_copy(observed, near_observed, sems.at[1]),
    ]
    for fetch in fetches:
        fetch.start()
    block = weighted.shape[0]
    place = Place(block, en)
    row = lax.broadcasted_iota(jnp.int32, (128, 128), 0)
    col = lax.broadcasted_iota(jnp.int32, (128, 128), 1)
    near = (row - col).astype(F32)
    always = row >= 0
    beside = []
    for n in range(4):
        shift = jnp.where(row // RMAX == LEFT[n], -RMAX - RMAX * LEFT[n], 128 - RMAX * RIGHT[n])
        held = (row // RMAX == LEFT[n]) | (row // RMAX == RIGHT[n])
        beside.append(((row + shift - col).astype(F32), held))

    def weight(i, j):
        at, to = place.clamp(i), place.clamp(j)
        inside = (i == at) & (j == to) & (low[at] <= j - i) & (j - i <= high[at])
        return jnp.where(inside, disp[at, to], 0.0)

    def make(g, n):
        for o in range(-REACH, REACH + 1):
            fold[5 * (g - place.first_bin + REACH) + o + REACH] = weight(g, g + o)
        column = weight(g, g)
        for o in (-2, -1, 1, 2):
            column = column + weight(g - o, g)
        numbers = profile(radius[place.clamp(g)], jnp.where(column > 0.0, column, 1.0))
        return tuple(
            jnp.concatenate(split(taper_values(diff, ok, *numbers)), axis=1) for diff, ok in ((near, always), beside[n])
        )

    for s in (0, 1, place.slots + 2, place.slots + 3):
        for o in range(5):
            fold[5 * s + o] = 0.0

    def some(g):
        made = [make(place.me * block + 4 * g + n, n) for n in range(4)]
        return [(band, 4 * g + n, made[n][0]) for n in range(4)] + [(edge, 4 * g + n, made[n][1]) for n in range(4)]

    def lon(g):
        return [(centre, 4 * g + n, lon_product(weighted[4 * g + n], band[4 * g + n])) for n in range(4)]

    run_stages(block // 4, 1, [(some, 0), (lon, 1)])
    for k in range(place.extra):
        band_x[k], edge_x[k] = make(place.first_bin + place.slot(k, place.wide), k % 4)
    for fetch in fetches:
        fetch.wait()


def lon_edges(centre, edge, before, after, g, at, n):
    return centre[at] + lon_product(edge_tile(before[g], after[g], n), edge[at])


def blur_kernel(centre, band, edge, before, after, blurred, whole):
    def lon(g):
        return [(whole, 4 * g + n, lon_edges(centre, edge, before, after, g, 4 * g + n, n)) for n in range(4)]

    def lat(g):
        return [(blurred, 4 * g + n, lat_product(band[4 * g + n], whole[4 * g + n])) for n in range(4)]

    size = min(2, before.shape[0])
    run_stages(before.shape[0] // size, size, [(lon, 0), (lat, 1)])


def middle_kernel(en, fold, centre, band, edge, blurred_a, before, after, background, observed, band_x, edge_x, before_x, after_x, energy,
                  back, last_a, first_a, last_b, first_b, loss, whole, blurred, resid, v_last, v_first, sums):
    groups = before.shape[0]
    half, block = 4 * groups, 8 * groups
    place = Place(block, en)
    extra, nears, slots, own = place.extra, place.nears, place.slots, place.own
    zero = jnp.zeros((128, 128), F32)
    for s in (0, 1, slots + 2, slots + 3):
        blurred[s] = zero
        resid[s] = zero
    sums[...] = jnp.zeros((8, 128), F32)
    blurred[pl.ds(own + 2, half)] = blurred_a[...]

    done = [lon_product(energy[k], band_x[k]) for k in range(extra)]
    done = [done[k] + lon_product(edge_tile(before_x[k // 4], after_x[k // 4], k % 4), edge_x[k]) for k in range(extra)]
    done = [lat_product(band_x[k], done[k]) for k in range(extra)]
    for k in range(extra):
        blurred[place.slot(k, place.wide) + 2] = done[k]

    def lon(g):
        return [(whole, 4 * g + n, lon_edges(centre, edge, before, after, g, half + 4 * g + n, n)) for n in range(4)]

    def lat(g):
        bins = [half + 4 * g + n for n in range(4)]
        return [(blurred, b + own + 2, lat_product(band[b], whole[b - half])) for b in bins]

    def mean_counts(slot, ground):
        mu = ground
        for o in range(5):
            mu = mu + fold[5 * (slot + 2) + o] * blurred[slot + o]
        return mu

    def residual(g):
        stores = []
        for b in [4 * g + n for n in range(4)]:
            slot = b + own
            mu = mean_counts(slot, background[b])
            counts = observed[b].astype(F32)
            terms = (mu - counts * jnp.log(mu)).reshape(16, 8, 128).sum(0)
            stores += [(resid, slot + 2, 1.0 - counts / mu), (sums, None, terms)]
        return stores

    def extra_residuals():
        values = []
        for k in range(nears):
            mu = mean_counts(place.slot(k, place.near), energy[extra + k])
            values.append(1.0 - energy[extra + nears + k] / mu)
        for k in range(nears):
            resid[place.slot(k, place.near) + 2] = values[k]

    def fold_back(g):
        tiles = []
        for b in [4 * g + n for n in range(4)]:
            slot = b + own
            total = None
            for o in range(5):
                term = fold[5 * (slot + 4 - o) + o] * resid[slot + 4 - o]
                total = term if total is None else total + term
            tiles.append(total)
        packed = pack_edges(tiles)
        return [(back, 4 * g + n, tiles[n]) for n in range(4)] + [(v_last, g, packed[0]), (v_first, g, packed[1])]

    wait = 3 - groups if groups < 3 else 0
    run_stages(
        groups, 1, [(lon, 0), (lat, 1), (residual, wait, 2 * groups), (fold_back, wait + 2, 2 * groups)],
        events=[(0, extra_residuals), (groups + 1, extra_residuals)],
    )
    last_a[...], last_b[...] = v_last[:groups], v_last[groups:]
    first_a[...], first_b[...] = v_first[:groups], v_first[groups:]
    loss[...] = jnp.full((1, 128), jnp.sum(sums[...]), F32)


def centre_kernel(back, band, total, last_in, first_in, out, passed, last, first):
    del last_in, first_in, last, first
    passed[...] = total[...]
    size = 8

    def some(g, carry):
        sums = [lon_product(back[size * g + i], band[size * g + i]) for i in range(size)]
        for i in range(size):
            out[size * g + i] = sums[i]
        return carry

    lax.fori_loop(0, back.shape[0] // size, some, 0)


def final_kernel(part, centre, band, edge, before, after, exposure, total, *rest):
    out, passed, whole, v_out, out_sems = rest[part:]
    groups = before.shape[0]
    first = part * 4 * groups
    size = min(2, groups)
    steps = groups // size
    passed[...] = total[...]

    def copy_out(p):
        count = 4 * size
        return pltpu.make_async_copy(v_out.at[pl.ds(p * count, count)], out.at[pl.ds(first + p * count, count)], out_sems.at[p])

    def lon(g):
        return [(whole, 4 * g + n, lon_edges(centre, edge, before, after, g, first + 4 * g + n, n)) for n in range(4)]

    def lat(g):
        bins = [4 * g + n for n in range(4)]
        return [(v_out, b, lat_product(band[first + b], whole[b]) * exposure[first + b]) for b in bins]

    run_stages(steps, size, [(lon, 0), (lat, 1)], events=[(p + 2, copy_out(p).start) for p in range(steps)])
    for p in range(steps):
        copy_out(p).wait()


def ring(size, shift):
    return [(i, (i + shift) % size) for i in range(size)]


def grid_ring(sky, en, sky_shift, en_shift):
    return [(s * en + e, (s + sky_shift) % sky * en + (e + en_shift) % en) for s in range(sky) for e in range(en)]


def local(flux, exposure, background, observed, psf_radius, band_low, band_high, disp_raw):
    block, rows, width = flux.shape
    bins = disp_raw.shape[0]
    sky, en = lax.axis_size("sky"), lax.axis_size("en")
    wide, near = 2 * REACH, REACH
    shifts = [1] if en == 2 else [1, -1]
    dirs = len(shifts)
    extra, nears = wide * dirs, near * dirs
    slots = block + extra
    parts = min(4, block // 4)

    def tiles(count, dtype=F32):
        return jax.ShapeDtypeStruct((count, rows, width), dtype)

    def edges(count):
        return jax.ShapeDtypeStruct((count // 4, 128, 128), F32)

    def weights(count):
        return jax.ShapeDtypeStruct((count, 128, 256), BF16)

    def scratch(shape):
        return pltpu.VMEM(shape.shape, shape.dtype)

    lanes = jax.ShapeDtypeStruct((1, 128), F32)

    flux, exposure_in, background, observed = [
        pltpu.with_memory_space_constraint(array, pltpu.HBM) for array in (flux, exposure, background, observed)
    ]
    half = block // 2

    def halo(last, first):
        return lax.ppermute(last, "sky", ring(sky, 1)), lax.ppermute(first, "sky", ring(sky, -1))

    weighted, last_a, first_a, last_b, first_b, *packed = pl.pallas_call(
        functools.partial(pack_kernel, parts, en),
        in_specs=[ANY] * 4,
        out_specs=[VMEM] * (5 + 3 * dirs),
        out_shape=[tiles(block)] + [edges(half)] * 4 + [tiles(wide + 2 * near)] * dirs + [edges(wide)] * (2 * dirs),
        scratch_shapes=[
            scratch(tiles(block)), scratch(tiles(block)), pltpu.VMEM((dirs, near, rows, width), jnp.int32),
            scratch(edges(block)), scratch(edges(block)),
            pltpu.SemaphoreType.DMA((2, parts)), pltpu.SemaphoreType.DMA((dirs, 2)),
        ],
        compiler_params=params(12),
        name="weight_and_pack",
    )(flux, exposure_in, background, observed)
    halo_a, halo_b = halo(last_a, first_a), halo(last_b, first_b)
    energies = []
    for d, shift in enumerate(shifts):
        energies.append(lax.ppermute(packed[d], "en", ring(en, shift)))
    if dirs > 1:
        energy = jnp.concatenate(
            [e[:wide] for e in energies] + [e[wide:wide + near] for e in energies] + [e[wide + near:] for e in energies]
        )
    else:
        energy = energies[0]

    centre, band, edge, band_x, edge_x, fold, background, observed, *packed = pl.pallas_call(
        functools.partial(weights_kernel, en),
        in_specs=[SMEM] * 4 + [VMEM] + [ANY] * (2 + 2 * dirs),
        out_specs=[VMEM] * 5 + [SMEM] + [VMEM] * 2 + [ANY] * (2 * dirs),
        out_shape=[tiles(block), weights(block), weights(block), weights(extra), weights(extra), jax.ShapeDtypeStruct((5 * (slots + 4),), F32), tiles(block), tiles(block, jnp.int32)] + [edges(wide)] * (2 * dirs),
        input_output_aliases={7 + n: 8 + n for n in range(2 * dirs)},
        scratch_shapes=[pltpu.SemaphoreType.DMA((2,))],
        compiler_params=params(4),
        cost_estimate=cost(block, 1, block * 2**15),
        name="weights_and_centre",
    )(psf_radius, band_low, band_high, disp_raw, weighted, background, observed, *packed[dirs:])
    befores = [lax.ppermute(packed[d], ("sky", "en"), grid_ring(sky, en, 1, shift)) for d, shift in enumerate(shifts)]
    afters = [lax.ppermute(packed[dirs + d], ("sky", "en"), grid_ring(sky, en, -1, shift)) for d, shift in enumerate(shifts)]
    before_x, after_x = [jnp.concatenate(a) if dirs > 1 else a[0] for a in (befores, afters)]
    blurred_a = pl.pallas_call(
        blur_kernel,
        in_specs=[VMEM] * 5,
        out_specs=VMEM,
        out_shape=tiles(half),
        scratch_shapes=[scratch(tiles(half))],
        compiler_params=params(6),
        cost_estimate=cost(half, 2),
        name="blur_first_half",
    )(centre, band, edge, *halo_a)
    back, *ends, total = pl.pallas_call(
        functools.partial(middle_kernel, en),
        in_specs=[SMEM] + [VMEM] * 13,
        out_specs=[VMEM] * 6,
        out_shape=[tiles(block)] + [edges(half)] * 4 + [lanes],
        scratch_shapes=[
            scratch(tiles(half)), scratch(tiles(slots + 4)), scratch(tiles(slots + 4)),
            scratch(edges(block)), scratch(edges(block)), pltpu.VMEM((8, 128), F32),
        ],
        compiler_params=params(14),
        cost_estimate=cost(block, 2, block * 2**15),
        name="blur_fold_residual_fold",
    )(fold, centre, band, edge, blurred_a, *halo_b, background, observed, band_x, edge_x, before_x, after_x, energy)

    masks = [en] + [1 << n for n in range(en.bit_length() - 1)]
    masks += [en << n for n in range(2, sky.bit_length() - 1)] + [2 * en]

    def partner(value, mask):
        return lax.ppermute(value, ("sky", "en"), [(i, i ^ mask) for i in range(sky * en)])

    halo_a = halo(*ends[:2])
    moved = partner(total, masks[0])
    centre, total, *ends = pl.pallas_call(
        centre_kernel,
        in_specs=[VMEM] * 3 + [ANY] * 2,
        out_specs=[VMEM] * 2 + [ANY] * 2,
        out_shape=[tiles(block), lanes, edges(half), edges(half)],
        input_output_aliases={3: 2, 4: 3},
        compiler_params=params(4),
        cost_estimate=cost(block, 1),
        name="back_centre",
    )(back, band, total, *ends[2:])
    halo_b = halo(*ends)
    total = total + moved
    for mask in masks[1:-2]:
        total = total + partner(total, mask)
    grad = []
    for part, (before, after) in enumerate((halo_a, halo_b)):
        moved = partner(total, masks[part - 2])
        *grad, passed = pl.pallas_call(
            functools.partial(final_kernel, part),
            in_specs=[VMEM] * 7 + [ANY] * part,
            out_specs=[ANY, VMEM],
            out_shape=[tiles(block), lanes],
            scratch_shapes=[scratch(tiles(half)), scratch(tiles(half)), pltpu.SemaphoreType.DMA((half // 4,))],
            input_output_aliases={7: 0} if part else {},
            compiler_params=params(8),
            cost_estimate=cost(half, 2),
            name="back_edges_lat_exposure",
        )(centre, band, edge, before, after, exposure, total, *grad)
        total = passed + moved
    return grad[0], total[0, 0] / F32(rows * width * bins * sky)


def solution(mesh):
    placed = (P("en", None, "sky"),) * 4 + (P(),) * 4
    return jax.shard_map(local, mesh=mesh, in_specs=placed, out_specs=(P("en", None, "sky"), P()), check_vma=False)
```

```python
import functools

import jax
import jax.numpy as jnp
from jax import lax
from jax.experimental import pallas as pl
from jax.experimental.pallas import tpu as pltpu
from jax.sharding import PartitionSpec as P

RMAX = 32
REACH = 2
F32 = jnp.float32
BF16 = jnp.bfloat16
SMEM = pl.BlockSpec(memory_space=pltpu.SMEM)
ANY = pl.BlockSpec(memory_space=pl.ANY)
VMEM = pl.BlockSpec(memory_space=pltpu.VMEM)
HBM = pl.BlockSpec(memory_space=pltpu.HBM)


def split(x):
    hi = x.astype(BF16)
    return hi, (x - hi.astype(F32)).astype(BF16)


def params(mib=56):
    return pltpu.CompilerParams(vmem_limit_bytes=mib * 2**20)


def blocks(count, rows, cols):
    return pl.BlockSpec((count, rows, cols), lambda i: (i, 0, 0))


def chunk_copy(source, target, sem, c, size):
    at = pl.ds(c * size, size)
    return pltpu.make_async_copy(source.at[at], target.at[at], sem)


def run_stages(groups, size, stages, events=(), arrive=None):
    stages = [(*stage, groups)[:3] for stage in stages]
    marks = {0} | {lag for _, lag, _ in stages} | {lag + count for _, lag, count in stages} | {at for at, _ in events}
    marks = sorted(marks)
    for start, stop in zip(marks, marks[1:] + [marks[-1]]):
        for at, event in events:
            if at == start:
                event()
        active = [(n, stage, lag) for n, (stage, lag, count) in enumerate(stages) if lag <= start < lag + count]
        if stop == start or not active:
            continue

        def step(p, carry):
            if arrive is not None:
                for n, _, lag in active:
                    arrive(n, p - lag)
            stores = []
            for _, stage, lag in active:
                for i in range(size):
                    stores += stage((p - lag) * size + i)
            for ref, index, value in stores:
                if index is None:
                    ref[...] += value
                else:
                    ref[index] = value
            return carry

        lax.fori_loop(start, stop, step, 0)


def cost(tiles, products, transcendentals=0):
    return pl.CostEstimate(flops=tiles * products * 2 * 128 * 256 * 256, bytes_accessed=tiles * 2**16, transcendentals=transcendentals)


class Place:
    def __init__(self, block, en):
        self.block, self.en = block, en
        self.me = lax.axis_index("en")
        self.dirs = 1 if en == 2 else 2
        self.extra = REACH * self.dirs
        self.slots, self.bins = block + self.extra, block * en
        self.own = jnp.where(self.me == 0, 0, REACH) if en == 2 else REACH
        self.first_bin = self.me * block - self.own

    def above(self, d):
        return jnp.where(self.me == 0, 1, 0) if self.en == 2 else 1 - d

    def sent(self, d, width):
        return self.above(d) * (self.block - width)

    def border(self, d):
        up = self.above(d) if self.en == 2 else d
        return up, up * (self.block + self.own - REACH)

    def clamp(self, g):
        return jnp.clip(g, 0, self.bins - 1)


def lanes_of(shape=(128, 128)):
    return lax.broadcasted_iota(jnp.int32, shape, 1)


def pack_edges(tiles):
    lane = lanes_of()
    outer = (lane < RMAX) | (lane >= 128 - RMAX)
    odd = (lane // RMAX) % 2 == 1
    early, late = [jnp.where(outer, tiles[n], pltpu.roll(tiles[n + 1], 64, 1)) for n in (0, 2)]
    late = pltpu.roll(late, RMAX, 1)
    return jnp.where(odd, early, late), jnp.where(odd, late, early)


LEFT = (3, 1, 0, 2)
RIGHT = (0, 2, 1, 3)


def edge_tile(before, after, n):
    lane = lanes_of()
    if LEFT[n] < RIGHT[n]:
        return jnp.where(lane < RMAX * RIGHT[n], before, after)
    return jnp.where(lane < RMAX * LEFT[n], after, before)


def twice(x):
    return jnp.concatenate([x, x], axis=0)


def lon_product(tile, weights):
    out = jnp.dot(jnp.concatenate(split(tile), axis=1), twice(weights), preferred_element_type=F32)
    return out[:, :128] + out[:, 128:]


def lat_product(weights, tile):
    out = jnp.dot(weights, twice(jnp.concatenate(split(tile), axis=1)), preferred_element_type=F32)
    return out[:, :128] + out[:, 128:]


def profile(radius, column):
    wide = jnp.full((1, 128), radius, jnp.int32).astype(F32)
    reach = wide * wide
    factor = -2.0 / reach
    lane = lax.broadcasted_iota(jnp.int32, (1, 128), 1)
    square = (lane * lane).astype(F32)
    values = jnp.where(square <= reach, jnp.exp(square * factor), 0.0)
    norm = 2.0 * jnp.sum(values, axis=1, keepdims=True) - 1.0
    root = jnp.sqrt(jnp.full((1, 128), column, F32))[:, :1]
    return factor[:, :1], 1.0 / (norm * root), reach[:, :1]


def taper_values(diff, ok, factor, scale, reach):
    square = diff * diff
    return jnp.where((square <= reach) & ok, jnp.exp(square * factor) * scale, 0.0)


def pack_kernel(parts, en, flux, exposure, background, observed, weighted, last, first, *rest):
    place = Place(flux.shape[0], en)
    dirs, block = place.dirs, place.block
    sent, (v_flux, v_exposure, v_observed, sems, near_sems) = rest[:dirs], rest[dirs:]
    chunk = block // parts

    def arrivals(c):
        return [chunk_copy(a, b, sems.at[n, c], c, chunk) for n, (a, b) in enumerate(((flux, v_flux), (exposure, v_exposure)))]

    def near_arrivals(d):
        at = pl.ds(place.sent(d, REACH), REACH)
        return [
            pltpu.make_async_copy(background.at[at], sent[d].at[pl.ds(0, REACH)], near_sems.at[d, 0]),
            pltpu.make_async_copy(observed.at[at], v_observed.at[d], near_sems.at[d, 1]),
        ]

    for c in range(parts):
        for copy in arrivals(c):
            copy.start()
    for d in range(dirs):
        for copy in near_arrivals(d):
            copy.start()

    def some(g, carry):
        tiles = [v_flux[4 * g + i] * v_exposure[4 * g + i] for i in range(4)]
        packed = pack_edges(tiles)
        for i in range(4):
            weighted[4 * g + i] = tiles[i]
        last[g], first[g] = packed
        return carry

    for c in range(parts):
        for copy in arrivals(c):
            copy.wait()
        lax.fori_loop(c * chunk // 4, (c + 1) * chunk // 4, some, 0)
    for d in range(dirs):
        for copy in near_arrivals(d):
            copy.wait()
        for k in range(REACH):
            sent[d][REACH + k] = v_observed[d, k].astype(F32)


def weights_kernel(en, radius, low, high, disp, weighted, background, observed,
                   centre, band, edge, fold, near_background, near_observed, sems):
    fetches = [
        pltpu.make_async_copy(background, near_background, sems.at[0]),
        pltpu.make_async_copy(observed, near_observed, sems.at[1]),
    ]
    for fetch in fetches:
        fetch.start()
    block = weighted.shape[0]
    place = Place(block, en)
    row = lax.broadcasted_iota(jnp.int32, (128, 128), 0)
    col = lax.broadcasted_iota(jnp.int32, (128, 128), 1)
    near = (row - col).astype(F32)
    always = row >= 0
    beside = []
    for n in range(4):
        shift = jnp.where(row // RMAX == LEFT[n], -RMAX - RMAX * LEFT[n], 128 - RMAX * RIGHT[n])
        held = (row // RMAX == LEFT[n]) | (row // RMAX == RIGHT[n])
        beside.append(((row + shift - col).astype(F32), held))

    def weight(i, j):
        at, to = place.clamp(i), place.clamp(j)
        inside = (i == at) & (j == to) & (low[at] <= j - i) & (j - i <= high[at])
        return jnp.where(inside, disp[at, to], 0.0)

    def fold_row(g):
        for o in range(-REACH, REACH + 1):
            fold[5 * (g - place.first_bin + REACH) + o + REACH] = weight(g, g + o)

    def make(g, n):
        fold_row(g)
        column = weight(g, g)
        for o in (-2, -1, 1, 2):
            column = column + weight(g - o, g)
        numbers = profile(radius[place.clamp(g)], jnp.where(column > 0.0, column, 1.0))
        return tuple(
            jnp.concatenate(split(taper_values(diff, ok, *numbers)), axis=1) for diff, ok in ((near, always), beside[n])
        )

    for s in (0, 1, place.slots + 2, place.slots + 3):
        for o in range(5):
            fold[5 * s + o] = 0.0

    def some(g):
        made = [make(place.me * block + 4 * g + n, n) for n in range(4)]
        return [(band, 4 * g + n, made[n][0]) for n in range(4)] + [(edge, 4 * g + n, made[n][1]) for n in range(4)]

    def lon(g):
        return [(centre, 4 * g + n, lon_product(weighted[4 * g + n], band[4 * g + n])) for n in range(4)]

    run_stages(block // 4, 1, [(some, 0), (lon, 1)])
    for d in range(place.dirs):
        up, slot = place.border(d)
        for k in range(REACH):
            fold_row(place.first_bin + slot + up * REACH + k)
    for fetch in fetches:
        fetch.wait()


def lon_edges(centre, edge, before, after, g, at, n):
    return centre[at] + lon_product(edge_tile(before[g], after[g], n), edge[at])


def blur_kernel(en, centre, band, edge, before, after, *blurred):
    place = Place(centre.shape[0], en)
    for d in range(place.dirs):
        start = place.sent(d, 4)
        g = lax.div(start, 4) if en == 2 else start // 4
        sums = [lon_edges(centre, edge, before, after, g, start + n, n) for n in range(4)]
        sums = [lat_product(band[start + n], sums[n]) for n in range(4)]
        for n in range(4):
            blurred[d][n] = sums[n]


def loss_terms(mu, counts):
    return (mu - counts * jnp.log(mu)).reshape(16, 8, 128).sum(0)


def middle_kernel(en, fold, centre, band, edge, before, after, background, observed, resid, loss, whole, blurred):
    block = centre.shape[0]
    place = Place(block, en)
    own = place.own
    zero = jnp.zeros((128, 128), F32)
    for s in (0, 1, block + 2, block + 3):
        blurred[s] = zero
    for s in (0, 1, place.slots + 2, place.slots + 3):
        resid[s] = zero
    loss[...] = jnp.zeros((8, 128), F32)
    inside = (own, own + block - REACH) if en == 2 else (REACH, block - REACH)

    def lon(g):
        return [(whole, 4 * g + n, lon_edges(centre, edge, before, after, g, 4 * g + n, n)) for n in range(4)]

    def lat(g):
        return [(blurred, 4 * g + n + 2, lat_product(band[4 * g + n], whole[4 * g + n])) for n in range(4)]

    def residual(g):
        stores = []
        for b in [4 * g + n for n in range(4)]:
            mu = background[b]
            for o in range(5):
                mu = mu + fold[5 * (b + own + 2) + o] * blurred[b + o]
            counts = observed[b].astype(F32)
            inner = (b >= inside[0]) & (b < inside[1])
            stores += [(resid, b + own + 2, 1.0 - counts / mu), (loss, None, jnp.where(inner, loss_terms(mu, counts), 0.0))]
        return stores

    run_stages(block // 8, 2, [(lon, 0), (lat, 1), (residual, 3)])


def border_kernel(en, fold, background, observed, resid_in, loss, *rest):
    block = background.shape[0]
    place = Place(block, en)
    sent, received, counts = [rest[n * place.dirs:(n + 1) * place.dirs] for n in range(3)]
    resid, total, blurred, ground, seen = rest[3 * place.dirs:]
    sums = loss[...]
    for d in range(place.dirs):
        up, slot = place.border(d)
        mine, theirs = 4 * (1 - up), 4 * up
        for k in range(4):
            blurred[mine + k] = sent[place.dirs - 1 - d][k]
            blurred[theirs + k] = received[d][k]
        first = place.sent(d, REACH) if en == 2 else up * (block - REACH)
        for k in range(REACH):
            ground[mine // 2 + k] = background[first + k]
            seen[mine // 2 + k] = observed[first + k].astype(F32)
            ground[theirs // 2 + k] = counts[d][k]
            seen[theirs // 2 + k] = counts[d][REACH + k]
        for j in range(2 * REACH):
            mu = ground[j]
            for o in range(5):
                mu = mu + fold[5 * (slot + j + 2) + o] * blurred[j + o]
            resid[slot + j + 2] = 1.0 - seen[j] / mu
            is_mine = (mine // 2 <= j) & (j < mine // 2 + REACH)
            sums = sums + jnp.where(is_mine, loss_terms(mu, seen[j]), 0.0)
    total[...] = jnp.full((1, 128), jnp.sum(sums), F32)


def fold_kernel(en, fold, resid, back, last, first):
    place = Place(back.shape[0], en)

    def fold_back(g):
        tiles = []
        for b in [4 * g + n for n in range(4)]:
            slot = b + place.own
            total = None
            for o in range(5):
                term = fold[5 * (slot + 4 - o) + o] * resid[slot + 4 - o]
                total = term if total is None else total + term
            tiles.append(total)
        packed = pack_edges(tiles)
        return [(back, 4 * g + n, tiles[n]) for n in range(4)] + [(last, g, packed[0]), (first, g, packed[1])]

    run_stages(back.shape[0] // 8, 2, [(fold_back, 0)])


def centre_kernel(back, band, total, moved, out, passed):
    passed[...] = total[...] + moved[...]
    size = 8

    def some(g, carry):
        sums = [lon_product(back[size * g + i], band[size * g + i]) for i in range(size)]
        for i in range(size):
            out[size * g + i] = sums[i]
        return carry

    lax.fori_loop(0, back.shape[0] // size, some, 0)


def final_kernel(part, centre, band, edge, before, after, exposure, total, *rest):
    out, passed, whole, v_out, out_sems = rest[part:]
    groups = before.shape[0] // 2
    first = part * 4 * groups
    size = min(2, groups)
    steps = groups // size
    passed[...] = total[...]

    def copy_out(p):
        count = 4 * size
        return pltpu.make_async_copy(v_out.at[pl.ds(p * count, count)], out.at[pl.ds(first + p * count, count)], out_sems.at[p])

    def lon(g):
        return [(whole, 4 * g + n, lon_edges(centre, edge, before, after, part * groups + g, first + 4 * g + n, n)) for n in range(4)]

    def lat(g):
        bins = [4 * g + n for n in range(4)]
        return [(v_out, b, lat_product(band[first + b], whole[b]) * exposure[first + b]) for b in bins]

    run_stages(steps, size, [(lon, 0), (lat, 1)], events=[(p + 2, copy_out(p).start) for p in range(steps)])
    for p in range(steps):
        copy_out(p).wait()


def ring(size, shift):
    return [(i, (i + shift) % size) for i in range(size)]


def grid_ring(sky, en, sky_shift, en_shift):
    return [(s * en + e, (s + sky_shift) % sky * en + (e + en_shift) % en) for s in range(sky) for e in range(en)]


def local(flux, exposure, background, observed, psf_radius, band_low, band_high, disp_raw):
    block, rows, width = flux.shape
    bins = disp_raw.shape[0]
    sky, en = lax.axis_size("sky"), lax.axis_size("en")
    shifts = [1] if en == 2 else [1, -1]
    dirs = len(shifts)
    slots = block + REACH * dirs
    parts = min(4, block // 4)

    def tiles(count, dtype=F32):
        return jax.ShapeDtypeStruct((count, rows, width), dtype)

    def edges(count):
        return jax.ShapeDtypeStruct((count // 4, 128, 128), F32)

    def weights(count):
        return jax.ShapeDtypeStruct((count, 128, 256), BF16)

    def scratch(shape):
        return pltpu.VMEM(shape.shape, shape.dtype)

    lanes = jax.ShapeDtypeStruct((1, 128), F32)

    flux, exposure_in, background, observed = [
        pltpu.with_memory_space_constraint(array, pltpu.HBM) for array in (flux, exposure, background, observed)
    ]
    half = block // 2

    def halo(last, first):
        return lax.ppermute(last, "sky", ring(sky, 1)), lax.ppermute(first, "sky", ring(sky, -1))

    def neighbours(arrays):
        return [lax.ppermute(array, "en", ring(en, shift)) for array, shift in zip(arrays, shifts)]

    weighted, last, first, *sent = pl.pallas_call(
        functools.partial(pack_kernel, parts, en),
        in_specs=[ANY] * 4,
        out_specs=[VMEM] * (3 + dirs),
        out_shape=[tiles(block), edges(block), edges(block)] + [tiles(2 * REACH)] * dirs,
        scratch_shapes=[
            scratch(tiles(block)), scratch(tiles(block)), pltpu.VMEM((dirs, REACH, rows, width), jnp.int32),
            pltpu.SemaphoreType.DMA((2, parts)), pltpu.SemaphoreType.DMA((dirs, 2)),
        ],
        compiler_params=params(12),
        name="weight_and_pack",
    )(flux, exposure_in, background, observed)
    before, after = halo(last, first)
    counts = neighbours(sent)

    centre, band, edge, fold, background, observed = pl.pallas_call(
        functools.partial(weights_kernel, en),
        in_specs=[SMEM] * 4 + [VMEM] + [ANY] * 2,
        out_specs=[VMEM] * 3 + [SMEM] + [VMEM] * 2,
        out_shape=[
            tiles(block), weights(block), weights(block), jax.ShapeDtypeStruct((5 * (slots + 4),), F32),
            tiles(block), tiles(block, jnp.int32),
        ],
        scratch_shapes=[pltpu.SemaphoreType.DMA((2,))],
        compiler_params=params(4),
        cost_estimate=cost(block, 1, block * 2**15),
        name="weights_and_centre",
    )(psf_radius, band_low, band_high, disp_raw, weighted, background, observed)
    sent = pl.pallas_call(
        functools.partial(blur_kernel, en),
        in_specs=[VMEM] * 5,
        out_specs=[VMEM] * dirs,
        out_shape=[tiles(4)] * dirs,
        compiler_params=params(4),
        cost_estimate=cost(4 * dirs, 2),
        name="blur_border",
    )(centre, band, edge, before, after)
    received = neighbours(sent)
    resid, loss = pl.pallas_call(
        functools.partial(middle_kernel, en),
        in_specs=[SMEM] + [VMEM] * 7,
        out_specs=[VMEM] * 2,
        out_shape=[tiles(slots + 4), jax.ShapeDtypeStruct((8, 128), F32)],
        scratch_shapes=[scratch(tiles(block)), scratch(tiles(block + 4))],
        compiler_params=params(10),
        cost_estimate=cost(block, 2, block * 2**15),
        name="blur_residual",
    )(fold, centre, band, edge, before, after, background, observed)
    resid, total = pl.pallas_call(
        functools.partial(border_kernel, en),
        in_specs=[SMEM] + [VMEM] * (4 + 3 * dirs),
        out_specs=[VMEM] * 2,
        out_shape=[tiles(slots + 4), lanes],
        input_output_aliases={3: 0},
        scratch_shapes=[scratch(tiles(8)), scratch(tiles(4)), scratch(tiles(4))],
        compiler_params=params(4),
        cost_estimate=cost(4 * dirs, 1),
        name="border_residual_loss",
    )(fold, background, observed, resid, loss, *sent, *received, *counts)
    back, last, first = pl.pallas_call(
        functools.partial(fold_kernel, en),
        in_specs=[SMEM, VMEM],
        out_specs=[VMEM] * 3,
        out_shape=[tiles(block), edges(block), edges(block)],
        compiler_params=params(4),
        cost_estimate=cost(block, 1),
        name="fold_back",
    )(fold, resid)

    masks = [en] + [1 << n for n in range(en.bit_length() - 1)]
    masks += [en << n for n in range(2, sky.bit_length() - 1)] + [2 * en]

    def partner(value, mask):
        return lax.ppermute(value, ("sky", "en"), [(i, i ^ mask) for i in range(sky * en)])

    moved = partner(total, masks[0])
    before, after = halo(last, first)
    centre, total = pl.pallas_call(
        centre_kernel,
        in_specs=[VMEM] * 4,
        out_specs=[VMEM] * 2,
        out_shape=[tiles(block), lanes],
        compiler_params=params(4),
        cost_estimate=cost(block, 1),
        name="back_centre",
    )(back, band, total, moved)
    for mask in masks[1:-2]:
        total = total + partner(total, mask)
    grad = []
    for part in range(2):
        moved = partner(total, masks[part - 2])
        *grad, passed = pl.pallas_call(
            functools.partial(final_kernel, part),
            in_specs=[VMEM] * 7 + [ANY] * part,
            out_specs=[ANY, VMEM],
            out_shape=[tiles(block), lanes],
            scratch_shapes=[scratch(tiles(half)), scratch(tiles(half)), pltpu.SemaphoreType.DMA((half // 4,))],
            input_output_aliases={7: 0} if part else {},
            compiler_params=params(8),
            cost_estimate=cost(half, 2),
            name="back_edges_lat_exposure",
        )(centre, band, edge, before, after, exposure, total, *grad)
        total = passed + moved
    return grad[0], total[0, 0] / F32(rows * width * bins * sky)


def solution(mesh):
    placed = (P("en", None, "sky"),) * 4 + (P(),) * 4
    return jax.shard_map(local, mesh=mesh, in_specs=placed, out_specs=(P("en", None, "sky"), P()), check_vma=False)
```

```python
import functools

import jax
import jax.numpy as jnp
from jax import lax
from jax.experimental import pallas as pl
from jax.experimental.pallas import tpu as pltpu
from jax.sharding import PartitionSpec as P

RMAX = 32
REACH = 2
F32 = jnp.float32
BF16 = jnp.bfloat16
SMEM = pl.BlockSpec(memory_space=pltpu.SMEM)
ANY = pl.BlockSpec(memory_space=pl.ANY)
VMEM = pl.BlockSpec(memory_space=pltpu.VMEM)
HBM = pl.BlockSpec(memory_space=pltpu.HBM)


def split(x):
    hi = x.astype(BF16)
    return hi, (x - hi.astype(F32)).astype(BF16)


def params(mib=56):
    return pltpu.CompilerParams(vmem_limit_bytes=mib * 2**20)


def blocks(count, rows, cols):
    return pl.BlockSpec((count, rows, cols), lambda i: (i, 0, 0))


def chunk_copy(source, target, sem, c, size):
    at = pl.ds(c * size, size)
    return pltpu.make_async_copy(source.at[at], target.at[at], sem)


def run_stages(groups, size, stages, events=(), arrive=None):
    stages = [(*stage, groups)[:3] for stage in stages]
    marks = {0} | {lag for _, lag, _ in stages} | {lag + count for _, lag, count in stages} | {at for at, _ in events}
    marks = sorted(marks)
    for start, stop in zip(marks, marks[1:] + [marks[-1]]):
        for at, event in events:
            if at == start:
                event()
        active = [(n, stage, lag) for n, (stage, lag, count) in enumerate(stages) if lag <= start < lag + count]
        if stop == start or not active:
            continue

        def step(p, carry):
            if arrive is not None:
                for n, _, lag in active:
                    arrive(n, p - lag)
            stores = []
            for _, stage, lag in active:
                for i in range(size):
                    stores += stage((p - lag) * size + i)
            for ref, index, value in stores:
                if index is None:
                    ref[...] += value
                else:
                    ref[index] = value
            return carry

        lax.fori_loop(start, stop, step, 0)


def cost(tiles, products, transcendentals=0):
    return pl.CostEstimate(flops=tiles * products * 2 * 128 * 256 * 256, bytes_accessed=tiles * 2**16, transcendentals=transcendentals)


class Place:
    def __init__(self, block, en):
        self.block, self.en = block, en
        self.me = lax.axis_index("en")
        self.dirs = 1 if en == 2 else 2
        self.extra = REACH * self.dirs
        self.slots, self.bins = block + self.extra, block * en
        self.own = jnp.where(self.me == 0, 0, REACH) if en == 2 else REACH
        self.first_bin = self.me * block - self.own

    def above(self, d):
        return jnp.where(self.me == 0, 1, 0) if self.en == 2 else 1 - d

    def sent(self, d, width):
        return self.above(d) * (self.block - width)

    def border(self, d):
        up = self.above(d) if self.en == 2 else d
        return up, up * (self.block + self.own - REACH)

    def clamp(self, g):
        return jnp.clip(g, 0, self.bins - 1)


def lanes_of(shape=(128, 128)):
    return lax.broadcasted_iota(jnp.int32, shape, 1)


def is_odd():
    return lax.axis_index("sky") % 2 == 1


def pack_edges(tiles):
    lane = lanes_of()
    outer = (lane < RMAX) | (lane >= 128 - RMAX)
    early, late = [jnp.where(outer, tiles[n], pltpu.roll(tiles[n + 1], 64, 1)) for n in (0, 2)]
    late = pltpu.roll(late, RMAX, 1)
    mask = ((lane // RMAX) % 2 == 1) != is_odd()
    return jnp.where(mask, early, late), jnp.where(mask, late, early)


LEFT = (3, 1, 0, 2)
RIGHT = (0, 2, 1, 3)


def edge_tile(near, far, n):
    lane = lanes_of()
    from_left = lane < RMAX * RIGHT[n] if LEFT[n] < RIGHT[n] else lane >= RMAX * LEFT[n]
    return jnp.where(from_left != is_odd(), far, near)


def twice(x):
    return jnp.concatenate([x, x], axis=0)


def lon_product(tile, weights):
    out = jnp.dot(jnp.concatenate(split(tile), axis=1), twice(weights), preferred_element_type=F32)
    return out[:, :128] + out[:, 128:]


def lat_product(weights, tile):
    out = jnp.dot(weights, twice(jnp.concatenate(split(tile), axis=1)), preferred_element_type=F32)
    return out[:, :128] + out[:, 128:]


def profile(radius, column):
    wide = jnp.full((1, 128), radius, jnp.int32).astype(F32)
    reach = wide * wide
    factor = -2.0 / reach
    lane = lax.broadcasted_iota(jnp.int32, (1, 128), 1)
    square = (lane * lane).astype(F32)
    values = jnp.where(square <= reach, jnp.exp(square * factor), 0.0)
    norm = 2.0 * jnp.sum(values, axis=1, keepdims=True) - 1.0
    root = jnp.sqrt(jnp.full((1, 128), column, F32))[:, :1]
    return factor[:, :1], 1.0 / (norm * root), reach[:, :1]


def taper_values(diff, ok, factor, scale, reach):
    square = diff * diff
    return jnp.where((square <= reach) & ok, jnp.exp(square * factor) * scale, 0.0)


def pack_kernel(parts, en, flux, exposure, background, observed, weighted, near, far, *rest):
    place = Place(flux.shape[0], en)
    dirs, block = place.dirs, place.block
    sent, (v_flux, v_exposure, v_observed, sems, near_sems) = rest[:dirs], rest[dirs:]
    chunk = block // parts

    def arrivals(c):
        return [chunk_copy(a, b, sems.at[n, c], c, chunk) for n, (a, b) in enumerate(((flux, v_flux), (exposure, v_exposure)))]

    def near_arrivals(d):
        at = pl.ds(place.sent(d, REACH), REACH)
        return [
            pltpu.make_async_copy(background.at[at], sent[d].at[pl.ds(0, REACH)], near_sems.at[d, 0]),
            pltpu.make_async_copy(observed.at[at], v_observed.at[d], near_sems.at[d, 1]),
        ]

    for c in range(parts):
        for copy in arrivals(c):
            copy.start()
    for d in range(dirs):
        for copy in near_arrivals(d):
            copy.start()

    def some(g, carry):
        tiles = [v_flux[4 * g + i] * v_exposure[4 * g + i] for i in range(4)]
        packed = pack_edges(tiles)
        for i in range(4):
            weighted[4 * g + i] = tiles[i]
        near[g], far[g] = packed
        return carry

    for c in range(parts):
        for copy in arrivals(c):
            copy.wait()
        lax.fori_loop(c * chunk // 4, (c + 1) * chunk // 4, some, 0)
    for d in range(dirs):
        for copy in near_arrivals(d):
            copy.wait()
        for k in range(REACH):
            sent[d][REACH + k] = v_observed[d, k].astype(F32)


def weights_kernel(en, radius, low, high, disp, weighted, background, observed,
                   centre, band, edge, fold, near_background, near_observed, sems):
    fetches = [
        pltpu.make_async_copy(background, near_background, sems.at[0]),
        pltpu.make_async_copy(observed, near_observed, sems.at[1]),
    ]
    for fetch in fetches:
        fetch.start()
    block = weighted.shape[0]
    place = Place(block, en)
    row = lax.broadcasted_iota(jnp.int32, (128, 128), 0)
    col = lax.broadcasted_iota(jnp.int32, (128, 128), 1)
    near = (row - col).astype(F32)
    always = row >= 0
    beside = []
    for n in range(4):
        shift = jnp.where(row // RMAX == LEFT[n], -RMAX - RMAX * LEFT[n], 128 - RMAX * RIGHT[n])
        held = (row // RMAX == LEFT[n]) | (row // RMAX == RIGHT[n])
        beside.append(((row + shift - col).astype(F32), held))

    def weight(i, j):
        at, to = place.clamp(i), place.clamp(j)
        inside = (i == at) & (j == to) & (low[at] <= j - i) & (j - i <= high[at])
        return jnp.where(inside, disp[at, to], 0.0)

    def fold_row(g):
        for o in range(-REACH, REACH + 1):
            fold[5 * (g - place.first_bin + REACH) + o + REACH] = weight(g, g + o)

    def make(g, n):
        fold_row(g)
        column = weight(g, g)
        for o in (-2, -1, 1, 2):
            column = column + weight(g - o, g)
        numbers = profile(radius[place.clamp(g)], jnp.where(column > 0.0, column, 1.0))
        return tuple(
            jnp.concatenate(split(taper_values(diff, ok, *numbers)), axis=1) for diff, ok in ((near, always), beside[n])
        )

    for s in (0, 1, place.slots + 2, place.slots + 3):
        for o in range(5):
            fold[5 * s + o] = 0.0

    def some(g):
        made = [make(place.me * block + 4 * g + n, n) for n in range(4)]
        return [(band, 4 * g + n, made[n][0]) for n in range(4)] + [(edge, 4 * g + n, made[n][1]) for n in range(4)]

    def lon(g):
        return [(centre, 4 * g + n, lon_product(weighted[4 * g + n], band[4 * g + n])) for n in range(4)]

    run_stages(block // 4, 1, [(some, 0), (lon, 1)])
    for d in range(place.dirs):
        up, slot = place.border(d)
        for k in range(REACH):
            fold_row(place.first_bin + slot + up * REACH + k)
    for fetch in fetches:
        fetch.wait()


def lon_edges(centre, edge, far, near, g, at, n):
    return centre[at] + lon_product(edge_tile(near[g], far[g], n), edge[at])


def blur_kernel(en, centre, band, edge, far, near, *blurred):
    place = Place(centre.shape[0], en)
    for d in range(place.dirs):
        start = place.sent(d, 4)
        g = lax.div(start, 4) if en == 2 else start // 4
        sums = [lon_edges(centre, edge, far, near, g, start + n, n) for n in range(4)]
        sums = [lat_product(band[start + n], sums[n]) for n in range(4)]
        for n in range(4):
            blurred[d][n] = sums[n]


def loss_terms(mu, counts):
    return (mu - counts * jnp.log(mu)).reshape(16, 8, 128).sum(0)


def middle_kernel(en, fold, centre, band, edge, far, near, background, observed, resid, loss, whole, blurred):
    block = centre.shape[0]
    place = Place(block, en)
    own = place.own
    zero = jnp.zeros((128, 128), F32)
    for s in (0, 1, block + 2, block + 3):
        blurred[s] = zero
    for s in (0, 1, place.slots + 2, place.slots + 3):
        resid[s] = zero
    loss[...] = jnp.zeros((8, 128), F32)
    inside = (own, own + block - REACH) if en == 2 else (REACH, block - REACH)

    def lon(g):
        return [(whole, 4 * g + n, lon_edges(centre, edge, far, near, g, 4 * g + n, n)) for n in range(4)]

    def lat(g):
        return [(blurred, 4 * g + n + 2, lat_product(band[4 * g + n], whole[4 * g + n])) for n in range(4)]

    def residual(g):
        stores = []
        for b in [4 * g + n for n in range(4)]:
            mu = background[b]
            for o in range(5):
                mu = mu + fold[5 * (b + own + 2) + o] * blurred[b + o]
            counts = observed[b].astype(F32)
            inner = (b >= inside[0]) & (b < inside[1])
            stores += [(resid, b + own + 2, 1.0 - counts / mu), (loss, None, jnp.where(inner, loss_terms(mu, counts), 0.0))]
        return stores

    run_stages(block // 8, 2, [(lon, 0), (lat, 1), (residual, 3)])


def border_kernel(en, fold, background, observed, resid_in, loss, *rest):
    block = background.shape[0]
    place = Place(block, en)
    sent, received, counts = [rest[n * place.dirs:(n + 1) * place.dirs] for n in range(3)]
    resid, total, blurred, ground, seen = rest[3 * place.dirs:]
    sums = loss[...]
    for d in range(place.dirs):
        up, slot = place.border(d)
        mine, theirs = 4 * (1 - up), 4 * up
        for k in range(4):
            blurred[mine + k] = sent[place.dirs - 1 - d][k]
            blurred[theirs + k] = received[d][k]
        first = place.sent(d, REACH) if en == 2 else up * (block - REACH)
        for k in range(REACH):
            ground[mine // 2 + k] = background[first + k]
            seen[mine // 2 + k] = observed[first + k].astype(F32)
            ground[theirs // 2 + k] = counts[d][k]
            seen[theirs // 2 + k] = counts[d][REACH + k]
        for j in range(2 * REACH):
            mu = ground[j]
            for o in range(5):
                mu = mu + fold[5 * (slot + j + 2) + o] * blurred[j + o]
            resid[slot + j + 2] = 1.0 - seen[j] / mu
            is_mine = (mine // 2 <= j) & (j < mine // 2 + REACH)
            sums = sums + jnp.where(is_mine, loss_terms(mu, seen[j]), 0.0)
    total[...] = jnp.full((1, 128), jnp.sum(sums), F32)


def fold_kernel(en, fold, resid, back, near, far):
    place = Place(back.shape[0], en)

    def fold_back(g):
        tiles = []
        for b in [4 * g + n for n in range(4)]:
            slot = b + place.own
            total = None
            for o in range(5):
                term = fold[5 * (slot + 4 - o) + o] * resid[slot + 4 - o]
                total = term if total is None else total + term
            tiles.append(total)
        packed = pack_edges(tiles)
        return [(back, 4 * g + n, tiles[n]) for n in range(4)] + [(near, g, packed[0]), (far, g, packed[1])]

    run_stages(back.shape[0] // 8, 2, [(fold_back, 0)])


def centre_kernel(back, band, total, moved, out, passed):
    passed[...] = total[...] + moved[...]
    size = 8

    def some(g, carry):
        sums = [lon_product(back[size * g + i], band[size * g + i]) for i in range(size)]
        for i in range(size):
            out[size * g + i] = sums[i]
        return carry

    lax.fori_loop(0, back.shape[0] // size, some, 0)


def final_kernel(part, centre, band, edge, far, near, exposure, total, *rest):
    out, passed, whole, v_out, out_sems = rest[part:]
    groups = near.shape[0] // 2
    first = part * 4 * groups
    size = min(2, groups)
    steps = groups // size
    passed[...] = total[...]

    def copy_out(p):
        count = 4 * size
        return pltpu.make_async_copy(v_out.at[pl.ds(p * count, count)], out.at[pl.ds(first + p * count, count)], out_sems.at[p])

    def lon(g):
        return [(whole, 4 * g + n, lon_edges(centre, edge, far, near, part * groups + g, first + 4 * g + n, n)) for n in range(4)]

    def lat(g):
        bins = [4 * g + n for n in range(4)]
        return [(v_out, b, lat_product(band[first + b], whole[b]) * exposure[first + b]) for b in bins]

    run_stages(steps, size, [(lon, 0), (lat, 1)], events=[(p + 2, copy_out(p).start) for p in range(steps)])
    for p in range(steps):
        copy_out(p).wait()


def ring(size, shift):
    return [(i, (i + shift) % size) for i in range(size)]


def local(flux, exposure, background, observed, psf_radius, band_low, band_high, disp_raw):
    block, rows, width = flux.shape
    bins = disp_raw.shape[0]
    sky, en = lax.axis_size("sky"), lax.axis_size("en")
    shifts = [1] if en == 2 else [1, -1]
    dirs = len(shifts)
    slots = block + REACH * dirs
    parts = min(4, block // 4)

    def tiles(count, dtype=F32):
        return jax.ShapeDtypeStruct((count, rows, width), dtype)

    def edges(count):
        return jax.ShapeDtypeStruct((count // 4, 128, 128), F32)

    def weights(count):
        return jax.ShapeDtypeStruct((count, 128, 256), BF16)

    def scratch(shape):
        return pltpu.VMEM(shape.shape, shape.dtype)

    lanes = jax.ShapeDtypeStruct((1, 128), F32)

    flux, exposure_in, background, observed = [
        pltpu.with_memory_space_constraint(array, pltpu.HBM) for array in (flux, exposure, background, observed)
    ]
    half = block // 2

    def swap_far(edges):
        return lax.ppermute(edges, "sky", [(s, (s + 1 if s % 2 else s - 1) % sky) for s in range(sky)])

    def swap_near(edges):
        return lax.ppermute(edges, "sky", [(s, s ^ 1) for s in range(sky)])

    def neighbours(arrays):
        return [lax.ppermute(array, "en", ring(en, shift)) for array, shift in zip(arrays, shifts)]

    weighted, near, far, *sent = pl.pallas_call(
        functools.partial(pack_kernel, parts, en),
        in_specs=[ANY] * 4,
        out_specs=[VMEM] * (3 + dirs),
        out_shape=[tiles(block), edges(block), edges(block)] + [tiles(2 * REACH)] * dirs,
        scratch_shapes=[
            scratch(tiles(block)), scratch(tiles(block)), pltpu.VMEM((dirs, REACH, rows, width), jnp.int32),
            pltpu.SemaphoreType.DMA((2, parts)), pltpu.SemaphoreType.DMA((dirs, 2)),
        ],
        compiler_params=params(12),
        name="weight_and_pack",
    )(flux, exposure_in, background, observed)
    far, near = swap_far(far), swap_near(near)
    counts = neighbours(sent)

    centre, band, edge, fold, background, observed = pl.pallas_call(
        functools.partial(weights_kernel, en),
        in_specs=[SMEM] * 4 + [VMEM] + [ANY] * 2,
        out_specs=[VMEM] * 3 + [SMEM] + [VMEM] * 2,
        out_shape=[
            tiles(block), weights(block), weights(block), jax.ShapeDtypeStruct((5 * (slots + 4),), F32),
            tiles(block), tiles(block, jnp.int32),
        ],
        scratch_shapes=[pltpu.SemaphoreType.DMA((2,))],
        compiler_params=params(4),
        cost_estimate=cost(block, 1, block * 2**15),
        name="weights_and_centre",
    )(psf_radius, band_low, band_high, disp_raw, weighted, background, observed)
    sent = pl.pallas_call(
        functools.partial(blur_kernel, en),
        in_specs=[VMEM] * 5,
        out_specs=[VMEM] * dirs,
        out_shape=[tiles(4)] * dirs,
        compiler_params=params(4),
        cost_estimate=cost(4 * dirs, 2),
        name="blur_border",
    )(centre, band, edge, far, near)
    received = neighbours(sent)
    resid, loss = pl.pallas_call(
        functools.partial(middle_kernel, en),
        in_specs=[SMEM] + [VMEM] * 7,
        out_specs=[VMEM] * 2,
        out_shape=[tiles(slots + 4), jax.ShapeDtypeStruct((8, 128), F32)],
        scratch_shapes=[scratch(tiles(block)), scratch(tiles(block + 4))],
        compiler_params=params(10),
        cost_estimate=cost(block, 2, block * 2**15),
        name="blur_residual",
    )(fold, centre, band, edge, far, near, background, observed)
    resid, total = pl.pallas_call(
        functools.partial(border_kernel, en),
        in_specs=[SMEM] + [VMEM] * (4 + 3 * dirs),
        out_specs=[VMEM] * 2,
        out_shape=[tiles(slots + 4), lanes],
        input_output_aliases={3: 0},
        scratch_shapes=[scratch(tiles(8)), scratch(tiles(4)), scratch(tiles(4))],
        compiler_params=params(4),
        cost_estimate=cost(4 * dirs, 1),
        name="border_residual_loss",
    )(fold, background, observed, resid, loss, *sent, *received, *counts)
    back, near, far = pl.pallas_call(
        functools.partial(fold_kernel, en),
        in_specs=[SMEM, VMEM],
        out_specs=[VMEM] * 3,
        out_shape=[tiles(block), edges(block), edges(block)],
        compiler_params=params(4),
        cost_estimate=cost(block, 1),
        name="fold_back",
    )(fold, resid)

    masks = [1 << n for n in range(en.bit_length() - 1)] + [en << n for n in range(2, sky.bit_length() - 1)] + [3 * en, en]

    def partner(value, mask):
        return lax.ppermute(value, ("sky", "en"), [(i, i ^ mask) for i in range(sky * en)])

    far, near = swap_far(far), swap_near(near)
    centre, total = pl.pallas_call(
        centre_kernel,
        in_specs=[VMEM] * 4,
        out_specs=[VMEM] * 2,
        out_shape=[tiles(block), lanes],
        compiler_params=params(4),
        cost_estimate=cost(block, 1),
        name="back_centre",
    )(back, band, total, partner(total, masks[0]))
    for mask in masks[1:-2]:
        total = total + partner(total, mask)
    grad = []
    for part in range(2):
        moved = partner(total, masks[part - 2])
        *grad, passed = pl.pallas_call(
            functools.partial(final_kernel, part),
            in_specs=[VMEM] * 7 + [ANY] * part,
            out_specs=[ANY, VMEM],
            out_shape=[tiles(block), lanes],
            scratch_shapes=[scratch(tiles(half)), scratch(tiles(half)), pltpu.SemaphoreType.DMA((half // 4,))],
            input_output_aliases={7: 0} if part else {},
            compiler_params=params(8),
            cost_estimate=cost(half, 2),
            name="back_edges_lat_exposure",
        )(centre, band, edge, far, near, exposure, total, *grad)
        total = passed + moved
    return grad[0], total[0, 0] / F32(rows * width * bins * sky)


def solution(mesh):
    placed = (P("en", None, "sky"),) * 4 + (P(),) * 4
    return jax.shard_map(local, mesh=mesh, in_specs=placed, out_specs=(P("en", None, "sky"), P()), check_vma=False)
```

```python
import functools

import jax
import jax.numpy as jnp
from jax import lax
from jax.experimental import pallas as pl
from jax.experimental.pallas import tpu as pltpu
from jax.sharding import PartitionSpec as P

RMAX = 32
REACH = 2
F32 = jnp.float32
BF16 = jnp.bfloat16
SMEM = pl.BlockSpec(memory_space=pltpu.SMEM)
ANY = pl.BlockSpec(memory_space=pl.ANY)
VMEM = pl.BlockSpec(memory_space=pltpu.VMEM)
HBM = pl.BlockSpec(memory_space=pltpu.HBM)


def split(x):
    hi = x.astype(BF16)
    return hi, (x - hi.astype(F32)).astype(BF16)


def params(mib=56):
    return pltpu.CompilerParams(vmem_limit_bytes=mib * 2**20)


def blocks(count, rows, cols):
    return pl.BlockSpec((count, rows, cols), lambda i: (i, 0, 0))


def chunk_copy(source, target, sem, c, size):
    at = pl.ds(c * size, size)
    return pltpu.make_async_copy(source.at[at], target.at[at], sem)


def run_stages(groups, size, stages, events=(), arrive=None):
    stages = [(*stage, groups)[:3] for stage in stages]
    marks = {0} | {lag for _, lag, _ in stages} | {lag + count for _, lag, count in stages} | {at for at, _ in events}
    marks = sorted(marks)
    for start, stop in zip(marks, marks[1:] + [marks[-1]]):
        for at, event in events:
            if at == start:
                event()
        active = [(n, stage, lag) for n, (stage, lag, count) in enumerate(stages) if lag <= start < lag + count]
        if stop == start or not active:
            continue

        def step(p, carry):
            if arrive is not None:
                for n, _, lag in active:
                    arrive(n, p - lag)
            stores = []
            for _, stage, lag in active:
                for i in range(size):
                    stores += stage((p - lag) * size + i)
            for ref, index, value in stores:
                if index is None:
                    ref[...] += value
                else:
                    ref[index] = value
            return carry

        lax.fori_loop(start, stop, step, 0)


def cost(tiles, products, transcendentals=0):
    return pl.CostEstimate(flops=tiles * products * 2 * 128 * 256 * 256, bytes_accessed=tiles * 2**16, transcendentals=transcendentals)


class Place:
    def __init__(self, block, en):
        self.block, self.en = block, en
        self.me = lax.axis_index("en")
        self.dirs = 1 if en == 2 else 2
        self.extra = REACH * self.dirs
        self.slots, self.bins = block + self.extra, block * en
        self.own = jnp.where(self.me == 0, 0, REACH) if en == 2 else REACH
        self.first_bin = self.me * block - self.own

    def above(self, d):
        return jnp.where(self.me == 0, 1, 0) if self.en == 2 else 1 - d

    def sent(self, d, width):
        return self.above(d) * (self.block - width)

    def border(self, d):
        up = self.above(d) if self.en == 2 else d
        return up, up * (self.block + self.own - REACH)

    def clamp(self, g):
        return jnp.clip(g, 0, self.bins - 1)


def lanes_of(shape=(128, 128)):
    return lax.broadcasted_iota(jnp.int32, shape, 1)


def is_odd():
    return lax.axis_index("sky") % 2 == 1


def pack_edges(tiles):
    lane = lanes_of()
    outer = (lane < RMAX) | (lane >= 128 - RMAX)
    early, late = [jnp.where(outer, tiles[n], pltpu.roll(tiles[n + 1], 64, 1)) for n in (0, 2)]
    late = pltpu.roll(late, RMAX, 1)
    mask = ((lane // RMAX) % 2 == 1) != is_odd()
    return jnp.where(mask, early, late), jnp.where(mask, late, early)


LEFT = (3, 1, 0, 2)
RIGHT = (0, 2, 1, 3)


def edge_tile(near, far, n):
    lane = lanes_of()
    from_left = lane < RMAX * RIGHT[n] if LEFT[n] < RIGHT[n] else lane >= RMAX * LEFT[n]
    return jnp.where(from_left != is_odd(), far, near)


def twice(x):
    return jnp.concatenate([x, x], axis=0)


def lon_product(tile, weights):
    out = jnp.dot(jnp.concatenate(split(tile), axis=1), twice(weights), preferred_element_type=F32)
    return out[:, :128] + out[:, 128:]


def lat_product(weights, tile):
    out = jnp.dot(weights, twice(jnp.concatenate(split(tile), axis=1)), preferred_element_type=F32)
    return out[:, :128] + out[:, 128:]


def profile(radius, column):
    wide = jnp.full((1, 128), radius, jnp.int32).astype(F32)
    reach = wide * wide
    factor = -2.0 / reach
    lane = lax.broadcasted_iota(jnp.int32, (1, 128), 1)
    square = (lane * lane).astype(F32)
    values = jnp.where(square <= reach, jnp.exp(square * factor), 0.0)
    norm = 2.0 * jnp.sum(values, axis=1, keepdims=True) - 1.0
    root = jnp.sqrt(jnp.full((1, 128), column, F32))[:, :1]
    return factor[:, :1], 1.0 / (norm * root), reach[:, :1]


def taper_values(diff, ok, factor, scale, reach):
    square = diff * diff
    return jnp.where((square <= reach) & ok, jnp.exp(square * factor) * scale, 0.0)


def pack_kernel(parts, en, flux, exposure, background, observed, weighted, near, far, *rest):
    place = Place(flux.shape[0], en)
    dirs, block = place.dirs, place.block
    sent, (v_flux, v_exposure, v_observed, sems, near_sems) = rest[:dirs], rest[dirs:]
    chunk = block // parts

    def arrivals(c):
        return [chunk_copy(a, b, sems.at[n, c], c, chunk) for n, (a, b) in enumerate(((flux, v_flux), (exposure, v_exposure)))]

    def near_arrivals(d):
        at = pl.ds(place.sent(d, REACH), REACH)
        return [
            pltpu.make_async_copy(background.at[at], sent[d].at[pl.ds(0, REACH)], near_sems.at[d, 0]),
            pltpu.make_async_copy(observed.at[at], v_observed.at[d], near_sems.at[d, 1]),
        ]

    for c in range(parts):
        for copy in arrivals(c):
            copy.start()
    for d in range(dirs):
        for copy in near_arrivals(d):
            copy.start()

    def some(g, carry):
        tiles = [v_flux[4 * g + i] * v_exposure[4 * g + i] for i in range(4)]
        packed = pack_edges(tiles)
        for i in range(4):
            weighted[4 * g + i] = tiles[i]
        near[g], far[g] = packed
        return carry

    for c in range(parts):
        for copy in arrivals(c):
            copy.wait()
        lax.fori_loop(c * chunk // 4, (c + 1) * chunk // 4, some, 0)
    for d in range(dirs):
        for copy in near_arrivals(d):
            copy.wait()
        for k in range(REACH):
            sent[d][REACH + k] = v_observed[d, k].astype(F32)


def weights_kernel(en, radius, low, high, disp, weighted, background, observed,
                   centre, band, edge, fold, near_background, near_observed, sems):
    fetches = [
        pltpu.make_async_copy(background, near_background, sems.at[0]),
        pltpu.make_async_copy(observed, near_observed, sems.at[1]),
    ]
    for fetch in fetches:
        fetch.start()
    block = weighted.shape[0]
    place = Place(block, en)
    row = lax.broadcasted_iota(jnp.int32, (128, 128), 0)
    col = lax.broadcasted_iota(jnp.int32, (128, 128), 1)
    near = (row - col).astype(F32)
    always = row >= 0
    beside = []
    for n in range(4):
        shift = jnp.where(row // RMAX == LEFT[n], -RMAX - RMAX * LEFT[n], 128 - RMAX * RIGHT[n])
        held = (row // RMAX == LEFT[n]) | (row // RMAX == RIGHT[n])
        beside.append(((row + shift - col).astype(F32), held))

    def weight(i, j):
        at, to = place.clamp(i), place.clamp(j)
        inside = (i == at) & (j == to) & (low[at] <= j - i) & (j - i <= high[at])
        return jnp.where(inside, disp[at, to], 0.0)

    def fold_row(g):
        for o in range(-REACH, REACH + 1):
            fold[5 * (g - place.first_bin + REACH) + o + REACH] = weight(g, g + o)

    def make(g, n):
        fold_row(g)
        column = weight(g, g)
        for o in (-2, -1, 1, 2):
            column = column + weight(g - o, g)
        numbers = profile(radius[place.clamp(g)], jnp.where(column > 0.0, column, 1.0))
        return tuple(
            jnp.concatenate(split(taper_values(diff, ok, *numbers)), axis=1) for diff, ok in ((near, always), beside[n])
        )

    for s in (0, 1, place.slots + 2, place.slots + 3):
        for o in range(5):
            fold[5 * s + o] = 0.0

    def some(g):
        made = [make(place.me * block + 4 * g + n, n) for n in range(4)]
        return [(band, 4 * g + n, made[n][0]) for n in range(4)] + [(edge, 4 * g + n, made[n][1]) for n in range(4)]

    def lon(g):
        return [(centre, 4 * g + n, lon_product(weighted[4 * g + n], band[4 * g + n])) for n in range(4)]

    run_stages(block // 4, 1, [(some, 0), (lon, 1)])
    for d in range(place.dirs):
        up, slot = place.border(d)
        for k in range(REACH):
            fold_row(place.first_bin + slot + up * REACH + k)
    for fetch in fetches:
        fetch.wait()


def lon_edges(centre, edge, far, near, g, at, n):
    return centre[at] + lon_product(edge_tile(near[g], far[g], n), edge[at])


def blur_kernel(en, centre, band, edge, far, near, *blurred):
    place = Place(centre.shape[0], en)
    for d in range(place.dirs):
        start = place.sent(d, 4)
        g = lax.div(start, 4) if en == 2 else start // 4
        sums = [lon_edges(centre, edge, far, near, g, start + n, n) for n in range(4)]
        sums = [lat_product(band[start + n], sums[n]) for n in range(4)]
        for n in range(4):
            blurred[2 * d + n // 2][n % 2] = sums[n]


def loss_terms(mu, counts):
    return (mu - counts * jnp.log(mu)).reshape(16, 8, 128).sum(0)


def middle_kernel(en, fold, centre, band, edge, far, near, background, observed, resid, loss, whole, blurred):
    block = centre.shape[0]
    place = Place(block, en)
    own = place.own
    zero = jnp.zeros((128, 128), F32)
    for s in (0, 1, block + 2, block + 3):
        blurred[s] = zero
    for s in (0, 1, place.slots + 2, place.slots + 3):
        resid[s] = zero
    loss[...] = jnp.zeros((8, 128), F32)
    inside = (own, own + block - REACH) if en == 2 else (REACH, block - REACH)

    def lon(g):
        return [(whole, 4 * g + n, lon_edges(centre, edge, far, near, g, 4 * g + n, n)) for n in range(4)]

    def lat(g):
        return [(blurred, 4 * g + n + 2, lat_product(band[4 * g + n], whole[4 * g + n])) for n in range(4)]

    def residual(g):
        stores = []
        for b in [4 * g + n for n in range(4)]:
            mu = background[b]
            for o in range(5):
                mu = mu + fold[5 * (b + own + 2) + o] * blurred[b + o]
            counts = observed[b].astype(F32)
            inner = (b >= inside[0]) & (b < inside[1])
            stores += [(resid, b + own + 2, 1.0 - counts / mu), (loss, None, jnp.where(inner, loss_terms(mu, counts), 0.0))]
        return stores

    run_stages(block // 8, 2, [(lon, 0), (lat, 1), (residual, 3)])


def border_kernel(en, fold, background, observed, resid_in, loss, *rest):
    block = background.shape[0]
    place = Place(block, en)
    dirs = place.dirs
    sent, received, counts = rest[:2 * dirs], rest[2 * dirs:4 * dirs], rest[4 * dirs:5 * dirs]
    resid, total, blurred, ground, seen = rest[5 * dirs:]
    sums = loss[...]
    for d in range(dirs):
        up, slot = place.border(d)
        mine, theirs = 4 * (1 - up), 4 * up
        for k in range(4):
            blurred[mine + k] = sent[2 * (dirs - 1 - d) + k // 2][k % 2]
            blurred[theirs + k] = received[2 * d + k // 2][k % 2]
        first = place.sent(d, REACH) if en == 2 else up * (block - REACH)
        for k in range(REACH):
            ground[mine // 2 + k] = background[first + k]
            seen[mine // 2 + k] = observed[first + k].astype(F32)
            ground[theirs // 2 + k] = counts[d][k]
            seen[theirs // 2 + k] = counts[d][REACH + k]
        for j in range(2 * REACH):
            mu = ground[j]
            for o in range(5):
                mu = mu + fold[5 * (slot + j + 2) + o] * blurred[j + o]
            resid[slot + j + 2] = 1.0 - seen[j] / mu
            is_mine = (mine // 2 <= j) & (j < mine // 2 + REACH)
            sums = sums + jnp.where(is_mine, loss_terms(mu, seen[j]), 0.0)
    total[...] = jnp.full((1, 128), jnp.sum(sums), F32)


def fold_kernel(en, fold, resid, back, near, far):
    place = Place(back.shape[0], en)

    def fold_back(g):
        tiles = []
        for b in [4 * g + n for n in range(4)]:
            slot = b + place.own
            total = None
            for o in range(5):
                term = fold[5 * (slot + 4 - o) + o] * resid[slot + 4 - o]
                total = term if total is None else total + term
            tiles.append(total)
        packed = pack_edges(tiles)
        return [(back, 4 * g + n, tiles[n]) for n in range(4)] + [(near, g, packed[0]), (far, g, packed[1])]

    run_stages(back.shape[0] // 8, 2, [(fold_back, 0)])


def centre_kernel(back, band, total, out, passed):
    passed[...] = total[...]
    size = 8

    def some(g, carry):
        sums = [lon_product(back[size * g + i], band[size * g + i]) for i in range(size)]
        for i in range(size):
            out[size * g + i] = sums[i]
        return carry

    lax.fori_loop(0, back.shape[0] // size, some, 0)


def final_kernel(part, centre, band, edge, far, near, exposure, total, *rest):
    out, passed, whole, v_out, out_sems = rest[part:]
    groups = near.shape[0] // 2
    first = part * 4 * groups
    size = min(2, groups)
    steps = groups // size
    passed[...] = total[...]

    def copy_out(p):
        count = 4 * size
        return pltpu.make_async_copy(v_out.at[pl.ds(p * count, count)], out.at[pl.ds(first + p * count, count)], out_sems.at[p])

    def lon(g):
        return [(whole, 4 * g + n, lon_edges(centre, edge, far, near, part * groups + g, first + 4 * g + n, n)) for n in range(4)]

    def lat(g):
        bins = [4 * g + n for n in range(4)]
        return [(v_out, b, lat_product(band[first + b], whole[b]) * exposure[first + b]) for b in bins]

    run_stages(steps, size, [(lon, 0), (lat, 1)], events=[(p + 2, copy_out(p).start) for p in range(steps)])
    for p in range(steps):
        copy_out(p).wait()


def tree_sum(values):
    while len(values) > 1:
        values = [a + b for a, b in zip(values[::2], values[1::2])]
    return values[0]


def ring(size, shift):
    return [(i, (i + shift) % size) for i in range(size)]


def local(flux, exposure, background, observed, psf_radius, band_low, band_high, disp_raw):
    block, rows, width = flux.shape
    bins = disp_raw.shape[0]
    sky, en = lax.axis_size("sky"), lax.axis_size("en")
    shifts = [1] if en == 2 else [1, -1]
    dirs = len(shifts)
    slots = block + REACH * dirs
    parts = min(4, block // 4)

    def tiles(count, dtype=F32):
        return jax.ShapeDtypeStruct((count, rows, width), dtype)

    def edges(count):
        return jax.ShapeDtypeStruct((count // 4, 128, 128), F32)

    def weights(count):
        return jax.ShapeDtypeStruct((count, 128, 256), BF16)

    def scratch(shape):
        return pltpu.VMEM(shape.shape, shape.dtype)

    lanes = jax.ShapeDtypeStruct((1, 128), F32)

    flux, exposure_in, background, observed = [
        pltpu.with_memory_space_constraint(array, pltpu.HBM) for array in (flux, exposure, background, observed)
    ]
    half = block // 2

    def swap_far(edges):
        return lax.ppermute(edges, "sky", [(s, (s + 1 if s % 2 else s - 1) % sky) for s in range(sky)])

    def swap_near(edges):
        return lax.ppermute(edges, "sky", [(s, s ^ 1) for s in range(sky)])

    def neighbours(arrays):
        return [lax.ppermute(array, "en", ring(en, shift)) for array, shift in zip(arrays, shifts)]

    weighted, near, far, *sent = pl.pallas_call(
        functools.partial(pack_kernel, parts, en),
        in_specs=[ANY] * 4,
        out_specs=[VMEM] * (3 + dirs),
        out_shape=[tiles(block), edges(block), edges(block)] + [tiles(2 * REACH)] * dirs,
        scratch_shapes=[
            scratch(tiles(block)), scratch(tiles(block)), pltpu.VMEM((dirs, REACH, rows, width), jnp.int32),
            pltpu.SemaphoreType.DMA((2, parts)), pltpu.SemaphoreType.DMA((dirs, 2)),
        ],
        compiler_params=params(12),
        name="weight_and_pack",
    )(flux, exposure_in, background, observed)
    far, near = swap_far(far), swap_near(near)
    counts = neighbours(sent)

    centre, band, edge, fold, background, observed = pl.pallas_call(
        functools.partial(weights_kernel, en),
        in_specs=[SMEM] * 4 + [VMEM] + [ANY] * 2,
        out_specs=[VMEM] * 3 + [SMEM] + [VMEM] * 2,
        out_shape=[
            tiles(block), weights(block), weights(block), jax.ShapeDtypeStruct((5 * (slots + 4),), F32),
            tiles(block), tiles(block, jnp.int32),
        ],
        scratch_shapes=[pltpu.SemaphoreType.DMA((2,))],
        compiler_params=params(4),
        cost_estimate=cost(block, 1, block * 2**15),
        name="weights_and_centre",
    )(psf_radius, band_low, band_high, disp_raw, weighted, background, observed)
    sent = pl.pallas_call(
        functools.partial(blur_kernel, en),
        in_specs=[VMEM] * 5,
        out_specs=[VMEM] * (2 * dirs),
        out_shape=[tiles(2)] * (2 * dirs),
        compiler_params=params(4),
        cost_estimate=cost(4 * dirs, 2),
        name="blur_border",
    )(centre, band, edge, far, near)
    received = [lax.ppermute(pair, "en", ring(en, shifts[n // 2])) for n, pair in enumerate(sent)]
    resid, loss = pl.pallas_call(
        functools.partial(middle_kernel, en),
        in_specs=[SMEM] + [VMEM] * 7,
        out_specs=[VMEM] * 2,
        out_shape=[tiles(slots + 4), jax.ShapeDtypeStruct((8, 128), F32)],
        scratch_shapes=[scratch(tiles(block)), scratch(tiles(block + 4))],
        compiler_params=params(10),
        cost_estimate=cost(block, 2, block * 2**15),
        name="blur_residual",
    )(fold, centre, band, edge, far, near, background, observed)
    resid, total = pl.pallas_call(
        functools.partial(border_kernel, en),
        in_specs=[SMEM] + [VMEM] * (4 + 5 * dirs),
        out_specs=[VMEM] * 2,
        out_shape=[tiles(slots + 4), lanes],
        input_output_aliases={3: 0},
        scratch_shapes=[scratch(tiles(8)), scratch(tiles(4)), scratch(tiles(4))],
        compiler_params=params(4),
        cost_estimate=cost(4 * dirs, 1),
        name="border_residual_loss",
    )(fold, background, observed, resid, loss, *sent, *received, *counts)
    back, near, far = pl.pallas_call(
        functools.partial(fold_kernel, en),
        in_specs=[SMEM, VMEM],
        out_specs=[VMEM] * 3,
        out_shape=[tiles(block), edges(block), edges(block)],
        compiler_params=params(4),
        cost_estimate=cost(block, 1),
        name="fold_back",
    )(fold, resid)

    def partners(value, masks):
        return [lax.ppermute(value, ("sky", "en"), [(i, i ^ mask) for i in range(sky * en)]) for mask in masks]

    far, near = swap_far(far), swap_near(near)
    moved = partners(total, [4 * en * k for k in range(1, sky // 4)])
    centre, total = pl.pallas_call(
        centre_kernel,
        in_specs=[VMEM] * 3,
        out_specs=[VMEM] * 2,
        out_shape=[tiles(block), lanes],
        compiler_params=params(4),
        cost_estimate=cost(block, 1),
        name="back_centre",
    )(back, band, total)
    grad = []
    for part, masks in enumerate(([k % en ^ (k // en * 3 * en) for k in range(1, 2 * en)], [en])):
        total = tree_sum([total] + moved)
        moved = partners(total, masks)
        *grad, total = pl.pallas_call(
            functools.partial(final_kernel, part),
            in_specs=[VMEM] * 7 + [ANY] * part,
            out_specs=[ANY, VMEM],
            out_shape=[tiles(block), lanes],
            scratch_shapes=[scratch(tiles(block // 2)), scratch(tiles(block // 2)), pltpu.SemaphoreType.DMA((block // 8,))],
            input_output_aliases={7: 0} if part else {},
            compiler_params=params(8),
            cost_estimate=cost(block // 2, 2),
            name="back_edges_lat_exposure",
        )(centre, band, edge, far, near, exposure, total, *grad)
    return grad[0], tree_sum([total] + moved)[0, 0] / F32(rows * width * bins * sky)


def solution(mesh):
    placed = (P("en", None, "sky"),) * 4 + (P(),) * 4
    return jax.shard_map(local, mesh=mesh, in_specs=placed, out_specs=(P("en", None, "sky"), P()), check_vma=False)
```

```python
import functools

import jax
import jax.numpy as jnp
from jax import lax
from jax.experimental import pallas as pl
from jax.experimental.pallas import tpu as pltpu
from jax.sharding import PartitionSpec as P

RMAX = 32
REACH = 2
F32 = jnp.float32
BF16 = jnp.bfloat16
SMEM = pl.BlockSpec(memory_space=pltpu.SMEM)
ANY = pl.BlockSpec(memory_space=pl.ANY)
VMEM = pl.BlockSpec(memory_space=pltpu.VMEM)
HBM = pl.BlockSpec(memory_space=pltpu.HBM)


def split(x):
    hi = x.astype(BF16)
    return hi, (x - hi.astype(F32)).astype(BF16)


def params(mib=56):
    return pltpu.CompilerParams(vmem_limit_bytes=mib * 2**20)


def blocks(count, rows, cols):
    return pl.BlockSpec((count, rows, cols), lambda i: (i, 0, 0))


def chunk_copy(source, target, sem, c, size):
    at = pl.ds(c * size, size)
    return pltpu.make_async_copy(source.at[at], target.at[at], sem)


def run_stages(groups, size, stages, events=(), arrive=None):
    stages = [(*stage, groups)[:3] for stage in stages]
    marks = {0} | {lag for _, lag, _ in stages} | {lag + count for _, lag, count in stages} | {at for at, _ in events}
    marks = sorted(marks)
    for start, stop in zip(marks, marks[1:] + [marks[-1]]):
        for at, event in events:
            if at == start:
                event()
        active = [(n, stage, lag) for n, (stage, lag, count) in enumerate(stages) if lag <= start < lag + count]
        if stop == start or not active:
            continue

        def step(p, carry):
            if arrive is not None:
                for n, _, lag in active:
                    arrive(n, p - lag)
            stores = []
            for _, stage, lag in active:
                for i in range(size):
                    stores += stage((p - lag) * size + i)
            for ref, index, value in stores:
                if index is None:
                    ref[...] += value
                else:
                    ref[index] = value
            return carry

        lax.fori_loop(start, stop, step, 0)


def cost(tiles, products, transcendentals=0):
    return pl.CostEstimate(flops=tiles * products * 2 * 128 * 256 * 256, bytes_accessed=tiles * 2**16, transcendentals=transcendentals)


class Place:
    def __init__(self, block, en):
        self.block, self.en = block, en
        self.me = lax.axis_index("en")
        self.dirs = 1 if en == 2 else 2
        self.extra = REACH * self.dirs
        self.slots, self.bins = block + self.extra, block * en
        self.own = jnp.where(self.me == 0, 0, REACH) if en == 2 else REACH
        self.first_bin = self.me * block - self.own

    def above(self, d):
        return jnp.where(self.me == 0, 1, 0) if self.en == 2 else 1 - d

    def sent(self, d, width):
        return self.above(d) * (self.block - width)

    def border(self, d):
        up = self.above(d) if self.en == 2 else d
        return up, up * (self.block + self.own - REACH)

    def clamp(self, g):
        return jnp.clip(g, 0, self.bins - 1)


def lanes_of(shape=(128, 128)):
    return lax.broadcasted_iota(jnp.int32, shape, 1)


def is_odd():
    return lax.axis_index("sky") % 2 == 1


def pack_edges(tiles):
    lane = lanes_of()
    outer = (lane < RMAX) | (lane >= 128 - RMAX)
    early, late = [jnp.where(outer, tiles[n], pltpu.roll(tiles[n + 1], 64, 1)) for n in (0, 2)]
    late = pltpu.roll(late, RMAX, 1)
    mask = ((lane // RMAX) % 2 == 1) != is_odd()
    return jnp.where(mask, early, late), jnp.where(mask, late, early)


LEFT = (3, 1, 0, 2)
RIGHT = (0, 2, 1, 3)


def edge_tile(near, far, n):
    lane = lanes_of()
    from_left = lane < RMAX * RIGHT[n] if LEFT[n] < RIGHT[n] else lane >= RMAX * LEFT[n]
    return jnp.where(from_left != is_odd(), far, near)


def twice(x):
    return jnp.concatenate([x, x], axis=0)


def lon_product(tile, weights):
    out = jnp.dot(jnp.concatenate(split(tile), axis=1), twice(weights), preferred_element_type=F32)
    return out[:, :128] + out[:, 128:]


def lat_product(weights, tile):
    out = jnp.dot(weights, twice(jnp.concatenate(split(tile), axis=1)), preferred_element_type=F32)
    return out[:, :128] + out[:, 128:]


def profile(radius, column):
    wide = jnp.full((1, 128), radius, jnp.int32).astype(F32)
    reach = wide * wide
    factor = -2.0 / reach
    lane = lax.broadcasted_iota(jnp.int32, (1, 128), 1)
    square = (lane * lane).astype(F32)
    values = jnp.where(square <= reach, jnp.exp(square * factor), 0.0)
    norm = 2.0 * jnp.sum(values, axis=1, keepdims=True) - 1.0
    root = jnp.sqrt(jnp.full((1, 128), column, F32))[:, :1]
    return factor[:, :1], 1.0 / (norm * root), reach[:, :1]


def taper_values(diff, ok, factor, scale, reach):
    square = diff * diff
    return jnp.where((square <= reach) & ok, jnp.exp(square * factor) * scale, 0.0)


def pack_kernel(parts, en, flux, exposure, background, observed, weighted, near, far, *rest):
    place = Place(flux.shape[0], en)
    dirs, block = place.dirs, place.block
    sent, (v_flux, v_exposure, v_observed, sems, near_sems) = rest[:dirs], rest[dirs:]
    chunk = block // parts

    def arrivals(c):
        return [chunk_copy(a, b, sems.at[n, c], c, chunk) for n, (a, b) in enumerate(((flux, v_flux), (exposure, v_exposure)))]

    def near_arrivals(d):
        at = pl.ds(place.sent(d, REACH), REACH)
        return [
            pltpu.make_async_copy(background.at[at], sent[d].at[pl.ds(0, REACH)], near_sems.at[d, 0]),
            pltpu.make_async_copy(observed.at[at], v_observed.at[d], near_sems.at[d, 1]),
        ]

    for c in range(parts):
        for copy in arrivals(c):
            copy.start()
    for d in range(dirs):
        for copy in near_arrivals(d):
            copy.start()

    def some(g, carry):
        tiles = [v_flux[4 * g + i] * v_exposure[4 * g + i] for i in range(4)]
        packed = pack_edges(tiles)
        for i in range(4):
            weighted[4 * g + i] = tiles[i]
        near[g], far[g] = packed
        return carry

    for c in range(parts):
        for copy in arrivals(c):
            copy.wait()
        lax.fori_loop(c * chunk // 4, (c + 1) * chunk // 4, some, 0)
    for d in range(dirs):
        for copy in near_arrivals(d):
            copy.wait()
        for k in range(REACH):
            sent[d][REACH + k] = v_observed[d, k].astype(F32)


def weights_kernel(en, radius, low, high, disp, weighted, background, observed,
                   centre, band, edge, fold, near_background, near_observed, sems):
    fetches = [
        pltpu.make_async_copy(background, near_background, sems.at[0]),
        pltpu.make_async_copy(observed, near_observed, sems.at[1]),
    ]
    for fetch in fetches:
        fetch.start()
    block = weighted.shape[0]
    place = Place(block, en)
    row = lax.broadcasted_iota(jnp.int32, (128, 128), 0)
    col = lax.broadcasted_iota(jnp.int32, (128, 128), 1)
    near = (row - col).astype(F32)
    always = row >= 0
    beside = []
    for n in range(4):
        shift = jnp.where(row // RMAX == LEFT[n], -RMAX - RMAX * LEFT[n], 128 - RMAX * RIGHT[n])
        held = (row // RMAX == LEFT[n]) | (row // RMAX == RIGHT[n])
        beside.append(((row + shift - col).astype(F32), held))

    def weight(i, j):
        at, to = place.clamp(i), place.clamp(j)
        inside = (i == at) & (j == to) & (low[at] <= j - i) & (j - i <= high[at])
        return jnp.where(inside, disp[at, to], 0.0)

    def fold_row(g):
        for o in range(-REACH, REACH + 1):
            fold[5 * (g - place.first_bin + REACH) + o + REACH] = weight(g, g + o)

    def make(g, n):
        fold_row(g)
        column = weight(g, g)
        for o in (-2, -1, 1, 2):
            column = column + weight(g - o, g)
        numbers = profile(radius[place.clamp(g)], jnp.where(column > 0.0, column, 1.0))
        return tuple(
            jnp.concatenate(split(taper_values(diff, ok, *numbers)), axis=1) for diff, ok in ((near, always), beside[n])
        )

    for s in (0, 1, place.slots + 2, place.slots + 3):
        for o in range(5):
            fold[5 * s + o] = 0.0

    def some(g):
        made = [make(place.me * block + 4 * g + n, n) for n in range(4)]
        return [(band, 4 * g + n, made[n][0]) for n in range(4)] + [(edge, 4 * g + n, made[n][1]) for n in range(4)]

    def lon(g):
        return [(centre, 4 * g + n, lon_product(weighted[4 * g + n], band[4 * g + n])) for n in range(4)]

    run_stages(block // 4, 1, [(some, 0), (lon, 1)])
    for d in range(place.dirs):
        up, slot = place.border(d)
        for k in range(REACH):
            fold_row(place.first_bin + slot + up * REACH + k)
    for fetch in fetches:
        fetch.wait()


def lon_edges(centre, edge, far, near, g, at, n):
    return centre[at] + lon_product(edge_tile(near[g], far[g], n), edge[at])


def blur_kernel(en, centre, band, edge, far, near, *blurred):
    place = Place(centre.shape[0], en)
    for d in range(place.dirs):
        start = place.sent(d, 4)
        g = lax.div(start, 4) if en == 2 else start // 4
        sums = [lon_edges(centre, edge, far, near, g, start + n, n) for n in range(4)]
        sums = [lat_product(band[start + n], sums[n]) for n in range(4)]
        for n in range(4):
            blurred[d][n] = sums[n]


def inverse(x):
    first = pl.reciprocal(x, approx=True)
    return first * (2.0 - x * first)


def loss_terms(mu, counts):
    return (mu - counts * jnp.log(mu)).reshape(16, 8, 128).sum(0)


def fold_one(fold, row, resid, at):
    total = None
    for o in range(5):
        term = fold[5 * (row - o) + o] * resid[at - o]
        total = term if total is None else total + term
    return total


def middle_kernel(en, fold, centre, band, edge, far, near, background, observed, resid, loss, back, near_out, far_out, whole, blurred):
    block = centre.shape[0]
    place = Place(block, en)
    own = place.own
    zero = jnp.zeros((128, 128), F32)
    for s in (0, 1, block + 2, block + 3):
        blurred[s] = zero
        resid[s] = zero
    loss[...] = jnp.zeros((8, 128), F32)
    inside = (own, own + block - REACH) if en == 2 else (REACH, block - REACH)

    def lon(g):
        return [(whole, 4 * g + n, lon_edges(centre, edge, far, near, g, 4 * g + n, n)) for n in range(4)]

    def lat(g):
        return [(blurred, 4 * g + n + 2, lat_product(band[4 * g + n], whole[4 * g + n])) for n in range(4)]

    def residual(g):
        stores = []
        for b in [4 * g + n for n in range(4)]:
            mu = background[b]
            for o in range(5):
                mu = mu + fold[5 * (b + own + 2) + o] * blurred[b + o]
            counts = observed[b].astype(F32)
            inner = (b >= inside[0]) & (b < inside[1])
            stores += [(resid, b + 2, 1.0 - counts * inverse(mu)), (loss, None, jnp.where(inner, loss_terms(mu, counts), 0.0))]
        return stores

    def fold_back(g):
        tiles = [fold_one(fold, 4 * g + n + own + 4, resid, 4 * g + n + 4) for n in range(4)]
        packed = pack_edges(tiles)
        return [(back, 4 * g + n, tiles[n]) for n in range(4)] + [(near_out, g, packed[0]), (far_out, g, packed[1])]

    run_stages(block // 8, 2, [(lon, 0), (lat, 1), (residual, 3), (fold_back, 5)])


def border_kernel(en, fold, background, observed, resid, loss, near_in, far_in, *rest):
    del near_in, far_in
    block = background.shape[0]
    place = Place(block, en)
    dirs, own = place.dirs, place.own
    sent, received, counts = [rest[n * dirs:(n + 1) * dirs] for n in range(3)]
    near, far, total = rest[3 * dirs:3 * dirs + 3]
    back, (blurred, ground, seen, rows, v_near, v_far, sems) = rest[3 * dirs + 3:4 * dirs + 3], rest[4 * dirs + 3:]
    sums = loss[...]
    copies = []
    for d in range(dirs):
        up, slot = place.border(d)
        mine, theirs = 4 * (1 - up), 4 * up
        for k in range(4):
            blurred[mine + k] = sent[dirs - 1 - d][k]
            blurred[theirs + k] = received[d][k]
            rows[mine + k] = resid[up * (block - 8) + 4 + k]
        first = up * (block - REACH)
        for k in range(REACH):
            ground[mine // 2 + k] = background[first + k]
            seen[mine // 2 + k] = observed[first + k].astype(F32)
            ground[theirs // 2 + k] = counts[d][k]
            seen[theirs // 2 + k] = counts[d][REACH + k]
        for j in range(2 * REACH):
            mu = ground[j]
            for o in range(5):
                mu = mu + fold[5 * (slot + j + 2) + o] * blurred[j + o]
            rows[theirs + j] = 1.0 - seen[j] * inverse(mu)
            is_mine = (mine // 2 <= j) & (j < mine // 2 + REACH)
            sums = sums + jnp.where(is_mine, loss_terms(mu, seen[j]), 0.0)
        first = up * (block - 4)
        tiles = [fold_one(fold, first + n + own + 4, rows, n + 4) for n in range(4)]
        v_near[d], v_far[d] = pack_edges(tiles)
        at = pl.ds(up * (block // 4 - 1), 1)
        for n, (source, target) in enumerate(((v_far, far), (v_near, near))):
            copies.append(pltpu.make_async_copy(source.at[pl.ds(d, 1)], target.at[at], sems.at[d, n]))
            copies[-1].start()
        for n in range(4):
            back[d][n] = tiles[n]
    total[...] = jnp.full((1, 128), jnp.sum(sums), F32)
    for copy in copies:
        copy.wait()


def centre_kernel(en, back, band, total, *rest):
    border, (out, passed) = rest[:-2], rest[-2:]
    passed[...] = total[...]
    size = 8

    def some(g, carry):
        sums = [lon_product(back[size * g + i], band[size * g + i]) for i in range(size)]
        for i in range(size):
            out[size * g + i] = sums[i]
        return carry

    lax.fori_loop(0, back.shape[0] // size, some, 0)
    place = Place(back.shape[0], en)
    for d in range(place.dirs):
        first = place.border(d)[0] * (back.shape[0] - 4)
        for n in range(4):
            out[first + n] = lon_product(border[d][n], band[first + n])


def final_kernel(part, centre, band, edge, far, near, exposure, total, *rest):
    out, passed, whole, v_out, out_sems = rest[part:]
    groups = near.shape[0] // 2
    first = part * 4 * groups
    size = min(2, groups)
    steps = groups // size
    passed[...] = total[...]

    def copy_out(p):
        count = 4 * size
        return pltpu.make_async_copy(v_out.at[pl.ds(p * count, count)], out.at[pl.ds(first + p * count, count)], out_sems.at[p])

    def lon(g):
        return [(whole, 4 * g + n, lon_edges(centre, edge, far, near, part * groups + g, first + 4 * g + n, n)) for n in range(4)]

    def lat(g):
        bins = [4 * g + n for n in range(4)]
        return [(v_out, b, lat_product(band[first + b], whole[b]) * exposure[first + b]) for b in bins]

    run_stages(steps, size, [(lon, 0), (lat, 1)], events=[(p + 2, copy_out(p).start) for p in range(steps)])
    for p in range(steps):
        copy_out(p).wait()


def tree_sum(values):
    while len(values) > 1:
        values = [a + b for a, b in zip(values[::2], values[1::2])]
    return values[0]


def ring(size, shift):
    return [(i, (i + shift) % size) for i in range(size)]


def local(flux, exposure, background, observed, psf_radius, band_low, band_high, disp_raw):
    block, rows, width = flux.shape
    bins = disp_raw.shape[0]
    sky, en = lax.axis_size("sky"), lax.axis_size("en")
    shifts = [1] if en == 2 else [1, -1]
    dirs = len(shifts)
    slots = block + REACH * dirs
    parts = min(8, block // 4)

    def tiles(count, dtype=F32):
        return jax.ShapeDtypeStruct((count, rows, width), dtype)

    def edges(count):
        return jax.ShapeDtypeStruct((count // 4, 128, 128), F32)

    def weights(count):
        return jax.ShapeDtypeStruct((count, 128, 256), BF16)

    def scratch(shape):
        return pltpu.VMEM(shape.shape, shape.dtype)

    lanes = jax.ShapeDtypeStruct((1, 128), F32)

    flux, exposure_in, background, observed = [
        pltpu.with_memory_space_constraint(array, pltpu.HBM) for array in (flux, exposure, background, observed)
    ]
    half = block // 2

    def swap_far(edges):
        return lax.ppermute(edges, "sky", [(s, (s + 1 if s % 2 else s - 1) % sky) for s in range(sky)])

    def swap_near(edges):
        return lax.ppermute(edges, "sky", [(s, s ^ 1) for s in range(sky)])

    def neighbours(arrays):
        return [lax.ppermute(array, "en", ring(en, shift)) for array, shift in zip(arrays, shifts)]

    weighted, near, far, *sent = pl.pallas_call(
        functools.partial(pack_kernel, parts, en),
        in_specs=[ANY] * 4,
        out_specs=[VMEM] * (3 + dirs),
        out_shape=[tiles(block), edges(block), edges(block)] + [tiles(2 * REACH)] * dirs,
        scratch_shapes=[
            scratch(tiles(block)), scratch(tiles(block)), pltpu.VMEM((dirs, REACH, rows, width), jnp.int32),
            pltpu.SemaphoreType.DMA((2, parts)), pltpu.SemaphoreType.DMA((dirs, 2)),
        ],
        compiler_params=params(12),
        name="weight_and_pack",
    )(flux, exposure_in, background, observed)
    far, near = swap_far(far), swap_near(near)
    counts = neighbours(sent)

    centre, band, edge, fold, background, observed = pl.pallas_call(
        functools.partial(weights_kernel, en),
        in_specs=[SMEM] * 4 + [VMEM] + [ANY] * 2,
        out_specs=[VMEM] * 3 + [SMEM] + [VMEM] * 2,
        out_shape=[
            tiles(block), weights(block), weights(block), jax.ShapeDtypeStruct((5 * (slots + 4),), F32),
            tiles(block), tiles(block, jnp.int32),
        ],
        scratch_shapes=[pltpu.SemaphoreType.DMA((2,))],
        compiler_params=params(4),
        cost_estimate=cost(block, 1, block * 2**15),
        name="weights_and_centre",
    )(psf_radius, band_low, band_high, disp_raw, weighted, background, observed)
    sent = pl.pallas_call(
        functools.partial(blur_kernel, en),
        in_specs=[VMEM] * 5,
        out_specs=[VMEM] * dirs,
        out_shape=[tiles(4)] * dirs,
        compiler_params=params(4),
        cost_estimate=cost(4 * dirs, 2),
        name="blur_border",
    )(centre, band, edge, far, near)
    received = neighbours(sent)
    resid, loss, *folded = pl.pallas_call(
        functools.partial(middle_kernel, en),
        in_specs=[SMEM] + [VMEM] * 7,
        out_specs=[VMEM] * 5,
        out_shape=[tiles(block + 4), jax.ShapeDtypeStruct((8, 128), F32), tiles(block), edges(block), edges(block)],
        scratch_shapes=[scratch(tiles(block)), scratch(tiles(block + 4))],
        compiler_params=params(10),
        cost_estimate=cost(block, 2, block * 2**15),
        name="blur_residual_fold",
    )(fold, centre, band, edge, far, near, background, observed)
    back, near, far = folded
    near, far, total, *border = pl.pallas_call(
        functools.partial(border_kernel, en),
        in_specs=[SMEM] + [VMEM] * 4 + [ANY] * 2 + [VMEM] * (3 * dirs),
        out_specs=[ANY] * 2 + [VMEM] * (1 + dirs),
        out_shape=[edges(block), edges(block), lanes] + [tiles(4)] * dirs,
        input_output_aliases={5: 0, 6: 1},
        scratch_shapes=[
            scratch(tiles(8)), scratch(tiles(4)), scratch(tiles(4)), scratch(tiles(8)),
            scratch(tiles(dirs)), scratch(tiles(dirs)), pltpu.SemaphoreType.DMA((dirs, 2)),
        ],
        compiler_params=params(4),
        cost_estimate=cost(4 * dirs, 1),
        name="border_residual_fold_loss",
    )(fold, background, observed, resid, loss, near, far, *sent, *received, *counts)

    def partners(value, masks):
        return [lax.ppermute(value, ("sky", "en"), [(i, i ^ mask) for i in range(sky * en)]) for mask in masks]

    far, near = swap_far(far), swap_near(near)
    moved = partners(total, [4 * en * k for k in range(1, sky // 4)])
    centre, total = pl.pallas_call(
        functools.partial(centre_kernel, en),
        in_specs=[VMEM] * (3 + dirs),
        out_specs=[VMEM] * 2,
        out_shape=[tiles(block), lanes],
        compiler_params=params(4),
        cost_estimate=cost(block, 1),
        name="back_centre",
    )(back, band, total, *border)
    grad = []
    for part, masks in enumerate(([k % en ^ (k // en * 3 * en) for k in range(1, 2 * en)], [en])):
        total = tree_sum([total] + moved)
        moved = partners(total, masks)
        *grad, total = pl.pallas_call(
            functools.partial(final_kernel, part),
            in_specs=[VMEM] * 7 + [ANY] * part,
            out_specs=[ANY, VMEM],
            out_shape=[tiles(block), lanes],
            scratch_shapes=[scratch(tiles(block // 2)), scratch(tiles(block // 2)), pltpu.SemaphoreType.DMA((block // 8,))],
            input_output_aliases={7: 0} if part else {},
            compiler_params=params(8),
            cost_estimate=cost(block // 2, 2),
            name="back_edges_lat_exposure",
        )(centre, band, edge, far, near, exposure, total, *grad)
    return grad[0], tree_sum([total] + moved)[0, 0] / F32(rows * width * bins * sky)


def solution(mesh):
    placed = (P("en", None, "sky"),) * 4 + (P(),) * 4
    return jax.shard_map(local, mesh=mesh, in_specs=placed, out_specs=(P("en", None, "sky"), P()), check_vma=False)
```

```python
import functools

import jax
import jax.numpy as jnp
from jax import lax
from jax.experimental import pallas as pl
from jax.experimental.pallas import tpu as pltpu
from jax.sharding import PartitionSpec as P

RMAX = 32
REACH = 2
F32 = jnp.float32
BF16 = jnp.bfloat16
SMEM = pl.BlockSpec(memory_space=pltpu.SMEM)
ANY = pl.BlockSpec(memory_space=pl.ANY)
VMEM = pl.BlockSpec(memory_space=pltpu.VMEM)
HBM = pl.BlockSpec(memory_space=pltpu.HBM)


def split(x):
    hi = x.astype(BF16)
    return hi, (x - hi.astype(F32)).astype(BF16)


def params(mib=56):
    return pltpu.CompilerParams(vmem_limit_bytes=mib * 2**20)


def blocks(count, rows, cols):
    return pl.BlockSpec((count, rows, cols), lambda i: (i, 0, 0))


def chunk_copy(source, target, sem, c, size):
    at = pl.ds(c * size, size)
    return pltpu.make_async_copy(source.at[at], target.at[at], sem)


def run_stages(groups, size, stages, events=(), arrive=None):
    stages = [(*stage, groups)[:3] for stage in stages]
    marks = {0} | {lag for _, lag, _ in stages} | {lag + count for _, lag, count in stages} | {at for at, _ in events}
    marks = sorted(marks)
    for start, stop in zip(marks, marks[1:] + [marks[-1]]):
        for at, event in events:
            if at == start:
                event()
        active = [(n, stage, lag) for n, (stage, lag, count) in enumerate(stages) if lag <= start < lag + count]
        if stop == start or not active:
            continue

        def step(p, carry):
            if arrive is not None:
                for n, _, lag in active:
                    arrive(n, p - lag)
            stores = []
            for _, stage, lag in active:
                for i in range(size):
                    stores += stage((p - lag) * size + i)
            for ref, index, value in stores:
                if index is None:
                    ref[...] += value
                else:
                    ref[index] = value
            return carry

        lax.fori_loop(start, stop, step, 0)


def cost(tiles, products, transcendentals=0):
    return pl.CostEstimate(flops=tiles * products * 2 * 128 * 256 * 256, bytes_accessed=tiles * 2**16, transcendentals=transcendentals)


class Place:
    def __init__(self, block, en):
        self.block, self.en = block, en
        self.me = lax.axis_index("en")
        self.dirs = 1 if en == 2 else 2
        self.extra = REACH * self.dirs
        self.slots, self.bins = block + self.extra, block * en
        self.own = jnp.where(self.me == 0, 0, REACH) if en == 2 else REACH
        self.first_bin = self.me * block - self.own

    def above(self, d):
        return jnp.where(self.me == 0, 1, 0) if self.en == 2 else 1 - d

    def sent(self, d, width):
        return self.above(d) * (self.block - width)

    def border(self, d):
        up = self.above(d) if self.en == 2 else d
        return up, up * (self.block + self.own - REACH)

    def clamp(self, g):
        return jnp.clip(g, 0, self.bins - 1)


def lanes_of(shape=(128, 128)):
    return lax.broadcasted_iota(jnp.int32, shape, 1)


def is_odd():
    return lax.axis_index("sky") % 2 == 1


def pack_edges(tiles):
    lane = lanes_of()
    outer = (lane < RMAX) | (lane >= 128 - RMAX)
    early, late = [jnp.where(outer, tiles[n], pltpu.roll(tiles[n + 1], 64, 1)) for n in (0, 2)]
    late = pltpu.roll(late, RMAX, 1)
    mask = ((lane // RMAX) % 2 == 1) != is_odd()
    return jnp.where(mask, early, late), jnp.where(mask, late, early)


LEFT = (3, 1, 0, 2)
RIGHT = (0, 2, 1, 3)


def edge_tile(near, far, n):
    lane = lanes_of()
    from_left = lane < RMAX * RIGHT[n] if LEFT[n] < RIGHT[n] else lane >= RMAX * LEFT[n]
    return jnp.where(from_left != is_odd(), far, near)


def twice(x):
    return jnp.concatenate([x, x], axis=0)


def lon_product(tile, weights):
    out = jnp.dot(jnp.concatenate(split(tile), axis=1), twice(weights), preferred_element_type=F32)
    return out[:, :128] + out[:, 128:]


def lat_product(weights, tile):
    out = jnp.dot(weights, twice(jnp.concatenate(split(tile), axis=1)), preferred_element_type=F32)
    return out[:, :128] + out[:, 128:]


def profile(radius, column):
    wide = jnp.full((1, 128), radius, jnp.int32).astype(F32)
    reach = wide * wide
    factor = -2.0 / reach
    lane = lax.broadcasted_iota(jnp.int32, (1, 128), 1)
    square = (lane * lane).astype(F32)
    values = jnp.where(square <= reach, jnp.exp(square * factor), 0.0)
    norm = 2.0 * jnp.sum(values, axis=1, keepdims=True) - 1.0
    root = jnp.sqrt(jnp.full((1, 128), column, F32))[:, :1]
    return factor[:, :1], 1.0 / (norm * root), reach[:, :1]


def taper_values(diff, ok, factor, scale, reach):
    square = diff * diff
    return jnp.where((square <= reach) & ok, jnp.exp(square * factor) * scale, 0.0)


def pack_kernel(parts, en, flux, exposure, background, observed, weighted, near, far, *rest):
    place = Place(flux.shape[0], en)
    dirs, block = place.dirs, place.block
    sent, (v_flux, v_exposure, v_observed, sems, near_sems) = rest[:dirs], rest[dirs:]
    chunk = block // parts

    def arrivals(c):
        return [chunk_copy(a, b, sems.at[n, c], c, chunk) for n, (a, b) in enumerate(((flux, v_flux), (exposure, v_exposure)))]

    def near_arrivals(d):
        at = pl.ds(place.sent(d, REACH), REACH)
        return [
            pltpu.make_async_copy(background.at[at], sent[d].at[pl.ds(0, REACH)], near_sems.at[d, 0]),
            pltpu.make_async_copy(observed.at[at], v_observed.at[d], near_sems.at[d, 1]),
        ]

    for c in range(parts):
        for copy in arrivals(c):
            copy.start()
    for d in range(dirs):
        for copy in near_arrivals(d):
            copy.start()

    def some(g, carry):
        tiles = [v_flux[4 * g + i] * v_exposure[4 * g + i] for i in range(4)]
        packed = pack_edges(tiles)
        for i in range(4):
            weighted[4 * g + i] = tiles[i]
        near[g], far[g] = packed
        return carry

    for c in range(parts):
        for copy in arrivals(c):
            copy.wait()
        lax.fori_loop(c * chunk // 4, (c + 1) * chunk // 4, some, 0)
    for d in range(dirs):
        for copy in near_arrivals(d):
            copy.wait()
        for k in range(REACH):
            sent[d][REACH + k] = v_observed[d, k].astype(F32)


def weights_kernel(en, radius, low, high, disp, weighted, background, observed,
                   centre, band, edge, fold, near_background, near_observed, sems):
    fetches = [
        pltpu.make_async_copy(background, near_background, sems.at[0]),
        pltpu.make_async_copy(observed, near_observed, sems.at[1]),
    ]
    for fetch in fetches:
        fetch.start()
    block = weighted.shape[0]
    place = Place(block, en)
    row = lax.broadcasted_iota(jnp.int32, (128, 128), 0)
    col = lax.broadcasted_iota(jnp.int32, (128, 128), 1)
    near = (row - col).astype(F32)
    always = row >= 0
    beside = []
    for n in range(4):
        shift = jnp.where(row // RMAX == LEFT[n], -RMAX - RMAX * LEFT[n], 128 - RMAX * RIGHT[n])
        held = (row // RMAX == LEFT[n]) | (row // RMAX == RIGHT[n])
        beside.append(((row + shift - col).astype(F32), held))

    def weight(i, j):
        at, to = place.clamp(i), place.clamp(j)
        inside = (i == at) & (j == to) & (low[at] <= j - i) & (j - i <= high[at])
        return jnp.where(inside, disp[at, to], 0.0)

    def fold_row(g):
        for o in range(-REACH, REACH + 1):
            fold[5 * (g - place.first_bin + REACH) + o + REACH] = weight(g, g + o)

    def make(g, n):
        fold_row(g)
        column = weight(g, g)
        for o in (-2, -1, 1, 2):
            column = column + weight(g - o, g)
        numbers = profile(radius[place.clamp(g)], jnp.where(column > 0.0, column, 1.0))
        return tuple(
            jnp.concatenate(split(taper_values(diff, ok, *numbers)), axis=1) for diff, ok in ((near, always), beside[n])
        )

    for s in (0, 1, place.slots + 2, place.slots + 3):
        for o in range(5):
            fold[5 * s + o] = 0.0

    def some(g):
        made = [make(place.me * block + 4 * g + n, n) for n in range(4)]
        return [(band, 4 * g + n, made[n][0]) for n in range(4)] + [(edge, 4 * g + n, made[n][1]) for n in range(4)]

    def lon(g):
        return [(centre, 4 * g + n, lon_product(weighted[4 * g + n], band[4 * g + n])) for n in range(4)]

    run_stages(block // 4, 1, [(some, 0), (lon, 1)])
    for d in range(place.dirs):
        up, slot = place.border(d)
        for k in range(REACH):
            fold_row(place.first_bin + slot + up * REACH + k)
    for fetch in fetches:
        fetch.wait()


def lon_edges(centre, edge, far, near, g, at, n):
    return centre[at] + lon_product(edge_tile(near[g], far[g], n), edge[at])


def blur_kernel(en, centre, band, edge, far, near, *blurred):
    place = Place(centre.shape[0], en)
    for d in range(place.dirs):
        start = place.sent(d, 4)
        g = lax.div(start, 4) if en == 2 else start // 4
        sums = [lon_edges(centre, edge, far, near, g, start + n, n) for n in range(4)]
        sums = [lat_product(band[start + n], sums[n]) for n in range(4)]
        for n in range(4):
            blurred[d][n] = sums[n]


def inverse(x):
    first = pl.reciprocal(x, approx=True)
    return first * (2.0 - x * first)


ROWS = [pl.ds(32 * r, 32) for r in range(4)]


def loss_terms(mu, counts):
    return (mu - counts * jnp.log(mu)).reshape(-1, 8, 128).sum(0)


def fold_one(fold, row, resid, at):
    total = None
    for o in range(5):
        term = fold[5 * (row - o) + o] * resid[at - o]
        total = term if total is None else total + term
    return total


def middle_kernel(en, fold, centre, band, edge, far, near, background, observed, resid, loss, back, near_out, far_out, whole, blurred):
    block = centre.shape[0]
    place = Place(block, en)
    own = place.own
    zero = jnp.zeros((128, 128), F32)
    for s in (0, 1, block + 2, block + 3):
        blurred[s] = zero
        resid[s] = zero
    loss[...] = jnp.zeros((8, 128), F32)
    inside = (own, own + block - REACH) if en == 2 else (REACH, block - REACH)

    def lon(g):
        return [(whole, 4 * g + n, lon_edges(centre, edge, far, near, g, 4 * g + n, n)) for n in range(4)]

    def lat(g):
        return [(blurred, 4 * g + n + 2, lat_product(band[4 * g + n], whole[4 * g + n])) for n in range(4)]

    def residual(g):
        sums = None
        for rows in ROWS:
            window = [blurred[4 * g + k, rows] for k in range(8)]
            for n in range(4):
                b = 4 * g + n
                mu = background[b, rows]
                for o in range(5):
                    mu = mu + fold[5 * (b + own + 2) + o] * window[n + o]
                counts = observed[b, rows].astype(F32)
                resid[b + 2, rows] = 1.0 - counts * inverse(mu)
                inner = (b >= inside[0]) & (b < inside[1])
                terms = jnp.where(inner, loss_terms(mu, counts), 0.0)
                sums = terms if sums is None else sums + terms
        return [(loss, None, sums)]

    def fold_back(g):
        tiles = [[] for _ in range(4)]
        for rows in ROWS:
            window = [resid[4 * g + k, rows] for k in range(8)]
            for n in range(4):
                total = None
                for o in range(5):
                    term = fold[5 * (4 * g + n + own + 4 - o) + o] * window[n + 4 - o]
                    total = term if total is None else total + term
                back[4 * g + n, rows] = total
                tiles[n].append(total)
        near_out[g], far_out[g] = pack_edges([jnp.concatenate(parts, axis=0) for parts in tiles])
        return []

    run_stages(block // 8, 2, [(fold_back, 5), (residual, 3), (lon, 0), (lat, 1)])


def border_kernel(en, fold, background, observed, resid, loss, near_in, far_in, *rest):
    block = background.shape[0]
    place = Place(block, en)
    dirs, own = place.dirs, place.own
    sent, received, counts = [rest[n * dirs:(n + 1) * dirs] for n in range(3)]
    near, far, total = rest[3 * dirs:3 * dirs + 3]
    back, (blurred, ground, seen, rows) = rest[3 * dirs + 3:4 * dirs + 3], rest[4 * dirs + 3:]
    sums = loss[...]
    near[...], far[...] = near_in[...], far_in[...]
    for d in range(dirs):
        up, slot = place.border(d)
        mine, theirs = 4 * (1 - up), 4 * up
        for k in range(4):
            blurred[mine + k] = sent[dirs - 1 - d][k]
            blurred[theirs + k] = received[d][k]
            rows[mine + k] = resid[up * (block - 8) + 4 + k]
        first = up * (block - REACH)
        for k in range(REACH):
            ground[mine // 2 + k] = background[first + k]
            seen[mine // 2 + k] = observed[first + k].astype(F32)
            ground[theirs // 2 + k] = counts[d][k]
            seen[theirs // 2 + k] = counts[d][REACH + k]
        for j in range(2 * REACH):
            mu = ground[j]
            for o in range(5):
                mu = mu + fold[5 * (slot + j + 2) + o] * blurred[j + o]
            rows[theirs + j] = 1.0 - seen[j] * inverse(mu)
            is_mine = (mine // 2 <= j) & (j < mine // 2 + REACH)
            sums = sums + jnp.where(is_mine, loss_terms(mu, seen[j]), 0.0)
        first = up * (block - 4)
        tiles = [fold_one(fold, first + n + own + 4, rows, n + 4) for n in range(4)]
        g = up * (block // 4 - 1)
        near[g], far[g] = pack_edges(tiles)
        for n in range(4):
            back[d][n] = tiles[n]
    total[...] = jnp.full((1, 128), jnp.sum(sums), F32)


def centre_kernel(en, back, band, total, *rest):
    border, (out, passed) = rest[:-2], rest[-2:]
    passed[...] = total[...]
    size = 8

    def some(g, carry):
        sums = [lon_product(back[size * g + i], band[size * g + i]) for i in range(size)]
        for i in range(size):
            out[size * g + i] = sums[i]
        return carry

    lax.fori_loop(0, back.shape[0] // size, some, 0)
    place = Place(back.shape[0], en)
    for d in range(place.dirs):
        first = place.border(d)[0] * (back.shape[0] - 4)
        for n in range(4):
            out[first + n] = lon_product(border[d][n], band[first + n])


def final_kernel(part, centre, band, edge, far, near, exposure, total, *rest):
    out, passed, whole, v_out, out_sems = rest[part:]
    groups = near.shape[0] // 2
    first = part * 4 * groups
    size = min(2, groups)
    steps = groups // size
    passed[...] = total[...]

    def copy_out(p):
        count = 4 * size
        return pltpu.make_async_copy(v_out.at[pl.ds(p * count, count)], out.at[pl.ds(first + p * count, count)], out_sems.at[p])

    def lon(g):
        return [(whole, 4 * g + n, lon_edges(centre, edge, far, near, part * groups + g, first + 4 * g + n, n)) for n in range(4)]

    def lat(g):
        bins = [4 * g + n for n in range(4)]
        return [(v_out, b, lat_product(band[first + b], whole[b]) * exposure[first + b]) for b in bins]

    run_stages(steps, size, [(lon, 0), (lat, 1)], events=[(p + 2, copy_out(p).start) for p in range(steps)])
    for p in range(steps):
        copy_out(p).wait()


def tree_sum(values):
    while len(values) > 1:
        values = [a + b for a, b in zip(values[::2], values[1::2])]
    return values[0]


def ring(size, shift):
    return [(i, (i + shift) % size) for i in range(size)]


def local(flux, exposure, background, observed, psf_radius, band_low, band_high, disp_raw):
    block, rows, width = flux.shape
    bins = disp_raw.shape[0]
    sky, en = lax.axis_size("sky"), lax.axis_size("en")
    shifts = [1] if en == 2 else [1, -1]
    dirs = len(shifts)
    slots = block + REACH * dirs
    parts = min(8, block // 4)

    def tiles(count, dtype=F32):
        return jax.ShapeDtypeStruct((count, rows, width), dtype)

    def edges(count):
        return jax.ShapeDtypeStruct((count // 4, 128, 128), F32)

    def weights(count):
        return jax.ShapeDtypeStruct((count, 128, 256), BF16)

    def scratch(shape):
        return pltpu.VMEM(shape.shape, shape.dtype)

    lanes = jax.ShapeDtypeStruct((1, 128), F32)

    flux, exposure_in, background, observed = [
        pltpu.with_memory_space_constraint(array, pltpu.HBM) for array in (flux, exposure, background, observed)
    ]
    half = block // 2

    def swap_far(edges):
        return lax.ppermute(edges, "sky", [(s, (s + 1 if s % 2 else s - 1) % sky) for s in range(sky)])

    def swap_near(edges):
        return lax.ppermute(edges, "sky", [(s, s ^ 1) for s in range(sky)])

    def neighbours(arrays):
        return [lax.ppermute(array, "en", ring(en, shift)) for array, shift in zip(arrays, shifts)]

    weighted, near, far, *sent = pl.pallas_call(
        functools.partial(pack_kernel, parts, en),
        in_specs=[ANY] * 4,
        out_specs=[VMEM] * (3 + dirs),
        out_shape=[tiles(block), edges(block), edges(block)] + [tiles(2 * REACH)] * dirs,
        scratch_shapes=[
            scratch(tiles(block)), scratch(tiles(block)), pltpu.VMEM((dirs, REACH, rows, width), jnp.int32),
            pltpu.SemaphoreType.DMA((2, parts)), pltpu.SemaphoreType.DMA((dirs, 2)),
        ],
        compiler_params=params(12),
        name="weight_and_pack",
    )(flux, exposure_in, background, observed)
    far, near = swap_far(far), swap_near(near)
    counts = neighbours(sent)

    centre, band, edge, fold, background, observed = pl.pallas_call(
        functools.partial(weights_kernel, en),
        in_specs=[SMEM] * 4 + [VMEM] + [ANY] * 2,
        out_specs=[VMEM] * 3 + [SMEM] + [VMEM] * 2,
        out_shape=[
            tiles(block), weights(block), weights(block), jax.ShapeDtypeStruct((5 * (slots + 4),), F32),
            tiles(block), tiles(block, jnp.int32),
        ],
        scratch_shapes=[pltpu.SemaphoreType.DMA((2,))],
        compiler_params=params(4),
        cost_estimate=cost(block, 1, block * 2**15),
        name="weights_and_centre",
    )(psf_radius, band_low, band_high, disp_raw, weighted, background, observed)
    sent = pl.pallas_call(
        functools.partial(blur_kernel, en),
        in_specs=[VMEM] * 5,
        out_specs=[VMEM] * dirs,
        out_shape=[tiles(4)] * dirs,
        compiler_params=params(4),
        cost_estimate=cost(4 * dirs, 2),
        name="blur_border",
    )(centre, band, edge, far, near)
    received = neighbours(sent)
    resid, loss, *folded = pl.pallas_call(
        functools.partial(middle_kernel, en),
        in_specs=[SMEM] + [VMEM] * 7,
        out_specs=[VMEM] * 5,
        out_shape=[tiles(block + 4), jax.ShapeDtypeStruct((8, 128), F32), tiles(block), edges(block), edges(block)],
        scratch_shapes=[scratch(tiles(block)), scratch(tiles(block + 4))],
        compiler_params=params(10),
        cost_estimate=cost(block, 2, block * 2**15),
        name="blur_residual_fold",
    )(fold, centre, band, edge, far, near, background, observed)
    back, near, far = folded
    near, far, total, *border = pl.pallas_call(
        functools.partial(border_kernel, en),
        in_specs=[SMEM] + [VMEM] * (6 + 3 * dirs),
        out_specs=[VMEM] * (3 + dirs),
        out_shape=[edges(block), edges(block), lanes] + [tiles(4)] * dirs,
        scratch_shapes=[scratch(tiles(8)), scratch(tiles(4)), scratch(tiles(4)), scratch(tiles(8))],
        compiler_params=params(4),
        cost_estimate=cost(4 * dirs, 1),
        name="border_residual_fold_loss",
    )(fold, background, observed, resid, loss, near, far, *sent, *received, *counts)

    def partners(value, masks):
        return [lax.ppermute(value, ("sky", "en"), [(i, i ^ mask) for i in range(sky * en)]) for mask in masks]

    far, near = swap_far(far), swap_near(near)
    moved = partners(total, [4 * en * k for k in range(1, sky // 4)])
    centre, total = pl.pallas_call(
        functools.partial(centre_kernel, en),
        in_specs=[VMEM] * (3 + dirs),
        out_specs=[VMEM] * 2,
        out_shape=[tiles(block), lanes],
        compiler_params=params(4),
        cost_estimate=cost(block, 1),
        name="back_centre",
    )(back, band, total, *border)
    grad = []
    for part, masks in enumerate(([k % en ^ (k // en * 3 * en) for k in range(1, 2 * en)], [en])):
        total = tree_sum([total] + moved)
        moved = partners(total, masks)
        *grad, total = pl.pallas_call(
            functools.partial(final_kernel, part),
            in_specs=[VMEM] * 7 + [ANY] * part,
            out_specs=[ANY, VMEM],
            out_shape=[tiles(block), lanes],
            scratch_shapes=[scratch(tiles(block // 2)), scratch(tiles(block // 2)), pltpu.SemaphoreType.DMA((block // 8,))],
            input_output_aliases={7: 0} if part else {},
            compiler_params=params(8),
            cost_estimate=cost(block // 2, 2),
            name="back_edges_lat_exposure",
        )(centre, band, edge, far, near, exposure, total, *grad)
    return grad[0], tree_sum([total] + moved)[0, 0] / F32(rows * width * bins * sky)


def solution(mesh):
    placed = (P("en", None, "sky"),) * 4 + (P(),) * 4
    return jax.shard_map(local, mesh=mesh, in_specs=placed, out_specs=(P("en", None, "sky"), P()), check_vma=False)
```

```python
import functools

import jax
import jax.numpy as jnp
from jax import lax
from jax.experimental import pallas as pl
from jax.experimental.pallas import tpu as pltpu
from jax.sharding import PartitionSpec as P

RMAX = 32
REACH = 2
F32 = jnp.float32
BF16 = jnp.bfloat16
SMEM = pl.BlockSpec(memory_space=pltpu.SMEM)
ANY = pl.BlockSpec(memory_space=pl.ANY)
VMEM = pl.BlockSpec(memory_space=pltpu.VMEM)
HBM = pl.BlockSpec(memory_space=pltpu.HBM)


def split(x):
    hi = x.astype(BF16)
    return hi, (x - hi.astype(F32)).astype(BF16)


def params(mib=56):
    return pltpu.CompilerParams(vmem_limit_bytes=mib * 2**20)


def blocks(count, rows, cols):
    return pl.BlockSpec((count, rows, cols), lambda i: (i, 0, 0))


def chunk_copy(source, target, sem, c, size):
    at = pl.ds(c * size, size)
    return pltpu.make_async_copy(source.at[at], target.at[at], sem)


def run_stages(groups, size, stages, events=(), arrive=None):
    stages = [(*stage, groups)[:3] for stage in stages]
    marks = {0} | {lag for _, lag, _ in stages} | {lag + count for _, lag, count in stages} | {at for at, _ in events}
    marks = sorted(marks)
    for start, stop in zip(marks, marks[1:] + [marks[-1]]):
        for at, event in events:
            if at == start:
                event()
        active = [(n, stage, lag) for n, (stage, lag, count) in enumerate(stages) if lag <= start < lag + count]
        if stop == start or not active:
            continue

        def step(p, carry):
            if arrive is not None:
                for n, _, lag in active:
                    arrive(n, p - lag)
            stores = []
            for _, stage, lag in active:
                for i in range(size):
                    stores += stage((p - lag) * size + i)
            for ref, index, value in stores:
                if index is None:
                    ref[...] += value
                else:
                    ref[index] = value
            return carry

        lax.fori_loop(start, stop, step, 0)


def cost(tiles, products, transcendentals=0):
    return pl.CostEstimate(flops=tiles * products * 2 * 128 * 256 * 256, bytes_accessed=tiles * 2**16, transcendentals=transcendentals)


class Place:
    def __init__(self, block, en):
        self.block, self.en = block, en
        self.me = lax.axis_index("en")
        self.dirs = 1 if en == 2 else 2
        self.extra = REACH * self.dirs
        self.slots, self.bins = block + self.extra, block * en
        self.own = jnp.where(self.me == 0, 0, REACH) if en == 2 else REACH
        self.first_bin = self.me * block - self.own

    def above(self, d):
        return jnp.where(self.me == 0, 1, 0) if self.en == 2 else 1 - d

    def sent(self, d, width):
        return self.above(d) * (self.block - width)

    def border(self, d):
        up = self.above(d) if self.en == 2 else d
        return up, up * (self.block + self.own - REACH)

    def clamp(self, g):
        return jnp.clip(g, 0, self.bins - 1)


def lanes_of(shape=(128, 128)):
    return lax.broadcasted_iota(jnp.int32, shape, 1)


def is_odd():
    return lax.axis_index("sky") % 2 == 1


def pack_edges(tiles):
    lane = lanes_of()
    outer = (lane < RMAX) | (lane >= 128 - RMAX)
    early, late = [jnp.where(outer, tiles[n], pltpu.roll(tiles[n + 1], 64, 1)) for n in (0, 2)]
    late = pltpu.roll(late, RMAX, 1)
    mask = ((lane // RMAX) % 2 == 1) != is_odd()
    return jnp.where(mask, early, late), jnp.where(mask, late, early)


LEFT = (3, 1, 0, 2)
RIGHT = (0, 2, 1, 3)


def edge_tile(near, far, n):
    lane = lanes_of()
    from_left = lane < RMAX * RIGHT[n] if LEFT[n] < RIGHT[n] else lane >= RMAX * LEFT[n]
    return jnp.where(from_left != is_odd(), far, near)


def twice(x):
    return jnp.concatenate([x, x], axis=0)


def lon_product(tile, weights):
    out = jnp.dot(jnp.concatenate(split(tile), axis=1), twice(weights), preferred_element_type=F32)
    return out[:, :128] + out[:, 128:]


def lat_product(weights, tile):
    out = jnp.dot(weights, twice(jnp.concatenate(split(tile), axis=1)), preferred_element_type=F32)
    return out[:, :128] + out[:, 128:]


def profile(radius, column):
    wide = jnp.full((1, 128), radius, jnp.int32).astype(F32)
    reach = wide * wide
    factor = -2.0 / reach
    lane = lax.broadcasted_iota(jnp.int32, (1, 128), 1)
    square = (lane * lane).astype(F32)
    values = jnp.where(square <= reach, jnp.exp(square * factor), 0.0)
    norm = 2.0 * jnp.sum(values, axis=1, keepdims=True) - 1.0
    root = jnp.sqrt(jnp.full((1, 128), column, F32))[:, :1]
    return factor[:, :1], 1.0 / (norm * root), reach[:, :1]


def taper_values(diff, ok, factor, scale, reach):
    square = diff * diff
    return jnp.where((square <= reach) & ok, jnp.exp(square * factor) * scale, 0.0)


def pack_kernel(parts, en, flux, exposure, background, observed, weighted, near, far, *rest):
    place = Place(flux.shape[0], en)
    dirs, block = place.dirs, place.block
    sent, (v_flux, v_exposure, v_observed, sems, near_sems) = rest[:dirs], rest[dirs:]
    chunk = block // parts

    def arrivals(c):
        return [chunk_copy(a, b, sems.at[n, c], c, chunk) for n, (a, b) in enumerate(((flux, v_flux), (exposure, v_exposure)))]

    def near_arrivals(d):
        at = pl.ds(place.sent(d, REACH), REACH)
        return [
            pltpu.make_async_copy(background.at[at], sent[d].at[pl.ds(0, REACH)], near_sems.at[d, 0]),
            pltpu.make_async_copy(observed.at[at], v_observed.at[d], near_sems.at[d, 1]),
        ]

    for c in range(parts):
        for copy in arrivals(c):
            copy.start()
    for d in range(dirs):
        for copy in near_arrivals(d):
            copy.start()

    def some(g, carry):
        tiles = [v_flux[4 * g + i] * v_exposure[4 * g + i] for i in range(4)]
        packed = pack_edges(tiles)
        for i in range(4):
            weighted[4 * g + i] = tiles[i]
        near[g], far[g] = packed
        return carry

    for c in range(parts):
        for copy in arrivals(c):
            copy.wait()
        lax.fori_loop(c * chunk // 4, (c + 1) * chunk // 4, some, 0)
    for d in range(dirs):
        for copy in near_arrivals(d):
            copy.wait()
        for k in range(REACH):
            sent[d][REACH + k] = v_observed[d, k].astype(F32)


def weights_kernel(en, radius, low, high, disp, weighted, background, observed,
                   centre, band, edge, fold, near_background, near_observed, sems):
    fetches = [
        pltpu.make_async_copy(background, near_background, sems.at[0]),
        pltpu.make_async_copy(observed, near_observed, sems.at[1]),
    ]
    for fetch in fetches:
        fetch.start()
    block = weighted.shape[0]
    place = Place(block, en)
    row = lax.broadcasted_iota(jnp.int32, (128, 128), 0)
    col = lax.broadcasted_iota(jnp.int32, (128, 128), 1)
    near = (row - col).astype(F32)
    always = row >= 0
    beside = []
    for n in range(4):
        shift = jnp.where(row // RMAX == LEFT[n], -RMAX - RMAX * LEFT[n], 128 - RMAX * RIGHT[n])
        held = (row // RMAX == LEFT[n]) | (row // RMAX == RIGHT[n])
        beside.append(((row + shift - col).astype(F32), held))

    def weight(i, j):
        at, to = place.clamp(i), place.clamp(j)
        inside = (i == at) & (j == to) & (low[at] <= j - i) & (j - i <= high[at])
        return jnp.where(inside, disp[at, to], 0.0)

    def fold_row(g):
        for o in range(-REACH, REACH + 1):
            fold[5 * (g - place.first_bin + REACH) + o + REACH] = weight(g, g + o)

    def make(g, n):
        fold_row(g)
        column = weight(g, g)
        for o in (-2, -1, 1, 2):
            column = column + weight(g - o, g)
        numbers = profile(radius[place.clamp(g)], jnp.where(column > 0.0, column, 1.0))
        return tuple(
            jnp.concatenate(split(taper_values(diff, ok, *numbers)), axis=1) for diff, ok in ((near, always), beside[n])
        )

    for s in (0, 1, place.slots + 2, place.slots + 3):
        for o in range(5):
            fold[5 * s + o] = 0.0

    def some(g):
        made = [make(place.me * block + 4 * g + n, n) for n in range(4)]
        return [(band, 4 * g + n, made[n][0]) for n in range(4)] + [(edge, 4 * g + n, made[n][1]) for n in range(4)]

    def lon(g):
        return [(centre, 4 * g + n, lon_product(weighted[4 * g + n], band[4 * g + n])) for n in range(4)]

    run_stages(block // 4, 1, [(some, 0), (lon, 1)])
    for d in range(place.dirs):
        up, slot = place.border(d)
        for k in range(REACH):
            fold_row(place.first_bin + slot + up * REACH + k)
    for fetch in fetches:
        fetch.wait()


def lon_edges(centre, edge, far, near, g, at, n):
    return centre[at] + lon_product(edge_tile(near[g], far[g], n), edge[at])


def blur_kernel(en, centre, band, edge, far, near, *blurred):
    place = Place(centre.shape[0], en)
    for d in range(place.dirs):
        start = place.sent(d, 4)
        g = lax.div(start, 4) if en == 2 else start // 4
        sums = [lon_edges(centre, edge, far, near, g, start + n, n) for n in range(4)]
        sums = [lat_product(band[start + n], sums[n]) for n in range(4)]
        for n in range(4):
            blurred[d][n] = sums[n]


def inverse(x):
    first = pl.reciprocal(x, approx=True)
    return first * (2.0 - x * first)


ROWS = [pl.ds(32 * r, 32) for r in range(4)]


def loss_terms(mu, counts):
    return (mu - counts * jnp.log(mu)).reshape(-1, 8, 128).sum(0)


def fold_one(fold, row, resid, at):
    total = None
    for o in range(5):
        term = fold[5 * (row - o) + o] * resid[at - o]
        total = term if total is None else total + term
    return total


def middle_kernel(en, fold, centre, band, edge, far, near, background, observed, resid, loss, back, near_out, far_out, whole, blurred):
    block = centre.shape[0]
    place = Place(block, en)
    own = place.own
    zero = jnp.zeros((128, 128), F32)
    for s in (0, 1, block + 2, block + 3):
        blurred[s] = zero
        resid[s] = zero
    loss[...] = jnp.zeros((8, 128), F32)
    inside = (own, own + block - REACH) if en == 2 else (REACH, block - REACH)

    def lon(g):
        return [(whole, 4 * g + n, lon_edges(centre, edge, far, near, g, 4 * g + n, n)) for n in range(4)]

    def lat(g):
        return [(blurred, 4 * g + n + 2, lat_product(band[4 * g + n], whole[4 * g + n])) for n in range(4)]

    def residual(g):
        sums = None
        for rows in ROWS:
            window = [blurred[4 * g + k, rows] for k in range(8)]
            for n in range(4):
                b = 4 * g + n
                mu = background[b, rows]
                for o in range(5):
                    mu = mu + fold[5 * (b + own + 2) + o] * window[n + o]
                counts = observed[b, rows].astype(F32)
                resid[b + 2, rows] = 1.0 - counts * inverse(mu)
                inner = (b >= inside[0]) & (b < inside[1])
                terms = jnp.where(inner, loss_terms(mu, counts), 0.0)
                sums = terms if sums is None else sums + terms
        return [(loss, None, sums)]

    def fold_back(g):
        tiles = [[] for _ in range(4)]
        for rows in ROWS:
            window = [resid[4 * g + k, rows] for k in range(8)]
            for n in range(4):
                total = None
                for o in range(5):
                    term = fold[5 * (4 * g + n + own + 4 - o) + o] * window[n + 4 - o]
                    total = term if total is None else total + term
                back[4 * g + n, rows] = total
                tiles[n].append(total)
        near_out[g], far_out[g] = pack_edges([jnp.concatenate(parts, axis=0) for parts in tiles])
        return []

    run_stages(block // 8, 2, [(fold_back, 5), (residual, 3), (lon, 0), (lat, 1)])


def border_kernel(en, fold, background, observed, resid, loss, near_in, far_in, *rest):
    block = background.shape[0]
    place = Place(block, en)
    dirs, own = place.dirs, place.own
    sent, received, counts = [rest[n * dirs:(n + 1) * dirs] for n in range(3)]
    near, far, total = rest[3 * dirs:3 * dirs + 3]
    back, (blurred, ground, seen, rows) = rest[3 * dirs + 3:4 * dirs + 3], rest[4 * dirs + 3:]
    sums = loss[...]
    near[...], far[...] = near_in[...], far_in[...]
    for d in range(dirs):
        up, slot = place.border(d)
        mine, theirs = 4 * (1 - up), 4 * up
        for k in range(4):
            blurred[mine + k] = sent[dirs - 1 - d][k]
            blurred[theirs + k] = received[d][k]
            rows[mine + k] = resid[up * (block - 8) + 4 + k]
        first = up * (block - REACH)
        for k in range(REACH):
            ground[mine // 2 + k] = background[first + k]
            seen[mine // 2 + k] = observed[first + k].astype(F32)
            ground[theirs // 2 + k] = counts[d][k]
            seen[theirs // 2 + k] = counts[d][REACH + k]
        for j in range(2 * REACH):
            mu = ground[j]
            for o in range(5):
                mu = mu + fold[5 * (slot + j + 2) + o] * blurred[j + o]
            rows[theirs + j] = 1.0 - seen[j] * inverse(mu)
            is_mine = (mine // 2 <= j) & (j < mine // 2 + REACH)
            sums = sums + jnp.where(is_mine, loss_terms(mu, seen[j]), 0.0)
        first = up * (block - 4)
        tiles = [fold_one(fold, first + n + own + 4, rows, n + 4) for n in range(4)]
        g = up * (block // 4 - 1)
        near[g], far[g] = pack_edges(tiles)
        for n in range(4):
            back[d][n] = tiles[n]
    total[...] = jnp.full((1, 128), jnp.sum(sums), F32)


def centre_kernel(en, back, band, total, *rest):
    border, (out, passed) = rest[:-2], rest[-2:]
    passed[...] = total[...]
    size = 8

    def some(g, carry):
        sums = [lon_product(back[size * g + i], band[size * g + i]) for i in range(size)]
        for i in range(size):
            out[size * g + i] = sums[i]
        return carry

    lax.fori_loop(0, back.shape[0] // size, some, 0)
    place = Place(back.shape[0], en)
    for d in range(place.dirs):
        first = place.border(d)[0] * (back.shape[0] - 4)
        for n in range(4):
            out[first + n] = lon_product(border[d][n], band[first + n])


def final_kernel(centre, band, edge, far, near, exposure, total, out, passed, whole, v_out, out_sems):
    groups = near.shape[0]
    size = 2
    steps = groups // size
    passed[...] = total[...]

    def copy_out(p):
        return chunk_copy(v_out, out, out_sems.at[p], p, 4 * size)

    def lon(g):
        return [(whole, 4 * g + n, lon_edges(centre, edge, far, near, g, 4 * g + n, n)) for n in range(4)]

    def lat(g):
        return [(v_out, 4 * g + n, lat_product(band[4 * g + n], whole[4 * g + n]) * exposure[4 * g + n]) for n in range(4)]

    run_stages(steps, size, [(lon, 0), (lat, 1)], events=[(p + 2, copy_out(p).start) for p in range(steps)])
    for p in range(steps):
        copy_out(p).wait()


def tree_sum(values):
    while len(values) > 1:
        values = [a + b for a, b in zip(values[::2], values[1::2])]
    return values[0]


def ring(size, shift):
    return [(i, (i + shift) % size) for i in range(size)]


def local(flux, exposure, background, observed, psf_radius, band_low, band_high, disp_raw):
    block, rows, width = flux.shape
    bins = disp_raw.shape[0]
    sky, en = lax.axis_size("sky"), lax.axis_size("en")
    shifts = [1] if en == 2 else [1, -1]
    dirs = len(shifts)
    slots = block + REACH * dirs
    parts = min(8, block // 4)

    def tiles(count, dtype=F32):
        return jax.ShapeDtypeStruct((count, rows, width), dtype)

    def edges(count):
        return jax.ShapeDtypeStruct((count // 4, 128, 128), F32)

    def weights(count):
        return jax.ShapeDtypeStruct((count, 128, 256), BF16)

    def scratch(shape):
        return pltpu.VMEM(shape.shape, shape.dtype)

    lanes = jax.ShapeDtypeStruct((1, 128), F32)

    flux, exposure_in, background, observed = [
        pltpu.with_memory_space_constraint(array, pltpu.HBM) for array in (flux, exposure, background, observed)
    ]
    half = block // 2

    def swap_far(edges):
        return lax.ppermute(edges, "sky", [(s, (s + 1 if s % 2 else s - 1) % sky) for s in range(sky)])

    def swap_near(edges):
        return lax.ppermute(edges, "sky", [(s, s ^ 1) for s in range(sky)])

    def neighbours(arrays):
        return [lax.ppermute(array, "en", ring(en, shift)) for array, shift in zip(arrays, shifts)]

    weighted, near, far, *sent = pl.pallas_call(
        functools.partial(pack_kernel, parts, en),
        in_specs=[ANY] * 4,
        out_specs=[VMEM] * (3 + dirs),
        out_shape=[tiles(block), edges(block), edges(block)] + [tiles(2 * REACH)] * dirs,
        scratch_shapes=[
            scratch(tiles(block)), scratch(tiles(block)), pltpu.VMEM((dirs, REACH, rows, width), jnp.int32),
            pltpu.SemaphoreType.DMA((2, parts)), pltpu.SemaphoreType.DMA((dirs, 2)),
        ],
        compiler_params=params(12),
        name="weight_and_pack",
    )(flux, exposure_in, background, observed)
    far, near = swap_far(far), swap_near(near)
    counts = neighbours(sent)

    centre, band, edge, fold, background, observed = pl.pallas_call(
        functools.partial(weights_kernel, en),
        in_specs=[SMEM] * 4 + [VMEM] + [ANY] * 2,
        out_specs=[VMEM] * 3 + [SMEM] + [VMEM] * 2,
        out_shape=[
            tiles(block), weights(block), weights(block), jax.ShapeDtypeStruct((5 * (slots + 4),), F32),
            tiles(block), tiles(block, jnp.int32),
        ],
        scratch_shapes=[pltpu.SemaphoreType.DMA((2,))],
        compiler_params=params(4),
        cost_estimate=cost(block, 1, block * 2**15),
        name="weights_and_centre",
    )(psf_radius, band_low, band_high, disp_raw, weighted, background, observed)
    sent = pl.pallas_call(
        functools.partial(blur_kernel, en),
        in_specs=[VMEM] * 5,
        out_specs=[VMEM] * dirs,
        out_shape=[tiles(4)] * dirs,
        compiler_params=params(4),
        cost_estimate=cost(4 * dirs, 2),
        name="blur_border",
    )(centre, band, edge, far, near)
    received = neighbours(sent)
    resid, loss, *folded = pl.pallas_call(
        functools.partial(middle_kernel, en),
        in_specs=[SMEM] + [VMEM] * 7,
        out_specs=[VMEM] * 5,
        out_shape=[tiles(block + 4), jax.ShapeDtypeStruct((8, 128), F32), tiles(block), edges(block), edges(block)],
        scratch_shapes=[scratch(tiles(block)), scratch(tiles(block + 4))],
        compiler_params=params(10),
        cost_estimate=cost(block, 2, block * 2**15),
        name="blur_residual_fold",
    )(fold, centre, band, edge, far, near, background, observed)
    back, near, far = folded
    near, far, total, *border = pl.pallas_call(
        functools.partial(border_kernel, en),
        in_specs=[SMEM] + [VMEM] * (6 + 3 * dirs),
        out_specs=[VMEM] * (3 + dirs),
        out_shape=[edges(block), edges(block), lanes] + [tiles(4)] * dirs,
        scratch_shapes=[scratch(tiles(8)), scratch(tiles(4)), scratch(tiles(4)), scratch(tiles(8))],
        compiler_params=params(4),
        cost_estimate=cost(4 * dirs, 1),
        name="border_residual_fold_loss",
    )(fold, background, observed, resid, loss, near, far, *sent, *received, *counts)

    def partners(value, masks):
        return [lax.ppermute(value, ("sky", "en"), [(i, i ^ mask) for i in range(sky * en)]) for mask in masks]

    far, near = swap_far(far), swap_near(near)
    moved = partners(total, [4 * en * k for k in range(1, sky // 4)])
    centre, total = pl.pallas_call(
        functools.partial(centre_kernel, en),
        in_specs=[VMEM] * (3 + dirs),
        out_specs=[VMEM] * 2,
        out_shape=[tiles(block), lanes],
        compiler_params=params(4),
        cost_estimate=cost(block, 1),
        name="back_centre",
    )(back, band, total, *border)
    total = tree_sum([total] + moved)
    total = tree_sum([total] + partners(total, [k % en ^ (k // en * 3 * en) for k in range(1, 2 * en)]))
    moved = partners(total, [en])
    grad, total = pl.pallas_call(
        final_kernel,
        in_specs=[VMEM] * 7,
        out_specs=[ANY, VMEM],
        out_shape=[tiles(block), lanes],
        scratch_shapes=[scratch(tiles(block)), scratch(tiles(block)), pltpu.SemaphoreType.DMA((block // 8,))],
        compiler_params=params(8),
        cost_estimate=cost(block, 2),
        name="back_edges_lat_exposure",
    )(centre, band, edge, far, near, exposure, total)
    return grad, tree_sum([total] + moved)[0, 0] / F32(rows * width * bins * sky)


def solution(mesh):
    placed = (P("en", None, "sky"),) * 4 + (P(),) * 4
    return jax.shard_map(local, mesh=mesh, in_specs=placed, out_specs=(P("en", None, "sky"), P()), check_vma=False)
```

```python
import functools

import jax
import jax.numpy as jnp
from jax import lax
from jax.experimental import pallas as pl
from jax.experimental.pallas import tpu as pltpu
from jax.sharding import PartitionSpec as P

RMAX = 32
REACH = 2
F32 = jnp.float32
BF16 = jnp.bfloat16
SMEM = pl.BlockSpec(memory_space=pltpu.SMEM)
ANY = pl.BlockSpec(memory_space=pl.ANY)
VMEM = pl.BlockSpec(memory_space=pltpu.VMEM)
HBM = pl.BlockSpec(memory_space=pltpu.HBM)


def split(x):
    hi = x.astype(BF16)
    return hi, (x - hi.astype(F32)).astype(BF16)


def params(mib=56):
    return pltpu.CompilerParams(vmem_limit_bytes=mib * 2**20)


def blocks(count, rows, cols):
    return pl.BlockSpec((count, rows, cols), lambda i: (i, 0, 0))


def chunk_copy(source, target, sem, c, size):
    at = pl.ds(c * size, size)
    return pltpu.make_async_copy(source.at[at], target.at[at], sem)


def run_stages(groups, size, stages, events=(), arrive=None):
    stages = [(*stage, groups)[:3] for stage in stages]
    marks = {0} | {lag for _, lag, _ in stages} | {lag + count for _, lag, count in stages} | {at for at, _ in events}
    marks = sorted(marks)
    for start, stop in zip(marks, marks[1:] + [marks[-1]]):
        for at, event in events:
            if at == start:
                event()
        active = [(n, stage, lag) for n, (stage, lag, count) in enumerate(stages) if lag <= start < lag + count]
        if stop == start or not active:
            continue

        def step(p, carry):
            if arrive is not None:
                for n, _, lag in active:
                    arrive(n, p - lag)
            stores = []
            for _, stage, lag in active:
                for i in range(size):
                    stores += stage((p - lag) * size + i)
            for ref, index, value in stores:
                if index is None:
                    ref[...] += value
                else:
                    ref[index] = value
            return carry

        lax.fori_loop(start, stop, step, 0)


def cost(tiles, products, transcendentals=0):
    return pl.CostEstimate(flops=tiles * products * 2 * 128 * 256 * 256, bytes_accessed=tiles * 2**16, transcendentals=transcendentals)


class Place:
    def __init__(self, block, en):
        self.block, self.en = block, en
        self.me = lax.axis_index("en")
        self.dirs = 1 if en == 2 else 2
        self.extra = REACH * self.dirs
        self.slots, self.bins = block + self.extra, block * en
        self.own = jnp.where(self.me == 0, 0, REACH) if en == 2 else REACH
        self.first_bin = self.me * block - self.own

    def above(self, d):
        return jnp.where(self.me == 0, 1, 0) if self.en == 2 else 1 - d

    def sent(self, d, width):
        return self.above(d) * (self.block - width)

    def border(self, d):
        up = self.above(d) if self.en == 2 else d
        return up, up * (self.block + self.own - REACH)

    def clamp(self, g):
        return jnp.clip(g, 0, self.bins - 1)


def lanes_of(shape=(128, 128)):
    return lax.broadcasted_iota(jnp.int32, shape, 1)


def is_odd():
    return lax.axis_index("sky") % 2 == 1


def pack_edges(tiles):
    lane = lanes_of()
    outer = (lane < RMAX) | (lane >= 128 - RMAX)
    early, late = [jnp.where(outer, tiles[n], pltpu.roll(tiles[n + 1], 64, 1)) for n in (0, 2)]
    late = pltpu.roll(late, RMAX, 1)
    mask = ((lane // RMAX) % 2 == 1) != is_odd()
    return jnp.where(mask, early, late), jnp.where(mask, late, early)


LEFT = (3, 1, 0, 2)
RIGHT = (0, 2, 1, 3)


def edge_tile(near, far, n):
    lane = lanes_of()
    from_left = lane < RMAX * RIGHT[n] if LEFT[n] < RIGHT[n] else lane >= RMAX * LEFT[n]
    return jnp.where(from_left != is_odd(), far, near)


def lon_product(tile, weights):
    hi, lo = split(tile)
    rows = jnp.concatenate([weights[:, :128], weights[:, :128], weights[:, 128:]], axis=0)
    return jnp.dot(jnp.concatenate([hi, lo, hi], axis=1), rows, preferred_element_type=F32)


def lat_product(weights, tile):
    hi, lo = split(tile)
    columns = jnp.concatenate([weights, weights[:, :128]], axis=1)
    return jnp.dot(columns, jnp.concatenate([hi, hi, lo], axis=0), preferred_element_type=F32)


def profile(radius, column):
    wide = jnp.full((1, 128), radius, jnp.int32).astype(F32)
    reach = wide * wide
    factor = -2.0 / reach
    lane = lax.broadcasted_iota(jnp.int32, (1, 128), 1)
    square = (lane * lane).astype(F32)
    values = jnp.where(square <= reach, jnp.exp(square * factor), 0.0)
    norm = 2.0 * jnp.sum(values, axis=1, keepdims=True) - 1.0
    root = jnp.sqrt(jnp.full((1, 128), column, F32))[:, :1]
    return factor[:, :1], 1.0 / (norm * root), reach[:, :1]


def taper_values(diff, ok, factor, scale, reach):
    square = diff * diff
    return jnp.where((square <= reach) & ok, jnp.exp(square * factor) * scale, 0.0)


def pack_kernel(parts, en, flux, exposure, background, observed, weighted, near, far, *rest):
    place = Place(flux.shape[0], en)
    dirs, block = place.dirs, place.block
    sent, (v_flux, v_exposure, v_observed, sems, near_sems) = rest[:dirs], rest[dirs:]
    chunk = block // parts

    def arrivals(c):
        return [chunk_copy(a, b, sems.at[n, c], c, chunk) for n, (a, b) in enumerate(((flux, v_flux), (exposure, v_exposure)))]

    def near_arrivals(d):
        at = pl.ds(place.sent(d, REACH), REACH)
        return [
            pltpu.make_async_copy(background.at[at], sent[d].at[pl.ds(0, REACH)], near_sems.at[d, 0]),
            pltpu.make_async_copy(observed.at[at], v_observed.at[d], near_sems.at[d, 1]),
        ]

    for c in range(parts):
        for copy in arrivals(c):
            copy.start()
    for d in range(dirs):
        for copy in near_arrivals(d):
            copy.start()

    def some(g, carry):
        tiles = [v_flux[4 * g + i] * v_exposure[4 * g + i] for i in range(4)]
        packed = pack_edges(tiles)
        for i in range(4):
            weighted[4 * g + i] = tiles[i]
        near[g], far[g] = packed
        return carry

    for c in range(parts):
        for copy in arrivals(c):
            copy.wait()
        lax.fori_loop(c * chunk // 4, (c + 1) * chunk // 4, some, 0)
    for d in range(dirs):
        for copy in near_arrivals(d):
            copy.wait()
        for k in range(REACH):
            sent[d][REACH + k] = v_observed[d, k].astype(F32)


def weights_kernel(en, radius, low, high, disp, weighted, background, observed,
                   centre, band, edge, fold, held_background, counts, v_observed, sems):
    fetches = [
        pltpu.make_async_copy(background, held_background, sems.at[0]),
        pltpu.make_async_copy(observed, v_observed, sems.at[1]),
    ]
    for fetch in fetches:
        fetch.start()
    block = weighted.shape[0]
    place = Place(block, en)
    row = lax.broadcasted_iota(jnp.int32, (128, 128), 0)
    col = lax.broadcasted_iota(jnp.int32, (128, 128), 1)
    near = (row - col).astype(F32)
    always = row >= 0
    beside = []
    for n in range(4):
        shift = jnp.where(row // RMAX == LEFT[n], -RMAX - RMAX * LEFT[n], 128 - RMAX * RIGHT[n])
        held = (row // RMAX == LEFT[n]) | (row // RMAX == RIGHT[n])
        beside.append(((row + shift - col).astype(F32), held))

    def weight(i, j):
        at, to = place.clamp(i), place.clamp(j)
        inside = (i == at) & (j == to) & (low[at] <= j - i) & (j - i <= high[at])
        return jnp.where(inside, disp[at, to], 0.0)

    def fold_row(g):
        for o in range(-REACH, REACH + 1):
            fold[5 * (g - place.first_bin + REACH) + o + REACH] = weight(g, g + o)

    def make(g, n):
        fold_row(g)
        column = weight(g, g)
        for o in (-2, -1, 1, 2):
            column = column + weight(g - o, g)
        numbers = profile(radius[place.clamp(g)], jnp.where(column > 0.0, column, 1.0))
        return tuple(
            jnp.concatenate(split(taper_values(diff, ok, *numbers)), axis=1) for diff, ok in ((near, always), beside[n])
        )

    for s in (0, 1, place.slots + 2, place.slots + 3):
        for o in range(5):
            fold[5 * s + o] = 0.0

    def some(g):
        made = [make(place.me * block + 4 * g + n, n) for n in range(4)]
        return [(band, 4 * g + n, made[n][0]) for n in range(4)] + [(edge, 4 * g + n, made[n][1]) for n in range(4)]

    def lon(g):
        return [(centre, 4 * g + n, lon_product(weighted[4 * g + n], band[4 * g + n])) for n in range(4)]

    run_stages(block // 4, 1, [(some, 0), (lon, 1)])
    for d in range(place.dirs):
        up, slot = place.border(d)
        for k in range(REACH):
            fold_row(place.first_bin + slot + up * REACH + k)
    for fetch in fetches:
        fetch.wait()

    def convert(g):
        return [(counts, 4 * g + n, v_observed[4 * g + n].astype(F32)) for n in range(4)]

    run_stages(block // 4, 1, [(convert, 0)])


def lon_edges(centre, edge, far, near, g, at, n):
    return centre[at] + lon_product(edge_tile(near[g], far[g], n), edge[at])


def blur_kernel(en, centre, band, edge, far, near, *blurred):
    place = Place(centre.shape[0], en)
    for d in range(place.dirs):
        start = place.sent(d, 4)
        g = lax.div(start, 4) if en == 2 else start // 4
        sums = [lon_edges(centre, edge, far, near, g, start + n, n) for n in range(4)]
        sums = [lat_product(band[start + n], sums[n]) for n in range(4)]
        for n in range(4):
            blurred[d][n] = sums[n]


def inverse(x):
    first = pl.reciprocal(x, approx=True)
    return first * (2.0 - x * first)


ROWS = [pl.ds(32 * r, 32) for r in range(4)]


def loss_terms(mu, counts):
    return (mu - counts * jnp.log(mu)).reshape(-1, 8, 128).sum(0)


def fold_one(fold, row, resid, at):
    total = None
    for o in range(5):
        term = fold[5 * (row - o) + o] * resid[at - o]
        total = term if total is None else total + term
    return total


def middle_kernel(en, fold, centre, band, edge, far, near, background, observed, resid, loss, back, near_out, far_out, whole, blurred):
    block = centre.shape[0]
    place = Place(block, en)
    own = place.own
    zero = jnp.zeros((128, 128), F32)
    for s in (0, 1, block + 2, block + 3):
        blurred[s] = zero
        resid[s] = zero
    loss[...] = jnp.zeros((8, 128), F32)
    inside = (own, own + block - REACH) if en == 2 else (REACH, block - REACH)

    def lon(g):
        return [(whole, 4 * g + n, lon_edges(centre, edge, far, near, g, 4 * g + n, n)) for n in range(4)]

    def lat(g):
        return [(blurred, 4 * g + n + 2, lat_product(band[4 * g + n], whole[4 * g + n])) for n in range(4)]

    def residual(g):
        sums = None
        for rows in ROWS:
            window = [blurred[4 * g + k, rows] for k in range(8)]
            for n in range(4):
                b = 4 * g + n
                mu = background[b, rows]
                for o in range(5):
                    mu = mu + fold[5 * (b + own + 2) + o] * window[n + o]
                counts = observed[b, rows]
                resid[b + 2, rows] = 1.0 - counts * inverse(mu)
                inner = (b >= inside[0]) & (b < inside[1])
                terms = jnp.where(inner, loss_terms(mu, counts), 0.0)
                sums = terms if sums is None else sums + terms
        return [(loss, None, sums)]

    def fold_back(g):
        tiles = [[] for _ in range(4)]
        for rows in ROWS:
            window = [resid[4 * g + k, rows] for k in range(8)]
            for n in range(4):
                total = None
                for o in range(5):
                    term = fold[5 * (4 * g + n + own + 4 - o) + o] * window[n + 4 - o]
                    total = term if total is None else total + term
                back[4 * g + n, rows] = total
                tiles[n].append(total)
        near_out[g], far_out[g] = pack_edges([jnp.concatenate(parts, axis=0) for parts in tiles])
        return []

    run_stages(block // 8, 2, [(fold_back, 5), (residual, 3), (lon, 0), (lat, 1)])


def border_kernel(en, fold, background, observed, resid, loss, near_in, far_in, *rest):
    block = background.shape[0]
    place = Place(block, en)
    dirs, own = place.dirs, place.own
    sent, received, counts = [rest[n * dirs:(n + 1) * dirs] for n in range(3)]
    near, far, total = rest[3 * dirs:3 * dirs + 3]
    back, (blurred, ground, seen, rows) = rest[3 * dirs + 3:4 * dirs + 3], rest[4 * dirs + 3:]
    sums = loss[...]
    near[...], far[...] = near_in[...], far_in[...]
    for d in range(dirs):
        up, slot = place.border(d)
        mine, theirs = 4 * (1 - up), 4 * up
        for k in range(4):
            blurred[mine + k] = sent[dirs - 1 - d][k]
            blurred[theirs + k] = received[d][k]
            rows[mine + k] = resid[up * (block - 8) + 4 + k]
        first = up * (block - REACH)
        for k in range(REACH):
            ground[mine // 2 + k] = background[first + k]
            seen[mine // 2 + k] = observed[first + k]
            ground[theirs // 2 + k] = counts[d][k]
            seen[theirs // 2 + k] = counts[d][REACH + k]
        for j in range(2 * REACH):
            mu = ground[j]
            for o in range(5):
                mu = mu + fold[5 * (slot + j + 2) + o] * blurred[j + o]
            rows[theirs + j] = 1.0 - seen[j] * inverse(mu)
            is_mine = (mine // 2 <= j) & (j < mine // 2 + REACH)
            sums = sums + jnp.where(is_mine, loss_terms(mu, seen[j]), 0.0)
        first = up * (block - 4)
        tiles = [fold_one(fold, first + n + own + 4, rows, n + 4) for n in range(4)]
        g = up * (block // 4 - 1)
        near[g], far[g] = pack_edges(tiles)
        for n in range(4):
            back[d][n] = tiles[n]
    total[...] = jnp.full((1, 128), jnp.sum(sums), F32)


def centre_kernel(en, back, band, total, *rest):
    border, (out, passed) = rest[:-2], rest[-2:]
    passed[...] = total[...]
    size = 8

    def some(g, carry):
        sums = [lon_product(back[size * g + i], band[size * g + i]) for i in range(size)]
        for i in range(size):
            out[size * g + i] = sums[i]
        return carry

    lax.fori_loop(0, back.shape[0] // size, some, 0)
    place = Place(back.shape[0], en)
    for d in range(place.dirs):
        first = place.border(d)[0] * (back.shape[0] - 4)
        for n in range(4):
            out[first + n] = lon_product(border[d][n], band[first + n])


def final_kernel(centre, band, edge, far, near, exposure, total, out, passed, whole, v_out, out_sems):
    groups = near.shape[0]
    size = 2
    steps = groups // size
    passed[...] = total[...]

    def copy_out(p):
        return chunk_copy(v_out, out, out_sems.at[p], p, 4 * size)

    def lon(g):
        return [(whole, 4 * g + n, lon_edges(centre, edge, far, near, g, 4 * g + n, n)) for n in range(4)]

    def lat(g):
        return [(v_out, 4 * g + n, lat_product(band[4 * g + n], whole[4 * g + n]) * exposure[4 * g + n]) for n in range(4)]

    run_stages(steps, size, [(lon, 0), (lat, 1)], events=[(p + 2, copy_out(p).start) for p in range(steps)])
    for p in range(steps):
        copy_out(p).wait()


def tree_sum(values):
    while len(values) > 1:
        values = [a + b for a, b in zip(values[::2], values[1::2])]
    return values[0]


def ring(size, shift):
    return [(i, (i + shift) % size) for i in range(size)]


def local(flux, exposure, background, observed, psf_radius, band_low, band_high, disp_raw):
    block, rows, width = flux.shape
    bins = disp_raw.shape[0]
    sky, en = lax.axis_size("sky"), lax.axis_size("en")
    shifts = [1] if en == 2 else [1, -1]
    dirs = len(shifts)
    slots = block + REACH * dirs
    parts = min(8, block // 4)

    def tiles(count, dtype=F32):
        return jax.ShapeDtypeStruct((count, rows, width), dtype)

    def edges(count):
        return jax.ShapeDtypeStruct((count // 4, 128, 128), F32)

    def weights(count):
        return jax.ShapeDtypeStruct((count, 128, 256), BF16)

    def scratch(shape):
        return pltpu.VMEM(shape.shape, shape.dtype)

    lanes = jax.ShapeDtypeStruct((1, 128), F32)

    flux, exposure_in, background, observed = [
        pltpu.with_memory_space_constraint(array, pltpu.HBM) for array in (flux, exposure, background, observed)
    ]
    half = block // 2

    def swap_far(edges):
        return lax.ppermute(edges, "sky", [(s, (s + 1 if s % 2 else s - 1) % sky) for s in range(sky)])

    def swap_near(edges):
        return lax.ppermute(edges, "sky", [(s, s ^ 1) for s in range(sky)])

    def neighbours(arrays):
        return [lax.ppermute(array, "en", ring(en, shift)) for array, shift in zip(arrays, shifts)]

    weighted, near, far, *sent = pl.pallas_call(
        functools.partial(pack_kernel, parts, en),
        in_specs=[ANY] * 4,
        out_specs=[VMEM] * (3 + dirs),
        out_shape=[tiles(block), edges(block), edges(block)] + [tiles(2 * REACH)] * dirs,
        scratch_shapes=[
            scratch(tiles(block)), scratch(tiles(block)), pltpu.VMEM((dirs, REACH, rows, width), jnp.int32),
            pltpu.SemaphoreType.DMA((2, parts)), pltpu.SemaphoreType.DMA((dirs, 2)),
        ],
        compiler_params=params(12),
        name="weight_and_pack",
    )(flux, exposure_in, background, observed)
    far, near = swap_far(far), swap_near(near)
    counts = neighbours(sent)

    centre, band, edge, fold, background, observed = pl.pallas_call(
        functools.partial(weights_kernel, en),
        in_specs=[SMEM] * 4 + [VMEM] + [ANY] * 2,
        out_specs=[VMEM] * 3 + [SMEM] + [VMEM] * 2,
        out_shape=[
            tiles(block), weights(block), weights(block), jax.ShapeDtypeStruct((5 * (slots + 4),), F32),
            tiles(block), tiles(block),
        ],
        scratch_shapes=[scratch(tiles(block, jnp.int32)), pltpu.SemaphoreType.DMA((2,))],
        compiler_params=params(6),
        cost_estimate=cost(block, 1, block * 2**15),
        name="weights_and_centre",
    )(psf_radius, band_low, band_high, disp_raw, weighted, background, observed)
    sent = pl.pallas_call(
        functools.partial(blur_kernel, en),
        in_specs=[VMEM] * 5,
        out_specs=[VMEM] * dirs,
        out_shape=[tiles(4)] * dirs,
        compiler_params=params(4),
        cost_estimate=cost(4 * dirs, 2),
        name="blur_border",
    )(centre, band, edge, far, near)
    received = neighbours(sent)
    resid, loss, *folded = pl.pallas_call(
        functools.partial(middle_kernel, en),
        in_specs=[SMEM] + [VMEM] * 7,
        out_specs=[VMEM] * 5,
        out_shape=[tiles(block + 4), jax.ShapeDtypeStruct((8, 128), F32), tiles(block), edges(block), edges(block)],
        scratch_shapes=[scratch(tiles(block)), scratch(tiles(block + 4))],
        compiler_params=params(10),
        cost_estimate=cost(block, 2, block * 2**15),
        name="blur_residual_fold",
    )(fold, centre, band, edge, far, near, background, observed)
    back, near, far = folded
    near, far, total, *border = pl.pallas_call(
        functools.partial(border_kernel, en),
        in_specs=[SMEM] + [VMEM] * (6 + 3 * dirs),
        out_specs=[VMEM] * (3 + dirs),
        out_shape=[edges(block), edges(block), lanes] + [tiles(4)] * dirs,
        scratch_shapes=[scratch(tiles(8)), scratch(tiles(4)), scratch(tiles(4)), scratch(tiles(8))],
        compiler_params=params(4),
        cost_estimate=cost(4 * dirs, 1),
        name="border_residual_fold_loss",
    )(fold, background, observed, resid, loss, near, far, *sent, *received, *counts)

    def partners(value, masks):
        return [lax.ppermute(value, ("sky", "en"), [(i, i ^ mask) for i in range(sky * en)]) for mask in masks]

    far, near = swap_far(far), swap_near(near)
    moved = partners(total, [4 * en * k for k in range(1, sky // 4)])
    centre, total = pl.pallas_call(
        functools.partial(centre_kernel, en),
        in_specs=[VMEM] * (3 + dirs),
        out_specs=[VMEM] * 2,
        out_shape=[tiles(block), lanes],
        compiler_params=params(4),
        cost_estimate=cost(block, 1),
        name="back_centre",
    )(back, band, total, *border)
    total = tree_sum([total] + moved)
    moved = partners(total, [k % en ^ (k // en * 3 * en) for k in range(1, 2 * en)])
    grad, total = pl.pallas_call(
        final_kernel,
        in_specs=[VMEM] * 7,
        out_specs=[ANY, VMEM],
        out_shape=[tiles(block), lanes],
        scratch_shapes=[scratch(tiles(block)), scratch(tiles(block)), pltpu.SemaphoreType.DMA((block // 8,))],
        compiler_params=params(8),
        cost_estimate=cost(block, 2),
        name="back_edges_lat_exposure",
    )(centre, band, edge, far, near, exposure, total)
    total = tree_sum([total] + moved)
    total = total + partners(total, [en])[0]
    return grad, total[0, 0] / F32(rows * width * bins * sky)


def solution(mesh):
    placed = (P("en", None, "sky"),) * 4 + (P(),) * 4
    return jax.shard_map(local, mesh=mesh, in_specs=placed, out_specs=(P("en", None, "sky"), P()), check_vma=False)
```

```python
import functools

import jax
import jax.numpy as jnp
from jax import lax
from jax.experimental import pallas as pl
from jax.experimental.pallas import tpu as pltpu
from jax.sharding import PartitionSpec as P

RMAX = 32
REACH = 2
F32 = jnp.float32
BF16 = jnp.bfloat16
SMEM = pl.BlockSpec(memory_space=pltpu.SMEM)
ANY = pl.BlockSpec(memory_space=pl.ANY)
VMEM = pl.BlockSpec(memory_space=pltpu.VMEM)
HBM = pl.BlockSpec(memory_space=pltpu.HBM)


def split(x):
    hi = x.astype(BF16)
    return hi, (x - hi.astype(F32)).astype(BF16)


def params(mib=56):
    return pltpu.CompilerParams(vmem_limit_bytes=mib * 2**20)


def blocks(count, rows, cols):
    return pl.BlockSpec((count, rows, cols), lambda i: (i, 0, 0))


def chunk_copy(source, target, sem, c, size):
    at = pl.ds(c * size, size)
    return pltpu.make_async_copy(source.at[at], target.at[at], sem)


def run_stages(groups, size, stages, events=(), arrive=None):
    stages = [(*stage, groups)[:3] for stage in stages]
    marks = {0} | {lag for _, lag, _ in stages} | {lag + count for _, lag, count in stages} | {at for at, _ in events}
    marks = sorted(marks)
    for start, stop in zip(marks, marks[1:] + [marks[-1]]):
        for at, event in events:
            if at == start:
                event()
        active = [(n, stage, lag) for n, (stage, lag, count) in enumerate(stages) if lag <= start < lag + count]
        if stop == start or not active:
            continue

        def step(p, carry):
            if arrive is not None:
                for n, _, lag in active:
                    arrive(n, p - lag)
            stores = []
            for _, stage, lag in active:
                for i in range(size):
                    stores += stage((p - lag) * size + i)
            for ref, index, value in stores:
                if index is None:
                    ref[...] += value
                else:
                    ref[index] = value
            return carry

        lax.fori_loop(start, stop, step, 0)


def cost(tiles, products, transcendentals=0):
    return pl.CostEstimate(flops=tiles * products * 2 * 128 * 256 * 256, bytes_accessed=tiles * 2**16, transcendentals=transcendentals)


class Place:
    def __init__(self, block, en):
        self.block, self.en = block, en
        self.me = lax.axis_index("en")
        self.dirs = 1 if en == 2 else 2
        self.extra = REACH * self.dirs
        self.slots, self.bins = block + self.extra, block * en
        self.own = jnp.where(self.me == 0, 0, REACH) if en == 2 else REACH
        self.first_bin = self.me * block - self.own

    def above(self, d):
        return jnp.where(self.me == 0, 1, 0) if self.en == 2 else 1 - d

    def sent(self, d, width):
        return self.above(d) * (self.block - width)

    def border(self, d):
        up = self.above(d) if self.en == 2 else d
        return up, up * (self.block + self.own - REACH)

    def clamp(self, g):
        return jnp.clip(g, 0, self.bins - 1)


def lanes_of(shape=(128, 128)):
    return lax.broadcasted_iota(jnp.int32, shape, 1)


def is_odd():
    return lax.axis_index("sky") % 2 == 1


def pack_edges(tiles):
    lane = lanes_of()
    outer = (lane < RMAX) | (lane >= 128 - RMAX)
    early, late = [jnp.where(outer, tiles[n], pltpu.roll(tiles[n + 1], 64, 1)) for n in (0, 2)]
    late = pltpu.roll(late, RMAX, 1)
    mask = ((lane // RMAX) % 2 == 1) != is_odd()
    return jnp.where(mask, early, late), jnp.where(mask, late, early)


LEFT = (3, 1, 0, 2)
RIGHT = (0, 2, 1, 3)


def edge_tile(near, far, n):
    lane = lanes_of()
    from_left = lane < RMAX * RIGHT[n] if LEFT[n] < RIGHT[n] else lane >= RMAX * LEFT[n]
    return jnp.where(from_left != is_odd(), far, near)


def twice(x):
    return jnp.concatenate([x, x], axis=0)


def lon_product(tile, weights):
    out = jnp.dot(jnp.concatenate(split(tile), axis=1), twice(weights), preferred_element_type=F32)
    return out[:, :128] + out[:, 128:]


def lat_product(weights, tile):
    out = jnp.dot(weights, twice(jnp.concatenate(split(tile), axis=1)), preferred_element_type=F32)
    return out[:, :128] + out[:, 128:]


def profile(radius, column):
    wide = jnp.full((1, 128), radius, jnp.int32).astype(F32)
    reach = wide * wide
    factor = -2.0 / reach
    lane = lax.broadcasted_iota(jnp.int32, (1, 128), 1)
    square = (lane * lane).astype(F32)
    values = jnp.where(square <= reach, jnp.exp(square * factor), 0.0)
    norm = 2.0 * jnp.sum(values, axis=1, keepdims=True) - 1.0
    root = jnp.sqrt(jnp.full((1, 128), column, F32))[:, :1]
    return factor[:, :1], 1.0 / (norm * root), reach[:, :1]


def taper_values(diff, ok, factor, scale, reach):
    square = diff * diff
    return jnp.where((square <= reach) & ok, jnp.exp(square * factor) * scale, 0.0)


def pack_kernel(parts, en, flux, exposure, background, observed, weighted, near, far, *rest):
    place = Place(flux.shape[0], en)
    dirs, block = place.dirs, place.block
    sent, (v_flux, v_exposure, v_observed, sems, near_sems) = rest[:dirs], rest[dirs:]
    chunk = block // parts

    def arrivals(c):
        return [chunk_copy(a, b, sems.at[n, c], c, chunk) for n, (a, b) in enumerate(((flux, v_flux), (exposure, v_exposure)))]

    def near_arrivals(d):
        at = pl.ds(place.sent(d, REACH), REACH)
        return [
            pltpu.make_async_copy(background.at[at], sent[d].at[pl.ds(0, REACH)], near_sems.at[d, 0]),
            pltpu.make_async_copy(observed.at[at], v_observed.at[d], near_sems.at[d, 1]),
        ]

    for c in range(parts):
        for copy in arrivals(c):
            copy.start()
    for d in range(dirs):
        for copy in near_arrivals(d):
            copy.start()

    def some(g, carry):
        tiles = [v_flux[4 * g + i] * v_exposure[4 * g + i] for i in range(4)]
        packed = pack_edges(tiles)
        for i in range(4):
            weighted[4 * g + i] = tiles[i]
        near[g], far[g] = packed
        return carry

    for c in range(parts):
        for copy in arrivals(c):
            copy.wait()
        lax.fori_loop(c * chunk // 4, (c + 1) * chunk // 4, some, 0)
    for d in range(dirs):
        for copy in near_arrivals(d):
            copy.wait()
        for k in range(REACH):
            sent[d][REACH + k] = v_observed[d, k].astype(F32)


def weights_kernel(en, radius, low, high, disp, weighted, background, observed,
                   centre, band, edge, fold, held_background, counts, v_observed, sems):
    fetches = [
        pltpu.make_async_copy(background, held_background, sems.at[0]),
        pltpu.make_async_copy(observed, v_observed, sems.at[1]),
    ]
    for fetch in fetches:
        fetch.start()
    block = weighted.shape[0]
    place = Place(block, en)
    row = lax.broadcasted_iota(jnp.int32, (128, 128), 0)
    col = lax.broadcasted_iota(jnp.int32, (128, 128), 1)
    near = (row - col).astype(F32)
    always = row >= 0
    beside = []
    for n in range(4):
        shift = jnp.where(row // RMAX == LEFT[n], -RMAX - RMAX * LEFT[n], 128 - RMAX * RIGHT[n])
        held = (row // RMAX == LEFT[n]) | (row // RMAX == RIGHT[n])
        beside.append(((row + shift - col).astype(F32), held))

    def weight(i, j):
        at, to = place.clamp(i), place.clamp(j)
        inside = (i == at) & (j == to) & (low[at] <= j - i) & (j - i <= high[at])
        return jnp.where(inside, disp[at, to], 0.0)

    def fold_row(g):
        for o in range(-REACH, REACH + 1):
            fold[5 * (g - place.first_bin + REACH) + o + REACH] = weight(g, g + o)

    def make(g, n):
        fold_row(g)
        column = weight(g, g)
        for o in (-2, -1, 1, 2):
            column = column + weight(g - o, g)
        numbers = profile(radius[place.clamp(g)], jnp.where(column > 0.0, column, 1.0))
        return tuple(
            jnp.concatenate(split(taper_values(diff, ok, *numbers)), axis=1) for diff, ok in ((near, always), beside[n])
        )

    for s in (0, 1, place.slots + 2, place.slots + 3):
        for o in range(5):
            fold[5 * s + o] = 0.0

    def some(g):
        made = [make(place.me * block + 4 * g + n, n) for n in range(4)]
        return [(band, 4 * g + n, made[n][0]) for n in range(4)] + [(edge, 4 * g + n, made[n][1]) for n in range(4)]

    def lon(g):
        return [(centre, 4 * g + n, lon_product(weighted[4 * g + n], band[4 * g + n])) for n in range(4)]

    run_stages(block // 4, 1, [(some, 0), (lon, 1)])
    for d in range(place.dirs):
        up, slot = place.border(d)
        for k in range(REACH):
            fold_row(place.first_bin + slot + up * REACH + k)
    for fetch in fetches:
        fetch.wait()

    def convert(g):
        return [(counts, 4 * g + n, v_observed[4 * g + n].astype(F32)) for n in range(4)]

    run_stages(block // 4, 1, [(convert, 0)])


def lon_edges(centre, edge, far, near, g, at, n):
    return centre[at] + lon_product(edge_tile(near[g], far[g], n), edge[at])


def blur_kernel(en, centre, band, edge, far, near, *blurred):
    place = Place(centre.shape[0], en)
    for d in range(place.dirs):
        start = place.sent(d, 4)
        g = lax.div(start, 4) if en == 2 else start // 4
        sums = [lon_edges(centre, edge, far, near, g, start + n, n) for n in range(4)]
        sums = [lat_product(band[start + n], sums[n]) for n in range(4)]
        for n in range(4):
            blurred[d][n] = sums[n]


def inverse(x):
    first = pl.reciprocal(x, approx=True)
    return first * (2.0 - x * first)


ROWS = [pl.ds(32 * r, 32) for r in range(4)]


def loss_terms(mu, counts):
    return (mu - counts * jnp.log(mu)).reshape(-1, 8, 128).sum(0)


def fold_one(fold, row, resid, at):
    total = None
    for o in range(5):
        term = fold[5 * (row - o) + o] * resid[at - o]
        total = term if total is None else total + term
    return total


def middle_kernel(en, fold, centre, band, edge, far, near, background, observed, resid, loss, back, near_out, far_out, whole, blurred):
    block = centre.shape[0]
    place = Place(block, en)
    own = place.own
    zero = jnp.zeros((128, 128), F32)
    for s in (0, 1, block + 2, block + 3):
        blurred[s] = zero
        resid[s] = zero
    loss[...] = jnp.zeros((8, 128), F32)
    inside = (own, own + block - REACH) if en == 2 else (REACH, block - REACH)

    def lon(g):
        return [(whole, 4 * g + n, lon_edges(centre, edge, far, near, g, 4 * g + n, n)) for n in range(4)]

    def lat(g):
        return [(blurred, 4 * g + n + 2, lat_product(band[4 * g + n], whole[4 * g + n])) for n in range(4)]

    def residual(g):
        sums = None
        for rows in ROWS:
            window = [blurred[4 * g + k, rows] for k in range(8)]
            for n in range(4):
                b = 4 * g + n
                mu = background[b, rows]
                for o in range(5):
                    mu = mu + fold[5 * (b + own + 2) + o] * window[n + o]
                counts = observed[b, rows]
                resid[b + 2, rows] = 1.0 - counts * inverse(mu)
                inner = (b >= inside[0]) & (b < inside[1])
                terms = jnp.where(inner, loss_terms(mu, counts), 0.0)
                sums = terms if sums is None else sums + terms
        return [(loss, None, sums)]

    def fold_back(g):
        tiles = [[] for _ in range(4)]
        for rows in ROWS:
            window = [resid[4 * g + k, rows] for k in range(8)]
            for n in range(4):
                total = None
                for o in range(5):
                    term = fold[5 * (4 * g + n + own + 4 - o) + o] * window[n + 4 - o]
                    total = term if total is None else total + term
                back[4 * g + n, rows] = total
                tiles[n].append(total)
        near_out[g], far_out[g] = pack_edges([jnp.concatenate(parts, axis=0) for parts in tiles])
        return []

    run_stages(block // 8, 2, [(fold_back, 5), (residual, 3), (lon, 0), (lat, 1)])


def border_kernel(en, fold, background, observed, resid, loss, near_in, far_in, *rest):
    block = background.shape[0]
    place = Place(block, en)
    dirs, own = place.dirs, place.own
    sent, received, counts = [rest[n * dirs:(n + 1) * dirs] for n in range(3)]
    near, far, total = rest[3 * dirs:3 * dirs + 3]
    back, (blurred, ground, seen, rows) = rest[3 * dirs + 3:4 * dirs + 3], rest[4 * dirs + 3:]
    sums = loss[...]
    near[...], far[...] = near_in[...], far_in[...]
    for d in range(dirs):
        up, slot = place.border(d)
        mine, theirs = 4 * (1 - up), 4 * up
        for k in range(4):
            blurred[mine + k] = sent[dirs - 1 - d][k]
            blurred[theirs + k] = received[d][k]
            rows[mine + k] = resid[up * (block - 8) + 4 + k]
        first = up * (block - REACH)
        for k in range(REACH):
            ground[mine // 2 + k] = background[first + k]
            seen[mine // 2 + k] = observed[first + k]
            ground[theirs // 2 + k] = counts[d][k]
            seen[theirs // 2 + k] = counts[d][REACH + k]
        for j in range(2 * REACH):
            mu = ground[j]
            for o in range(5):
                mu = mu + fold[5 * (slot + j + 2) + o] * blurred[j + o]
            rows[theirs + j] = 1.0 - seen[j] * inverse(mu)
            is_mine = (mine // 2 <= j) & (j < mine // 2 + REACH)
            sums = sums + jnp.where(is_mine, loss_terms(mu, seen[j]), 0.0)
        first = up * (block - 4)
        tiles = [fold_one(fold, first + n + own + 4, rows, n + 4) for n in range(4)]
        g = up * (block // 4 - 1)
        near[g], far[g] = pack_edges(tiles)
        for n in range(4):
            back[d][n] = tiles[n]
    total[...] = jnp.full((1, 128), jnp.sum(sums), F32)


def centre_kernel(en, back, band, total, *rest):
    border, (out, passed) = rest[:-2], rest[-2:]
    passed[...] = total[...]
    size = 8

    def some(g, carry):
        sums = [lon_product(back[size * g + i], band[size * g + i]) for i in range(size)]
        for i in range(size):
            out[size * g + i] = sums[i]
        return carry

    lax.fori_loop(0, back.shape[0] // size, some, 0)
    place = Place(back.shape[0], en)
    for d in range(place.dirs):
        first = place.border(d)[0] * (back.shape[0] - 4)
        for n in range(4):
            out[first + n] = lon_product(border[d][n], band[first + n])


def final_kernel(centre, band, edge, far, near, exposure, total, out, passed, whole, v_out, out_sems):
    groups = near.shape[0]
    size = 2
    steps = groups // size
    passed[...] = total[...]

    def copy_out(p):
        return chunk_copy(v_out, out, out_sems.at[p], p, 4 * size)

    def lon(g):
        return [(whole, 4 * g + n, lon_edges(centre, edge, far, near, g, 4 * g + n, n)) for n in range(4)]

    def lat(g):
        return [(v_out, 4 * g + n, lat_product(band[4 * g + n], whole[4 * g + n]) * exposure[4 * g + n]) for n in range(4)]

    run_stages(steps, size, [(lon, 0), (lat, 1)], events=[(p + 2, copy_out(p).start) for p in range(steps)])
    for p in range(steps):
        copy_out(p).wait()


def tree_sum(values):
    while len(values) > 1:
        values = [a + b for a, b in zip(values[::2], values[1::2])]
    return values[0]


def ring(size, shift):
    return [(i, (i + shift) % size) for i in range(size)]


def local(flux, exposure, background, observed, psf_radius, band_low, band_high, disp_raw):
    block, rows, width = flux.shape
    bins = disp_raw.shape[0]
    sky, en = lax.axis_size("sky"), lax.axis_size("en")
    shifts = [1] if en == 2 else [1, -1]
    dirs = len(shifts)
    slots = block + REACH * dirs
    parts = min(8, block // 4)

    def tiles(count, dtype=F32):
        return jax.ShapeDtypeStruct((count, rows, width), dtype)

    def edges(count):
        return jax.ShapeDtypeStruct((count // 4, 128, 128), F32)

    def weights(count):
        return jax.ShapeDtypeStruct((count, 128, 256), BF16)

    def scratch(shape):
        return pltpu.VMEM(shape.shape, shape.dtype)

    lanes = jax.ShapeDtypeStruct((1, 128), F32)

    flux, exposure_in, background, observed = [
        pltpu.with_memory_space_constraint(array, pltpu.HBM) for array in (flux, exposure, background, observed)
    ]
    half = block // 2

    def swap_far(edges):
        return lax.ppermute(edges, "sky", [(s, (s + 1 if s % 2 else s - 1) % sky) for s in range(sky)])

    def swap_near(edges):
        return lax.ppermute(edges, "sky", [(s, s ^ 1) for s in range(sky)])

    def neighbours(arrays):
        return [lax.ppermute(array, "en", ring(en, shift)) for array, shift in zip(arrays, shifts)]

    weighted, near, far, *sent = pl.pallas_call(
        functools.partial(pack_kernel, parts, en),
        in_specs=[ANY] * 4,
        out_specs=[VMEM] * (3 + dirs),
        out_shape=[tiles(block), edges(block), edges(block)] + [tiles(2 * REACH)] * dirs,
        scratch_shapes=[
            scratch(tiles(block)), scratch(tiles(block)), pltpu.VMEM((dirs, REACH, rows, width), jnp.int32),
            pltpu.SemaphoreType.DMA((2, parts)), pltpu.SemaphoreType.DMA((dirs, 2)),
        ],
        compiler_params=params(12),
        name="weight_and_pack",
    )(flux, exposure_in, background, observed)
    far, near = swap_far(far), swap_near(near)
    counts = neighbours(sent)

    centre, band, edge, fold, background, observed = pl.pallas_call(
        functools.partial(weights_kernel, en),
        in_specs=[SMEM] * 4 + [VMEM] + [ANY] * 2,
        out_specs=[VMEM] * 3 + [SMEM] + [VMEM] * 2,
        out_shape=[
            tiles(block), weights(block), weights(block), jax.ShapeDtypeStruct((5 * (slots + 4),), F32),
            tiles(block), tiles(block),
        ],
        scratch_shapes=[scratch(tiles(block, jnp.int32)), pltpu.SemaphoreType.DMA((2,))],
        compiler_params=params(6),
        cost_estimate=cost(block, 1, block * 2**15),
        name="weights_and_centre",
    )(psf_radius, band_low, band_high, disp_raw, weighted, background, observed)
    sent = pl.pallas_call(
        functools.partial(blur_kernel, en),
        in_specs=[VMEM] * 5,
        out_specs=[VMEM] * dirs,
        out_shape=[tiles(4)] * dirs,
        compiler_params=params(4),
        cost_estimate=cost(4 * dirs, 2),
        name="blur_border",
    )(centre, band, edge, far, near)
    received = neighbours(sent)
    resid, loss, *folded = pl.pallas_call(
        functools.partial(middle_kernel, en),
        in_specs=[SMEM] + [VMEM] * 7,
        out_specs=[VMEM] * 5,
        out_shape=[tiles(block + 4), jax.ShapeDtypeStruct((8, 128), F32), tiles(block), edges(block), edges(block)],
        scratch_shapes=[scratch(tiles(block)), scratch(tiles(block + 4))],
        compiler_params=params(10),
        cost_estimate=cost(block, 2, block * 2**15),
        name="blur_residual_fold",
    )(fold, centre, band, edge, far, near, background, observed)
    back, near, far = folded
    near, far, total, *border = pl.pallas_call(
        functools.partial(border_kernel, en),
        in_specs=[SMEM] + [VMEM] * (6 + 3 * dirs),
        out_specs=[VMEM] * (3 + dirs),
        out_shape=[edges(block), edges(block), lanes] + [tiles(4)] * dirs,
        scratch_shapes=[scratch(tiles(8)), scratch(tiles(4)), scratch(tiles(4)), scratch(tiles(8))],
        compiler_params=params(4),
        cost_estimate=cost(4 * dirs, 1),
        name="border_residual_fold_loss",
    )(fold, background, observed, resid, loss, near, far, *sent, *received, *counts)

    def partners(value, masks):
        return [lax.ppermute(value, ("sky", "en"), [(i, i ^ mask) for i in range(sky * en)]) for mask in masks]

    far, near = swap_far(far), swap_near(near)
    moved = partners(total, [4 * en * k for k in range(1, sky // 4)])
    centre, total = pl.pallas_call(
        functools.partial(centre_kernel, en),
        in_specs=[VMEM] * (3 + dirs),
        out_specs=[VMEM] * 2,
        out_shape=[tiles(block), lanes],
        compiler_params=params(4),
        cost_estimate=cost(block, 1),
        name="back_centre",
    )(back, band, total, *border)
    total = tree_sum([total] + moved)
    moved = partners(total, [k % en ^ (k // en * 3 * en) for k in range(1, 2 * en)])
    grad, total = pl.pallas_call(
        final_kernel,
        in_specs=[VMEM] * 7,
        out_specs=[ANY, VMEM],
        out_shape=[tiles(block), lanes],
        scratch_shapes=[scratch(tiles(block)), scratch(tiles(block)), pltpu.SemaphoreType.DMA((block // 8,))],
        compiler_params=params(8),
        cost_estimate=cost(block, 2),
        name="back_edges_lat_exposure",
    )(centre, band, edge, far, near, exposure, total)
    total = tree_sum([total] + moved)
    total = total + partners(total, [en])[0]
    return grad, total[0, 0] / F32(rows * width * bins * sky)


def solution(mesh):
    placed = (P("en", None, "sky"),) * 4 + (P(),) * 4
    return jax.shard_map(local, mesh=mesh, in_specs=placed, out_specs=(P("en", None, "sky"), P()), check_vma=False)
```

```python
import functools

import jax
import jax.numpy as jnp
from jax import lax
from jax.experimental import pallas as pl
from jax.experimental.pallas import tpu as pltpu
from jax.sharding import PartitionSpec as P

RMAX = 32
REACH = 2
F32 = jnp.float32
BF16 = jnp.bfloat16
SMEM = pl.BlockSpec(memory_space=pltpu.SMEM)
ANY = pl.BlockSpec(memory_space=pl.ANY)
VMEM = pl.BlockSpec(memory_space=pltpu.VMEM)
HBM = pl.BlockSpec(memory_space=pltpu.HBM)


def split(x):
    hi = x.astype(BF16)
    return hi, (x - hi.astype(F32)).astype(BF16)


def params(mib=56):
    return pltpu.CompilerParams(vmem_limit_bytes=mib * 2**20)


def blocks(count, rows, cols):
    return pl.BlockSpec((count, rows, cols), lambda i: (i, 0, 0))


def chunk_copy(source, target, sem, c, size):
    at = pl.ds(c * size, size)
    return pltpu.make_async_copy(source.at[at], target.at[at], sem)


def run_stages(groups, size, stages, events=(), written_out=False):
    stages = [(*stage, groups)[:3] for stage in stages]
    marks = {0} | {lag for _, lag, _ in stages} | {lag + count for _, lag, count in stages} | {at for at, _ in events}
    marks = sorted(marks)
    for start, stop in zip(marks, marks[1:] + [marks[-1]]):
        for at, event in events:
            if at == start:
                event()
        active = [(n, stage, lag) for n, (stage, lag, count) in enumerate(stages) if lag <= start < lag + count]
        if stop == start or not active:
            continue

        def step(p, carry):
            stores = []
            for _, stage, lag in active:
                for i in range(size):
                    stores += stage((p - lag) * size + i)
            for ref, index, value in stores:
                if index is None:
                    ref[...] += value
                else:
                    ref[index] = value
            return carry

        if written_out:
            for p in range(start, stop):
                step(p, 0)
        else:
            lax.fori_loop(start, stop, step, 0)


def cost(tiles, products, transcendentals=0):
    return pl.CostEstimate(flops=tiles * products * 2 * 128 * 256 * 256, bytes_accessed=tiles * 2**16, transcendentals=transcendentals)


class Place:
    def __init__(self, block, en):
        self.block, self.en = block, en
        self.me = lax.axis_index("en")
        self.dirs = 1 if en == 2 else 2
        self.extra = REACH * self.dirs
        self.slots, self.bins = block + self.extra, block * en
        self.own = jnp.where(self.me == 0, 0, REACH) if en == 2 else REACH
        self.first_bin = self.me * block - self.own

    def above(self, d):
        return jnp.where(self.me == 0, 1, 0) if self.en == 2 else 1 - d

    def sent(self, d, width):
        return self.above(d) * (self.block - width)

    def border(self, d):
        up = self.above(d) if self.en == 2 else d
        return up, up * (self.block + self.own - REACH)

    def clamp(self, g):
        return jnp.clip(g, 0, self.bins - 1)


def lanes_of(shape=(128, 128)):
    return lax.broadcasted_iota(jnp.int32, shape, 1)


def is_odd():
    return lax.axis_index("sky") % 2 == 1


def pack_edges(tiles):
    lane = lanes_of()
    outer = (lane < RMAX) | (lane >= 128 - RMAX)
    early, late = [jnp.where(outer, tiles[n], pltpu.roll(tiles[n + 1], 64, 1)) for n in (0, 2)]
    late = pltpu.roll(late, RMAX, 1)
    mask = ((lane // RMAX) % 2 == 1) != is_odd()
    return jnp.where(mask, early, late), jnp.where(mask, late, early)


LEFT = (3, 1, 0, 2)
RIGHT = (0, 2, 1, 3)


def edge_tile(near, far, n):
    lane = lanes_of()
    from_left = lane < RMAX * RIGHT[n] if LEFT[n] < RIGHT[n] else lane >= RMAX * LEFT[n]
    return jnp.where(from_left != is_odd(), far, near)


def twice(x):
    return jnp.concatenate([x, x], axis=0)


def lon_product(tile, weights):
    out = jnp.dot(jnp.concatenate(split(tile), axis=1), twice(weights), preferred_element_type=F32)
    return out[:, :128] + out[:, 128:]


def lat_product(weights, tile):
    out = jnp.dot(weights, twice(jnp.concatenate(split(tile), axis=1)), preferred_element_type=F32)
    return out[:, :128] + out[:, 128:]


def profile(radius, column):
    wide = jnp.full((1, 128), radius, jnp.int32).astype(F32)
    reach = wide * wide
    factor = -2.0 / reach
    lane = lax.broadcasted_iota(jnp.int32, (1, 128), 1)
    square = (lane * lane).astype(F32)
    values = jnp.where(square <= reach, jnp.exp(square * factor), 0.0)
    norm = 2.0 * jnp.sum(values, axis=1, keepdims=True) - 1.0
    root = jnp.sqrt(jnp.full((1, 128), column, F32))[:, :1]
    return factor[:, :1], 1.0 / (norm * root), reach[:, :1]


def taper_values(diff, ok, factor, scale, reach):
    square = diff * diff
    return jnp.where((square <= reach) & ok, jnp.exp(square * factor) * scale, 0.0)


def pack_kernel(parts, en, flux, exposure, background, observed, weighted, near, far, *rest):
    place = Place(flux.shape[0], en)
    dirs, block = place.dirs, place.block
    sent, (v_flux, v_exposure, v_observed, sems, near_sems) = rest[:dirs], rest[dirs:]
    chunk = block // parts

    def arrivals(c):
        return [chunk_copy(a, b, sems.at[n, c], c, chunk) for n, (a, b) in enumerate(((flux, v_flux), (exposure, v_exposure)))]

    def near_arrivals(d):
        at = pl.ds(place.sent(d, REACH), REACH)
        return [
            pltpu.make_async_copy(background.at[at], sent[d].at[pl.ds(0, REACH)], near_sems.at[d, 0]),
            pltpu.make_async_copy(observed.at[at], v_observed.at[d], near_sems.at[d, 1]),
        ]

    for c in range(parts):
        for copy in arrivals(c):
            copy.start()
    for d in range(dirs):
        for copy in near_arrivals(d):
            copy.start()

    def some(g, carry):
        tiles = [v_flux[4 * g + i] * v_exposure[4 * g + i] for i in range(4)]
        packed = pack_edges(tiles)
        for i in range(4):
            weighted[4 * g + i] = tiles[i]
        near[g], far[g] = packed
        return carry

    for c in range(parts):
        for copy in arrivals(c):
            copy.wait()
        lax.fori_loop(c * chunk // 4, (c + 1) * chunk // 4, some, 0)
    for d in range(dirs):
        for copy in near_arrivals(d):
            copy.wait()
        for k in range(REACH):
            sent[d][REACH + k] = v_observed[d, k].astype(F32)


def weights_kernel(en, radius, low, high, disp, weighted, background, observed,
                   centre, band, edge, fold, held_background, counts, v_observed, sems):
    fetches = [
        pltpu.make_async_copy(background, held_background, sems.at[0]),
        pltpu.make_async_copy(observed, v_observed, sems.at[1]),
    ]
    for fetch in fetches:
        fetch.start()
    block = weighted.shape[0]
    place = Place(block, en)
    row = lax.broadcasted_iota(jnp.int32, (128, 128), 0)
    col = lax.broadcasted_iota(jnp.int32, (128, 128), 1)
    near = (row - col).astype(F32)
    always = row >= 0
    beside = []
    for n in range(4):
        shift = jnp.where(row // RMAX == LEFT[n], -RMAX - RMAX * LEFT[n], 128 - RMAX * RIGHT[n])
        held = (row // RMAX == LEFT[n]) | (row // RMAX == RIGHT[n])
        beside.append(((row + shift - col).astype(F32), held))

    def weight(i, j):
        at, to = place.clamp(i), place.clamp(j)
        inside = (i == at) & (j == to) & (low[at] <= j - i) & (j - i <= high[at])
        return jnp.where(inside, disp[at, to], 0.0)

    def fold_row(g):
        for o in range(-REACH, REACH + 1):
            fold[5 * (g - place.first_bin + REACH) + o + REACH] = weight(g, g + o)

    def make(g, n):
        fold_row(g)
        column = weight(g, g)
        for o in (-2, -1, 1, 2):
            column = column + weight(g - o, g)
        numbers = profile(radius[place.clamp(g)], jnp.where(column > 0.0, column, 1.0))
        return tuple(
            jnp.concatenate(split(taper_values(diff, ok, *numbers)), axis=1) for diff, ok in ((near, always), beside[n])
        )

    for s in (0, 1, place.slots + 2, place.slots + 3):
        for o in range(5):
            fold[5 * s + o] = 0.0

    def some(g):
        made = [make(place.me * block + 4 * g + n, n) for n in range(4)]
        return [(band, 4 * g + n, made[n][0]) for n in range(4)] + [(edge, 4 * g + n, made[n][1]) for n in range(4)]

    def lon(g):
        return [(centre, 4 * g + n, lon_product(weighted[4 * g + n], band[4 * g + n])) for n in range(4)]

    run_stages(block // 4, 1, [(some, 0), (lon, 1)])
    for d in range(place.dirs):
        up, slot = place.border(d)
        for k in range(REACH):
            fold_row(place.first_bin + slot + up * REACH + k)
    for fetch in fetches:
        fetch.wait()

    def convert(g):
        return [(counts, 4 * g + n, v_observed[4 * g + n].astype(F32)) for n in range(4)]

    run_stages(block // 4, 1, [(convert, 0)])


def lon_edges(centre, edge, far, near, g, at, n):
    return centre[at] + lon_product(edge_tile(near[g], far[g], n), edge[at])


def blur_kernel(en, centre, band, edge, far, near, *blurred):
    place = Place(centre.shape[0], en)
    for d in range(place.dirs):
        start = place.sent(d, 4)
        g = lax.div(start, 4) if en == 2 else start // 4
        sums = [lon_edges(centre, edge, far, near, g, start + n, n) for n in range(4)]
        sums = [lat_product(band[start + n], sums[n]) for n in range(4)]
        for n in range(4):
            blurred[d][n] = sums[n]


def inverse(x):
    first = pl.reciprocal(x, approx=True)
    return first * (2.0 - x * first)


ROWS = [pl.ds(32 * r, 32) for r in range(4)]


def loss_terms(mu, counts):
    return (mu - counts * jnp.log(mu)).reshape(-1, 8, 128).sum(0)


def fold_one(fold, row, resid, at):
    total = None
    for o in range(5):
        term = fold[5 * (row - o) + o] * resid[at - o]
        total = term if total is None else total + term
    return total


def middle_kernel(en, fold, centre, band, edge, far, near, background, observed, resid, loss, back, near_out, far_out, whole, blurred):
    block = centre.shape[0]
    place = Place(block, en)
    own = place.own
    zero = jnp.zeros((128, 128), F32)
    for s in (0, 1, block + 2, block + 3):
        blurred[s] = zero
        resid[s] = zero
    loss[...] = jnp.zeros((8, 128), F32)
    inside = (own, own + block - REACH) if en == 2 else (REACH, block - REACH)

    def lon(g):
        return [(whole, 4 * g + n, lon_edges(centre, edge, far, near, g, 4 * g + n, n)) for n in range(4)]

    def lat(g):
        return [(blurred, 4 * g + n + 2, lat_product(band[4 * g + n], whole[4 * g + n])) for n in range(4)]

    def residual(g):
        sums = None
        for rows in ROWS:
            window = [blurred[4 * g + k, rows] for k in range(8)]
            for n in range(4):
                b = 4 * g + n
                mu = background[b, rows]
                for o in range(5):
                    mu = mu + fold[5 * (b + own + 2) + o] * window[n + o]
                counts = observed[b, rows]
                resid[b + 2, rows] = 1.0 - counts * inverse(mu)
                inner = (b >= inside[0]) & (b < inside[1])
                terms = jnp.where(inner, loss_terms(mu, counts), 0.0)
                sums = terms if sums is None else sums + terms
        return [(loss, None, sums)]

    def fold_back(g):
        tiles = [[] for _ in range(4)]
        for rows in ROWS:
            window = [resid[4 * g + k, rows] for k in range(8)]
            for n in range(4):
                total = None
                for o in range(5):
                    term = fold[5 * (4 * g + n + own + 4 - o) + o] * window[n + 4 - o]
                    total = term if total is None else total + term
                back[4 * g + n, rows] = total
                tiles[n].append(total)
        near_out[g], far_out[g] = pack_edges([jnp.concatenate(parts, axis=0) for parts in tiles])
        return []

    run_stages(block // 8, 2, [(fold_back, 5), (residual, 3), (lon, 0), (lat, 1)], written_out=True)


def border_kernel(en, fold, background, observed, resid, loss, near_in, far_in, *rest):
    block = background.shape[0]
    place = Place(block, en)
    dirs, own = place.dirs, place.own
    sent, received, counts = [rest[n * dirs:(n + 1) * dirs] for n in range(3)]
    near, far, total = rest[3 * dirs:3 * dirs + 3]
    back, (blurred, ground, seen, rows) = rest[3 * dirs + 3:4 * dirs + 3], rest[4 * dirs + 3:]
    sums = loss[...]
    near[...], far[...] = near_in[...], far_in[...]
    for d in range(dirs):
        up, slot = place.border(d)
        mine, theirs = 4 * (1 - up), 4 * up
        for k in range(4):
            blurred[mine + k] = sent[dirs - 1 - d][k]
            blurred[theirs + k] = received[d][k]
            rows[mine + k] = resid[up * (block - 8) + 4 + k]
        first = up * (block - REACH)
        for k in range(REACH):
            ground[mine // 2 + k] = background[first + k]
            seen[mine // 2 + k] = observed[first + k]
            ground[theirs // 2 + k] = counts[d][k]
            seen[theirs // 2 + k] = counts[d][REACH + k]
        for j in range(2 * REACH):
            mu = ground[j]
            for o in range(5):
                mu = mu + fold[5 * (slot + j + 2) + o] * blurred[j + o]
            rows[theirs + j] = 1.0 - seen[j] * inverse(mu)
            is_mine = (mine // 2 <= j) & (j < mine // 2 + REACH)
            sums = sums + jnp.where(is_mine, loss_terms(mu, seen[j]), 0.0)
        first = up * (block - 4)
        tiles = [fold_one(fold, first + n + own + 4, rows, n + 4) for n in range(4)]
        g = up * (block // 4 - 1)
        near[g], far[g] = pack_edges(tiles)
        for n in range(4):
            back[d][n] = tiles[n]
    total[...] = jnp.full((1, 128), jnp.sum(sums), F32)


def centre_kernel(en, back, band, total, *rest):
    border, (out, passed) = rest[:-2], rest[-2:]
    passed[...] = total[...]
    size = 8

    def some(g, carry):
        sums = [lon_product(back[size * g + i], band[size * g + i]) for i in range(size)]
        for i in range(size):
            out[size * g + i] = sums[i]
        return carry

    lax.fori_loop(0, back.shape[0] // size, some, 0)
    place = Place(back.shape[0], en)
    for d in range(place.dirs):
        first = place.border(d)[0] * (back.shape[0] - 4)
        for n in range(4):
            out[first + n] = lon_product(border[d][n], band[first + n])


def final_kernel(centre, band, edge, far, near, exposure, total, out, passed, whole, v_out, out_sems):
    groups = near.shape[0]
    size = 2
    steps = groups // size
    passed[...] = total[...]

    def copy_out(p):
        return chunk_copy(v_out, out, out_sems.at[p], p, 4 * size)

    def lon(g):
        return [(whole, 4 * g + n, lon_edges(centre, edge, far, near, g, 4 * g + n, n)) for n in range(4)]

    def lat(g):
        return [(v_out, 4 * g + n, lat_product(band[4 * g + n], whole[4 * g + n]) * exposure[4 * g + n]) for n in range(4)]

    run_stages(steps, size, [(lon, 0), (lat, 1)], events=[(p + 2, copy_out(p).start) for p in range(steps)], written_out=True)
    for p in range(steps):
        copy_out(p).wait()


def tree_sum(values):
    while len(values) > 1:
        values = [a + b for a, b in zip(values[::2], values[1::2])]
    return values[0]


def ring(size, shift):
    return [(i, (i + shift) % size) for i in range(size)]


def local(flux, exposure, background, observed, psf_radius, band_low, band_high, disp_raw):
    block, rows, width = flux.shape
    bins = disp_raw.shape[0]
    sky, en = lax.axis_size("sky"), lax.axis_size("en")
    shifts = [1] if en == 2 else [1, -1]
    dirs = len(shifts)
    slots = block + REACH * dirs
    parts = min(8, block // 4)

    def tiles(count, dtype=F32):
        return jax.ShapeDtypeStruct((count, rows, width), dtype)

    def edges(count):
        return jax.ShapeDtypeStruct((count // 4, 128, 128), F32)

    def weights(count):
        return jax.ShapeDtypeStruct((count, 128, 256), BF16)

    def scratch(shape):
        return pltpu.VMEM(shape.shape, shape.dtype)

    lanes = jax.ShapeDtypeStruct((1, 128), F32)

    flux, exposure_in, background, observed = [
        pltpu.with_memory_space_constraint(array, pltpu.HBM) for array in (flux, exposure, background, observed)
    ]
    half = block // 2

    def swap_far(edges):
        return lax.ppermute(edges, "sky", [(s, (s + 1 if s % 2 else s - 1) % sky) for s in range(sky)])

    def swap_near(edges):
        return lax.ppermute(edges, "sky", [(s, s ^ 1) for s in range(sky)])

    def neighbours(arrays):
        return [lax.ppermute(array, "en", ring(en, shift)) for array, shift in zip(arrays, shifts)]

    weighted, near, far, *sent = pl.pallas_call(
        functools.partial(pack_kernel, parts, en),
        in_specs=[ANY] * 4,
        out_specs=[VMEM] * (3 + dirs),
        out_shape=[tiles(block), edges(block), edges(block)] + [tiles(2 * REACH)] * dirs,
        scratch_shapes=[
            scratch(tiles(block)), scratch(tiles(block)), pltpu.VMEM((dirs, REACH, rows, width), jnp.int32),
            pltpu.SemaphoreType.DMA((2, parts)), pltpu.SemaphoreType.DMA((dirs, 2)),
        ],
        compiler_params=params(12),
        name="weight_and_pack",
    )(flux, exposure_in, background, observed)
    far, near = swap_far(far), swap_near(near)
    counts = neighbours(sent)

    centre, band, edge, fold, background, observed = pl.pallas_call(
        functools.partial(weights_kernel, en),
        in_specs=[SMEM] * 4 + [VMEM] + [ANY] * 2,
        out_specs=[VMEM] * 3 + [SMEM] + [VMEM] * 2,
        out_shape=[
            tiles(block), weights(block), weights(block), jax.ShapeDtypeStruct((5 * (slots + 4),), F32),
            tiles(block), tiles(block),
        ],
        scratch_shapes=[scratch(tiles(block, jnp.int32)), pltpu.SemaphoreType.DMA((2,))],
        compiler_params=params(6),
        cost_estimate=cost(block, 1, block * 2**15),
        name="weights_and_centre",
    )(psf_radius, band_low, band_high, disp_raw, weighted, background, observed)
    sent = pl.pallas_call(
        functools.partial(blur_kernel, en),
        in_specs=[VMEM] * 5,
        out_specs=[VMEM] * dirs,
        out_shape=[tiles(4)] * dirs,
        compiler_params=params(4),
        cost_estimate=cost(4 * dirs, 2),
        name="blur_border",
    )(centre, band, edge, far, near)
    received = neighbours(sent)
    resid, loss, *folded = pl.pallas_call(
        functools.partial(middle_kernel, en),
        in_specs=[SMEM] + [VMEM] * 7,
        out_specs=[VMEM] * 5,
        out_shape=[tiles(block + 4), jax.ShapeDtypeStruct((8, 128), F32), tiles(block), edges(block), edges(block)],
        scratch_shapes=[scratch(tiles(block)), scratch(tiles(block + 4))],
        compiler_params=params(10),
        cost_estimate=cost(block, 2, block * 2**15),
        name="blur_residual_fold",
    )(fold, centre, band, edge, far, near, background, observed)
    back, near, far = folded
    near, far, total, *border = pl.pallas_call(
        functools.partial(border_kernel, en),
        in_specs=[SMEM] + [VMEM] * (6 + 3 * dirs),
        out_specs=[VMEM] * (3 + dirs),
        out_shape=[edges(block), edges(block), lanes] + [tiles(4)] * dirs,
        scratch_shapes=[scratch(tiles(8)), scratch(tiles(4)), scratch(tiles(4)), scratch(tiles(8))],
        compiler_params=params(4),
        cost_estimate=cost(4 * dirs, 1),
        name="border_residual_fold_loss",
    )(fold, background, observed, resid, loss, near, far, *sent, *received, *counts)

    def partners(value, masks):
        return [lax.ppermute(value, ("sky", "en"), [(i, i ^ mask) for i in range(sky * en)]) for mask in masks]

    far, near = swap_far(far), swap_near(near)
    moved = partners(total, [4 * en * k for k in range(1, sky // 4)])
    centre, total = pl.pallas_call(
        functools.partial(centre_kernel, en),
        in_specs=[VMEM] * (3 + dirs),
        out_specs=[VMEM] * 2,
        out_shape=[tiles(block), lanes],
        compiler_params=params(4),
        cost_estimate=cost(block, 1),
        name="back_centre",
    )(back, band, total, *border)
    total = tree_sum([total] + moved)
    moved = partners(total, [k % en ^ (k // en * 3 * en) for k in range(1, 2 * en)])
    grad, total = pl.pallas_call(
        final_kernel,
        in_specs=[VMEM] * 7,
        out_specs=[ANY, VMEM],
        out_shape=[tiles(block), lanes],
        scratch_shapes=[scratch(tiles(block)), scratch(tiles(block)), pltpu.SemaphoreType.DMA((block // 8,))],
        compiler_params=params(8),
        cost_estimate=cost(block, 2),
        name="back_edges_lat_exposure",
    )(centre, band, edge, far, near, exposure, total)
    total = tree_sum([total] + moved)
    total = total + partners(total, [en])[0]
    return grad, total[0, 0] / F32(rows * width * bins * sky)


def solution(mesh):
    placed = (P("en", None, "sky"),) * 4 + (P(),) * 4
    return jax.shard_map(local, mesh=mesh, in_specs=placed, out_specs=(P("en", None, "sky"), P()), check_vma=False)
```

```python
import functools

import jax
import jax.numpy as jnp
from jax import lax
from jax.experimental import pallas as pl
from jax.experimental.pallas import tpu as pltpu
from jax.sharding import PartitionSpec as P

RMAX = 32
REACH = 2
F32 = jnp.float32
BF16 = jnp.bfloat16
SMEM = pl.BlockSpec(memory_space=pltpu.SMEM)
ANY = pl.BlockSpec(memory_space=pl.ANY)
VMEM = pl.BlockSpec(memory_space=pltpu.VMEM)
HBM = pl.BlockSpec(memory_space=pltpu.HBM)


def split(x):
    hi = x.astype(BF16)
    return hi, (x - hi.astype(F32)).astype(BF16)


def params(mib=56):
    return pltpu.CompilerParams(vmem_limit_bytes=mib * 2**20)


def blocks(count, rows, cols):
    return pl.BlockSpec((count, rows, cols), lambda i: (i, 0, 0))


def chunk_copy(source, target, sem, c, size):
    at = pl.ds(c * size, size)
    return pltpu.make_async_copy(source.at[at], target.at[at], sem)


def run_stages(groups, size, stages, events=(), written_out=False):
    stages = [(*stage, groups)[:3] for stage in stages]
    marks = {0} | {lag for _, lag, _ in stages} | {lag + count for _, lag, count in stages} | {at for at, _ in events}
    marks = sorted(marks)
    for start, stop in zip(marks, marks[1:] + [marks[-1]]):
        for at, event in events:
            if at == start:
                event()
        active = [(n, stage, lag) for n, (stage, lag, count) in enumerate(stages) if lag <= start < lag + count]
        if stop == start or not active:
            continue

        def step(p, carry):
            stores = []
            for _, stage, lag in active:
                for i in range(size):
                    stores += stage((p - lag) * size + i)
            for ref, index, value in stores:
                if index is None:
                    ref[...] += value
                else:
                    ref[index] = value
            return carry

        if written_out:
            for p in range(start, stop):
                step(p, 0)
        else:
            lax.fori_loop(start, stop, step, 0)


def cost(tiles, products, transcendentals=0):
    return pl.CostEstimate(flops=tiles * products * 2 * 128 * 256 * 256, bytes_accessed=tiles * 2**16, transcendentals=transcendentals)


class Place:
    def __init__(self, block, en):
        self.block, self.en = block, en
        self.me = lax.axis_index("en")
        self.dirs = 1 if en == 2 else 2
        self.extra = REACH * self.dirs
        self.slots, self.bins = block + self.extra, block * en
        self.own = jnp.where(self.me == 0, 0, REACH) if en == 2 else REACH
        self.first_bin = self.me * block - self.own

    def above(self, d):
        return jnp.where(self.me == 0, 1, 0) if self.en == 2 else 1 - d

    def sent(self, d, width):
        return self.above(d) * (self.block - width)

    def border(self, d):
        up = self.above(d) if self.en == 2 else d
        return up, up * (self.block + self.own - REACH)

    def clamp(self, g):
        return jnp.clip(g, 0, self.bins - 1)


def lanes_of(shape=(128, 128)):
    return lax.broadcasted_iota(jnp.int32, shape, 1)


def is_odd():
    return lax.axis_index("sky") % 2 == 1


def pack_edges(tiles):
    lane = lanes_of()
    outer = (lane < RMAX) | (lane >= 128 - RMAX)
    early, late = [jnp.where(outer, tiles[n], pltpu.roll(tiles[n + 1], 64, 1)) for n in (0, 2)]
    late = pltpu.roll(late, RMAX, 1)
    mask = ((lane // RMAX) % 2 == 1) != is_odd()
    return jnp.where(mask, early, late), jnp.where(mask, late, early)


LEFT = (3, 1, 0, 2)
RIGHT = (0, 2, 1, 3)


def edge_tile(near, far, n):
    lane = lanes_of()
    from_left = lane < RMAX * RIGHT[n] if LEFT[n] < RIGHT[n] else lane >= RMAX * LEFT[n]
    return jnp.where(from_left != is_odd(), far, near)


def twice(x):
    return jnp.concatenate([x, x], axis=0)


def lon_product(tile, weights):
    out = jnp.dot(jnp.concatenate(split(tile), axis=1), twice(weights), preferred_element_type=F32)
    return out[:, :128] + out[:, 128:]


def lat_product(weights, tile):
    out = jnp.dot(weights, twice(jnp.concatenate(split(tile), axis=1)), preferred_element_type=F32)
    return out[:, :128] + out[:, 128:]


def profile(radius, column):
    wide = jnp.full((1, 128), radius, jnp.int32).astype(F32)
    reach = wide * wide
    factor = -2.0 / reach
    lane = lax.broadcasted_iota(jnp.int32, (1, 128), 1)
    square = (lane * lane).astype(F32)
    values = jnp.where(square <= reach, jnp.exp(square * factor), 0.0)
    norm = 2.0 * jnp.sum(values, axis=1, keepdims=True) - 1.0
    root = jnp.sqrt(jnp.full((1, 128), column, F32))[:, :1]
    return factor[:, :1], 1.0 / (norm * root), reach[:, :1]


def taper_values(diff, ok, factor, scale, reach):
    square = diff * diff
    return jnp.where((square <= reach) & ok, jnp.exp(square * factor) * scale, 0.0)


def pack_kernel(parts, en, flux, exposure, background, observed, weighted, near, far, *rest):
    place = Place(flux.shape[0], en)
    dirs, block = place.dirs, place.block
    sent, (v_flux, v_exposure, v_observed, sems, near_sems) = rest[:dirs], rest[dirs:]
    chunk = block // parts

    def arrivals(c):
        return [chunk_copy(a, b, sems.at[n, c], c, chunk) for n, (a, b) in enumerate(((flux, v_flux), (exposure, v_exposure)))]

    def near_arrivals(d):
        at = pl.ds(place.sent(d, REACH), REACH)
        return [
            pltpu.make_async_copy(background.at[at], sent[d].at[pl.ds(0, REACH)], near_sems.at[d, 0]),
            pltpu.make_async_copy(observed.at[at], v_observed.at[d], near_sems.at[d, 1]),
        ]

    for c in range(parts):
        for copy in arrivals(c):
            copy.start()
    for d in range(dirs):
        for copy in near_arrivals(d):
            copy.start()

    def some(g, carry):
        tiles = [v_flux[4 * g + i] * v_exposure[4 * g + i] for i in range(4)]
        packed = pack_edges(tiles)
        for i in range(4):
            weighted[4 * g + i] = tiles[i]
        near[g], far[g] = packed
        return carry

    for c in range(parts):
        for copy in arrivals(c):
            copy.wait()
        lax.fori_loop(c * chunk // 4, (c + 1) * chunk // 4, some, 0)
    for d in range(dirs):
        for copy in near_arrivals(d):
            copy.wait()
        for k in range(REACH):
            sent[d][REACH + k] = v_observed[d, k].astype(F32)


def weights_kernel(en, radius, low, high, disp, weighted, background, observed,
                   centre, band, edge, fold, held_background, counts, v_observed, sems):
    fetches = [
        pltpu.make_async_copy(background, held_background, sems.at[0]),
        pltpu.make_async_copy(observed, v_observed, sems.at[1]),
    ]
    for fetch in fetches:
        fetch.start()
    block = weighted.shape[0]
    place = Place(block, en)
    row = lax.broadcasted_iota(jnp.int32, (128, 128), 0)
    col = lax.broadcasted_iota(jnp.int32, (128, 128), 1)
    near = (row - col).astype(F32)
    always = row >= 0
    beside = []
    for n in range(4):
        shift = jnp.where(row // RMAX == LEFT[n], -RMAX - RMAX * LEFT[n], 128 - RMAX * RIGHT[n])
        held = (row // RMAX == LEFT[n]) | (row // RMAX == RIGHT[n])
        beside.append(((row + shift - col).astype(F32), held))

    def weight(i, j):
        at, to = place.clamp(i), place.clamp(j)
        inside = (i == at) & (j == to) & (low[at] <= j - i) & (j - i <= high[at])
        return jnp.where(inside, disp[at, to], 0.0)

    def fold_row(g):
        for o in range(-REACH, REACH + 1):
            fold[5 * (g - place.first_bin + REACH) + o + REACH] = weight(g, g + o)

    def make(g, n):
        fold_row(g)
        column = weight(g, g)
        for o in (-2, -1, 1, 2):
            column = column + weight(g - o, g)
        numbers = profile(radius[place.clamp(g)], jnp.where(column > 0.0, column, 1.0))
        return tuple(
            jnp.concatenate(split(taper_values(diff, ok, *numbers)), axis=1) for diff, ok in ((near, always), beside[n])
        )

    for s in (0, 1, place.slots + 2, place.slots + 3):
        for o in range(5):
            fold[5 * s + o] = 0.0

    def some(g):
        made = [make(place.me * block + 4 * g + n, n) for n in range(4)]
        return [(band, 4 * g + n, made[n][0]) for n in range(4)] + [(edge, 4 * g + n, made[n][1]) for n in range(4)]

    def lon(g):
        return [(centre, 4 * g + n, lon_product(weighted[4 * g + n], band[4 * g + n])) for n in range(4)]

    run_stages(block // 4, 1, [(some, 0), (lon, 1)])
    for d in range(place.dirs):
        up, slot = place.border(d)
        for k in range(REACH):
            fold_row(place.first_bin + slot + up * REACH + k)
    for fetch in fetches:
        fetch.wait()

    def convert(g):
        return [(counts, 4 * g + n, v_observed[4 * g + n].astype(F32)) for n in range(4)]

    run_stages(block // 4, 1, [(convert, 0)])


def lon_edges(centre, edge, far, near, g, at, n):
    return centre[at] + lon_product(edge_tile(near[g], far[g], n), edge[at])


def blur_kernel(en, centre, band, edge, far, near, *blurred):
    place = Place(centre.shape[0], en)
    for d in range(place.dirs):
        start = place.sent(d, 4)
        g = lax.div(start, 4) if en == 2 else start // 4
        sums = [lon_edges(centre, edge, far, near, g, start + n, n) for n in range(4)]
        sums = [lat_product(band[start + n], sums[n]) for n in range(4)]
        for n in range(4):
            blurred[d][n] = sums[n]


def inverse(x):
    first = pl.reciprocal(x, approx=True)
    return first * (2.0 - x * first)


ROWS = [pl.ds(32 * r, 32) for r in range(4)]


def loss_terms(mu, counts):
    return (mu - counts * jnp.log(mu)).reshape(-1, 8, 128).sum(0)


def fold_one(fold, row, resid, at):
    total = None
    for o in range(5):
        term = fold[5 * (row - o) + o] * resid[at - o]
        total = term if total is None else total + term
    return total


def middle_kernel(en, fold, centre, band, edge, far, near, background, observed, resid, loss, back, near_out, far_out, whole, blurred):
    block = centre.shape[0]
    place = Place(block, en)
    own = place.own
    zero = jnp.zeros((128, 128), F32)
    for s in (0, 1, block + 2, block + 3):
        blurred[s] = zero
        resid[s] = zero
    loss[...] = jnp.zeros((8, 128), F32)
    inside = (own, own + block - REACH) if en == 2 else (REACH, block - REACH)

    def lon(g):
        return [(whole, 4 * g + n, lon_edges(centre, edge, far, near, g, 4 * g + n, n)) for n in range(4)]

    def lat(g):
        return [(blurred, 4 * g + n + 2, lat_product(band[4 * g + n], whole[4 * g + n])) for n in range(4)]

    def residual(g):
        sums = None
        for rows in ROWS:
            window = [blurred[4 * g + k, rows] for k in range(8)]
            for n in range(4):
                b = 4 * g + n
                mu = background[b, rows]
                for o in range(5):
                    mu = mu + fold[5 * (b + own + 2) + o] * window[n + o]
                counts = observed[b, rows]
                resid[b + 2, rows] = 1.0 - counts * inverse(mu)
                inner = (b >= inside[0]) & (b < inside[1])
                terms = jnp.where(inner, loss_terms(mu, counts), 0.0)
                sums = terms if sums is None else sums + terms
        return [(loss, None, sums)]

    def fold_back(g):
        tiles = [[] for _ in range(4)]
        for rows in ROWS:
            window = [resid[4 * g + k, rows] for k in range(8)]
            for n in range(4):
                total = None
                for o in range(5):
                    term = fold[5 * (4 * g + n + own + 4 - o) + o] * window[n + 4 - o]
                    total = term if total is None else total + term
                back[4 * g + n, rows] = total
                tiles[n].append(total)
        near_out[g], far_out[g] = pack_edges([jnp.concatenate(parts, axis=0) for parts in tiles])
        return []

    run_stages(block // 8, 2, [(fold_back, 5), (residual, 3), (lon, 0), (lat, 1)], written_out=True)


def border_kernel(en, fold, background, observed, resid, loss, near_in, far_in, *rest):
    block = background.shape[0]
    place = Place(block, en)
    dirs, own = place.dirs, place.own
    sent, received, counts = [rest[n * dirs:(n + 1) * dirs] for n in range(3)]
    near, far, total = rest[3 * dirs:3 * dirs + 3]
    back, (blurred, ground, seen, rows) = rest[3 * dirs + 3:4 * dirs + 3], rest[4 * dirs + 3:]
    sums = loss[...]
    near[...], far[...] = near_in[...], far_in[...]
    for d in range(dirs):
        up, slot = place.border(d)
        mine, theirs = 4 * (1 - up), 4 * up
        for k in range(4):
            blurred[mine + k] = sent[dirs - 1 - d][k]
            blurred[theirs + k] = received[d][k]
            rows[mine + k] = resid[up * (block - 8) + 4 + k]
        first = up * (block - REACH)
        for k in range(REACH):
            ground[mine // 2 + k] = background[first + k]
            seen[mine // 2 + k] = observed[first + k]
            ground[theirs // 2 + k] = counts[d][k]
            seen[theirs // 2 + k] = counts[d][REACH + k]
        for j in range(2 * REACH):
            mu = ground[j]
            for o in range(5):
                mu = mu + fold[5 * (slot + j + 2) + o] * blurred[j + o]
            rows[theirs + j] = 1.0 - seen[j] * inverse(mu)
            is_mine = (mine // 2 <= j) & (j < mine // 2 + REACH)
            sums = sums + jnp.where(is_mine, loss_terms(mu, seen[j]), 0.0)
        first = up * (block - 4)
        tiles = [fold_one(fold, first + n + own + 4, rows, n + 4) for n in range(4)]
        g = up * (block // 4 - 1)
        near[g], far[g] = pack_edges(tiles)
        for n in range(4):
            back[d][n] = tiles[n]
    total[...] = jnp.full((1, 128), jnp.sum(sums), F32)


def centre_kernel(en, back, band, total, *rest):
    border, (out, passed) = rest[:-2], rest[-2:]
    passed[...] = total[...]
    size = 8

    def some(g, carry):
        sums = [lon_product(back[size * g + i], band[size * g + i]) for i in range(size)]
        for i in range(size):
            out[size * g + i] = sums[i]
        return carry

    lax.fori_loop(0, back.shape[0] // size, some, 0)
    place = Place(back.shape[0], en)
    for d in range(place.dirs):
        first = place.border(d)[0] * (back.shape[0] - 4)
        for n in range(4):
            out[first + n] = lon_product(border[d][n], band[first + n])


def final_kernel(start, count, centre, band, edge, far, near, exposure, total, *rest):
    out, passed, whole, v_out, out_sems = rest[1 if start else 0:]
    size = 2 if count % 2 == 0 else 1
    steps = count // size
    passed[...] = total[...]

    def copy_out(p):
        bins = 4 * size
        return pltpu.make_async_copy(v_out.at[pl.ds(p * bins, bins)], out.at[pl.ds(4 * start + p * bins, bins)], out_sems.at[p])

    def lon(g):
        return [(whole, 4 * g + n, lon_edges(centre, edge, far, near, start + g, 4 * (start + g) + n, n)) for n in range(4)]

    def lat(g):
        stores = []
        for n in range(4):
            b = 4 * (start + g) + n
            stores.append((v_out, 4 * g + n, lat_product(band[b], whole[4 * g + n]) * exposure[b]))
        return stores

    run_stages(steps, size, [(lon, 0), (lat, 1)], events=[(p + 2, copy_out(p).start) for p in range(steps)], written_out=True)
    for p in range(steps):
        copy_out(p).wait()


def tree_sum(values):
    while len(values) > 1:
        values = [a + b for a, b in zip(values[::2], values[1::2])]
    return values[0]


def ring(size, shift):
    return [(i, (i + shift) % size) for i in range(size)]


def local(flux, exposure, background, observed, psf_radius, band_low, band_high, disp_raw):
    block, rows, width = flux.shape
    bins = disp_raw.shape[0]
    sky, en = lax.axis_size("sky"), lax.axis_size("en")
    shifts = [1] if en == 2 else [1, -1]
    dirs = len(shifts)
    slots = block + REACH * dirs
    parts = min(8, block // 4)

    def tiles(count, dtype=F32):
        return jax.ShapeDtypeStruct((count, rows, width), dtype)

    def edges(count):
        return jax.ShapeDtypeStruct((count // 4, 128, 128), F32)

    def weights(count):
        return jax.ShapeDtypeStruct((count, 128, 256), BF16)

    def scratch(shape):
        return pltpu.VMEM(shape.shape, shape.dtype)

    lanes = jax.ShapeDtypeStruct((1, 128), F32)

    flux, exposure_in, background, observed = [
        pltpu.with_memory_space_constraint(array, pltpu.HBM) for array in (flux, exposure, background, observed)
    ]
    half = block // 2

    def swap_far(edges):
        return lax.ppermute(edges, "sky", [(s, (s + 1 if s % 2 else s - 1) % sky) for s in range(sky)])

    def swap_near(edges):
        return lax.ppermute(edges, "sky", [(s, s ^ 1) for s in range(sky)])

    def neighbours(arrays):
        return [lax.ppermute(array, "en", ring(en, shift)) for array, shift in zip(arrays, shifts)]

    weighted, near, far, *sent = pl.pallas_call(
        functools.partial(pack_kernel, parts, en),
        in_specs=[ANY] * 4,
        out_specs=[VMEM] * (3 + dirs),
        out_shape=[tiles(block), edges(block), edges(block)] + [tiles(2 * REACH)] * dirs,
        scratch_shapes=[
            scratch(tiles(block)), scratch(tiles(block)), pltpu.VMEM((dirs, REACH, rows, width), jnp.int32),
            pltpu.SemaphoreType.DMA((2, parts)), pltpu.SemaphoreType.DMA((dirs, 2)),
        ],
        compiler_params=params(12),
        name="weight_and_pack",
    )(flux, exposure_in, background, observed)
    far, near = swap_far(far), swap_near(near)
    counts = neighbours(sent)

    centre, band, edge, fold, background, observed = pl.pallas_call(
        functools.partial(weights_kernel, en),
        in_specs=[SMEM] * 4 + [VMEM] + [ANY] * 2,
        out_specs=[VMEM] * 3 + [SMEM] + [VMEM] * 2,
        out_shape=[
            tiles(block), weights(block), weights(block), jax.ShapeDtypeStruct((5 * (slots + 4),), F32),
            tiles(block), tiles(block),
        ],
        scratch_shapes=[scratch(tiles(block, jnp.int32)), pltpu.SemaphoreType.DMA((2,))],
        compiler_params=params(6),
        cost_estimate=cost(block, 1, block * 2**15),
        name="weights_and_centre",
    )(psf_radius, band_low, band_high, disp_raw, weighted, background, observed)
    sent = pl.pallas_call(
        functools.partial(blur_kernel, en),
        in_specs=[VMEM] * 5,
        out_specs=[VMEM] * dirs,
        out_shape=[tiles(4)] * dirs,
        compiler_params=params(4),
        cost_estimate=cost(4 * dirs, 2),
        name="blur_border",
    )(centre, band, edge, far, near)
    received = neighbours(sent)
    resid, loss, *folded = pl.pallas_call(
        functools.partial(middle_kernel, en),
        in_specs=[SMEM] + [VMEM] * 7,
        out_specs=[VMEM] * 5,
        out_shape=[tiles(block + 4), jax.ShapeDtypeStruct((8, 128), F32), tiles(block), edges(block), edges(block)],
        scratch_shapes=[scratch(tiles(block)), scratch(tiles(block + 4))],
        compiler_params=params(10),
        cost_estimate=cost(block, 2, block * 2**15),
        name="blur_residual_fold",
    )(fold, centre, band, edge, far, near, background, observed)
    back, near, far = folded
    near, far, total, *border = pl.pallas_call(
        functools.partial(border_kernel, en),
        in_specs=[SMEM] + [VMEM] * (6 + 3 * dirs),
        out_specs=[VMEM] * (3 + dirs),
        out_shape=[edges(block), edges(block), lanes] + [tiles(4)] * dirs,
        scratch_shapes=[scratch(tiles(8)), scratch(tiles(4)), scratch(tiles(4)), scratch(tiles(8))],
        compiler_params=params(4),
        cost_estimate=cost(4 * dirs, 1),
        name="border_residual_fold_loss",
    )(fold, background, observed, resid, loss, near, far, *sent, *received, *counts)

    def partners(value, masks):
        return [lax.ppermute(value, ("sky", "en"), [(i, i ^ mask) for i in range(sky * en)]) for mask in masks]

    far, near = swap_far(far), swap_near(near)
    moved = partners(total, [4 * en * k for k in range(1, sky // 4)])
    centre, total = pl.pallas_call(
        functools.partial(centre_kernel, en),
        in_specs=[VMEM] * (3 + dirs),
        out_specs=[VMEM] * 2,
        out_shape=[tiles(block), lanes],
        compiler_params=params(4),
        cost_estimate=cost(block, 1),
        name="back_centre",
    )(back, band, total, *border)
    groups = block // 4
    most = max(groups * 3 // 4, 1)
    grad = []
    for start, count, masks in ((0, most, [k % en ^ (k // en * 3 * en) for k in range(1, 2 * en)]), (most, groups - most, [en])):
        total = tree_sum([total] + moved)
        moved = partners(total, masks)
        *grad, total = pl.pallas_call(
            functools.partial(final_kernel, start, count),
            in_specs=[VMEM] * 7 + [ANY] * len(grad),
            out_specs=[ANY, VMEM],
            out_shape=[tiles(block), lanes],
            scratch_shapes=[scratch(tiles(4 * count)), scratch(tiles(4 * count)), pltpu.SemaphoreType.DMA((count,))],
            input_output_aliases={7: 0} if start else {},
            compiler_params=params(8),
            cost_estimate=cost(4 * count, 2),
            name="back_edges_lat_exposure",
        )(centre, band, edge, far, near, exposure, total, *grad)
    return grad[0], tree_sum([total] + moved)[0, 0] / F32(rows * width * bins * sky)


def solution(mesh):
    placed = (P("en", None, "sky"),) * 4 + (P(),) * 4
    return jax.shard_map(local, mesh=mesh, in_specs=placed, out_specs=(P("en", None, "sky"), P()), check_vma=False)
```

```python
import functools

import jax
import jax.numpy as jnp
from jax import lax
from jax.experimental import pallas as pl
from jax.experimental.pallas import tpu as pltpu
from jax.sharding import PartitionSpec as P

RMAX = 32
REACH = 2
F32 = jnp.float32
BF16 = jnp.bfloat16
SMEM = pl.BlockSpec(memory_space=pltpu.SMEM)
ANY = pl.BlockSpec(memory_space=pl.ANY)
VMEM = pl.BlockSpec(memory_space=pltpu.VMEM)
HBM = pl.BlockSpec(memory_space=pltpu.HBM)


def split(x):
    hi = x.astype(BF16)
    return hi, (x - hi.astype(F32)).astype(BF16)


def params(mib=56):
    return pltpu.CompilerParams(vmem_limit_bytes=mib * 2**20)


def blocks(count, rows, cols):
    return pl.BlockSpec((count, rows, cols), lambda i: (i, 0, 0))


def chunk_copy(source, target, sem, c, size):
    at = pl.ds(c * size, size)
    return pltpu.make_async_copy(source.at[at], target.at[at], sem)


def run_stages(groups, size, stages, events=(), written_out=False):
    stages = [(*stage, groups)[:3] for stage in stages]
    marks = {0} | {lag for _, lag, _ in stages} | {lag + count for _, lag, count in stages} | {at for at, _ in events}
    marks = sorted(marks)
    for start, stop in zip(marks, marks[1:] + [marks[-1]]):
        for at, event in events:
            if at == start:
                event()
        active = [(n, stage, lag) for n, (stage, lag, count) in enumerate(stages) if lag <= start < lag + count]
        if stop == start or not active:
            continue

        def step(p, carry):
            stores = []
            for _, stage, lag in active:
                for i in range(size):
                    stores += stage((p - lag) * size + i)
            for ref, index, value in stores:
                if index is None:
                    ref[...] += value
                else:
                    ref[index] = value
            return carry

        if written_out:
            for p in range(start, stop):
                step(p, 0)
        else:
            lax.fori_loop(start, stop, step, 0)


def cost(tiles, products, transcendentals=0):
    return pl.CostEstimate(flops=tiles * products * 2 * 128 * 256 * 256, bytes_accessed=tiles * 2**16, transcendentals=transcendentals)


class Place:
    def __init__(self, block, en):
        self.block, self.en = block, en
        self.me = lax.axis_index("en")
        self.dirs = 1 if en == 2 else 2
        self.extra = REACH * self.dirs
        self.slots, self.bins = block + self.extra, block * en
        self.own = jnp.where(self.me == 0, 0, REACH) if en == 2 else REACH
        self.first_bin = self.me * block - self.own

    def above(self, d):
        return jnp.where(self.me == 0, 1, 0) if self.en == 2 else 1 - d

    def sent(self, d, width):
        return self.above(d) * (self.block - width)

    def border(self, d):
        up = self.above(d) if self.en == 2 else d
        return up, up * (self.block + self.own - REACH)

    def clamp(self, g):
        return jnp.clip(g, 0, self.bins - 1)


def lanes_of(shape=(128, 128)):
    return lax.broadcasted_iota(jnp.int32, shape, 1)


def is_odd():
    return lax.axis_index("sky") % 2 == 1


def pack_edges(tiles):
    lane = lanes_of()
    outer = (lane < RMAX) | (lane >= 128 - RMAX)
    early, late = [jnp.where(outer, tiles[n], pltpu.roll(tiles[n + 1], 64, 1)) for n in (0, 2)]
    late = pltpu.roll(late, RMAX, 1)
    mask = ((lane // RMAX) % 2 == 1) != is_odd()
    return jnp.where(mask, early, late), jnp.where(mask, late, early)


LEFT = (3, 1, 0, 2)
RIGHT = (0, 2, 1, 3)


def edge_tile(near, far, n):
    lane = lanes_of()
    from_left = lane < RMAX * RIGHT[n] if LEFT[n] < RIGHT[n] else lane >= RMAX * LEFT[n]
    return jnp.where(from_left != is_odd(), far, near)


def twice(x):
    return jnp.concatenate([x, x], axis=0)


def lon_product(tile, weights):
    out = jnp.dot(jnp.concatenate(split(tile), axis=1), twice(weights), preferred_element_type=F32)
    return out[:, :128] + out[:, 128:]


def lat_product(weights, tile):
    out = jnp.dot(weights, twice(jnp.concatenate(split(tile), axis=1)), preferred_element_type=F32)
    return out[:, :128] + out[:, 128:]


def profile(radius, column):
    wide = jnp.full((1, 128), radius, jnp.int32).astype(F32)
    reach = wide * wide
    factor = -2.0 / reach
    lane = lax.broadcasted_iota(jnp.int32, (1, 128), 1)
    square = (lane * lane).astype(F32)
    values = jnp.where(square <= reach, jnp.exp(square * factor), 0.0)
    norm = 2.0 * jnp.sum(values, axis=1, keepdims=True) - 1.0
    root = jnp.sqrt(jnp.full((1, 128), column, F32))[:, :1]
    return factor[:, :1], 1.0 / (norm * root), reach[:, :1]


def taper_values(diff, ok, factor, scale, reach):
    square = diff * diff
    return jnp.where((square <= reach) & ok, jnp.exp(square * factor) * scale, 0.0)


def pack_kernel(parts, en, flux, exposure, background, observed, weighted, near, far, *rest):
    place = Place(flux.shape[0], en)
    dirs, block = place.dirs, place.block
    sent, (v_flux, v_exposure, v_observed, sems, near_sems) = rest[:dirs], rest[dirs:]
    chunk = block // parts

    def arrivals(c):
        return [chunk_copy(a, b, sems.at[n, c], c, chunk) for n, (a, b) in enumerate(((flux, v_flux), (exposure, v_exposure)))]

    def near_arrivals(d):
        at = pl.ds(place.sent(d, REACH), REACH)
        return [
            pltpu.make_async_copy(background.at[at], sent[d].at[pl.ds(0, REACH)], near_sems.at[d, 0]),
            pltpu.make_async_copy(observed.at[at], v_observed.at[d], near_sems.at[d, 1]),
        ]

    for c in range(parts):
        for copy in arrivals(c):
            copy.start()
    for d in range(dirs):
        for copy in near_arrivals(d):
            copy.start()

    def some(g, carry):
        tiles = [v_flux[4 * g + i] * v_exposure[4 * g + i] for i in range(4)]
        packed = pack_edges(tiles)
        for i in range(4):
            weighted[4 * g + i] = tiles[i]
        near[g], far[g] = packed
        return carry

    for c in range(parts):
        for copy in arrivals(c):
            copy.wait()
        lax.fori_loop(c * chunk // 4, (c + 1) * chunk // 4, some, 0)
    for d in range(dirs):
        for copy in near_arrivals(d):
            copy.wait()
        for k in range(REACH):
            sent[d][REACH + k] = v_observed[d, k].astype(F32)


def weights_kernel(en, radius, low, high, disp, weighted, background, observed,
                   centre, band, edge, fold, held_background, counts, v_observed, sems):
    fetches = [
        pltpu.make_async_copy(background, held_background, sems.at[0]),
        pltpu.make_async_copy(observed, v_observed, sems.at[1]),
    ]
    for fetch in fetches:
        fetch.start()
    block = weighted.shape[0]
    place = Place(block, en)
    row = lax.broadcasted_iota(jnp.int32, (128, 128), 0)
    col = lax.broadcasted_iota(jnp.int32, (128, 128), 1)
    near = (row - col).astype(F32)
    always = row >= 0
    beside = []
    for n in range(4):
        shift = jnp.where(row // RMAX == LEFT[n], -RMAX - RMAX * LEFT[n], 128 - RMAX * RIGHT[n])
        held = (row // RMAX == LEFT[n]) | (row // RMAX == RIGHT[n])
        beside.append(((row + shift - col).astype(F32), held))

    def weight(i, j):
        at, to = place.clamp(i), place.clamp(j)
        inside = (i == at) & (j == to) & (low[at] <= j - i) & (j - i <= high[at])
        return jnp.where(inside, disp[at, to], 0.0)

    def fold_row(g):
        for o in range(-REACH, REACH + 1):
            fold[5 * (g - place.first_bin + REACH) + o + REACH] = weight(g, g + o)

    def make(g, n):
        fold_row(g)
        column = weight(g, g)
        for o in (-2, -1, 1, 2):
            column = column + weight(g - o, g)
        numbers = profile(radius[place.clamp(g)], jnp.where(column > 0.0, column, 1.0))
        return tuple(
            jnp.concatenate(split(taper_values(diff, ok, *numbers)), axis=1) for diff, ok in ((near, always), beside[n])
        )

    for s in (0, 1, place.slots + 2, place.slots + 3):
        for o in range(5):
            fold[5 * s + o] = 0.0

    def some(g):
        made = [make(place.me * block + 4 * g + n, n) for n in range(4)]
        return [(band, 4 * g + n, made[n][0]) for n in range(4)] + [(edge, 4 * g + n, made[n][1]) for n in range(4)]

    def lon(g):
        return [(centre, 4 * g + n, lon_product(weighted[4 * g + n], band[4 * g + n])) for n in range(4)]

    run_stages(block // 4, 1, [(some, 0), (lon, 1)])
    for d in range(place.dirs):
        up, slot = place.border(d)
        for k in range(REACH):
            fold_row(place.first_bin + slot + up * REACH + k)
    for fetch in fetches:
        fetch.wait()

    def convert(g):
        return [(counts, 4 * g + n, v_observed[4 * g + n].astype(F32)) for n in range(4)]

    run_stages(block // 4, 1, [(convert, 0)])


def lon_edges(centre, edge, far, near, g, at, n):
    return centre[at] + lon_product(edge_tile(near[g], far[g], n), edge[at])


def blur_kernel(en, centre, band, edge, far, near, *blurred):
    place = Place(centre.shape[0], en)
    for d in range(place.dirs):
        start = place.sent(d, 4)
        g = lax.div(start, 4) if en == 2 else start // 4
        sums = [lon_edges(centre, edge, far, near, g, start + n, n) for n in range(4)]
        sums = [lat_product(band[start + n], sums[n]) for n in range(4)]
        for n in range(4):
            blurred[d][n] = sums[n]


def inverse(x):
    first = pl.reciprocal(x, approx=True)
    return first * (2.0 - x * first)


ROWS = [pl.ds(32 * r, 32) for r in range(4)]


def loss_terms(mu, counts):
    return (mu - counts * jnp.log(mu)).reshape(-1, 8, 128).sum(0)


def fold_one(fold, row, resid, at):
    total = None
    for o in range(5):
        term = fold[5 * (row - o) + o] * resid[at - o]
        total = term if total is None else total + term
    return total


def middle_kernel(en, fold, centre, band, edge, far, near, background, observed, resid, loss, back, near_out, far_out, whole, blurred):
    block = centre.shape[0]
    place = Place(block, en)
    own = place.own
    zero = jnp.zeros((128, 128), F32)
    for s in (0, 1, block + 2, block + 3):
        blurred[s] = zero
        resid[s] = zero
    loss[...] = jnp.zeros((8, 128), F32)
    inside = (own, own + block - REACH) if en == 2 else (REACH, block - REACH)

    def lon(g):
        return [(whole, 4 * g + n, lon_edges(centre, edge, far, near, g, 4 * g + n, n)) for n in range(4)]

    def lat(g):
        return [(blurred, 4 * g + n + 2, lat_product(band[4 * g + n], whole[4 * g + n])) for n in range(4)]

    def residual(g):
        sums = None
        for rows in ROWS:
            window = [blurred[4 * g + k, rows] for k in range(8)]
            for n in range(4):
                b = 4 * g + n
                mu = background[b, rows]
                for o in range(5):
                    mu = mu + fold[5 * (b + own + 2) + o] * window[n + o]
                counts = observed[b, rows]
                resid[b + 2, rows] = 1.0 - counts * inverse(mu)
                inner = (b >= inside[0]) & (b < inside[1])
                terms = jnp.where(inner, loss_terms(mu, counts), 0.0)
                sums = terms if sums is None else sums + terms
        return [(loss, None, sums)]

    def fold_back(g):
        tiles = [[] for _ in range(4)]
        for rows in ROWS:
            window = [resid[4 * g + k, rows] for k in range(8)]
            for n in range(4):
                total = None
                for o in range(5):
                    term = fold[5 * (4 * g + n + own + 4 - o) + o] * window[n + 4 - o]
                    total = term if total is None else total + term
                back[4 * g + n, rows] = total
                tiles[n].append(total)
        near_out[g], far_out[g] = pack_edges([jnp.concatenate(parts, axis=0) for parts in tiles])
        return []

    run_stages(block // 8, 2, [(fold_back, 5), (residual, 3), (lon, 0), (lat, 1)], written_out=True)


def border_kernel(en, fold, background, observed, resid, loss, near_in, far_in, *rest):
    block = background.shape[0]
    place = Place(block, en)
    dirs, own = place.dirs, place.own
    sent, received, counts = [rest[n * dirs:(n + 1) * dirs] for n in range(3)]
    near, far, total = rest[3 * dirs:3 * dirs + 3]
    back, (blurred, ground, seen, rows) = rest[3 * dirs + 3:4 * dirs + 3], rest[4 * dirs + 3:]
    sums = loss[...]
    near[...], far[...] = near_in[...], far_in[...]
    for d in range(dirs):
        up, slot = place.border(d)
        mine, theirs = 4 * (1 - up), 4 * up
        for k in range(4):
            blurred[mine + k] = sent[dirs - 1 - d][k]
            blurred[theirs + k] = received[d][k]
            rows[mine + k] = resid[up * (block - 8) + 4 + k]
        first = up * (block - REACH)
        for k in range(REACH):
            ground[mine // 2 + k] = background[first + k]
            seen[mine // 2 + k] = observed[first + k]
            ground[theirs // 2 + k] = counts[d][k]
            seen[theirs // 2 + k] = counts[d][REACH + k]
        for part in ROWS:
            window = [blurred[k, part] for k in range(8)]
            for j in range(2 * REACH):
                mu = ground[j, part]
                for o in range(5):
                    mu = mu + fold[5 * (slot + j + 2) + o] * window[j + o]
                rows[theirs + j, part] = 1.0 - seen[j, part] * inverse(mu)
                ground[j, part] = mu
        first = up * (block - 4)
        parts = [[] for _ in range(4)]
        for part in ROWS:
            window = [rows[k, part] for k in range(8)]
            for n in range(4):
                parts[n].append(fold_one(fold, first + n + own + 4, window, n + 4))
        tiles = [jnp.concatenate(chunks, axis=0) for chunks in parts]
        for k in range(REACH):
            sums = sums + loss_terms(ground[mine // 2 + k], seen[mine // 2 + k])
        g = up * (block // 4 - 1)
        near[g], far[g] = pack_edges(tiles)
        for n in range(4):
            back[d][n] = tiles[n]
    total[...] = jnp.full((1, 128), jnp.sum(sums), F32)


def centre_kernel(en, back, band, total, *rest):
    border, (out, passed) = rest[:-2], rest[-2:]
    passed[...] = total[...]
    size = 8

    def some(g, carry):
        sums = [lon_product(back[size * g + i], band[size * g + i]) for i in range(size)]
        for i in range(size):
            out[size * g + i] = sums[i]
        return carry

    lax.fori_loop(0, back.shape[0] // size, some, 0)
    place = Place(back.shape[0], en)
    for d in range(place.dirs):
        first = place.border(d)[0] * (back.shape[0] - 4)
        for n in range(4):
            out[first + n] = lon_product(border[d][n], band[first + n])


def final_kernel(centre, band, edge, far, near, exposure, total, out, passed, whole, v_out, out_sems):
    groups = near.shape[0]
    size = 2
    steps = groups // size
    passed[...] = total[...]

    def copy_out(p):
        return chunk_copy(v_out, out, out_sems.at[p], p, 4 * size)

    def lon(g):
        return [(whole, 4 * g + n, lon_edges(centre, edge, far, near, g, 4 * g + n, n)) for n in range(4)]

    def lat(g):
        return [(v_out, 4 * g + n, lat_product(band[4 * g + n], whole[4 * g + n]) * exposure[4 * g + n]) for n in range(4)]

    run_stages(steps, size, [(lon, 0), (lat, 1)], events=[(p + 2, copy_out(p).start) for p in range(steps)], written_out=True)
    for p in range(steps):
        copy_out(p).wait()


def tree_sum(values):
    while len(values) > 1:
        values = [a + b for a, b in zip(values[::2], values[1::2])]
    return values[0]


def ring(size, shift):
    return [(i, (i + shift) % size) for i in range(size)]


def local(flux, exposure, background, observed, psf_radius, band_low, band_high, disp_raw):
    block, rows, width = flux.shape
    bins = disp_raw.shape[0]
    sky, en = lax.axis_size("sky"), lax.axis_size("en")
    shifts = [1] if en == 2 else [1, -1]
    dirs = len(shifts)
    slots = block + REACH * dirs
    parts = min(8, block // 4)

    def tiles(count, dtype=F32):
        return jax.ShapeDtypeStruct((count, rows, width), dtype)

    def edges(count):
        return jax.ShapeDtypeStruct((count // 4, 128, 128), F32)

    def weights(count):
        return jax.ShapeDtypeStruct((count, 128, 256), BF16)

    def scratch(shape):
        return pltpu.VMEM(shape.shape, shape.dtype)

    lanes = jax.ShapeDtypeStruct((1, 128), F32)

    flux, exposure_in, background, observed = [
        pltpu.with_memory_space_constraint(array, pltpu.HBM) for array in (flux, exposure, background, observed)
    ]
    half = block // 2

    def swap_far(edges):
        return lax.ppermute(edges, "sky", [(s, (s + 1 if s % 2 else s - 1) % sky) for s in range(sky)])

    def swap_near(edges):
        return lax.ppermute(edges, "sky", [(s, s ^ 1) for s in range(sky)])

    def neighbours(arrays):
        return [lax.ppermute(array, "en", ring(en, shift)) for array, shift in zip(arrays, shifts)]

    weighted, near, far, *sent = pl.pallas_call(
        functools.partial(pack_kernel, parts, en),
        in_specs=[ANY] * 4,
        out_specs=[VMEM] * (3 + dirs),
        out_shape=[tiles(block), edges(block), edges(block)] + [tiles(2 * REACH)] * dirs,
        scratch_shapes=[
            scratch(tiles(block)), scratch(tiles(block)), pltpu.VMEM((dirs, REACH, rows, width), jnp.int32),
            pltpu.SemaphoreType.DMA((2, parts)), pltpu.SemaphoreType.DMA((dirs, 2)),
        ],
        compiler_params=params(12),
        name="weight_and_pack",
    )(flux, exposure_in, background, observed)
    far, near = swap_far(far), swap_near(near)
    counts = neighbours(sent)

    centre, band, edge, fold, background, observed = pl.pallas_call(
        functools.partial(weights_kernel, en),
        in_specs=[SMEM] * 4 + [VMEM] + [ANY] * 2,
        out_specs=[VMEM] * 3 + [SMEM] + [VMEM] * 2,
        out_shape=[
            tiles(block), weights(block), weights(block), jax.ShapeDtypeStruct((5 * (slots + 4),), F32),
            tiles(block), tiles(block),
        ],
        scratch_shapes=[scratch(tiles(block, jnp.int32)), pltpu.SemaphoreType.DMA((2,))],
        compiler_params=params(6),
        cost_estimate=cost(block, 1, block * 2**15),
        name="weights_and_centre",
    )(psf_radius, band_low, band_high, disp_raw, weighted, background, observed)
    sent = pl.pallas_call(
        functools.partial(blur_kernel, en),
        in_specs=[VMEM] * 5,
        out_specs=[VMEM] * dirs,
        out_shape=[tiles(4)] * dirs,
        compiler_params=params(4),
        cost_estimate=cost(4 * dirs, 2),
        name="blur_border",
    )(centre, band, edge, far, near)
    received = neighbours(sent)
    resid, loss, *folded = pl.pallas_call(
        functools.partial(middle_kernel, en),
        in_specs=[SMEM] + [VMEM] * 7,
        out_specs=[VMEM] * 5,
        out_shape=[tiles(block + 4), jax.ShapeDtypeStruct((8, 128), F32), tiles(block), edges(block), edges(block)],
        scratch_shapes=[scratch(tiles(block)), scratch(tiles(block + 4))],
        compiler_params=params(10),
        cost_estimate=cost(block, 2, block * 2**15),
        name="blur_residual_fold",
    )(fold, centre, band, edge, far, near, background, observed)
    back, near, far = folded
    near, far, total, *border = pl.pallas_call(
        functools.partial(border_kernel, en),
        in_specs=[SMEM] + [VMEM] * (6 + 3 * dirs),
        out_specs=[VMEM] * (3 + dirs),
        out_shape=[edges(block), edges(block), lanes] + [tiles(4)] * dirs,
        scratch_shapes=[scratch(tiles(8)), scratch(tiles(4)), scratch(tiles(4)), scratch(tiles(8))],
        compiler_params=params(4),
        cost_estimate=cost(4 * dirs, 1),
        name="border_residual_fold_loss",
    )(fold, background, observed, resid, loss, near, far, *sent, *received, *counts)

    def partners(value, masks):
        return [lax.ppermute(value, ("sky", "en"), [(i, i ^ mask) for i in range(sky * en)]) for mask in masks]

    far, near = swap_far(far), swap_near(near)
    moved = partners(total, [4 * en * k for k in range(1, sky // 4)])
    centre, total = pl.pallas_call(
        functools.partial(centre_kernel, en),
        in_specs=[VMEM] * (3 + dirs),
        out_specs=[VMEM] * 2,
        out_shape=[tiles(block), lanes],
        compiler_params=params(4),
        cost_estimate=cost(block, 1),
        name="back_centre",
    )(back, band, total, *border)
    total = tree_sum([total] + moved)
    moved = partners(total, [k % en ^ (k // en * 3 * en) for k in range(1, 2 * en)])
    grad, total = pl.pallas_call(
        final_kernel,
        in_specs=[VMEM] * 7,
        out_specs=[ANY, VMEM],
        out_shape=[tiles(block), lanes],
        scratch_shapes=[scratch(tiles(block)), scratch(tiles(block)), pltpu.SemaphoreType.DMA((block // 8,))],
        compiler_params=params(8),
        cost_estimate=cost(block, 2),
        name="back_edges_lat_exposure",
    )(centre, band, edge, far, near, exposure, total)
    total = tree_sum([total] + moved)
    total = total + partners(total, [en])[0]
    return grad, total[0, 0] / F32(rows * width * bins * sky)


def solution(mesh):
    placed = (P("en", None, "sky"),) * 4 + (P(),) * 4
    return jax.shard_map(local, mesh=mesh, in_specs=placed, out_specs=(P("en", None, "sky"), P()), check_vma=False)
```

```python
import functools

import jax
import jax.numpy as jnp
from jax import lax
from jax.experimental import pallas as pl
from jax.experimental.pallas import tpu as pltpu
from jax.sharding import PartitionSpec as P

RMAX = 32
REACH = 2
F32 = jnp.float32
BF16 = jnp.bfloat16
SMEM = pl.BlockSpec(memory_space=pltpu.SMEM)
ANY = pl.BlockSpec(memory_space=pl.ANY)
VMEM = pl.BlockSpec(memory_space=pltpu.VMEM)
HBM = pl.BlockSpec(memory_space=pltpu.HBM)


def split(x):
    hi = x.astype(BF16)
    return hi, (x - hi.astype(F32)).astype(BF16)


def params(mib=56):
    return pltpu.CompilerParams(vmem_limit_bytes=mib * 2**20)


def blocks(count, rows, cols):
    return pl.BlockSpec((count, rows, cols), lambda i: (i, 0, 0))


def chunk_copy(source, target, sem, c, size):
    at = pl.ds(c * size, size)
    return pltpu.make_async_copy(source.at[at], target.at[at], sem)


def run_stages(groups, size, stages, events=(), written_out=False):
    stages = [(*stage, groups)[:3] for stage in stages]
    marks = {0} | {lag for _, lag, _ in stages} | {lag + count for _, lag, count in stages} | {at for at, _ in events}
    marks = sorted(marks)
    for start, stop in zip(marks, marks[1:] + [marks[-1]]):
        for at, event in events:
            if at == start:
                event()
        active = [(n, stage, lag) for n, (stage, lag, count) in enumerate(stages) if lag <= start < lag + count]
        if stop == start or not active:
            continue

        def step(p, carry):
            stores = []
            for _, stage, lag in active:
                for i in range(size):
                    stores += stage((p - lag) * size + i)
            for ref, index, value in stores:
                if index is None:
                    ref[...] += value
                else:
                    ref[index] = value
            return carry

        if written_out:
            for p in range(start, stop):
                step(p, 0)
        else:
            lax.fori_loop(start, stop, step, 0)


def cost(tiles, products, transcendentals=0):
    return pl.CostEstimate(flops=tiles * products * 2 * 128 * 256 * 256, bytes_accessed=tiles * 2**16, transcendentals=transcendentals)


class Place:
    def __init__(self, block, en):
        self.block, self.en = block, en
        self.me = lax.axis_index("en")
        self.dirs = 1 if en == 2 else 2
        self.extra = REACH * self.dirs
        self.slots, self.bins = block + self.extra, block * en
        self.own = jnp.where(self.me == 0, 0, REACH) if en == 2 else REACH
        self.first_bin = self.me * block - self.own

    def above(self, d):
        return jnp.where(self.me == 0, 1, 0) if self.en == 2 else 1 - d

    def sent(self, d, width):
        return self.above(d) * (self.block - width)

    def border(self, d):
        up = self.above(d) if self.en == 2 else d
        return up, up * (self.block + self.own - REACH)

    def clamp(self, g):
        return jnp.clip(g, 0, self.bins - 1)


def lanes_of(shape=(128, 128)):
    return lax.broadcasted_iota(jnp.int32, shape, 1)


def is_odd():
    return lax.axis_index("sky") % 2 == 1


def pack_edges(tiles):
    lane = lanes_of()
    outer = (lane < RMAX) | (lane >= 128 - RMAX)
    early, late = [jnp.where(outer, tiles[n], pltpu.roll(tiles[n + 1], 64, 1)) for n in (0, 2)]
    late = pltpu.roll(late, RMAX, 1)
    mask = ((lane // RMAX) % 2 == 1) != is_odd()
    return jnp.where(mask, early, late), jnp.where(mask, late, early)


LEFT = (3, 1, 0, 2)
RIGHT = (0, 2, 1, 3)


def edge_tile(near, far, n):
    lane = lanes_of()
    from_left = lane < RMAX * RIGHT[n] if LEFT[n] < RIGHT[n] else lane >= RMAX * LEFT[n]
    return jnp.where(from_left != is_odd(), far, near)


def twice(x):
    return jnp.concatenate([x, x], axis=0)


def lon_product(tile, weights):
    out = jnp.dot(jnp.concatenate(split(tile), axis=1), twice(weights), preferred_element_type=F32)
    return out[:, :128] + out[:, 128:]


def lat_product(weights, tile):
    out = jnp.dot(weights, twice(jnp.concatenate(split(tile), axis=1)), preferred_element_type=F32)
    return out[:, :128] + out[:, 128:]


def profile(radius, column):
    wide = jnp.full((1, 128), radius, jnp.int32).astype(F32)
    reach = wide * wide
    factor = -2.0 / reach
    lane = lax.broadcasted_iota(jnp.int32, (1, 128), 1)
    square = (lane * lane).astype(F32)
    values = jnp.where(square <= reach, jnp.exp(square * factor), 0.0)
    norm = 2.0 * jnp.sum(values, axis=1, keepdims=True) - 1.0
    root = jnp.sqrt(jnp.full((1, 128), column, F32))[:, :1]
    return factor[:, :1], 1.0 / (norm * root), reach[:, :1]


def taper_values(diff, ok, factor, scale, reach):
    square = diff * diff
    return jnp.where((square <= reach) & ok, jnp.exp(square * factor) * scale, 0.0)


def pack_kernel(parts, en, flux, exposure, background, observed, weighted, near, far, *rest):
    place = Place(flux.shape[0], en)
    dirs, block = place.dirs, place.block
    sent, (v_flux, v_exposure, v_observed, sems, near_sems) = rest[:dirs], rest[dirs:]
    chunk = block // parts

    def arrivals(c):
        return [chunk_copy(a, b, sems.at[n, c], c, chunk) for n, (a, b) in enumerate(((flux, v_flux), (exposure, v_exposure)))]

    def near_arrivals(d):
        at = pl.ds(place.sent(d, REACH), REACH)
        return [
            pltpu.make_async_copy(background.at[at], sent[d].at[pl.ds(0, REACH)], near_sems.at[d, 0]),
            pltpu.make_async_copy(observed.at[at], v_observed.at[d], near_sems.at[d, 1]),
        ]

    for c in range(parts):
        for copy in arrivals(c):
            copy.start()
    for d in range(dirs):
        for copy in near_arrivals(d):
            copy.start()

    def some(g, carry):
        tiles = [v_flux[4 * g + i] * v_exposure[4 * g + i] for i in range(4)]
        packed = pack_edges(tiles)
        for i in range(4):
            weighted[4 * g + i] = tiles[i]
        near[g], far[g] = packed
        return carry

    for c in range(parts):
        for copy in arrivals(c):
            copy.wait()
        lax.fori_loop(c * chunk // 4, (c + 1) * chunk // 4, some, 0)
    for d in range(dirs):
        for copy in near_arrivals(d):
            copy.wait()
        for k in range(REACH):
            sent[d][REACH + k] = v_observed[d, k].astype(F32)


def weights_kernel(en, radius, low, high, disp, weighted, background, observed,
                   centre, band, edge, fold, held_background, counts, v_observed, sems):
    fetches = [
        pltpu.make_async_copy(background, held_background, sems.at[0]),
        pltpu.make_async_copy(observed, v_observed, sems.at[1]),
    ]
    for fetch in fetches:
        fetch.start()
    block = weighted.shape[0]
    place = Place(block, en)
    row = lax.broadcasted_iota(jnp.int32, (128, 128), 0)
    col = lax.broadcasted_iota(jnp.int32, (128, 128), 1)
    near = (row - col).astype(F32)
    always = row >= 0
    beside = []
    for n in range(4):
        shift = jnp.where(row // RMAX == LEFT[n], -RMAX - RMAX * LEFT[n], 128 - RMAX * RIGHT[n])
        held = (row // RMAX == LEFT[n]) | (row // RMAX == RIGHT[n])
        beside.append(((row + shift - col).astype(F32), held))

    def weight(i, j):
        at, to = place.clamp(i), place.clamp(j)
        inside = (i == at) & (j == to) & (low[at] <= j - i) & (j - i <= high[at])
        return jnp.where(inside, disp[at, to], 0.0)

    def fold_row(g):
        for o in range(-REACH, REACH + 1):
            fold[5 * (g - place.first_bin + REACH) + o + REACH] = weight(g, g + o)

    def make(g, n):
        fold_row(g)
        column = weight(g, g)
        for o in (-2, -1, 1, 2):
            column = column + weight(g - o, g)
        numbers = profile(radius[place.clamp(g)], jnp.where(column > 0.0, column, 1.0))
        return tuple(
            jnp.concatenate(split(taper_values(diff, ok, *numbers)), axis=1) for diff, ok in ((near, always), beside[n])
        )

    for s in (0, 1, place.slots + 2, place.slots + 3):
        for o in range(5):
            fold[5 * s + o] = 0.0

    def some(g):
        made = [make(place.me * block + 4 * g + n, n) for n in range(4)]
        return [(band, 4 * g + n, made[n][0]) for n in range(4)] + [(edge, 4 * g + n, made[n][1]) for n in range(4)]

    def lon(g):
        return [(centre, 4 * g + n, lon_product(weighted[4 * g + n], band[4 * g + n])) for n in range(4)]

    run_stages(block // 4, 1, [(some, 0), (lon, 1)])
    for d in range(place.dirs):
        up, slot = place.border(d)
        for k in range(REACH):
            fold_row(place.first_bin + slot + up * REACH + k)
    for fetch in fetches:
        fetch.wait()

    def convert(g):
        return [(counts, 4 * g + n, v_observed[4 * g + n].astype(F32)) for n in range(4)]

    run_stages(block // 4, 1, [(convert, 0)])


def lon_edges(centre, edge, far, near, g, at, n):
    return centre[at] + lon_product(edge_tile(near[g], far[g], n), edge[at])


def blur_kernel(en, centre, band, edge, far, near, *blurred):
    place = Place(centre.shape[0], en)
    for d in range(place.dirs):
        start = place.sent(d, 4)
        g = lax.div(start, 4) if en == 2 else start // 4
        sums = [lon_edges(centre, edge, far, near, g, start + n, n) for n in range(4)]
        sums = [lat_product(band[start + n], sums[n]) for n in range(4)]
        for n in range(4):
            blurred[d][n] = sums[n]


def inverse(x):
    first = pl.reciprocal(x, approx=True)
    return first * (2.0 - x * first)


ROWS = [pl.ds(32 * r, 32) for r in range(4)]


def loss_terms(mu, counts):
    return (mu - counts * jnp.log(mu)).reshape(-1, 8, 128).sum(0)


def fold_one(fold, row, resid, at):
    total = None
    for o in range(5):
        term = fold[5 * (row - o) + o] * resid[at - o]
        total = term if total is None else total + term
    return total


def middle_kernel(en, fold, centre, band, edge, far, near, background, observed, resid, loss, back, near_out, far_out, whole, blurred):
    block = centre.shape[0]
    place = Place(block, en)
    own = place.own
    zero = jnp.zeros((128, 128), F32)
    for s in (0, 1, block + 2, block + 3):
        blurred[s] = zero
        resid[s] = zero
    loss[...] = jnp.zeros((8, 128), F32)
    inside = (own, own + block - REACH) if en == 2 else (REACH, block - REACH)

    def lon(g):
        return [(whole, 4 * g + n, lon_edges(centre, edge, far, near, g, 4 * g + n, n)) for n in range(4)]

    def lat(g):
        return [(blurred, 4 * g + n + 2, lat_product(band[4 * g + n], whole[4 * g + n])) for n in range(4)]

    def residual(g):
        sums = None
        for rows in ROWS:
            window = [blurred[4 * g + k, rows] for k in range(8)]
            for n in range(4):
                b = 4 * g + n
                mu = background[b, rows]
                for o in range(5):
                    mu = mu + fold[5 * (b + own + 2) + o] * window[n + o]
                counts = observed[b, rows]
                resid[b + 2, rows] = 1.0 - counts * inverse(mu)
                inner = (b >= inside[0]) & (b < inside[1])
                terms = jnp.where(inner, loss_terms(mu, counts), 0.0)
                sums = terms if sums is None else sums + terms
        return [(loss, None, sums)]

    def fold_back(g):
        tiles = [[] for _ in range(4)]
        for rows in ROWS:
            window = [resid[4 * g + k, rows] for k in range(8)]
            for n in range(4):
                total = None
                for o in range(5):
                    term = fold[5 * (4 * g + n + own + 4 - o) + o] * window[n + 4 - o]
                    total = term if total is None else total + term
                back[4 * g + n, rows] = total
                tiles[n].append(total)
        near_out[g], far_out[g] = pack_edges([jnp.concatenate(parts, axis=0) for parts in tiles])
        return []

    run_stages(block // 4, 1, [(fold_back, 5), (residual, 3), (lon, 0), (lat, 1)], written_out=True)


def border_kernel(en, fold, background, observed, resid, loss, near_in, far_in, *rest):
    block = background.shape[0]
    place = Place(block, en)
    dirs, own = place.dirs, place.own
    sent, received, counts = [rest[n * dirs:(n + 1) * dirs] for n in range(3)]
    near, far, total = rest[3 * dirs:3 * dirs + 3]
    back, (blurred, ground, seen, rows) = rest[3 * dirs + 3:4 * dirs + 3], rest[4 * dirs + 3:]
    sums = loss[...]
    near[...], far[...] = near_in[...], far_in[...]
    for d in range(dirs):
        up, slot = place.border(d)
        mine, theirs = 4 * (1 - up), 4 * up
        for k in range(4):
            blurred[mine + k] = sent[dirs - 1 - d][k]
            blurred[theirs + k] = received[d][k]
            rows[mine + k] = resid[up * (block - 8) + 4 + k]
        first = up * (block - REACH)
        for k in range(REACH):
            ground[mine // 2 + k] = background[first + k]
            seen[mine // 2 + k] = observed[first + k]
            ground[theirs // 2 + k] = counts[d][k]
            seen[theirs // 2 + k] = counts[d][REACH + k]
        for j in range(2 * REACH):
            mu = ground[j]
            for o in range(5):
                mu = mu + fold[5 * (slot + j + 2) + o] * blurred[j + o]
            rows[theirs + j] = 1.0 - seen[j] * inverse(mu)
            is_mine = (mine // 2 <= j) & (j < mine // 2 + REACH)
            sums = sums + jnp.where(is_mine, loss_terms(mu, seen[j]), 0.0)
        first = up * (block - 4)
        tiles = [fold_one(fold, first + n + own + 4, rows, n + 4) for n in range(4)]
        g = up * (block // 4 - 1)
        near[g], far[g] = pack_edges(tiles)
        for n in range(4):
            back[d][n] = tiles[n]
    total[...] = jnp.full((1, 128), jnp.sum(sums), F32)


def centre_kernel(en, back, band, total, *rest):
    border, (out, passed) = rest[:-2], rest[-2:]
    passed[...] = total[...]
    size = 8

    def some(g, carry):
        sums = [lon_product(back[size * g + i], band[size * g + i]) for i in range(size)]
        for i in range(size):
            out[size * g + i] = sums[i]
        return carry

    lax.fori_loop(0, back.shape[0] // size, some, 0)
    place = Place(back.shape[0], en)
    for d in range(place.dirs):
        first = place.border(d)[0] * (back.shape[0] - 4)
        for n in range(4):
            out[first + n] = lon_product(border[d][n], band[first + n])


def final_kernel(centre, band, edge, far, near, exposure, total, out, passed, whole, v_out, out_sems):
    groups = near.shape[0]
    size = 1
    steps = groups // size
    passed[...] = total[...]

    def copy_out(p):
        return chunk_copy(v_out, out, out_sems.at[p], p, 4 * size)

    def lon(g):
        return [(whole, 4 * g + n, lon_edges(centre, edge, far, near, g, 4 * g + n, n)) for n in range(4)]

    def lat(g):
        return [(v_out, 4 * g + n, lat_product(band[4 * g + n], whole[4 * g + n]) * exposure[4 * g + n]) for n in range(4)]

    run_stages(steps, size, [(lon, 0), (lat, 1)], events=[(p + 2, copy_out(p).start) for p in range(steps)], written_out=True)
    for p in range(steps):
        copy_out(p).wait()


def tree_sum(values):
    while len(values) > 1:
        values = [a + b for a, b in zip(values[::2], values[1::2])]
    return values[0]


def ring(size, shift):
    return [(i, (i + shift) % size) for i in range(size)]


def local(flux, exposure, background, observed, psf_radius, band_low, band_high, disp_raw):
    block, rows, width = flux.shape
    bins = disp_raw.shape[0]
    sky, en = lax.axis_size("sky"), lax.axis_size("en")
    shifts = [1] if en == 2 else [1, -1]
    dirs = len(shifts)
    slots = block + REACH * dirs
    parts = min(8, block // 4)

    def tiles(count, dtype=F32):
        return jax.ShapeDtypeStruct((count, rows, width), dtype)

    def edges(count):
        return jax.ShapeDtypeStruct((count // 4, 128, 128), F32)

    def weights(count):
        return jax.ShapeDtypeStruct((count, 128, 256), BF16)

    def scratch(shape):
        return pltpu.VMEM(shape.shape, shape.dtype)

    lanes = jax.ShapeDtypeStruct((1, 128), F32)

    flux, exposure_in, background, observed = [
        pltpu.with_memory_space_constraint(array, pltpu.HBM) for array in (flux, exposure, background, observed)
    ]
    half = block // 2

    def swap_far(edges):
        return lax.ppermute(edges, "sky", [(s, (s + 1 if s % 2 else s - 1) % sky) for s in range(sky)])

    def swap_near(edges):
        return lax.ppermute(edges, "sky", [(s, s ^ 1) for s in range(sky)])

    def neighbours(arrays):
        return [lax.ppermute(array, "en", ring(en, shift)) for array, shift in zip(arrays, shifts)]

    weighted, near, far, *sent = pl.pallas_call(
        functools.partial(pack_kernel, parts, en),
        in_specs=[ANY] * 4,
        out_specs=[VMEM] * (3 + dirs),
        out_shape=[tiles(block), edges(block), edges(block)] + [tiles(2 * REACH)] * dirs,
        scratch_shapes=[
            scratch(tiles(block)), scratch(tiles(block)), pltpu.VMEM((dirs, REACH, rows, width), jnp.int32),
            pltpu.SemaphoreType.DMA((2, parts)), pltpu.SemaphoreType.DMA((dirs, 2)),
        ],
        compiler_params=params(12),
        name="weight_and_pack",
    )(flux, exposure_in, background, observed)
    far, near = swap_far(far), swap_near(near)
    counts = neighbours(sent)

    centre, band, edge, fold, background, observed = pl.pallas_call(
        functools.partial(weights_kernel, en),
        in_specs=[SMEM] * 4 + [VMEM] + [ANY] * 2,
        out_specs=[VMEM] * 3 + [SMEM] + [VMEM] * 2,
        out_shape=[
            tiles(block), weights(block), weights(block), jax.ShapeDtypeStruct((5 * (slots + 4),), F32),
            tiles(block), tiles(block),
        ],
        scratch_shapes=[scratch(tiles(block, jnp.int32)), pltpu.SemaphoreType.DMA((2,))],
        compiler_params=params(6),
        cost_estimate=cost(block, 1, block * 2**15),
        name="weights_and_centre",
    )(psf_radius, band_low, band_high, disp_raw, weighted, background, observed)
    sent = pl.pallas_call(
        functools.partial(blur_kernel, en),
        in_specs=[VMEM] * 5,
        out_specs=[VMEM] * dirs,
        out_shape=[tiles(4)] * dirs,
        compiler_params=params(4),
        cost_estimate=cost(4 * dirs, 2),
        name="blur_border",
    )(centre, band, edge, far, near)
    received = neighbours(sent)
    resid, loss, *folded = pl.pallas_call(
        functools.partial(middle_kernel, en),
        in_specs=[SMEM] + [VMEM] * 7,
        out_specs=[VMEM] * 5,
        out_shape=[tiles(block + 4), jax.ShapeDtypeStruct((8, 128), F32), tiles(block), edges(block), edges(block)],
        scratch_shapes=[scratch(tiles(block)), scratch(tiles(block + 4))],
        compiler_params=params(10),
        cost_estimate=cost(block, 2, block * 2**15),
        name="blur_residual_fold",
    )(fold, centre, band, edge, far, near, background, observed)
    back, near, far = folded
    near, far, total, *border = pl.pallas_call(
        functools.partial(border_kernel, en),
        in_specs=[SMEM] + [VMEM] * (6 + 3 * dirs),
        out_specs=[VMEM] * (3 + dirs),
        out_shape=[edges(block), edges(block), lanes] + [tiles(4)] * dirs,
        scratch_shapes=[scratch(tiles(8)), scratch(tiles(4)), scratch(tiles(4)), scratch(tiles(8))],
        compiler_params=params(4),
        cost_estimate=cost(4 * dirs, 1),
        name="border_residual_fold_loss",
    )(fold, background, observed, resid, loss, near, far, *sent, *received, *counts)

    def partners(value, masks):
        return [lax.ppermute(value, ("sky", "en"), [(i, i ^ mask) for i in range(sky * en)]) for mask in masks]

    far, near = swap_far(far), swap_near(near)
    moved = partners(total, [4 * en * k for k in range(1, sky // 4)])
    centre, total = pl.pallas_call(
        functools.partial(centre_kernel, en),
        in_specs=[VMEM] * (3 + dirs),
        out_specs=[VMEM] * 2,
        out_shape=[tiles(block), lanes],
        compiler_params=params(4),
        cost_estimate=cost(block, 1),
        name="back_centre",
    )(back, band, total, *border)
    total = tree_sum([total] + moved)
    moved = partners(total, [k % en ^ (k // en * 3 * en) for k in range(1, 2 * en)])
    grad, total = pl.pallas_call(
        final_kernel,
        in_specs=[VMEM] * 7,
        out_specs=[ANY, VMEM],
        out_shape=[tiles(block), lanes],
        scratch_shapes=[scratch(tiles(block)), scratch(tiles(block)), pltpu.SemaphoreType.DMA((block // 4,))],
        compiler_params=params(8),
        cost_estimate=cost(block, 2),
        name="back_edges_lat_exposure",
    )(centre, band, edge, far, near, exposure, total)
    total = tree_sum([total] + moved)
    total = total + partners(total, [en])[0]
    return grad, total[0, 0] / F32(rows * width * bins * sky)


def solution(mesh):
    placed = (P("en", None, "sky"),) * 4 + (P(),) * 4
    return jax.shard_map(local, mesh=mesh, in_specs=placed, out_specs=(P("en", None, "sky"), P()), check_vma=False)
```
